32 devices in a mesh: batch: 8 (over y, x, core), frames: 4 (over z).
Axes of the slice: x: 2, y: 2, z: 4, core: 2. Of those that a mesh axis runs over, the one named last changes fastest.
Arguments:
- params: float32 [869376], P('batch'), may hold values from -8 to 8
- first_moment: float32 [869376], P('batch'), may hold values from -6.4349833e-06 to 6.4349833e-06
- second_moment: float32 [869376], P('batch'), may hold values from 1.1502503e-12 to 4.601001e-12
- mixture: float32 [16, 2000], P('batch', 'frames'), may hold values from -6 to 6
- sources: float32 [16, 3, 2000], P('batch', None, 'frames'), may hold values from -6 to 6
- speakers: int32 [16], P('batch'), may hold values from 2 to 3
- lengths: int32 [16], P('batch'), may hold values from 500 to 2000, as said below
Outputs:
- new_params: float32 [869376], P('batch')
- half_params: bfloat16 [869376], P('batch')
- new_first: float32 [869376], P('batch')
- new_second: float32 [869376], P('batch')
- grad_norm: float32 [], replicated
- loss_parts: float32 [2], replicated
The draws below stay inside these ranges and needn't reach their ends.
Inputs may be any that keep to these rules, and one draw needn't show every extreme that they name: `lengths`: in each run of 2 items of the same index of batch, one item drawn from the seed has length 2000.
All inputs are finite; a program needn't handle non-finite values.
Results may differ from the reference program's by a relative error of at most 0.001.
Values sent between devices are 32-bit elements; how exact they have to be, the bound alone decides.
A program may use at most 384 MiB of HBM per device.

```python
import math
import jax
import jax.numpy as jnp
from jax import lax

FILTERS = 64
UNITS = 128
HOP = 50
SOURCES = 3
BLOCKS = 2
STEP = 5
ITEMS_DEV = 2
ITEMS = 16
SAMPLES = 2000
PARAMS = 869376


def layout_drawn():
    entries = [('encoder', (FILTERS, 2))]
    for layer_no in range(2 * BLOCKS):
        for side_no in range(2):
            entries += [('input', (FILTERS, 4 * UNITS)), ('recurrent', (UNITS, 4 * UNITS)), ('gate_bias', (4 * UNITS,))]
        entries += [('project', (2 * UNITS, FILTERS)), ('offset', (FILTERS,)), ('gain', (FILTERS,)), ('shift', (FILTERS,))]
    entries += [('masker', (FILTERS, SOURCES * FILTERS)), ('decoder', (FILTERS, 2))]
    return entries


def draw_params(key, part):
    key = jax.random.fold_in(key, 11)
    segments = []
    for number, (kind_name, dims) in enumerate(layout_drawn()):
        length_of = math.prod(dims)
        sub_key = jax.random.fold_in(key, number)
        base = jnp.clip(jax.random.normal(sub_key, (length_of,), jnp.float32), -6.0, 6.0)
        evenly = jax.random.uniform(jax.random.fold_in(sub_key, 1), (length_of,), jnp.float32)
        if kind_name == 'input':
            piece = base / math.sqrt(FILTERS)
        elif kind_name == 'recurrent':
            piece = base / math.sqrt(UNITS)
        elif kind_name == 'gate_bias':
            quarter = length_of // 4
            piece = jnp.concatenate([0.3 * base[:quarter], -1.0 + 5.0 * evenly[quarter:2 * quarter], 0.3 * base[2 * quarter:]])
        elif kind_name == 'project':
            piece = base / math.sqrt(2 * UNITS)
        elif kind_name == 'gain':
            piece = jnp.exp((2.0 * evenly - 1.0) * 0.7)
        elif kind_name == 'masker':
            piece = base / math.sqrt(FILTERS)
        elif kind_name == 'decoder':
            piece = 2.0 * base / math.sqrt(FILTERS)
        elif kind_name == 'encoder':
            piece = base
        else:
            piece = 0.3 * base
        segments.append(piece)
    return jnp.concatenate(segments)


def draw_lengths(key, part):
    key = jax.random.fold_in(key, 7)
    drawn = jax.random.randint(jax.random.fold_in(key, 1), (ITEMS,), SAMPLES // 4, SAMPLES + 1)
    chosen = jax.random.randint(jax.random.fold_in(key, 2), (ITEMS // ITEMS_DEV,), 0, ITEMS_DEV)
    position = jnp.arange(ITEMS) % ITEMS_DEV
    return jnp.where(position == jnp.repeat(chosen, ITEMS_DEV), SAMPLES, drawn).astype(jnp.int32)


def touch_ends(result, stream_key, smallest, largest):
    shape = result.shape
    index_at = [jax.random.randint(jax.random.fold_in(stream_key, axis), (), 0, shape[axis]) for axis in range(len(shape))]
    result = result.at[tuple(index_at)].set(smallest)
    longest = shape.index(max(shape))
    index_at[longest] = (index_at[longest] + 1) % shape[longest]
    return result.at[tuple(index_at)].set(largest)


def block_scale(stream_key, shape, cuts, least, top_value):
    level = 1.0
    for dim, parts in cuts:
        steps = jax.random.uniform(jax.random.fold_in(jax.random.fold_in(stream_key, 6), dim), (parts,), jnp.float32, least / len(cuts), top_value / len(cuts))
        level = level * jnp.repeat(jnp.exp(steps), shape[dim] // parts).reshape((-1,) + (1,) * (len(shape) - 1 - dim))
    return level


def bell_draw(own_key, shape, scale, most, cuts=(), held_as=jnp.bfloat16):
    loudness = block_scale(own_key, shape, cuts, -0.22, 0.18) if cuts else 1.0
    values = jax.random.normal(own_key, shape, jnp.float32) * scale * loudness
    return jnp.minimum(jnp.maximum(values, -most), most).astype(held_as)


def setup_inputs(seed: int = 0) -> dict:
    arg_keys = jax.random.split(jax.random.key(seed), 8)
    params = draw_params(jax.random.fold_in(arg_keys[7], 71), 0)
    first_moment = bell_draw(arg_keys[1], (PARAMS,), (0.001 / PARAMS ** 0.5), 6.434983333747368e-06, ((0, 8),), jnp.float32)
    second_moment = jnp.clip(jnp.exp(math.log(4.6010010038011195e-12) - 1.3862944 * jax.random.uniform(arg_keys[2], (PARAMS,), jnp.float32) ** block_scale(arg_keys[2], (PARAMS,), ((0, 8),), -0.2, 0.2)), 1.1502502509502799e-12, 4.6010010038011195e-12)
    mixture = bell_draw(arg_keys[3], (ITEMS, SAMPLES), 1.0, 6.0, ((0, 8), (1, 4)), jnp.float32)
    sources = bell_draw(arg_keys[4], (ITEMS, SOURCES, SAMPLES), 1.0, 6.0, ((0, 8), (2, 4)), jnp.float32)
    speakers = touch_ends(jax.random.randint(arg_keys[5], (ITEMS,), 2, 4), jax.random.fold_in(arg_keys[5], 1), 2, 3).astype(jnp.int32)
    lengths = draw_lengths(jax.random.fold_in(arg_keys[7], 71), 0)
    return dict(params=params, first_moment=first_moment, second_moment=second_moment, mixture=mixture, sources=sources, speakers=speakers, lengths=lengths)


HIGHEST = lax.Precision.HIGHEST
NORM_EPS = 1e-08
CLIP_AT = 0.001
BETA_ONE = 0.5
BETA_TWO = 0.5
LEARN_RATE = 0.05
DECAY_RATE = 0.01
ADAM_EPS = 1e-08

@jax.custom_vjp
def low(v):
    return lax.optimization_barrier(v.astype(jnp.bfloat16)).astype(jnp.float32)

@jax.custom_vjp
def low_back(v):
    return v

def low_keep(v):
    return (low(v), None)

def low_pass(kept, grad):
    return (grad,)

def back_keep(v):
    return (v, None)

def back_low(kept, grad):
    return (low(grad),)
low.defvjp(low_keep, low_pass)
low_back.defvjp(back_keep, back_low)

def layout():
    entries = [('encoder', (FILTERS, 2))]
    for layer_no in range(2 * BLOCKS):
        for side_no in range(2):
            entries += [('input', (FILTERS, 4 * UNITS)), ('recurrent', (UNITS, 4 * UNITS)), ('gate_bias', (4 * UNITS,))]
        entries += [('project', (2 * UNITS, FILTERS)), ('offset', (FILTERS,)), ('gain', (FILTERS,)), ('shift', (FILTERS,))]
    entries += [('masker', (FILTERS, SOURCES * FILTERS)), ('decoder', (FILTERS, 2))]
    return entries

def unpack(flat):
    pieces = []
    offset_at = 0
    for kind_name, dims in layout():
        length_of = math.prod(dims)
        pieces.append(flat[offset_at:offset_at + length_of].reshape(dims))
        offset_at += length_of
    return pieces

def lstm_pass(inputs, w_in, w_rec, bias, state):
    gates_all = jnp.einsum('tbc,cg->tbg', inputs, w_in, precision=HIGHEST) + bias

    def advance(carry, gates_in):
        hidden_now, cell_now = carry
        gates = gates_in + jnp.dot(hidden_now, w_rec, precision=HIGHEST, preferred_element_type=jnp.float32)
        in_gate, forget, candidate, out_gate = jnp.split(gates, 4, axis=-1)
        cell_now = jax.nn.sigmoid(forget) * cell_now + jax.nn.sigmoid(in_gate) * jnp.tanh(candidate)
        hidden_now = jax.nn.sigmoid(out_gate) * jnp.tanh(cell_now)
        return ((hidden_now, cell_now), hidden_now)
    state, outputs = lax.scan(jax.checkpoint(advance), state, gates_all)
    return (outputs, state)

def bilstm(inputs, weights, fwd_state, bwd_state):
    ahead, fwd_end = lstm_pass(inputs, weights[0], weights[1], weights[2], fwd_state)
    behind, bwd_end = lstm_pass(inputs[::-1], weights[3], weights[4], weights[5], bwd_state)
    return (jnp.concatenate([ahead, behind[::-1]], -1), fwd_end, bwd_end)

def arrange(tensor, across):
    item_count, group_count, width_in, depth_of = tensor.shape
    if across:
        return tensor.transpose(1, 0, 2, 3).reshape(group_count, item_count * width_in, depth_of)
    return tensor.transpose(2, 0, 1, 3).reshape(width_in, item_count * group_count, depth_of)

def unarrange(sequence, dims, across):
    item_count, group_count, width_in = (dims[0], dims[1], dims[2])
    if across:
        return sequence.reshape(group_count, item_count, width_in, -1).transpose(1, 0, 2, 3)
    return sequence.reshape(width_in, item_count, group_count, -1).transpose(1, 2, 0, 3)

def sub_layer(tensor, weights, across):
    sequence = arrange(tensor, across)
    zero_state = jnp.zeros((sequence.shape[1], UNITS), jnp.float32)
    outputs, _, _ = bilstm(sequence, weights[:6], (zero_state, zero_state), (zero_state, zero_state))
    outputs = unarrange(outputs, tensor.shape, across)
    mixed = jnp.einsum('iskh,hc->iskc', outputs, weights[6], precision=HIGHEST) + weights[7]
    mean_of = lax.optimization_barrier(jnp.mean(mixed, axis=(1, 2, 3), keepdims=True))
    spread = lax.optimization_barrier(jnp.mean(mixed * mixed, axis=(1, 2, 3), keepdims=True)) - mean_of * mean_of
    normed = (mixed - mean_of) * lax.rsqrt(spread + NORM_EPS)
    return tensor + weights[8] * normed + weights[9]

def forward(flat, mixture, sources, speakers, lengths):
    pieces = unpack(flat)
    item_count = mixture.shape[0]
    sample_count = mixture.shape[1]
    group_count = sample_count // HOP
    following = jnp.concatenate([mixture[:, 1:], jnp.zeros((item_count, 1), jnp.float32)], 1)
    encoder = pieces[0]
    encoded = jax.nn.softplus(mixture[:, :, None] * encoder[:, 0] + following[:, :, None] * encoder[:, 1])
    padded = jnp.concatenate([encoded, jnp.zeros((item_count, HOP, FILTERS), jnp.float32)], 1)
    padded = padded.reshape(item_count, group_count + 1, HOP, FILTERS)
    tensor = jnp.concatenate([padded[:, :-1], padded[:, 1:]], 2)
    for layer_no in range(2 * BLOCKS):
        tensor = sub_layer(tensor, pieces[1 + 10 * layer_no:11 + 10 * layer_no], layer_no % 2 == 1)
    firsts = tensor[:, :, :HOP]
    seconds = jnp.concatenate([jnp.zeros((item_count, 1, HOP, FILTERS), jnp.float32), tensor[:, :-1, HOP:]], 1)
    summed = (firsts + seconds).reshape(item_count, sample_count, FILTERS)
    logits = jnp.einsum('inc,cm->inm', summed, pieces[-2], precision=HIGHEST).reshape(item_count, sample_count, SOURCES, FILTERS)
    active = (jnp.arange(SOURCES)[None, :] < speakers[:, None]).astype(jnp.float32)
    masked = jax.nn.sigmoid(logits) * active[:, None, :, None] * encoded[:, :, None, :]
    previous = jnp.concatenate([jnp.zeros((item_count, 1, SOURCES, FILTERS), jnp.float32), masked[:, :-1]], 1)
    decoder = pieces[-1]
    estimate = jnp.einsum('injc,c->inj', masked, decoder[:, 0], precision=HIGHEST) + jnp.einsum('injc,c->inj', previous, decoder[:, 1], precision=HIGHEST)
    target = sources.transpose(0, 2, 1) * active[:, None, :]
    valid = (jnp.arange(sample_count)[None, :] < lengths[:, None]).astype(jnp.float32)
    differ = estimate - target
    return jnp.sum(valid[:, :, None] * (jnp.sqrt(differ * differ + 1.0) - 1.0))

def reference(params, first_moment, second_moment, mixture, sources, speakers, lengths):
    loss_sum, pull_back = jax.vjp(lambda flat: forward(flat, mixture, sources, speakers, lengths), params)
    gradient = pull_back(jnp.ones((), loss_sum.dtype))[0]
    count = jnp.sum(lengths).astype(loss_sum.dtype)
    gradient = gradient / count
    grad_norm = jnp.sqrt(jnp.sum(gradient * gradient))
    clipped = gradient * (CLIP_AT / jnp.maximum(grad_norm, CLIP_AT))
    new_first = BETA_ONE * first_moment + (1.0 - BETA_ONE) * clipped
    new_second = BETA_TWO * second_moment + (1.0 - BETA_TWO) * clipped * clipped
    step_size = new_first / (1.0 - BETA_ONE ** STEP) / (jnp.sqrt(new_second / (1.0 - BETA_TWO ** STEP)) + ADAM_EPS)
    new_params = params - LEARN_RATE * (step_size + DECAY_RATE * params)
    return (new_params, new_params.astype(jnp.bfloat16), new_first, new_second, grad_norm, jnp.stack([loss_sum, count]))
```

```python
import functools
import math

import jax
import jax.numpy as jnp
from jax import lax
from jax.experimental import pallas as pl
from jax.experimental.pallas import tpu as pltpu
from jax.sharding import PartitionSpec as P

FILTERS = 64
UNITS = 128
HOP = 50
HALF_PAD = 56
SOURCES = 3
BLOCKS = 2
STEP = 5
GATES = 4 * UNITS

HIGHEST = lax.Precision.HIGHEST
NORM_EPS = 1e-08
CLIP_AT = 0.001
BETA_ONE = 0.5
BETA_TWO = 0.5
LEARN_RATE = 0.05
DECAY_RATE = 0.01
ADAM_EPS = 1e-08
F32 = jnp.float32
BF16 = jnp.bfloat16
VMEM_MAX = 60 * 2**20


def split(a):
    hi = a.astype(BF16)
    return hi, (a - hi.astype(F32)).astype(BF16)


def dot(a, b):
    return jnp.dot(a, b, preferred_element_type=F32)


def dot3(a, w_twice, w_low):
    hi, lo = split(a)
    return dot(jnp.concatenate([hi, lo], 1), w_twice) + dot(hi, w_low)


def dot_rows(a, b):
    return lax.dot_general(a, b, (((0,), (0,)), ((), ())), preferred_element_type=F32)


def dot_rows3(a, b):
    a_hi, a_lo = split(a)
    b_hi, b_lo = split(b)
    return dot_rows(a_hi, b_hi) + dot_rows(a_lo, b_hi) + dot_rows(a_hi, b_lo)


def put_split(w, twice_ref, low_ref):
    hi, lo = split(w)
    twice_ref[...] = jnp.concatenate([hi, hi], 0)
    low_ref[...] = lo


def place(dir_no, chunk_no, count, steps, inter, groups):
    first = jnp.where(dir_no == 0, chunk_no * steps, (count - 1 - chunk_no) * steps)
    if inter:
        return first, 0, 0
    half = first // HOP
    return first, half, pl.multiple_of((first - HOP * half) * groups, 8)


def forward_kernel(inter, first_layer, groups, steps, *refs):
    if first_layer:
        (dir_ref, x_ref, win_ref, wrec_ref, bias_ref, proj_ref,
         h_ref, coef_ref, part_ref,
         wi2, wil, wr2, wrl, pj2, pjl, bias_s, gin, c_s, h_s) = refs
    else:
        (dir_ref, prev_ref, pa_ref, pb_ref, vec_ref, win_ref, wrec_ref, bias_ref, proj_ref,
         x_ref, normed_ref, scale_ref, h_ref, coef_ref, part_ref,
         wi2, wil, wr2, wrl, pj2, pjl, bias_s, gin, c_s, h_s) = refs
    chunk_no = pl.program_id(0)
    count = pl.num_programs(0)
    dir_no = dir_ref[0]
    rows = 2 * HALF_PAD if inter else groups
    valid = HOP * groups

    @pl.when(chunk_no == 0)
    def _():
        column = lax.broadcasted_iota(jnp.int32, (1, GATES), 1)
        scaling = jnp.where((column >= 2 * UNITS) & (column < 3 * UNITS), 1.0, 0.5)
        win = win_ref[...] * scaling
        none = jnp.zeros_like(win)
        for half in range(2):
            put_split(jnp.concatenate([win, none] if half == 0 else [none, win], 0), wi2.at[half], wil.at[half])
        put_split(wrec_ref[...] * scaling, wr2, wrl)
        bias_s[...] = jnp.broadcast_to(bias_ref[...] * scaling, bias_s.shape)
        proj = proj_ref[...]
        none = jnp.zeros_like(proj)
        for half in range(2):
            put_split(jnp.concatenate([proj, none] if half == 0 else [none, proj], 1), pj2.at[half], pjl.at[half])
        c_s[...] = jnp.zeros_like(c_s)
        h_s[...] = jnp.zeros_like(h_s)
        h_ref[0] = jnp.zeros((rows, UNITS), F32)
        h_ref[h_ref.shape[0] - 1] = jnp.zeros((rows, UNITS), F32)
        if not first_layer:
            mixed = pa_ref[:valid] + pb_ref[:valid] + vec_ref[0:1]
            total = 2.0 * valid * FILTERS
            mean = jnp.sum(mixed) / total
            spread = jnp.sum(mixed * mixed) / total - mean * mean
            scale = lax.rsqrt(jnp.full((1, 128), spread + NORM_EPS, F32))
            normed = (mixed - mean) * scale
            normed_ref[:valid] = normed
            x_ref[:valid] = prev_ref[:valid] + vec_ref[1:2] * normed + vec_ref[2:3]
            x_ref[valid:] = jnp.zeros((x_ref.shape[0] - valid, 128), F32)
            normed_ref[valid:] = jnp.zeros((x_ref.shape[0] - valid, 128), F32)
            scale_ref[...] = jnp.broadcast_to(scale, scale_ref.shape)

    first, half, row = place(dir_no, chunk_no, count, steps, inter, groups)
    if inter:
        xs = jnp.concatenate(
            [x_ref[pl.ds(first + u, HALF_PAD, stride=groups), :] for u in range(steps)], 0
        )
        for side in range(2):
            found = dot3(xs, wi2[side], wil[side]) + bias_s[0:1]
            for u in range(steps):
                gin[pl.ds(u * rows + side * HALF_PAD, HALF_PAD)] = found[u * HALF_PAD:(u + 1) * HALF_PAD]
    else:
        xs = x_ref[pl.ds(row, steps * groups), :]
        gin[...] = dot3(xs, wi2[half], wil[half]) + bias_s[0:1]

    h = h_s[...]
    c = c_s[...]
    for u in range(steps):
        v = jnp.where(dir_no == 0, u, steps - 1 - u)
        hi, lo = split(h)
        z = (
            gin[pl.ds(pl.multiple_of(v * rows, 8), rows)]
            + dot(jnp.concatenate([hi, lo], 1), wr2[...])
            + dot(hi, wrl[...])
        )
        th = jnp.tanh(z)
        ti, tf, g, to = (th[:, q * UNITS:(q + 1) * UNITS] for q in range(4))
        i_g = 0.5 * ti + 0.5
        f_g = 0.5 * tf + 0.5
        o_g = 0.5 * to + 0.5
        c_prev = c
        c = f_g * c + i_g * g
        tc = jnp.tanh(c)
        h = o_g * tc
        h_ref[first + v + 1] = h
        coef_ref[u, 0] = tc * (0.25 - 0.25 * to * to)
        coef_ref[u, 1] = o_g * (1.0 - tc * tc)
        coef_ref[u, 2] = g * (0.25 - 0.25 * ti * ti)
        coef_ref[u, 3] = c_prev * (0.25 - 0.25 * tf * tf)
        coef_ref[u, 4] = i_g * (1.0 - g * g)
        coef_ref[u, 5] = f_g
    h_s[...] = h
    c_s[...] = c

    hs = h_ref[pl.ds(first + 1, steps)]
    if inter:
        low_half = hs[:, :HALF_PAD].reshape(steps * HALF_PAD, UNITS)
        top_half = hs[:, HALF_PAD:].reshape(steps * HALF_PAD, UNITS)
        found = dot3(low_half, pj2[0], pjl[0]) + dot3(top_half, pj2[1], pjl[1])
        for u in range(steps):
            part_ref[pl.ds(first + u, HALF_PAD, stride=groups), :] = found[u * HALF_PAD:(u + 1) * HALF_PAD]
    else:
        found = dot3(hs.reshape(steps * groups, UNITS), pj2[half], pjl[half])
        here = pl.ds(row, steps * groups)

        @pl.when(2 * chunk_no < count)
        def _():
            part_ref[here] = found

        @pl.when(2 * chunk_no >= count)
        def _():
            part_ref[here] = part_ref[here] + found


def backward_kernel(inter, last_layer, groups, steps, *refs):
    if last_layer:
        (dir_ref, g_ref, normed_ref, scale_ref, vec_ref, x_ref, h_ref, coef_ref, win_ref, wrec_ref, proj_ref,
         dx_ref, dwin_ref, dwrec_ref, db_ref, dproj_ref, dvec_ref,
         wi2, wil, wrw, wrt, pj2, pjl, dmx, dhc, dzs, dz_s, dc_s, awin, aproj) = refs
    else:
        (dir_ref, res_ref, da_ref, db2_ref, normed_ref, scale_ref, vec_ref, x_ref, h_ref, coef_ref,
         win_ref, wrec_ref, proj_ref,
         g_ref, dx_ref, dwin_ref, dwrec_ref, db_ref, dproj_ref, dvec_ref,
         wi2, wil, wrw, wrt, pj2, pjl, dmx, dhc, dzs, dz_s, dc_s, awin, aproj) = refs
    back_no = pl.program_id(0)
    count = pl.num_programs(0)
    chunk_no = count - 1 - back_no
    dir_no = dir_ref[0]
    rows = 2 * HALF_PAD if inter else groups
    valid = HOP * groups

    @pl.when(back_no == 0)
    def _():
        win_t = win_ref[...].T
        none = jnp.zeros_like(win_t)
        for half in range(2):
            put_split(jnp.concatenate([win_t, none] if half == 0 else [none, win_t], 1), wi2.at[half], wil.at[half])
        hi, lo = split(wrec_ref[...].T)
        wrw[...] = jnp.concatenate([hi, lo], 1)
        wrt[...] = hi
        proj_t = proj_ref[...].T
        none = jnp.zeros_like(proj_t)
        for half in range(2):
            put_split(jnp.concatenate([proj_t, none] if half == 0 else [none, proj_t], 0), pj2.at[half], pjl.at[half])
        dz_s[...] = jnp.zeros_like(dz_s)
        dc_s[...] = jnp.zeros_like(dc_s)
        awin[...] = jnp.zeros_like(awin)
        aproj[...] = jnp.zeros_like(aproj)
        db_ref[...] = jnp.zeros_like(db_ref)
        if not last_layer:
            g_ref[:valid] = res_ref[:valid] + da_ref[:valid] + db2_ref[:valid]
            g_ref[valid:] = jnp.zeros((g_ref.shape[0] - valid, 128), F32)
        g = g_ref[:valid]
        normed = normed_ref[:valid]
        g_n = g * vec_ref[1:2]
        total = 2.0 * valid * FILTERS
        mean_one = jnp.sum(g_n) / total
        mean_two = jnp.sum(g_n * normed) / total
        dmixed = scale_ref[0:1] * (g_n - mean_one - normed * mean_two)
        dmx[:valid] = dmixed
        dmx[valid:] = jnp.zeros((dmx.shape[0] - valid, 128), F32)
        dvec_ref[...] = jnp.zeros_like(dvec_ref)
        dvec_ref[0:1] = jnp.sum(dmixed, 0, keepdims=True)
        dvec_ref[1:2] = jnp.sum(g * normed, 0, keepdims=True)
        dvec_ref[2:3] = jnp.sum(g, 0, keepdims=True)

    first, half, row = place(dir_no, chunk_no, count, steps, inter, groups)
    here = pl.ds(row, steps * groups)
    if inter:
        dms = jnp.concatenate(
            [dmx[pl.ds(first + u, HALF_PAD, stride=groups), :] for u in range(steps)], 0
        )
        for side in range(2):
            found = dot3(dms, pj2[side], pjl[side])
            for u in range(steps):
                dhc[pl.ds(u * rows + side * HALF_PAD, HALF_PAD)] = found[u * HALF_PAD:(u + 1) * HALF_PAD]
    else:
        dms = dmx[here, :]
        dhc[...] = dot3(dms, pj2[half], pjl[half])

    dz = dz_s[...]
    dc_next = dc_s[...]
    for u in reversed(range(steps)):
        v = jnp.where(dir_no == 0, u, steps - 1 - u)
        hi, lo = split(dz)
        wide = dot(hi, wrw[...])
        dh = (
            dhc[pl.ds(pl.multiple_of(v * rows, 8), rows)]
            + wide[:, :UNITS] + wide[:, UNITS:] + dot(lo, wrt[...])
        )
        dc = dh * coef_ref[u, 1] + dc_next
        dz = jnp.concatenate(
            [dc * coef_ref[u, 2], dc * coef_ref[u, 3], dc * coef_ref[u, 4], dh * coef_ref[u, 0]], 1
        )
        dc_next = dc * coef_ref[u, 5]
        if inter:
            dzs[0, pl.ds(pl.multiple_of(v * HALF_PAD, 8), HALF_PAD)] = dz[:HALF_PAD]
            dzs[1, pl.ds(pl.multiple_of(v * HALF_PAD, 8), HALF_PAD)] = dz[HALF_PAD:]
        else:
            dzs[0, pl.ds(pl.multiple_of(v * rows, 8), rows)] = dz
    dz_s[...] = dz
    dc_s[...] = dc_next

    hs = h_ref[pl.ds(first + 1, steps)]
    hp = h_ref[pl.ds(first + 2 * dir_no, steps)]
    if inter:
        xs = jnp.concatenate(
            [x_ref[pl.ds(first + u, HALF_PAD, stride=groups), :] for u in range(steps)], 0
        )
        found = 0.0
        for side in range(2):
            cut = slice(side * HALF_PAD, (side + 1) * HALF_PAD)
            dzc = dzs[side]
            found = found + dot3(dzc, wi2[side], wil[side])
            turned = xs if side == 0 else pltpu.roll(xs, FILTERS, 1)
            awin[...] += dot_rows3(
                jnp.concatenate([turned, hp[:, cut].reshape(steps * HALF_PAD, UNITS)], 1), dzc
            )
            aproj[side] += dot_rows3(hs[:, cut].reshape(steps * HALF_PAD, UNITS), dms)
            db_ref[0:1] += jnp.sum(dzc, 0, keepdims=True)
        for u in range(steps):
            dx_ref[pl.ds(first + u, HALF_PAD, stride=groups), :] = found[u * HALF_PAD:(u + 1) * HALF_PAD]
    else:
        xs = x_ref[here, :]
        dzc = dzs[0]
        turned = jnp.where(half == 0, xs, pltpu.roll(xs, FILTERS, 1))
        awin[...] += dot_rows3(jnp.concatenate([turned, hp.reshape(steps * groups, UNITS)], 1), dzc)
        aproj[half] += dot_rows3(hs.reshape(steps * groups, UNITS), dms)
        db_ref[0:1] += jnp.sum(dzc, 0, keepdims=True)
        found = dot3(dzc, wi2[half], wil[half])

        @pl.when(2 * back_no < count)
        def _():
            dx_ref[here] = found

        @pl.when(2 * back_no >= count)
        def _():
            dx_ref[here] = dx_ref[here] + found

    @pl.when(back_no == count - 1)
    def _():
        dwin_ref[...] = awin[:FILTERS]
        dwrec_ref[...] = awin[2 * FILTERS:]
        dproj_ref[...] = aproj[0, :, :FILTERS] + aproj[1, :, FILTERS:]


def sizes(inter, groups):
    if inter:
        return groups, 2 * HALF_PAD, 8
    return 2 * HOP, groups, 10


def whole(shape):
    return pl.BlockSpec(shape, lambda j: (0,) * len(shape))


def run_forward(layer_no, groups, dir_no, stream, weights):
    inter = layer_no % 2 == 1
    first_layer = layer_no == 0
    length, rows, steps = sizes(inter, groups)
    stream_shape = (HALF_PAD * groups, 128)
    count = length // steps
    coef_block = (steps, 6, rows, UNITS)
    out = [
        ((length + 2, rows, UNITS), whole((length + 2, rows, UNITS))),
        ((length, 6, rows, UNITS), pl.BlockSpec(coef_block, lambda j: (j, 0, 0, 0))),
        (stream_shape, whole(stream_shape)),
    ]
    if not first_layer:
        out = [(stream_shape, whole(stream_shape)), (stream_shape, whole(stream_shape)), ((8, 128), whole((8, 128)))] + out
    operands = list(stream) + list(weights)
    gin_rows = steps * rows
    return pl.pallas_call(
        functools.partial(forward_kernel, inter, first_layer, groups, steps),
        grid=(count,),
        in_specs=[pl.BlockSpec(memory_space=pltpu.SMEM)] + [whole(a.shape) for a in operands],
        out_specs=[spec for _, spec in out],
        out_shape=[jax.ShapeDtypeStruct(shape, F32) for shape, _ in out],
        scratch_shapes=[
            pltpu.VMEM((2, 256, GATES), BF16), pltpu.VMEM((2, 128, GATES), BF16),
            pltpu.VMEM((256, GATES), BF16), pltpu.VMEM((128, GATES), BF16),
            pltpu.VMEM((2, 256, 128), BF16), pltpu.VMEM((2, 128, 128), BF16),
            pltpu.VMEM((8, GATES), F32), pltpu.VMEM((gin_rows, GATES), F32),
            pltpu.VMEM((rows, UNITS), F32), pltpu.VMEM((rows, UNITS), F32),
        ],
        compiler_params=pltpu.CompilerParams(vmem_limit_bytes=VMEM_MAX),
        name="forward_inter" if inter else "forward_intra",
    )(dir_no, *operands)


def run_backward(layer_no, groups, dir_no, grads, normed, scale, vec, x, h_all, coef, weights):
    inter = layer_no % 2 == 1
    last_layer = layer_no == 2 * BLOCKS - 1
    length, rows, steps = sizes(inter, groups)
    stream_shape = (HALF_PAD * groups, 128)
    count = length // steps
    coef_block = (steps, 6, rows, UNITS)
    out = [stream_shape, (FILTERS, GATES), (UNITS, GATES), (8, GATES), (UNITS, FILTERS), (8, 128)]
    if not last_layer:
        out = [stream_shape] + out
    before = list(grads) + [normed, scale, vec, x, h_all]
    return pl.pallas_call(
        functools.partial(backward_kernel, inter, last_layer, groups, steps),
        grid=(count,),
        in_specs=[pl.BlockSpec(memory_space=pltpu.SMEM)]
        + [whole(a.shape) for a in before]
        + [pl.BlockSpec(coef_block, lambda j: (count - 1 - j, 0, 0, 0))]
        + [whole(a.shape) for a in weights],
        out_specs=[whole(shape) for shape in out],
        out_shape=[jax.ShapeDtypeStruct(shape, F32) for shape in out],
        scratch_shapes=[
            pltpu.VMEM((2, 2 * GATES, 128), BF16), pltpu.VMEM((2, GATES, 128), BF16),
            pltpu.VMEM((GATES, 256), BF16), pltpu.VMEM((GATES, 128), BF16),
            pltpu.VMEM((2, 256, 128), BF16), pltpu.VMEM((2, 128, 128), BF16),
            pltpu.VMEM(stream_shape, F32), pltpu.VMEM((steps * rows, UNITS), F32),
            pltpu.VMEM((2, steps * HALF_PAD, GATES) if inter else (1, steps * rows, GATES), F32),
            pltpu.VMEM((rows, GATES), F32), pltpu.VMEM((rows, UNITS), F32),
            pltpu.VMEM((256, GATES), F32), pltpu.VMEM((2, UNITS, 128), F32),
        ],
        compiler_params=pltpu.CompilerParams(vmem_limit_bytes=VMEM_MAX),
        name="backward_inter" if inter else "backward_intra",
    )(dir_no, *before, coef, *weights)


def layout():
    entries = [("encoder", (FILTERS, 2))]
    for layer_no in range(2 * BLOCKS):
        for side_no in range(2):
            entries += [
                ("input", (FILTERS, 4 * UNITS)),
                ("recurrent", (UNITS, 4 * UNITS)),
                ("gate_bias", (4 * UNITS,)),
            ]
        entries += [
            ("project", (2 * UNITS, FILTERS)),
            ("offset", (FILTERS,)),
            ("gain", (FILTERS,)),
            ("shift", (FILTERS,)),
        ]
    entries += [("masker", (FILTERS, SOURCES * FILTERS)), ("decoder", (FILTERS, 2))]
    return entries


SIDE = FILTERS * GATES + UNITS * GATES + GATES
LAYER = 2 * SIDE + 2 * UNITS * FILTERS + 3 * FILTERS


def layer_weights(flat, layer_no, dir_no):
    start = 2 * FILTERS + LAYER * layer_no
    mine = lax.dynamic_slice(flat, (start + SIDE * dir_no,), (SIDE,))
    cut = FILTERS * GATES
    win = mine[:cut].reshape(FILTERS, GATES)
    wrec = mine[cut:cut + UNITS * GATES].reshape(UNITS, GATES)
    bias = mine[cut + UNITS * GATES:].reshape(1, GATES)
    at = start + 2 * SIDE
    proj = lax.dynamic_slice(flat, (at + UNITS * FILTERS * dir_no,), (UNITS * FILTERS,)).reshape(UNITS, FILTERS)
    at += 2 * UNITS * FILTERS
    vec = flat[at:at + 3 * FILTERS].reshape(3, FILTERS)
    vec = jnp.pad(jnp.concatenate([vec, vec], 1), ((0, 5), (0, 0)))
    return win, wrec, bias, proj, vec


def local(params, first_moment, second_moment, mixture, sources, speakers, lengths):
    flat = lax.all_gather(params, "batch", axis=0, tiled=True)
    items = mixture.shape[0]
    frames_size = lax.axis_size("frames")
    samples = mixture.shape[1] * frames_size
    groups = samples // HOP
    core = lax.axis_index("batch") % 2
    depth = lax.axis_index("frames")
    column = 2 * items
    copies = frames_size // column
    mine = depth // copies
    weight = jnp.where(depth % copies == 0, 1.0, 0.0).astype(F32)
    pairs = [[2 * b, 2 * b + 1] for b in range(lax.axis_size("batch") // 2)]
    swap = [(b, b + 1 if b % 2 == 0 else b - 1) for b in range(lax.axis_size("batch"))]

    signals = jnp.concatenate([mixture[:, None], sources], 1)
    signals = lax.all_gather(signals, "frames", axis=2, tiled=True)
    scalars = jnp.stack([speakers, lengths], 1).astype(F32)
    signals = lax.all_gather(signals, "batch", axis=0, tiled=True, axis_index_groups=pairs)
    scalars = lax.all_gather(scalars, "batch", axis=0, tiled=True, axis_index_groups=pairs)
    signal = lax.dynamic_slice_in_dim(signals, mine, 1, 0)[0]
    scalar = lax.dynamic_slice_in_dim(scalars, mine, 1, 0)[0]
    mix = signal[0]
    following = jnp.concatenate([mix[1:], jnp.zeros((1,), F32)])

    def by_row(array):
        return array.reshape(array.shape[:-1] + (groups, HOP)).swapaxes(-1, -2).reshape(array.shape[:-1] + (groups * HOP,))

    mix_row = by_row(mix)
    follow_row = by_row(following)
    encoder = flat[:2 * FILTERS].reshape(FILTERS, 2)
    raw = mix_row[:, None] * encoder[:, 0] + follow_row[:, None] * encoder[:, 1]
    encoded = jax.nn.softplus(raw)

    def later(array):
        three = array.reshape(HOP, groups, -1)
        return jnp.concatenate([three[:, 1:], jnp.zeros_like(three[:, :1])], 1).reshape(array.shape)

    def earlier(array):
        three = array.reshape(HOP, groups, -1)
        return jnp.concatenate([jnp.zeros_like(three[:, :1]), three[:, :-1]], 1).reshape(array.shape)

    pad = ((0, (HALF_PAD - HOP) * groups), (0, 0))
    stream = jnp.pad(jnp.concatenate([encoded, later(encoded)], 1), pad)
    dir_no = core.reshape(1).astype(jnp.int32)

    def exchange(array):
        return lax.ppermute(array, "batch", swap)

    kept = []
    weights = []
    below = (stream,)
    for layer_no in range(2 * BLOCKS):
        *lstm, vec = layer_weights(flat, layer_no, core)
        found = run_forward(layer_no, groups, dir_no, below, lstm)
        if layer_no == 0:
            x = stream
        else:
            x, normed, scale = found[:3]
            kept[-1] += [normed, scale]
        h_all, coef, part = found[-3:]
        kept.append([x, h_all, coef])
        weights.append((lstm, vec))
        below = (x, part, exchange(part), vec)

    prev, pa, pb, vec = below
    valid_rows = HOP * groups
    mixed = (pa + pb + vec[0:1])[:valid_rows]
    total = 2.0 * valid_rows * FILTERS
    mean = jnp.sum(mixed) / total
    spread = jnp.sum(mixed * mixed) / total - mean * mean
    scale = lax.rsqrt(spread + NORM_EPS)
    normed = (mixed - mean) * scale
    separated = prev[:valid_rows] + vec[1:2] * normed + vec[2:3]
    kept[-1] += [jnp.pad(normed, pad), jnp.full((8, 128), scale, F32)]

    position = by_row(jnp.arange(samples).astype(F32))
    valid = jnp.where(position < scalar[1], 1.0, 0.0) * weight
    active = jnp.where(jnp.arange(SOURCES).astype(F32) < scalar[0], 1.0, 0.0)
    target = by_row(signal[1:]) * active[:, None]
    tail = FILTERS * SOURCES * FILTERS
    masker = flat[-tail - 2 * FILTERS:-2 * FILTERS].reshape(FILTERS, SOURCES * FILTERS)
    decoder = flat[-2 * FILTERS:].reshape(FILTERS, 2)

    def previous_frame(array):
        three = array.reshape(HOP, groups, -1)
        top = jnp.concatenate([jnp.zeros_like(three[-1:, :1]), three[-1:, :-1]], 1)
        return jnp.concatenate([top, three[:-1]], 0).reshape(array.shape)

    def head(masker, decoder, separated, encoded):
        summed = separated[:, :FILTERS] + earlier(separated[:, FILTERS:])
        logits = jnp.dot(summed, masker, precision=HIGHEST).reshape(-1, SOURCES, FILTERS)
        masked = jax.nn.sigmoid(logits) * active[:, None] * encoded[:, None, :]
        previous = previous_frame(masked)
        estimate = jnp.einsum("njc,c->nj", masked, decoder[:, 0], precision=HIGHEST) + jnp.einsum(
            "njc,c->nj", previous, decoder[:, 1], precision=HIGHEST
        )
        differ = estimate - target.T
        return jnp.sum(valid[:, None] * (jnp.sqrt(differ * differ + 1.0) - 1.0))

    loss_local, (grad_masker, grad_decoder, grad, grad_encoded) = jax.value_and_grad(head, (0, 1, 2, 3))(
        masker, decoder, separated, encoded
    )
    grads = (jnp.pad(grad, pad),)
    layer_grads = [None] * (2 * BLOCKS)
    lead = jnp.where(core == 0, 1.0, 0.0).astype(F32)
    sides = jnp.stack([lead, 1.0 - lead])
    for layer_no in reversed(range(2 * BLOCKS)):
        lstm, vec = weights[layer_no]
        x, h_all, coef, normed, scale = kept[layer_no]
        win, wrec, _, proj = lstm
        found = run_backward(layer_no, groups, dir_no, grads, normed, scale, vec, x, h_all, coef, (win, wrec, proj))
        g = found[0] if len(found) == 7 else grads[0]
        dx, dwin, dwrec, db, dproj, dvec = found[-6:]
        side = jnp.concatenate([dwin.reshape(-1), dwrec.reshape(-1), db[0]])
        folded = dvec[:3, :FILTERS] + dvec[:3, FILTERS:]
        layer_grads[layer_no] = jnp.concatenate(
            [(sides[:, None] * side).reshape(-1), (sides[:, None] * dproj.reshape(-1)).reshape(-1), lead * folded.reshape(-1)]
        )
        if layer_no:
            grads = (g, dx, exchange(dx))
    grad_groups = (lead * g + dx)[:valid_rows]
    grad_enc = grad_groups[:, :FILTERS] + earlier(grad_groups[:, FILTERS:]) + lead * grad_encoded
    grad_raw = grad_enc * jax.nn.sigmoid(raw)
    grad_encoder = jnp.stack(
        [jnp.sum(grad_raw * mix_row[:, None], 0), jnp.sum(grad_raw * follow_row[:, None], 0)], 1
    )
    gradient = jnp.concatenate(
        [grad_encoder.reshape(-1)] + layer_grads + [lead * grad_masker.reshape(-1), lead * grad_decoder.reshape(-1)]
    )
    loss_sum, count = lax.psum(
        (loss_local * lead, jnp.sum(lengths).astype(F32) / frames_size), ("batch", "frames")
    )
    shard = lax.psum_scatter(gradient, "batch", scatter_dimension=0, tiled=True)
    shard = lax.psum(shard, "frames") / count
    grad_norm = jnp.sqrt(lax.psum(jnp.sum(shard * shard), "batch"))
    clipped = shard * (CLIP_AT / jnp.maximum(grad_norm, CLIP_AT))
    new_first = BETA_ONE * first_moment + (1.0 - BETA_ONE) * clipped
    new_second = BETA_TWO * second_moment + (1.0 - BETA_TWO) * clipped * clipped
    step_size = (
        new_first / (1.0 - BETA_ONE**STEP) / (jnp.sqrt(new_second / (1.0 - BETA_TWO**STEP)) + ADAM_EPS)
    )
    new_params = params - LEARN_RATE * (step_size + DECAY_RATE * params)
    return (
        new_params,
        new_params.astype(BF16),
        new_first,
        new_second,
        grad_norm,
        jnp.stack([loss_sum, count]),
    )


def solution(mesh):
    placed = (
        P("batch"),
        P("batch"),
        P("batch"),
        P("batch", "frames"),
        P("batch", None, "frames"),
        P("batch"),
        P("batch"),
    )
    return jax.shard_map(
        local,
        mesh=mesh,
        in_specs=placed,
        out_specs=(P("batch"), P("batch"), P("batch"), P("batch"), P(), P()),
        check_vma=False,
    )
```

```python
import functools
import math

import jax
import jax.numpy as jnp
from jax import lax
from jax.experimental import pallas as pl
from jax.experimental.pallas import tpu as pltpu
from jax.sharding import PartitionSpec as P

FILTERS = 64
UNITS = 128
HOP = 50
HALF_PAD = 56
SOURCES = 3
BLOCKS = 2
STEP = 5
GATES = 4 * UNITS

HIGHEST = lax.Precision.HIGHEST
NORM_EPS = 1e-08
CLIP_AT = 0.001
BETA_ONE = 0.5
BETA_TWO = 0.5
LEARN_RATE = 0.05
DECAY_RATE = 0.01
ADAM_EPS = 1e-08
F32 = jnp.float32
BF16 = jnp.bfloat16
VMEM_MAX = 60 * 2**20


def split(a):
    hi = a.astype(BF16)
    return hi, (a - hi.astype(F32)).astype(BF16)


def dot(a, b):
    return jnp.dot(a, b, preferred_element_type=F32)


def dot3(a, w_twice, w_low):
    hi, lo = split(a)
    return dot(jnp.concatenate([hi, lo], 1), w_twice) + dot(hi, w_low)


def dot_rows(a, b):
    return lax.dot_general(a, b, (((0,), (0,)), ((), ())), preferred_element_type=F32)


def dot_rows3(a, b):
    a_hi, a_lo = split(a)
    b_hi, b_lo = split(b)
    return dot_rows(a_hi, b_hi) + dot_rows(a_lo, b_hi) + dot_rows(a_hi, b_lo)


SIDE_ROWS = 772
PROJ_ROWS = 2 * SIDE_ROWS
VEC_ROW = PROJ_ROWS + 128
LAYER_ROWS = 1680
HEAD_ROWS = 160
WINDOW = 1688


def window(layer_no):
    at = 2 + 3347 * layer_no
    return at // 16 * 8, at // 2 % 8, at % 2


def pick(ref, base, odd, start, count, stride=1):
    def load(at):
        return ref[pl.ds(at, count, stride=stride), :] if stride > 1 else ref[pl.ds(at, count), :]

    first = load(base + start)
    if not odd:
        return first
    return jnp.concatenate([first[:, 64:], load(base + start + 1)[:, :64]], 1)


def load_weights(ref, base, odd, dir_no, proj_s):
    at = SIDE_ROWS * dir_no
    win = jnp.concatenate([pick(ref, base, odd, at + q, FILTERS, 4) for q in range(4)], 1)
    wrec = jnp.concatenate([pick(ref, base, odd, at + 256 + q, UNITS, 4) for q in range(4)], 1)
    bias = jnp.concatenate([pick(ref, base, odd, at + 768 + q, 1) for q in range(4)], 1)
    pairs = pick(ref, base, odd, PROJ_ROWS + 64 * dir_no, 64)
    proj_s[pl.ds(0, 64, stride=2), :] = pairs
    proj_s[pl.ds(1, 64, stride=2), :] = pltpu.roll(pairs, 64, 1)
    return win, wrec, bias, proj_s[:, :FILTERS]


def load_vec(ref, base, odd):
    first = pick(ref, base, odd, VEC_ROW, 1)
    turned = pltpu.roll(jnp.broadcast_to(first, (8, 128)), 64, 1)[0:1]
    if odd:
        last = ref[base + VEC_ROW + 1:base + VEC_ROW + 2, :]
        last = jnp.concatenate([last[:, 64:], last[:, 64:]], 1)
    else:
        last = ref[base + VEC_ROW + 1:base + VEC_ROW + 2, :]
        last = jnp.concatenate([last[:, :64], last[:, :64]], 1)
    low = lax.broadcasted_iota(jnp.int32, (1, 128), 1) < 64
    return jnp.where(low, first, turned), jnp.where(low, turned, first), last


def put_split(w, twice_ref, low_ref):
    hi, lo = split(w)
    twice_ref[...] = jnp.concatenate([hi, hi], 0)
    low_ref[...] = lo


def place(dir_no, chunk_no, count, steps, inter, groups):
    first = jnp.where(dir_no == 0, chunk_no * steps, (count - 1 - chunk_no) * steps)
    if inter:
        return first, 0, 0
    half = first // HOP
    return first, half, pl.multiple_of((first - HOP * half) * groups, 8)


def norm_stage(prev_ref, pa_ref, pb_ref, flat_ref, base, odd, valid, normed_ref, scale_ref, x_ref):
    offset, gain, shift = load_vec(flat_ref, base, odd)
    mixed = pa_ref[:valid] + pb_ref[:valid] + offset
    total = 2.0 * valid * FILTERS
    mean = jnp.sum(mixed) / total
    spread = jnp.sum(mixed * mixed) / total - mean * mean
    scale = lax.rsqrt(jnp.full((1, 128), spread + NORM_EPS, F32))
    normed = (mixed - mean) * scale
    normed_ref[:valid] = normed
    normed_ref[valid:] = jnp.zeros((normed_ref.shape[0] - valid, 128), F32)
    x_ref[:valid] = prev_ref[:valid] + gain * normed + shift
    x_ref[valid:] = jnp.zeros((x_ref.shape[0] - valid, 128), F32)
    scale_ref[...] = jnp.broadcast_to(scale, scale_ref.shape)


def forward_kernel(layer_no, groups, steps, *refs):
    inter = layer_no % 2 == 1
    first_layer = layer_no == 0
    if first_layer:
        (dir_ref, x_ref, flat_ref,
         h_ref, coef_ref, part_ref,
         wi2, wil, wr2, wrl, pj2, pjl, proj_s, bias_s, gin, c_s, h_s) = refs
    else:
        (dir_ref, prev_ref, pa_ref, pb_ref, below_ref, flat_ref,
         x_ref, normed_ref, scale_ref, h_ref, coef_ref, part_ref,
         wi2, wil, wr2, wrl, pj2, pjl, proj_s, bias_s, gin, c_s, h_s) = refs
    chunk_no = pl.program_id(0)
    count = pl.num_programs(0)
    dir_no = dir_ref[0]
    rows = 2 * HALF_PAD if inter else groups
    valid = HOP * groups

    @pl.when(chunk_no == 0)
    def _():
        column = lax.broadcasted_iota(jnp.int32, (1, GATES), 1)
        scaling = jnp.where((column >= 2 * UNITS) & (column < 3 * UNITS), 1.0, 0.5)
        _, base, odd = window(layer_no)
        win, wrec, bias, proj = load_weights(flat_ref, base, odd, dir_no, proj_s)
        win = win * scaling
        none = jnp.zeros_like(win)
        for half in range(2):
            put_split(jnp.concatenate([win, none] if half == 0 else [none, win], 0), wi2.at[half], wil.at[half])
        put_split(wrec * scaling, wr2, wrl)
        bias_s[...] = jnp.broadcast_to(bias * scaling, bias_s.shape)
        none = jnp.zeros_like(proj)
        for half in range(2):
            put_split(jnp.concatenate([proj, none] if half == 0 else [none, proj], 1), pj2.at[half], pjl.at[half])
        c_s[...] = jnp.zeros_like(c_s)
        h_s[...] = jnp.zeros_like(h_s)
        h_ref[0] = jnp.zeros((rows, UNITS), F32)
        h_ref[h_ref.shape[0] - 1] = jnp.zeros((rows, UNITS), F32)
        if not first_layer:
            _, below_base, below_odd = window(layer_no - 1)
            norm_stage(
                prev_ref, pa_ref, pb_ref, below_ref, below_base, below_odd, valid, normed_ref, scale_ref, x_ref
            )

    first, half, row = place(dir_no, chunk_no, count, steps, inter, groups)
    if inter:
        xs = jnp.concatenate(
            [x_ref[pl.ds(first + u, HALF_PAD, stride=groups), :] for u in range(steps)], 0
        )
        for side in range(2):
            found = dot3(xs, wi2[side], wil[side]) + bias_s[0:1]
            for u in range(steps):
                gin[pl.ds(u * rows + side * HALF_PAD, HALF_PAD)] = found[u * HALF_PAD:(u + 1) * HALF_PAD]
    else:
        xs = x_ref[pl.ds(row, steps * groups), :]
        gin[...] = dot3(xs, wi2[half], wil[half]) + bias_s[0:1]

    h = h_s[...]
    c = c_s[...]
    for u in range(steps):
        v = jnp.where(dir_no == 0, u, steps - 1 - u)
        hi, lo = split(h)
        z = (
            gin[pl.ds(pl.multiple_of(v * rows, 8), rows)]
            + dot(jnp.concatenate([hi, lo], 1), wr2[...])
            + dot(hi, wrl[...])
        )
        th = jnp.tanh(z)
        ti, tf, g, to = (th[:, q * UNITS:(q + 1) * UNITS] for q in range(4))
        i_g = 0.5 * ti + 0.5
        f_g = 0.5 * tf + 0.5
        o_g = 0.5 * to + 0.5
        c_prev = c
        c = f_g * c + i_g * g
        tc = jnp.tanh(c)
        h = o_g * tc
        h_ref[first + v + 1] = h
        coef_ref[u, 0] = tc * (0.25 - 0.25 * to * to)
        coef_ref[u, 1] = o_g * (1.0 - tc * tc)
        coef_ref[u, 2] = g * (0.25 - 0.25 * ti * ti)
        coef_ref[u, 3] = c_prev * (0.25 - 0.25 * tf * tf)
        coef_ref[u, 4] = i_g * (1.0 - g * g)
        coef_ref[u, 5] = f_g
    h_s[...] = h
    c_s[...] = c

    hs = h_ref[pl.ds(first + 1, steps)]
    if inter:
        low_half = hs[:, :HALF_PAD].reshape(steps * HALF_PAD, UNITS)
        top_half = hs[:, HALF_PAD:].reshape(steps * HALF_PAD, UNITS)
        found = dot3(low_half, pj2[0], pjl[0]) + dot3(top_half, pj2[1], pjl[1])
        for u in range(steps):
            part_ref[pl.ds(first + u, HALF_PAD, stride=groups), :] = found[u * HALF_PAD:(u + 1) * HALF_PAD]
    else:
        found = dot3(hs.reshape(steps * groups, UNITS), pj2[half], pjl[half])
        here = pl.ds(row, steps * groups)

        @pl.when(2 * chunk_no < count)
        def _():
            part_ref[here] = found

        @pl.when(2 * chunk_no >= count)
        def _():
            part_ref[here] = part_ref[here] + found


def backward_kernel(layer_no, groups, steps, *refs):
    inter = layer_no % 2 == 1
    last_layer = layer_no == 2 * BLOCKS - 1
    if last_layer:
        (dir_ref, g_ref, hg_ref, normed_ref, scale_ref, x_ref, h_ref, coef_ref, flat_ref,
         dx_ref, grad_ref,
         wi2, wil, wrw, wrt, pj2, pjl, proj_s, dmx, dhc, dzs, dz_s, dc_s, awin, aproj, abias) = refs
    elif layer_no:
        (dir_ref, res_ref, da_ref, db2_ref, normed_ref, scale_ref, x_ref, h_ref, coef_ref, flat_ref,
         g_ref, dx_ref, grad_ref,
         wi2, wil, wrw, wrt, pj2, pjl, proj_s, dmx, dhc, dzs, dz_s, dc_s, awin, aproj, abias) = refs
    else:
        (dir_ref, res_ref, da_ref, db2_ref, column_ref, denc_ref, encoder_ref, loss_ref,
         normed_ref, scale_ref, x_ref, h_ref, coef_ref, flat_ref,
         grad_ref,
         wi2, wil, wrw, wrt, pj2, pjl, proj_s, dmx, dhc, dzs, dz_s, dc_s, awin, aproj, abias, g_ref, dx_ref) = refs
    back_no = pl.program_id(0)
    count = pl.num_programs(0)
    chunk_no = count - 1 - back_no
    dir_no = dir_ref[0]
    rows = 2 * HALF_PAD if inter else groups
    valid = HOP * groups

    @pl.when(back_no == 0)
    def _():
        _, base, odd = window(layer_no)
        win, wrec, _, proj = load_weights(flat_ref, base, odd, dir_no, proj_s)
        win_t = win.T
        none = jnp.zeros_like(win_t)
        for half in range(2):
            put_split(jnp.concatenate([win_t, none] if half == 0 else [none, win_t], 1), wi2.at[half], wil.at[half])
        hi, lo = split(wrec.T)
        wrw[...] = jnp.concatenate([hi, lo], 1)
        wrt[...] = hi
        proj_t = proj.T
        none = jnp.zeros_like(proj_t)
        for half in range(2):
            put_split(jnp.concatenate([proj_t, none] if half == 0 else [none, proj_t], 0), pj2.at[half], pjl.at[half])
        dz_s[...] = jnp.zeros_like(dz_s)
        dc_s[...] = jnp.zeros_like(dc_s)
        awin[...] = jnp.zeros_like(awin)
        aproj[...] = jnp.zeros_like(aproj)
        abias[...] = jnp.zeros_like(abias)
        grad_ref[...] = jnp.zeros_like(grad_ref)
        if not last_layer:
            g_ref[:valid] = res_ref[:valid] + da_ref[:valid] + db2_ref[:valid]
            g_ref[valid:] = jnp.zeros((g_ref.shape[0] - valid, 128), F32)
        g = g_ref[:valid]
        normed = normed_ref[:valid]
        _, gain, _ = load_vec(flat_ref, base, odd)
        g_n = g * gain
        total = 2.0 * valid * FILTERS
        mean_one = jnp.sum(g_n) / total
        mean_two = jnp.sum(g_n * normed) / total
        dmixed = scale_ref[0:1] * (g_n - mean_one - normed * mean_two)
        dmx[:valid] = dmixed
        dmx[valid:] = jnp.zeros((dmx.shape[0] - valid, 128), F32)
        lead = jnp.where(dir_no == 0, 1.0, 0.0)

        def fold(array):
            found = lead * jnp.sum(array, 0, keepdims=True)
            return found[:, :FILTERS] + found[:, FILTERS:]

        grad_ref[VEC_ROW:VEC_ROW + 1] = jnp.concatenate([fold(dmixed), fold(g * normed)], 1)
        grad_ref[VEC_ROW + 1:VEC_ROW + 2] = jnp.concatenate([fold(g), jnp.zeros((1, FILTERS), F32)], 1)
        if last_layer:
            grad_ref[LAYER_ROWS:] = hg_ref[...] * lead

    first, half, row = place(dir_no, chunk_no, count, steps, inter, groups)
    here = pl.ds(row, steps * groups)
    if inter:
        dms = jnp.concatenate(
            [dmx[pl.ds(first + u, HALF_PAD, stride=groups), :] for u in range(steps)], 0
        )
        for side in range(2):
            found = dot3(dms, pj2[side], pjl[side])
            for u in range(steps):
                dhc[pl.ds(u * rows + side * HALF_PAD, HALF_PAD)] = found[u * HALF_PAD:(u + 1) * HALF_PAD]
    else:
        dms = dmx[here, :]
        dhc[...] = dot3(dms, pj2[half], pjl[half])

    dz = dz_s[...]
    dc_next = dc_s[...]
    for u in reversed(range(steps)):
        v = jnp.where(dir_no == 0, u, steps - 1 - u)
        hi, lo = split(dz)
        wide = dot(hi, wrw[...])
        dh = (
            dhc[pl.ds(pl.multiple_of(v * rows, 8), rows)]
            + wide[:, :UNITS] + wide[:, UNITS:] + dot(lo, wrt[...])
        )
        dc = dh * coef_ref[u, 1] + dc_next
        dz = jnp.concatenate(
            [dc * coef_ref[u, 2], dc * coef_ref[u, 3], dc * coef_ref[u, 4], dh * coef_ref[u, 0]], 1
        )
        dc_next = dc * coef_ref[u, 5]
        if inter:
            dzs[0, pl.ds(pl.multiple_of(v * HALF_PAD, 8), HALF_PAD)] = dz[:HALF_PAD]
            dzs[1, pl.ds(pl.multiple_of(v * HALF_PAD, 8), HALF_PAD)] = dz[HALF_PAD:]
        else:
            dzs[0, pl.ds(pl.multiple_of(v * rows, 8), rows)] = dz
    dz_s[...] = dz
    dc_s[...] = dc_next

    hs = h_ref[pl.ds(first + 1, steps)]
    hp = h_ref[pl.ds(first + 2 * dir_no, steps)]
    if inter:
        xs = jnp.concatenate(
            [x_ref[pl.ds(first + u, HALF_PAD, stride=groups), :] for u in range(steps)], 0
        )
        found = 0.0
        for side in range(2):
            cut = slice(side * HALF_PAD, (side + 1) * HALF_PAD)
            dzc = dzs[side]
            found = found + dot3(dzc, wi2[side], wil[side])
            turned = xs if side == 0 else pltpu.roll(xs, FILTERS, 1)
            awin[...] += dot_rows3(
                jnp.concatenate([turned, hp[:, cut].reshape(steps * HALF_PAD, UNITS)], 1), dzc
            )
            aproj[side] += dot_rows3(hs[:, cut].reshape(steps * HALF_PAD, UNITS), dms)
            abias[0:1] += jnp.sum(dzc, 0, keepdims=True)
        for u in range(steps):
            dx_ref[pl.ds(first + u, HALF_PAD, stride=groups), :] = found[u * HALF_PAD:(u + 1) * HALF_PAD]
    else:
        xs = x_ref[here, :]
        dzc = dzs[0]
        turned = jnp.where(half == 0, xs, pltpu.roll(xs, FILTERS, 1))
        awin[...] += dot_rows3(jnp.concatenate([turned, hp.reshape(steps * groups, UNITS)], 1), dzc)
        aproj[half] += dot_rows3(hs.reshape(steps * groups, UNITS), dms)
        abias[0:1] += jnp.sum(dzc, 0, keepdims=True)
        found = dot3(dzc, wi2[half], wil[half])

        @pl.when(2 * back_no < count)
        def _():
            dx_ref[here] = found

        @pl.when(2 * back_no >= count)
        def _():
            dx_ref[here] = dx_ref[here] + found

    @pl.when(back_no == count - 1)
    def _():
        at = SIDE_ROWS * dir_no
        for q in range(4):
            cut = slice(q * UNITS, (q + 1) * UNITS)
            grad_ref[pl.ds(at + q, FILTERS, stride=4), :] = awin[:FILTERS, cut]
            grad_ref[pl.ds(at + 256 + q, UNITS, stride=4), :] = awin[2 * FILTERS:, cut]
            grad_ref[pl.ds(at + 768 + q, 1), :] = abias[0:1, cut]
        proj_s[...] = aproj[0] + pltpu.roll(aproj[1], FILTERS, 1)
        even = proj_s[pl.ds(0, 64, stride=2), :]
        odd_rows = proj_s[pl.ds(1, 64, stride=2), :]
        grad_ref[pl.ds(PROJ_ROWS + 64 * dir_no, 64), :] = jnp.concatenate(
            [even[:, :FILTERS], odd_rows[:, :FILTERS]], 1
        )
        if layer_no == 0:
            lead = jnp.where(dir_no == 0, 1.0, 0.0)
            streams = lead * g_ref[:valid] + dx_ref[:valid]
            column = column_ref[...]
            mix, following = column[:, 0:1], column[:, 1:2]
            raw = mix * encoder_ref[0:1] + following * encoder_ref[1:2]
            group_at = lax.broadcasted_iota(jnp.int32, (valid, FILTERS), 0) % groups
            shifted = jnp.where(group_at == 0, 0.0, pltpu.roll(pltpu.roll(streams, FILTERS, 1), 1, 0)[:, :FILTERS])
            grad_raw = (streams[:, :FILTERS] + shifted + lead * denc_ref[...]) * jax.nn.sigmoid(raw)
            grad_ref[LAYER_ROWS:LAYER_ROWS + 1] = jnp.concatenate(
                [jnp.sum(grad_raw * mix, 0, keepdims=True), jnp.sum(grad_raw * following, 0, keepdims=True)], 1
            )
            grad_ref[LAYER_ROWS + 1:LAYER_ROWS + 2] = loss_ref[0:1] * lead


def head_kernel(groups, prev_ref, pa_ref, pb_ref, below_ref, stream_ref, column_ref, active_ref, masker_ref, decoder_ref,
                normed_ref, scale_ref, g_ref, hg_ref, denc_ref, loss_ref,
                sep, sig_s, now_s, before_s, slope_s, mk2, mkl, mt2, mtl, dk2, dkl, dt2, dtl, amask, adec, m_low, m_top):
    valid = HOP * groups
    block = 10 * groups
    _, below_base, below_odd = window(2 * BLOCKS - 1)
    norm_stage(prev_ref, pa_ref, pb_ref, below_ref, below_base, below_odd, valid, normed_ref, scale_ref, sep)
    put_split(masker_ref[...], mk2, mkl)
    put_split(masker_ref[...].T, mt2, mtl)
    put_split(decoder_ref[...], dk2, dkl)
    put_split(decoder_ref[...].T, dt2, dtl)
    amask[...] = jnp.zeros_like(amask)
    adec[...] = jnp.zeros_like(adec)
    active = active_ref[0:1]

    def rows(n):
        return pl.ds(pl.multiple_of(n * block, 8), block)

    def summed_of(n):
        here = sep[rows(n), :]
        group_at = lax.broadcasted_iota(jnp.int32, (block, FILTERS), 0) % groups
        shifted = pltpu.roll(pltpu.roll(here, FILTERS, 1), 1, 0)[:, :FILTERS]
        return here[:, :FILTERS] + jnp.where(group_at == 0, 0.0, shifted)

    def frames_of(n):
        encoded = stream_ref[rows(n), :][:, :FILTERS]
        return jnp.concatenate([encoded, encoded, encoded], 1)

    def ahead(n, carry):
        logits = dot3(summed_of(n), mk2[...], mkl[...])
        sig = jax.nn.sigmoid(logits)
        sig_s[rows(n), :] = sig
        both = dot3(sig * active * frames_of(n), dk2[...], dkl[...])
        now_s[rows(n), :] = both[:, :128]
        before_s[pl.ds(pl.multiple_of(n * block + groups, 8), block), :] = both[:, 128:]
        return carry

    lax.fori_loop(0, HOP // 10, ahead, 0)
    at = lax.broadcasted_iota(jnp.int32, (groups, 128), 0)
    before_s[:groups] = jnp.where(at == 0, 0.0, pltpu.roll(before_s[valid:], 1, 0))

    def losses(n, total):
        column = column_ref[rows(n), :]
        lane = lax.broadcasted_iota(jnp.int32, (block, 128), 1)
        target = jnp.where(lane < SOURCES, column, 0.0)
        kept = jnp.broadcast_to(column[:, SOURCES:SOURCES + 1], (block, 128))
        differ = now_s[rows(n), :] + before_s[rows(n), :] - target
        root = jnp.sqrt(differ * differ + 1.0)
        slope_s[rows(n), :] = kept * differ / root
        return total + jnp.sum(kept * (root - 1.0), 0, keepdims=True)

    total = lax.fori_loop(0, HOP // 10, losses, jnp.zeros((1, 128), F32))
    loss_ref[...] = jnp.broadcast_to(jnp.sum(total, 1, keepdims=True), loss_ref.shape)
    slope_s[valid:] = jnp.where(at == groups - 1, 0.0, pltpu.roll(slope_s[:groups], groups - 1, 0))

    def back(n, carry):
        slopes = jnp.concatenate(
            [slope_s[rows(n), :], slope_s[pl.ds(pl.multiple_of(n * block + groups, 8), block), :]], 1
        )
        sig = sig_s[rows(n), :]
        frames = frames_of(n)
        dmasked = dot3(slopes, dt2[...], dtl[...]) * active
        by_sig = dmasked * sig
        denc_ref[rows(n), :] = (
            by_sig[:, :FILTERS] + by_sig[:, FILTERS:2 * FILTERS] + by_sig[:, 2 * FILTERS:]
        )
        dlogits = by_sig * frames * (1.0 - sig)
        dsummed = dot3(dlogits, mt2[...], mtl[...])
        group_at = lax.broadcasted_iota(jnp.int32, (block, FILTERS), 0) % groups
        shifted = jnp.where(group_at == groups - 1, 0.0, pltpu.roll(dsummed, block - 1, 0))
        g_ref[rows(n), :] = jnp.concatenate([dsummed, shifted], 1)
        amask[...] += dot_rows3(summed_of(n), dlogits)
        adec[...] += dot_rows3(sig * active * frames, slopes)
        return carry

    lax.fori_loop(0, HOP // 10, back, 0)
    g_ref[valid:] = jnp.zeros((g_ref.shape[0] - valid, 128), F32)
    m_low[...] = amask[:, :128]
    m_top[...] = jnp.concatenate([amask[:, 128:], jnp.zeros((FILTERS, FILTERS), F32)], 1)
    low_even, low_odd = m_low[pl.ds(0, 32, stride=2), :], m_low[pl.ds(1, 32, stride=2), :]
    top_even, top_odd = m_top[pl.ds(0, 32, stride=2), :], m_top[pl.ds(1, 32, stride=2), :]
    hg_ref[pl.ds(0, 32, stride=3), :] = low_even
    hg_ref[pl.ds(1, 32, stride=3), :] = jnp.concatenate([top_even[:, :FILTERS], low_odd[:, :FILTERS]], 1)
    hg_ref[pl.ds(2, 32, stride=3), :] = jnp.concatenate([low_odd[:, FILTERS:], top_odd[:, :FILTERS]], 1)
    columns = []
    for tap in range(2):
        found = 0.0
        for j in range(SOURCES):
            found = found + adec[j * FILTERS:(j + 1) * FILTERS, 128 * tap + j:128 * tap + j + 1]
        columns.append(jnp.broadcast_to(found, (FILTERS, 128)))
    lane = lax.broadcasted_iota(jnp.int32, (FILTERS, 128), 1)
    hg_ref[96:HEAD_ROWS] = jnp.where(lane == 0, columns[0], jnp.where(lane == 1, columns[1], 0.0))


def assemble(flat, layers):
    lane = lax.broadcasted_iota(jnp.int32, (FILTERS, 128), 1)
    row = lax.broadcasted_iota(jnp.int32, (FILTERS, 128), 0)
    encoder = jnp.broadcast_to(layers[0][LAYER_ROWS:LAYER_ROWS + 1], (FILTERS, 128))
    first_tap = jnp.sum(jnp.where(lane == row, encoder, 0.0), 1, keepdims=True)
    second_tap = jnp.sum(jnp.where(lane == row + FILTERS, encoder, 0.0), 1, keepdims=True)

    def interleave(a, b):
        return jnp.sum(jnp.where(lane == 2 * row, a, jnp.where(lane == 2 * row + 1, b, 0.0)), 0, keepdims=True)

    flat[0:1] = interleave(first_tap, second_tap)
    for layer_no, ref in enumerate(layers):
        first, inner, odd = window(layer_no)
        base = first + inner
        if odd:
            whole_rows = ref[:LAYER_ROWS - 6]
            turned = pltpu.roll(whole_rows, FILTERS, 1)
            flat[base:base + 1, FILTERS:] = turned[0:1, FILTERS:]
            wide_low = lax.broadcasted_iota(jnp.int32, (LAYER_ROWS - 7, 128), 1) < FILTERS
            flat[base + 1:base + LAYER_ROWS - 6] = jnp.where(wide_low, turned[:-1], turned[1:])
        else:
            flat[base:base + LAYER_ROWS - 6] = ref[:LAYER_ROWS - 6]
    flat[6695:6791] = layers[3][LAYER_ROWS:LAYER_ROWS + 96]
    decoder = layers[3][LAYER_ROWS + 96:LAYER_ROWS + HEAD_ROWS]
    flat[6791:6792] = interleave(decoder[:, 0:1], decoder[:, 1:2])
    flat[6792:] = jnp.zeros((flat.shape[0] - 6792, 128), F32)


def finish_kernel(chips, depths, entries, width, r0, r1, r2, r3, p_ref, m_ref, v_ref,
                  new_ref, half_ref, first_ref, second_ref, stats_ref,
                  flat, pair_in, sent, plane_in, held, depth_in, mine, found, note, depth_notes, notes,
                  pair_sem, plane_sem, depth_sem, spread_sem, note_sem, notes_sem):
    b = lax.axis_index("batch")
    z = lax.axis_index("frames")
    core = lax.rem(b, 2)
    chip = b // 2
    piece = width // depths
    rows = p_ref.shape[0]

    def start(shard):
        return pl.multiple_of(shard * entries // 1024 * 8, 8)

    def send(src, dst, sems, slot, device):
        copy = pltpu.make_async_remote_copy(
            src_ref=src, dst_ref=dst, send_sem=sems.at[0, slot], recv_sem=sems.at[1, slot],
            device_id=device, device_id_type=pl.DeviceIdType.MESH,
        )
        copy.start()
        return copy

    barrier = pltpu.get_barrier_semaphore()
    for step in range(1, 2 * chips):
        pl.semaphore_signal(
            barrier, inc=1, device_id=(lax.rem(b + step, 2 * chips), z), device_id_type=pl.DeviceIdType.MESH
        )
    for step in range(1, depths):
        pl.semaphore_signal(
            barrier, inc=1, device_id=(b, lax.rem(z + step, depths)), device_id_type=pl.DeviceIdType.MESH
        )
    assemble(flat, (r0, r1, r2, r3))
    note[...] = jnp.broadcast_to(r0[LAYER_ROWS + 1:LAYER_ROWS + 2], note.shape)
    pl.semaphore_wait(barrier, 2 * chips - 1 + depths - 1)

    order = list(range(1, chips)) + [0]
    pairs = {}
    for step in order:
        other = 2 * lax.rem(chip + step, chips) + 1 - core
        pairs[step] = send(
            flat.at[pl.ds(start(other), width)], pair_in.at[step], pair_sem, step, (2 * chip + 1 - core, z)
        )
    loss_copies = [
        send(note, depth_notes.at[step - 1], note_sem, step - 1, (b, lax.rem(z + step, depths)))
        for step in range(1, depths)
    ]
    planes = []
    for step in order:
        pairs[step].wait_recv()
        owner = 2 * lax.rem(chip + step, chips) + core
        total = flat[pl.ds(start(owner), width), :] + pair_in[step]
        if step:
            sent[step - 1] = total
            planes.append(send(sent.at[step - 1], plane_in.at[step - 1], plane_sem, step - 1, (owner, z)))
        else:
            held[...] = total
    for step in order:
        pairs[step].wait_send()
    total = held[...]
    for step in range(1, chips):
        planes[step - 1].wait()
        total = total + plane_in[step - 1]
    held[...] = total
    copies = []
    for step in range(1, depths):
        other = lax.rem(z + step, depths)
        copies.append(
            send(held.at[pl.ds(pl.multiple_of(other * piece, 8), piece)], depth_in.at[step - 1], depth_sem, step - 1, (b, other))
        )
    here = pl.ds(pl.multiple_of(z * piece, 8), piece)
    total = held[here, :]
    for step in range(1, depths):
        copies[step - 1].wait()
        total = total + depth_in[step - 1]
    mine[...] = total
    copies = [
        send(mine, found.at[here], spread_sem, step - 1, (b, lax.rem(z + step, depths)))
        for step in range(1, depths)
    ]
    losses = note[...]
    for step in range(1, depths):
        loss_copies[step - 1].wait()
        losses = losses + depth_notes[step - 1]
    for copy in copies:
        copy.wait()
    found[here, :] = mine[...]

    at = b * entries - start(b) * 128
    row_at, lane_at = at // 128, lax.rem(at, 128)
    gradient = found[pl.ds(row_at, rows), :]
    counted = gradient
    if entries % 128:
        lane = lax.broadcasted_iota(jnp.int32, (rows, 128), 1)
        row = lax.broadcasted_iota(jnp.int32, (rows, 128), 0)
        turn = lax.rem(128 - lane_at, 128)
        gradient = jnp.where(
            lane < 128 - lane_at, pltpu.roll(gradient, turn, 1), pltpu.roll(found[pl.ds(row_at + 1, rows), :], turn, 1)
        )
        counted = jnp.where(128 * row + lane < entries, gradient, 0.0)
    squares = jnp.sum(jnp.sum(counted * counted, 0, keepdims=True), 1, keepdims=True)
    lane = lax.broadcasted_iota(jnp.int32, note.shape, 1)
    note[...] = jnp.where(lane == 2, squares, losses)
    copies = [
        send(note, notes.at[b], notes_sem, step - 1, (lax.rem(b + step, 2 * chips), z))
        for step in range(1, 2 * chips)
    ]
    for copy in copies:
        copy.wait()
    notes[b] = note[...]
    totals = notes[0]
    for other in range(1, 2 * chips):
        totals = totals + notes[other]
    count = jnp.sum(jnp.where(lane == 1, totals, 0.0), 1, keepdims=True)[0:1]
    norm = jnp.sqrt(jnp.sum(jnp.where(lane == 2, totals, 0.0), 1, keepdims=True)[0:1]) / count
    stats_ref[...] = jnp.where(lane == 2, norm, totals)
    clipped = gradient / count * (CLIP_AT / jnp.maximum(norm, CLIP_AT))
    new_first = BETA_ONE * m_ref[...] + (1.0 - BETA_ONE) * clipped
    new_second = BETA_TWO * v_ref[...] + (1.0 - BETA_TWO) * clipped * clipped
    step_size = (
        new_first / (1.0 - BETA_ONE**STEP) / (jnp.sqrt(new_second / (1.0 - BETA_TWO**STEP)) + ADAM_EPS)
    )
    params = p_ref[...]
    new_params = params - LEARN_RATE * (step_size + DECAY_RATE * params)
    new_ref[...] = new_params
    half_ref[...] = new_params.astype(BF16)
    first_ref[...] = new_first
    second_ref[...] = new_second


def sizes(inter, groups):
    if inter:
        return groups, 2 * HALF_PAD, 8
    return 2 * HOP, groups, 10


def whole(shape):
    return pl.BlockSpec(shape, lambda j: (0,) * len(shape))


def layer_spec(layer_no):
    first, _, _ = window(layer_no)
    return pl.BlockSpec((pl.Element(WINDOW), pl.Element(128)), lambda j: (first, 0))


def run_forward(layer_no, groups, dir_no, stream, flat):
    inter = layer_no % 2 == 1
    length, rows, steps = sizes(inter, groups)
    stream_shape = (HALF_PAD * groups, 128)
    coef_block = (steps, 6, rows, UNITS)
    out = [
        ((length + 2, rows, UNITS), whole((length + 2, rows, UNITS))),
        ((length, 6, rows, UNITS), pl.BlockSpec(coef_block, lambda j: (j, 0, 0, 0))),
        (stream_shape, whole(stream_shape)),
    ]
    layers = [layer_no]
    if layer_no:
        out = [(stream_shape, whole(stream_shape)), (stream_shape, whole(stream_shape)), ((8, 128), whole((8, 128)))] + out
        layers = [layer_no - 1, layer_no]
    return pl.pallas_call(
        functools.partial(forward_kernel, layer_no, groups, steps),
        grid=(length // steps,),
        in_specs=[pl.BlockSpec(memory_space=pltpu.SMEM)]
        + [whole(a.shape) for a in stream]
        + [layer_spec(n) for n in layers],
        out_specs=[spec for _, spec in out],
        out_shape=[jax.ShapeDtypeStruct(shape, F32) for shape, _ in out],
        scratch_shapes=[
            pltpu.VMEM((2, 256, GATES), BF16), pltpu.VMEM((2, 128, GATES), BF16),
            pltpu.VMEM((256, GATES), BF16), pltpu.VMEM((128, GATES), BF16),
            pltpu.VMEM((2, 256, 128), BF16), pltpu.VMEM((2, 128, 128), BF16),
            pltpu.VMEM((UNITS, 128), F32),
            pltpu.VMEM((8, GATES), F32), pltpu.VMEM((steps * rows, GATES), F32),
            pltpu.VMEM((rows, UNITS), F32), pltpu.VMEM((rows, UNITS), F32),
        ],
        compiler_params=pltpu.CompilerParams(vmem_limit_bytes=VMEM_MAX),
        name="forward_inter" if inter else "forward_intra",
    )(dir_no, *stream, *[flat for _ in layers])


def run_backward(layer_no, groups, dir_no, before, coef, flat):
    inter = layer_no % 2 == 1
    last_layer = layer_no == 2 * BLOCKS - 1
    length, rows, steps = sizes(inter, groups)
    stream_shape = (HALF_PAD * groups, 128)
    count = length // steps
    coef_block = (steps, 6, rows, UNITS)
    if last_layer:
        out = [stream_shape, (LAYER_ROWS + HEAD_ROWS, 128)]
    elif layer_no:
        out = [stream_shape, stream_shape, (LAYER_ROWS, 128)]
    else:
        out = [(LAYER_ROWS + 8, 128)]
    streams = [] if layer_no else [pltpu.VMEM(stream_shape, F32), pltpu.VMEM(stream_shape, F32)]
    return pl.pallas_call(
        functools.partial(backward_kernel, layer_no, groups, steps),
        grid=(count,),
        in_specs=[pl.BlockSpec(memory_space=pltpu.SMEM)]
        + [whole(a.shape) for a in before]
        + [pl.BlockSpec(coef_block, lambda j: (count - 1 - j, 0, 0, 0)), layer_spec(layer_no)],
        out_specs=[whole(shape) for shape in out],
        out_shape=[jax.ShapeDtypeStruct(shape, F32) for shape in out],
        scratch_shapes=[
            pltpu.VMEM((2, 2 * GATES, 128), BF16), pltpu.VMEM((2, GATES, 128), BF16),
            pltpu.VMEM((GATES, 256), BF16), pltpu.VMEM((GATES, 128), BF16),
            pltpu.VMEM((2, 256, 128), BF16), pltpu.VMEM((2, 128, 128), BF16),
            pltpu.VMEM((UNITS, 128), F32),
            pltpu.VMEM(stream_shape, F32), pltpu.VMEM((steps * rows, UNITS), F32),
            pltpu.VMEM((2, steps * HALF_PAD, GATES) if inter else (1, steps * rows, GATES), F32),
            pltpu.VMEM((rows, GATES), F32), pltpu.VMEM((rows, UNITS), F32),
            pltpu.VMEM((256, GATES), F32), pltpu.VMEM((2, UNITS, 128), F32), pltpu.VMEM((8, GATES), F32),
        ]
        + streams,
        compiler_params=pltpu.CompilerParams(vmem_limit_bytes=VMEM_MAX),
        name="backward_inter" if inter else "backward_intra",
    )(dir_no, *before, coef, flat)


def run_head(groups, streams, flat, stream, column, active, masker, decoder):
    valid = HOP * groups
    stream_shape = (HALF_PAD * groups, 128)
    first, _, _ = window(2 * BLOCKS - 1)
    out = [stream_shape, (8, 128), stream_shape, (HEAD_ROWS, 128), (valid, FILTERS), (8, 128)]
    wide = SOURCES * FILTERS
    return pl.pallas_call(
        functools.partial(head_kernel, groups),
        grid=(1,),
        in_specs=[whole(a.shape) for a in streams]
        + [layer_spec(2 * BLOCKS - 1)]
        + [whole(a.shape) for a in (stream, column, active, masker, decoder)],
        out_specs=[whole(shape) for shape in out],
        out_shape=[jax.ShapeDtypeStruct(shape, F32) for shape in out],
        scratch_shapes=[
            pltpu.VMEM(stream_shape, F32), pltpu.VMEM((valid, wide), F32), pltpu.VMEM((valid, 128), F32),
            pltpu.VMEM((valid + groups, 128), F32), pltpu.VMEM((valid + groups, 128), F32),
            pltpu.VMEM((2 * FILTERS, wide), BF16), pltpu.VMEM((FILTERS, wide), BF16),
            pltpu.VMEM((2 * wide, FILTERS), BF16), pltpu.VMEM((wide, FILTERS), BF16),
            pltpu.VMEM((2 * wide, 256), BF16), pltpu.VMEM((wide, 256), BF16),
            pltpu.VMEM((512, wide), BF16), pltpu.VMEM((256, wide), BF16),
            pltpu.VMEM((FILTERS, wide), F32), pltpu.VMEM((wide, 256), F32),
            pltpu.VMEM((FILTERS, 128), F32), pltpu.VMEM((FILTERS, 128), F32),
        ],
        compiler_params=pltpu.CompilerParams(vmem_limit_bytes=VMEM_MAX),
        name="head",
    )(*streams, flat, stream, column, active, masker, decoder)


def run_finish(layers, params, first_moment, second_moment):
    entries = params.shape[0]
    rows = -(-entries // 128)
    depths = lax.axis_size("frames")
    chips = lax.axis_size("batch") // 2
    width = -(-(rows + 8) // (8 * depths)) * 8 * depths
    shards = [
        jnp.pad(a, (0, rows * 128 - entries)).reshape(rows, 128) for a in (params, first_moment, second_moment)
    ]
    out = [((rows, 128), F32), ((rows, 128), BF16), ((rows, 128), F32), ((rows, 128), F32), ((8, 128), F32)]
    vmem = pl.BlockSpec(memory_space=pltpu.VMEM)
    block = (width, 128)
    piece = (width // depths, 128)
    sems = pltpu.SemaphoreType.DMA
    found = pl.pallas_call(
        functools.partial(finish_kernel, chips, depths, entries, width),
        in_specs=[vmem] * 7,
        out_specs=[vmem] * 5,
        out_shape=[jax.ShapeDtypeStruct(shape, dtype) for shape, dtype in out],
        scratch_shapes=[
            pltpu.VMEM((6792 + width, 128), F32),
            pltpu.VMEM((chips,) + block, F32), pltpu.VMEM((chips - 1,) + block, F32),
            pltpu.VMEM((chips - 1,) + block, F32), pltpu.VMEM(block, F32),
            pltpu.VMEM((depths - 1,) + piece, F32), pltpu.VMEM(piece, F32), pltpu.VMEM(block, F32),
            pltpu.VMEM((8, 128), F32), pltpu.VMEM((depths - 1, 8, 128), F32), pltpu.VMEM((2 * chips, 8, 128), F32),
            sems((2, chips)), sems((2, chips - 1)), sems((2, depths - 1)), sems((2, depths - 1)),
            sems((2, depths - 1)), sems((2, 2 * chips - 1)),
        ],
        compiler_params=pltpu.CompilerParams(
            vmem_limit_bytes=VMEM_MAX, collective_id=1, has_side_effects=True
        ),
        name="finish",
    )(*layers, *shards)
    return [a.reshape(-1)[:entries] for a in found[:4]] + [found[4]]


def local(params, first_moment, second_moment, mixture, sources, speakers, lengths):
    flat = lax.all_gather(params, "batch", axis=0, tiled=True)
    items = mixture.shape[0]
    frames_size = lax.axis_size("frames")
    samples = mixture.shape[1] * frames_size
    groups = samples // HOP
    core = lax.axis_index("batch") % 2
    depth = lax.axis_index("frames")
    column = 2 * items
    copies = frames_size // column
    mine = depth // copies
    weight = jnp.where(depth % copies == 0, 1.0, 0.0).astype(F32)
    pairs = [[2 * b, 2 * b + 1] for b in range(lax.axis_size("batch") // 2)]
    swap = [(b, b + 1 if b % 2 == 0 else b - 1) for b in range(lax.axis_size("batch"))]

    signals = jnp.concatenate([mixture[:, None], sources], 1)
    signals = lax.all_gather(signals, "frames", axis=2, tiled=True)
    scalars = jnp.stack([speakers, lengths], 1).astype(F32)
    signals = lax.all_gather(signals, "batch", axis=0, tiled=True, axis_index_groups=pairs)
    scalars = lax.all_gather(scalars, "batch", axis=0, tiled=True, axis_index_groups=pairs)
    signal = lax.dynamic_slice_in_dim(signals, mine, 1, 0)[0]
    scalar = lax.dynamic_slice_in_dim(scalars, mine, 1, 0)[0]
    mix = signal[0]
    following = jnp.concatenate([mix[1:], jnp.zeros((1,), F32)])

    def by_row(array):
        return array.reshape(array.shape[:-1] + (groups, HOP)).swapaxes(-1, -2).reshape(array.shape[:-1] + (groups * HOP,))

    mix_row = by_row(mix)
    follow_row = by_row(following)
    encoder = flat[:2 * FILTERS].reshape(FILTERS, 2)
    raw = mix_row[:, None] * encoder[:, 0] + follow_row[:, None] * encoder[:, 1]
    encoded = jax.nn.softplus(raw)

    def later(array):
        three = array.reshape(HOP, groups, -1)
        return jnp.concatenate([three[:, 1:], jnp.zeros_like(three[:, :1])], 1).reshape(array.shape)

    def earlier(array):
        three = array.reshape(HOP, groups, -1)
        return jnp.concatenate([jnp.zeros_like(three[:, :1]), three[:, :-1]], 1).reshape(array.shape)

    pad = ((0, (HALF_PAD - HOP) * groups), (0, 0))
    stream = jnp.pad(jnp.concatenate([encoded, later(encoded)], 1), pad)
    dir_no = core.reshape(1).astype(jnp.int32)
    view = flat.reshape(-1, 128)

    def exchange(array):
        return lax.ppermute(array, "batch", swap)

    kept = []
    below = (stream,)
    for layer_no in range(2 * BLOCKS):
        found = run_forward(layer_no, groups, dir_no, below, view)
        x = found[0] if layer_no else stream
        if layer_no:
            kept[-1][:0] = found[1:3]
        h_all, coef, part = found[-3:]
        kept.append([x, h_all, coef])
        below = (x, part, exchange(part))

    position = by_row(jnp.arange(samples).astype(F32))
    valid = jnp.where(position < scalar[1], 1.0, 0.0) * weight
    active = jnp.where(jnp.arange(SOURCES).astype(F32) < scalar[0], 1.0, 0.0)
    target = by_row(signal[1:]) * active[:, None]
    wide = SOURCES * FILTERS
    masker = flat[-FILTERS * wide - 2 * FILTERS:-2 * FILTERS].reshape(FILTERS, wide)
    decoder = flat[-2 * FILTERS:].reshape(FILTERS, 2)
    column = jnp.pad(jnp.concatenate([target, valid[None]], 0).T, ((0, 0), (0, 124)))
    by_source = jnp.pad(jnp.eye(SOURCES, dtype=F32), ((0, 0), (0, 128 - SOURCES)))
    taps = (by_source[:, None, None, :] * decoder[None, :, :, None]).reshape(wide, 256)
    active_wide = jnp.broadcast_to(jnp.repeat(active, FILTERS)[None], (8, wide))
    normed, scale, grad, head_grads, grad_encoded, loss = run_head(
        groups, below, view, stream, column, active_wide, masker, taps
    )
    kept[-1][:0] = [normed, scale]
    lane = jnp.arange(128)
    count_part = jnp.sum(scalars[:, 1]) / frames_size
    loss = jnp.where(lane == 0, loss, jnp.where(lane == 1, count_part, 0.0))
    signal_column = jnp.pad(jnp.stack([mix_row, follow_row], 1), ((0, 0), (0, 126)))
    encoder_rows = jnp.pad(encoder.T, ((0, 6), (0, 0)))
    sums = [None] * (2 * BLOCKS)
    before = (grad, head_grads)
    for layer_no in reversed(range(2 * BLOCKS)):
        normed, scale, x, h_all, coef = kept[layer_no]
        if layer_no == 0:
            before = before + (signal_column, grad_encoded, encoder_rows, loss)
        found = run_backward(layer_no, groups, dir_no, before + (normed, scale, x, h_all), coef, view)
        sums[layer_no] = found[-1]
        if layer_no == 2 * BLOCKS - 1:
            dx = found[0]
        elif layer_no:
            grad, dx = found[:2]
        if layer_no:
            before = (grad, dx, exchange(dx))
    *updated, stats = run_finish(sums, params, first_moment, second_moment)
    return (*updated, stats[0, 2], stats[0, :2])


def solution(mesh):
    placed = (
        P("batch"),
        P("batch"),
        P("batch"),
        P("batch", "frames"),
        P("batch", None, "frames"),
        P("batch"),
        P("batch"),
    )
    return jax.shard_map(
        local,
        mesh=mesh,
        in_specs=placed,
        out_specs=(P("batch"), P("batch"), P("batch"), P("batch"), P(), P()),
        check_vma=False,
    )
```

```python
import functools
import math

import jax
import jax.numpy as jnp
from jax import lax
from jax.experimental import pallas as pl
from jax.experimental.pallas import tpu as pltpu
from jax.sharding import PartitionSpec as P

FILTERS = 64
UNITS = 128
HOP = 50
HALF_PAD = 56
SOURCES = 3
BLOCKS = 2
STEP = 5
GATES = 4 * UNITS

HIGHEST = lax.Precision.HIGHEST
NORM_EPS = 1e-08
CLIP_AT = 0.001
BETA_ONE = 0.5
BETA_TWO = 0.5
LEARN_RATE = 0.05
DECAY_RATE = 0.01
ADAM_EPS = 1e-08
F32 = jnp.float32
BF16 = jnp.bfloat16
VMEM_MAX = 60 * 2**20


def split(a):
    hi = a.astype(BF16)
    return hi, (a - hi.astype(F32)).astype(BF16)


def dot(a, b):
    return jnp.dot(a, b, preferred_element_type=F32)


def dot3(a, w_twice, w_low):
    hi, lo = split(a)
    return dot(jnp.concatenate([hi, lo], 1), w_twice) + dot(hi, w_low)


def dot_rows(a, b):
    return lax.dot_general(a, b, (((0,), (0,)), ((), ())), preferred_element_type=F32)


def dot_rows3(a, b):
    a_hi, a_lo = split(a)
    b_hi, b_lo = split(b)
    return dot_rows(a_hi, b_hi) + dot_rows(a_lo, b_hi) + dot_rows(a_hi, b_lo)


SIDE_ROWS = 772
PROJ_ROWS = 2 * SIDE_ROWS
VEC_ROW = PROJ_ROWS + 128
LAYER_ROWS = 1680
HEAD_ROWS = 160
WINDOW = 1688


def window(layer_no):
    at = 2 + 3347 * layer_no
    return at // 16 * 8, at // 2 % 8, at % 2


def pick(ref, base, odd, start, count, stride=1):
    def load(at):
        return ref[pl.ds(at, count, stride=stride), :] if stride > 1 else ref[pl.ds(at, count), :]

    first = load(base + start)
    if not odd:
        return first
    return jnp.concatenate([first[:, 64:], load(base + start + 1)[:, :64]], 1)


def load_weights(ref, base, odd, dir_no, proj_s):
    at = SIDE_ROWS * dir_no
    win = jnp.concatenate([pick(ref, base, odd, at + q, FILTERS, 4) for q in range(4)], 1)
    wrec = jnp.concatenate([pick(ref, base, odd, at + 256 + q, UNITS, 4) for q in range(4)], 1)
    bias = jnp.concatenate([pick(ref, base, odd, at + 768 + q, 1) for q in range(4)], 1)
    pairs = pick(ref, base, odd, PROJ_ROWS + 64 * dir_no, 64)
    proj_s[pl.ds(0, 64, stride=2), :] = pairs
    proj_s[pl.ds(1, 64, stride=2), :] = pltpu.roll(pairs, 64, 1)
    return win, wrec, bias, proj_s[:, :FILTERS]


def load_vec(ref, base, odd):
    first = pick(ref, base, odd, VEC_ROW, 1)
    turned = pltpu.roll(jnp.broadcast_to(first, (8, 128)), 64, 1)[0:1]
    if odd:
        last = ref[base + VEC_ROW + 1:base + VEC_ROW + 2, :]
        last = jnp.concatenate([last[:, 64:], last[:, 64:]], 1)
    else:
        last = ref[base + VEC_ROW + 1:base + VEC_ROW + 2, :]
        last = jnp.concatenate([last[:, :64], last[:, :64]], 1)
    low = lax.broadcasted_iota(jnp.int32, (1, 128), 1) < 64
    return jnp.where(low, first, turned), jnp.where(low, turned, first), last


def put_split(w, twice_ref, low_ref):
    hi, lo = split(w)
    twice_ref[...] = jnp.concatenate([hi, hi], 0)
    low_ref[...] = lo


def times(dir_no, chunk_no, length, steps):
    return [dir_no * (length - 1) + (1 - 2 * dir_no) * (chunk_no * steps + u) for u in range(steps)]


def stream_rows(inter, groups, at):
    if inter:
        return pl.ds(at, HALF_PAD, stride=groups)
    return pl.ds(pl.multiple_of(lax.rem(at, HOP) * groups, 8), groups)


def gather(ref, inter, groups, positions):
    return jnp.concatenate([ref[stream_rows(inter, groups, at), :] for at in positions], 0)


def to_sides(inter, steps, array):
    if not inter:
        return [array]
    three = array.reshape(steps, 2 * HALF_PAD, array.shape[-1])
    return [
        three[:, side * HALF_PAD:(side + 1) * HALF_PAD].reshape(steps * HALF_PAD, array.shape[-1]) for side in range(2)
    ]


SIDE_ROWS = 772
PROJ_ROWS = 2 * SIDE_ROWS
VEC_ROW = PROJ_ROWS + 128
LAYER_ROWS = 1680
HEAD_ROWS = 160
WINDOW = 1688


def window(layer_no):
    at = 2 + 3347 * layer_no
    return at // 16 * 8, at // 2 % 8, at % 2


def pick(ref, base, odd, start, count, stride=1):
    def load(at):
        return ref[pl.ds(at, count, stride=stride), :] if stride > 1 else ref[pl.ds(at, count), :]

    first = load(base + start)
    if not odd:
        return first
    return jnp.concatenate([first[:, 64:], load(base + start + 1)[:, :64]], 1)


def load_weights(ref, base, odd, dir_no, proj_s):
    at = SIDE_ROWS * dir_no
    win = jnp.concatenate([pick(ref, base, odd, at + q, FILTERS, 4) for q in range(4)], 1)
    wrec = jnp.concatenate([pick(ref, base, odd, at + 256 + q, UNITS, 4) for q in range(4)], 1)
    bias = jnp.concatenate([pick(ref, base, odd, at + 768 + q, 1) for q in range(4)], 1)
    pairs = pick(ref, base, odd, PROJ_ROWS + 64 * dir_no, 64)
    proj_s[pl.ds(0, 64, stride=2), :] = pairs
    proj_s[pl.ds(1, 64, stride=2), :] = pltpu.roll(pairs, 64, 1)
    return win, wrec, bias, proj_s[:, :FILTERS]


def load_vec(ref, base, odd):
    first = pick(ref, base, odd, VEC_ROW, 1)
    turned = pltpu.roll(jnp.broadcast_to(first, (8, 128)), 64, 1)[0:1]
    if odd:
        last = ref[base + VEC_ROW + 1:base + VEC_ROW + 2, :]
        last = jnp.concatenate([last[:, 64:], last[:, 64:]], 1)
    else:
        last = ref[base + VEC_ROW + 1:base + VEC_ROW + 2, :]
        last = jnp.concatenate([last[:, :64], last[:, :64]], 1)
    low = lax.broadcasted_iota(jnp.int32, (1, 128), 1) < 64
    return jnp.where(low, first, turned), jnp.where(low, turned, first), last


def put_split(w, twice_ref, low_ref):
    hi, lo = split(w)
    twice_ref[...] = jnp.concatenate([hi, hi], 0)
    low_ref[...] = lo


def place(dir_no, chunk_no, count, steps, inter, groups):
    first = jnp.where(dir_no == 0, chunk_no * steps, (count - 1 - chunk_no) * steps)
    if inter:
        return first, 0, 0
    half = first // HOP
    return first, half, pl.multiple_of((first - HOP * half) * groups, 8)


def norm_stage(prev_ref, pa_ref, pb_ref, flat_ref, base, odd, valid, normed_ref, scale_ref, x_ref):
    offset, gain, shift = load_vec(flat_ref, base, odd)
    mixed = pa_ref[:valid] + pb_ref[:valid] + offset
    total = 2.0 * valid * FILTERS
    mean = jnp.sum(mixed) / total
    spread = jnp.sum(mixed * mixed) / total - mean * mean
    scale = lax.rsqrt(jnp.full((1, 128), spread + NORM_EPS, F32))
    normed = (mixed - mean) * scale
    normed_ref[:valid] = normed
    normed_ref[valid:] = jnp.zeros((normed_ref.shape[0] - valid, 128), F32)
    x_ref[:valid] = prev_ref[:valid] + gain * normed + shift
    x_ref[valid:] = jnp.zeros((x_ref.shape[0] - valid, 128), F32)
    scale_ref[...] = jnp.broadcast_to(scale, scale_ref.shape)


def greet_sibling():
    b = lax.axis_index("batch")
    device = (b + 1 - 2 * lax.rem(b, 2), lax.axis_index("frames"))
    return device, pltpu.get_barrier_semaphore()


def fetch(flat_ref, layer_no, window_s, sem):
    first, _, _ = window(layer_no)
    copy = pltpu.make_async_copy(flat_ref.at[pl.ds(first, WINDOW)], window_s, sem)
    copy.start()
    return copy


def swap_with_sibling(src_ref, dst_ref, sems):
    device, barrier = greet_sibling()
    pl.semaphore_wait(barrier, 1)
    copy = pltpu.make_async_remote_copy(
        src_ref=src_ref, dst_ref=dst_ref, send_sem=sems.at[0], recv_sem=sems.at[1],
        device_id=device, device_id_type=pl.DeviceIdType.MESH,
    )
    copy.start()
    copy.wait()


def forward_kernel(layer_no, groups, steps, *refs):
    inter = layer_no % 2 == 1
    (x_ref, flat_ref,
     next_ref, normed_ref, scale_ref, h_ref, coef_ref,
     wi2, wil, wr2, wrl, pj2, pjl, proj_s, bias_s, gin_a, gin_b, h_a, h_b, c_s, part_ref, peer_ref, sems, window_s, fetch_sem) = refs
    turn_no = pl.program_id(0)
    last_turn = pl.num_programs(0) - 1
    chunks = 2 * pl.num_programs(0)
    length = chunks * steps
    dir_no = lax.rem(lax.axis_index("batch"), 2)
    rows = 2 * HALF_PAD if inter else groups
    valid = HOP * groups

    def before(chunk_no, gin):
        chunk_no = lax.rem(chunk_no, chunks)
        positions = times(dir_no, chunk_no, length, steps)
        xs_hi, xs_lo = split(gather(x_ref, inter, groups, positions))
        both = jnp.concatenate([xs_hi, xs_lo], 1)
        half = 0 if inter else lax.div(positions[0], HOP)

        def gate(q):
            cut = slice(q * UNITS, (q + 1) * UNITS)
            for side in range(2) if inter else [half]:
                found = dot(both, wi2[side, :, cut]) + dot(xs_hi, wil[side, :, cut]) + bias_s[0:1, cut]
                if inter:
                    for u in range(steps):
                        at = u * rows + side * HALF_PAD
                        gin[at:at + HALF_PAD, cut] = found[u * HALF_PAD:(u + 1) * HALF_PAD]
                else:
                    gin[:, cut] = found

        return [functools.partial(gate, q) for q in range(4)]

    def after(chunk_no, hs):
        chunk_no = lax.rem(chunk_no + chunks, chunks)
        positions = times(dir_no, chunk_no, length, steps)

        def project():
            if inter:
                found = 0.0
                for side, part in enumerate(to_sides(inter, steps, hs[...])):
                    found = found + dot3(part, pj2[side], pjl[side])
                for u in range(steps):
                    part_ref[stream_rows(inter, groups, positions[u]), :] = found[u * HALF_PAD:(u + 1) * HALF_PAD]
            else:
                half = lax.div(positions[0], HOP)
                found = dot3(hs[...], pj2[half], pjl[half])
                for u in range(steps):
                    here = stream_rows(inter, groups, positions[u])
                    part_ref[here, :] = part_ref[here, :] + found[u * groups:(u + 1) * groups]

        return [project]

    def walk(gin, hs, h, c, sub, beside):
        for u in range(steps):
            hi, lo = split(h)
            z = dot(jnp.concatenate([hi, lo], 1), wr2[...]) + dot(hi, wrl[...])
            for task in beside[u::steps]:
                task()
            z = z + gin[u * rows:(u + 1) * rows]
            th = jnp.tanh(z)
            ti, tf, g, to = (th[:, q * UNITS:(q + 1) * UNITS] for q in range(4))
            i_g = 0.5 * ti + 0.5
            f_g = 0.5 * tf + 0.5
            o_g = 0.5 * to + 0.5
            c_prev = c
            c = f_g * c + i_g * g
            tc = jnp.tanh(c)
            h = o_g * tc
            at = sub * steps + u
            hs[u * rows:(u + 1) * rows] = h
            h_ref[at] = h
            coef_ref[at, 0] = tc * (0.25 - 0.25 * to * to)
            coef_ref[at, 1] = o_g * (1.0 - tc * tc)
            coef_ref[at, 2] = g * (0.25 - 0.25 * ti * ti)
            coef_ref[at, 3] = c_prev * (0.25 - 0.25 * tf * tf)
            coef_ref[at, 4] = i_g * (1.0 - g * g)
            coef_ref[at, 5] = f_g
        return h, c

    @pl.when(turn_no == 0)
    def _():
        device, barrier = greet_sibling()
        pl.semaphore_signal(barrier, inc=1, device_id=device, device_id_type=pl.DeviceIdType.MESH)
        fetch(flat_ref, layer_no, window_s, fetch_sem).wait()
        part_ref[...] = jnp.zeros_like(part_ref)
        column = lax.broadcasted_iota(jnp.int32, (1, GATES), 1)
        scaling = jnp.where((column >= 2 * UNITS) & (column < 3 * UNITS), 1.0, 0.5)
        _, base, odd = window(layer_no)
        win, wrec, bias, proj = load_weights(window_s, base, odd, dir_no, proj_s)
        win = win * scaling
        none = jnp.zeros_like(win)
        for half in range(2):
            put_split(jnp.concatenate([win, none] if half == 0 else [none, win], 0), wi2.at[half], wil.at[half])
        put_split(wrec * scaling, wr2, wrl)
        bias_s[...] = jnp.broadcast_to(bias * scaling, bias_s.shape)
        none = jnp.zeros_like(proj)
        for half in range(2):
            put_split(jnp.concatenate([proj, none] if half == 0 else [none, proj], 1), pj2.at[half], pjl.at[half])
        c_s[...] = jnp.zeros_like(c_s)
        h_b[...] = jnp.zeros_like(h_b)
        for task in before(0, gin_a):
            task()

    h, c = h_b[(steps - 1) * rows:], c_s[...]
    h, c = walk(gin_a, h_a, h, c, 0, after(2 * turn_no - 1, h_b) + before(2 * turn_no + 1, gin_b))
    h, c = walk(gin_b, h_b, h, c, 1, after(2 * turn_no, h_a) + before(2 * turn_no + 2, gin_a))
    c_s[...] = c

    @pl.when(turn_no == last_turn)
    def _():
        for task in after(chunks - 1, h_b):
            task()
        swap_with_sibling(part_ref, peer_ref, sems)
        _, base, odd = window(layer_no)
        norm_stage(x_ref, part_ref, peer_ref, window_s, base, odd, valid, normed_ref, scale_ref, next_ref)


def backward_kernel(layer_no, groups, steps, *refs):
    inter = layer_no % 2 == 1
    last_layer = layer_no == 2 * BLOCKS - 1
    g_ref, normed_ref, scale_ref, x_ref, h_ref, coef_ref, flat_ref, *rest = refs
    if last_layer:
        hg_ref, *rest = rest
    if layer_no == 0:
        column_ref, denc_ref, encoder_ref, loss_ref, *rest = rest
    else:
        below_ref, *rest = rest
    (grad_ref,
     wi2, wil, wrw, wrt, pj2, pjl, proj_s, dmx, dh_a, dh_b, dz_a, dz_b, dc_s, awin, aproj, abias,
     dx_ref, peer_ref, sems, window_s, fetch_sem) = rest
    turn_no = pl.program_id(0)
    last_turn = pl.num_programs(0) - 1
    chunks = 2 * pl.num_programs(0)
    length = chunks * steps
    dir_no = lax.rem(lax.axis_index("batch"), 2)
    rows = 2 * HALF_PAD if inter else groups
    valid = HOP * groups

    def before(back_no, dhc):
        chunk_no = chunks - 1 - lax.rem(back_no, chunks)
        positions = times(dir_no, chunk_no, length, steps)

        def outward():
            dms = gather(dmx, inter, groups, positions)
            if inter:
                for side in range(2):
                    found = dot3(dms, pj2[side], pjl[side])
                    for u in range(steps):
                        at = u * rows + side * HALF_PAD
                        dhc[at:at + HALF_PAD] = found[u * HALF_PAD:(u + 1) * HALF_PAD]
            else:
                half = lax.div(positions[0], HOP)
                dhc[...] = dot3(dms, pj2[half], pjl[half])

        return [outward]

    def after(back_no, dzs):
        used = back_no >= 0
        chunk_no = chunks - 1 - lax.rem(back_no + chunks, chunks)
        positions = times(dir_no, chunk_no, length, steps)
        half = 0 if inter else lax.div(positions[0], HOP)
        xs = gather(x_ref, inter, groups, positions)
        at = chunk_no * steps
        hs = h_ref[pl.ds(at, steps)].reshape(steps * rows, UNITS)
        early = h_ref[lax.rem(at + length - 1, length)] * jnp.where(at == 0, 0.0, 1.0)
        hp = jnp.concatenate([early, hs[:(steps - 1) * rows]], 0)
        if inter:
            lhs = [
                jnp.concatenate([xs if side == 0 else pltpu.roll(xs, FILTERS, 1), hp_side], 1)
                for side, hp_side in enumerate(to_sides(inter, steps, hp))
            ]
            lhs = jnp.concatenate(lhs, 0)
        else:
            lhs = jnp.concatenate([jnp.where(half == 0, xs, pltpu.roll(xs, FILTERS, 1)), hp], 1)
        lhs_t = lhs.T
        lhs_hi, lhs_lo = split(lhs_t)

        def gate(q):
            cut = slice(q * UNITS, (q + 1) * UNITS)
            dz = dzs[:, cut]
            abias[0:1, cut] += jnp.sum(dz, 0, keepdims=True)
            if inter:
                dz = jnp.concatenate(to_sides(inter, steps, dz), 0)
            dz_hi, dz_lo = split(dz)
            awin[:, cut] += dot(lhs_hi, dz_hi) + dot(lhs_lo, dz_hi) + dot(lhs_hi, dz_lo)

        def project():
            dms = gather(dmx, inter, groups, positions) * jnp.where(used, 1.0, 0.0)
            if inter:
                aproj[...] += dot_rows3(jnp.concatenate(to_sides(inter, steps, hs), 1), dms)
            else:
                turned = jnp.where(half == 0, dms, pltpu.roll(dms, FILTERS, 1))
                aproj[...] += dot_rows3(hs, turned)

        def inward():
            if inter:
                found = 0.0
                for side, dz_side in enumerate(to_sides(inter, steps, dzs[...])):
                    found = found + dot3(dz_side, wi2[side], wil[side])
                for u in range(steps):
                    dx_ref[stream_rows(inter, groups, positions[u]), :] = found[u * HALF_PAD:(u + 1) * HALF_PAD]
            else:
                found = dot3(dzs[...], wi2[half], wil[half])
                for u in range(steps):
                    here = stream_rows(inter, groups, positions[u])
                    dx_ref[here, :] = dx_ref[here, :] + found[u * groups:(u + 1) * groups]

        return [functools.partial(gate, q) for q in range(4)] + [inward, project]

    def walk(dhc, dzs, dz, dc_next, sub, beside):
        for u in reversed(range(steps)):
            at = sub * steps + u
            hi, lo = split(dz)
            wide = dot(hi, wrw[...])
            dh = wide[:, :UNITS] + wide[:, UNITS:] + dot(lo, wrt[...])
            for task in beside[steps - 1 - u::steps]:
                task()
            dh = dh + dhc[u * rows:(u + 1) * rows]
            dc = dh * coef_ref[at, 1] + dc_next
            dz = jnp.concatenate(
                [dc * coef_ref[at, 2], dc * coef_ref[at, 3], dc * coef_ref[at, 4], dh * coef_ref[at, 0]], 1
            )
            dc_next = dc * coef_ref[at, 5]
            dzs[u * rows:(u + 1) * rows] = dz
        return dz, dc_next

    @pl.when(turn_no == 0)
    def _():
        if layer_no:
            device, barrier = greet_sibling()
            pl.semaphore_signal(barrier, inc=1, device_id=device, device_id_type=pl.DeviceIdType.MESH)
        fetch(flat_ref, layer_no, window_s, fetch_sem).wait()
        dx_ref[...] = jnp.zeros_like(dx_ref)
        _, base, odd = window(layer_no)
        win, wrec, _, proj = load_weights(window_s, base, odd, dir_no, proj_s)
        win_t = win.T
        none = jnp.zeros_like(win_t)
        for half in range(2):
            put_split(jnp.concatenate([win_t, none] if half == 0 else [none, win_t], 1), wi2.at[half], wil.at[half])
        hi, lo = split(wrec.T)
        wrw[...] = jnp.concatenate([hi, lo], 1)
        wrt[...] = hi
        proj_t = proj.T
        none = jnp.zeros_like(proj_t)
        for half in range(2):
            put_split(jnp.concatenate([proj_t, none] if half == 0 else [none, proj_t], 0), pj2.at[half], pjl.at[half])
        dz_b[...] = jnp.zeros_like(dz_b)
        dc_s[...] = jnp.zeros_like(dc_s)
        awin[...] = jnp.zeros_like(awin)
        aproj[...] = jnp.zeros_like(aproj)
        abias[...] = jnp.zeros_like(abias)
        grad_ref[...] = jnp.zeros_like(grad_ref)
        g = g_ref[:valid]
        normed = normed_ref[:valid]
        _, gain, _ = load_vec(window_s, base, odd)
        g_n = g * gain
        total = 2.0 * valid * FILTERS
        mean_one = jnp.sum(g_n) / total
        mean_two = jnp.sum(g_n * normed) / total
        dmixed = scale_ref[0:1] * (g_n - mean_one - normed * mean_two)
        dmx[:valid] = dmixed
        dmx[valid:] = jnp.zeros((dmx.shape[0] - valid, 128), F32)
        lead = jnp.where(dir_no == 0, 1.0, 0.0)

        def fold(array):
            found = lead * jnp.sum(array, 0, keepdims=True)
            return found[:, :FILTERS] + found[:, FILTERS:]

        grad_ref[VEC_ROW:VEC_ROW + 1] = jnp.concatenate([fold(dmixed), fold(g * normed)], 1)
        grad_ref[VEC_ROW + 1:VEC_ROW + 2] = jnp.concatenate([fold(g), jnp.zeros((1, FILTERS), F32)], 1)
        if last_layer:
            grad_ref[LAYER_ROWS:] = hg_ref[...] * lead

        for task in before(0, dh_a):
            task()

    dz, dc_next = dz_b[:rows], dc_s[...]
    dz, dc_next = walk(dh_a, dz_a, dz, dc_next, 1, after(2 * turn_no - 1, dz_b) + before(2 * turn_no + 1, dh_b))
    dz, dc_next = walk(dh_b, dz_b, dz, dc_next, 0, after(2 * turn_no, dz_a) + before(2 * turn_no + 2, dh_a))
    dc_s[...] = dc_next

    @pl.when(turn_no == last_turn)
    def _():
        for task in after(chunks - 1, dz_b):
            task()
        if layer_no:
            swap_with_sibling(dx_ref, peer_ref, sems)
            below_ref[:valid] = g_ref[:valid] + dx_ref[:valid] + peer_ref[:valid]
            below_ref[valid:] = jnp.zeros((below_ref.shape[0] - valid, 128), F32)
        at = SIDE_ROWS * dir_no
        for q in range(4):
            cut = slice(q * UNITS, (q + 1) * UNITS)
            grad_ref[pl.ds(at + q, FILTERS, stride=4), :] = awin[:FILTERS, cut]
            grad_ref[pl.ds(at + 256 + q, UNITS, stride=4), :] = awin[2 * FILTERS:, cut]
            grad_ref[pl.ds(at + 768 + q, 1), :] = abias[0:1, cut]
        proj_s[...] = aproj[:UNITS] + pltpu.roll(aproj[UNITS:], FILTERS, 1) if inter else aproj[...]
        even = proj_s[pl.ds(0, 64, stride=2), :]
        odd_rows = proj_s[pl.ds(1, 64, stride=2), :]
        grad_ref[pl.ds(PROJ_ROWS + 64 * dir_no, 64), :] = jnp.concatenate(
            [even[:, :FILTERS], odd_rows[:, :FILTERS]], 1
        )
        if layer_no == 0:
            lead = jnp.where(dir_no == 0, 1.0, 0.0)
            streams = lead * g_ref[:valid] + dx_ref[:valid]
            column = column_ref[...]
            mix, following = column[:, 0:1], column[:, 1:2]
            raw = mix * encoder_ref[0:1] + following * encoder_ref[1:2]
            group_at = lax.broadcasted_iota(jnp.int32, (valid, FILTERS), 0) % groups
            shifted = jnp.where(group_at == 0, 0.0, pltpu.roll(pltpu.roll(streams, FILTERS, 1), 1, 0)[:, :FILTERS])
            grad_raw = (streams[:, :FILTERS] + shifted + lead * denc_ref[...]) * jax.nn.sigmoid(raw)
            grad_ref[LAYER_ROWS:LAYER_ROWS + 1] = jnp.concatenate(
                [jnp.sum(grad_raw * mix, 0, keepdims=True), jnp.sum(grad_raw * following, 0, keepdims=True)], 1
            )
            grad_ref[LAYER_ROWS + 1:LAYER_ROWS + 2] = loss_ref[0:1] * lead


def head_kernel(groups, sep, stream_ref, column_ref, active_ref, masker_ref, decoder_ref,
                g_ref, hg_ref, denc_ref, loss_ref,
                sig_s, now_s, before_s, slope_s, mk2, mkl, mt2, mtl, dk2, dkl, dt2, dtl, amask, adec, m_low, m_top):
    valid = HOP * groups
    block = 10 * groups
    put_split(masker_ref[...], mk2, mkl)
    put_split(masker_ref[...].T, mt2, mtl)
    put_split(decoder_ref[...], dk2, dkl)
    put_split(decoder_ref[...].T, dt2, dtl)
    amask[...] = jnp.zeros_like(amask)
    adec[...] = jnp.zeros_like(adec)
    active = active_ref[0:1]

    def rows(n):
        return pl.ds(pl.multiple_of(n * block, 8), block)

    def summed_of(n):
        here = sep[rows(n), :]
        group_at = lax.broadcasted_iota(jnp.int32, (block, FILTERS), 0) % groups
        shifted = pltpu.roll(pltpu.roll(here, FILTERS, 1), 1, 0)[:, :FILTERS]
        return here[:, :FILTERS] + jnp.where(group_at == 0, 0.0, shifted)

    def frames_of(n):
        encoded = stream_ref[rows(n), :][:, :FILTERS]
        return jnp.concatenate([encoded, encoded, encoded], 1)

    def ahead(n, carry):
        logits = dot3(summed_of(n), mk2[...], mkl[...])
        sig = jax.nn.sigmoid(logits)
        sig_s[rows(n), :] = sig
        both = dot3(sig * active * frames_of(n), dk2[...], dkl[...])
        now_s[rows(n), :] = both[:, :128]
        before_s[pl.ds(pl.multiple_of(n * block + groups, 8), block), :] = both[:, 128:]
        return carry

    lax.fori_loop(0, HOP // 10, ahead, 0)
    at = lax.broadcasted_iota(jnp.int32, (groups, 128), 0)
    before_s[:groups] = jnp.where(at == 0, 0.0, pltpu.roll(before_s[valid:], 1, 0))

    def losses(n, total):
        column = column_ref[rows(n), :]
        lane = lax.broadcasted_iota(jnp.int32, (block, 128), 1)
        target = jnp.where(lane < SOURCES, column, 0.0)
        kept = jnp.broadcast_to(column[:, SOURCES:SOURCES + 1], (block, 128))
        differ = now_s[rows(n), :] + before_s[rows(n), :] - target
        root = jnp.sqrt(differ * differ + 1.0)
        slope_s[rows(n), :] = kept * differ / root
        return total + jnp.sum(kept * (root - 1.0), 0, keepdims=True)

    total = lax.fori_loop(0, HOP // 10, losses, jnp.zeros((1, 128), F32))
    loss_ref[...] = jnp.broadcast_to(jnp.sum(total, 1, keepdims=True), loss_ref.shape)
    slope_s[valid:] = jnp.where(at == groups - 1, 0.0, pltpu.roll(slope_s[:groups], groups - 1, 0))

    def back(n, carry):
        slopes = jnp.concatenate(
            [slope_s[rows(n), :], slope_s[pl.ds(pl.multiple_of(n * block + groups, 8), block), :]], 1
        )
        sig = sig_s[rows(n), :]
        frames = frames_of(n)
        dmasked = dot3(slopes, dt2[...], dtl[...]) * active
        by_sig = dmasked * sig
        denc_ref[rows(n), :] = (
            by_sig[:, :FILTERS] + by_sig[:, FILTERS:2 * FILTERS] + by_sig[:, 2 * FILTERS:]
        )
        dlogits = by_sig * frames * (1.0 - sig)
        dsummed = dot3(dlogits, mt2[...], mtl[...])
        group_at = lax.broadcasted_iota(jnp.int32, (block, FILTERS), 0) % groups
        shifted = jnp.where(group_at == groups - 1, 0.0, pltpu.roll(dsummed, block - 1, 0))
        g_ref[rows(n), :] = jnp.concatenate([dsummed, shifted], 1)
        amask[...] += dot_rows3(summed_of(n), dlogits)
        adec[...] += dot_rows3(sig * active * frames, slopes)
        return carry

    lax.fori_loop(0, HOP // 10, back, 0)
    g_ref[valid:] = jnp.zeros((g_ref.shape[0] - valid, 128), F32)
    m_low[...] = amask[:, :128]
    m_top[...] = jnp.concatenate([amask[:, 128:], jnp.zeros((FILTERS, FILTERS), F32)], 1)
    low_even, low_odd = m_low[pl.ds(0, 32, stride=2), :], m_low[pl.ds(1, 32, stride=2), :]
    top_even, top_odd = m_top[pl.ds(0, 32, stride=2), :], m_top[pl.ds(1, 32, stride=2), :]
    hg_ref[pl.ds(0, 32, stride=3), :] = low_even
    hg_ref[pl.ds(1, 32, stride=3), :] = jnp.concatenate([top_even[:, :FILTERS], low_odd[:, :FILTERS]], 1)
    hg_ref[pl.ds(2, 32, stride=3), :] = jnp.concatenate([low_odd[:, FILTERS:], top_odd[:, :FILTERS]], 1)
    columns = []
    for tap in range(2):
        found = 0.0
        for j in range(SOURCES):
            found = found + adec[j * FILTERS:(j + 1) * FILTERS, 128 * tap + j:128 * tap + j + 1]
        columns.append(jnp.broadcast_to(found, (FILTERS, 128)))
    lane = lax.broadcasted_iota(jnp.int32, (FILTERS, 128), 1)
    hg_ref[96:HEAD_ROWS] = jnp.where(lane == 0, columns[0], jnp.where(lane == 1, columns[1], 0.0))


def assemble(flat, layers):
    lane = lax.broadcasted_iota(jnp.int32, (FILTERS, 128), 1)
    row = lax.broadcasted_iota(jnp.int32, (FILTERS, 128), 0)
    encoder = jnp.broadcast_to(layers[0][LAYER_ROWS:LAYER_ROWS + 1], (FILTERS, 128))
    first_tap = jnp.sum(jnp.where(lane == row, encoder, 0.0), 1, keepdims=True)
    second_tap = jnp.sum(jnp.where(lane == row + FILTERS, encoder, 0.0), 1, keepdims=True)

    def interleave(a, b):
        return jnp.sum(jnp.where(lane == 2 * row, a, jnp.where(lane == 2 * row + 1, b, 0.0)), 0, keepdims=True)

    flat[0:1] = interleave(first_tap, second_tap)
    for layer_no, ref in enumerate(layers):
        first, inner, odd = window(layer_no)
        base = first + inner
        if odd:
            whole_rows = ref[:LAYER_ROWS - 6]
            turned = pltpu.roll(whole_rows, FILTERS, 1)
            flat[base:base + 1, FILTERS:] = turned[0:1, FILTERS:]
            wide_low = lax.broadcasted_iota(jnp.int32, (LAYER_ROWS - 7, 128), 1) < FILTERS
            flat[base + 1:base + LAYER_ROWS - 6] = jnp.where(wide_low, turned[:-1], turned[1:])
        else:
            flat[base:base + LAYER_ROWS - 6] = ref[:LAYER_ROWS - 6]
    flat[6695:6791] = layers[3][LAYER_ROWS:LAYER_ROWS + 96]
    decoder = layers[3][LAYER_ROWS + 96:LAYER_ROWS + HEAD_ROWS]
    flat[6791:6792] = interleave(decoder[:, 0:1], decoder[:, 1:2])
    flat[6792:] = jnp.zeros((flat.shape[0] - 6792, 128), F32)


def finish_kernel(chips, depths, entries, width, r0, r1, r2, r3, p_ref, m_ref, v_ref,
                  new_ref, half_ref, first_ref, second_ref, stats_ref,
                  flat, pair_in, sent, plane_in, held, depth_in, mine, found, note, depth_notes, notes,
                  pair_sem, plane_sem, depth_sem, spread_sem, note_sem, notes_sem):
    b = lax.axis_index("batch")
    z = lax.axis_index("frames")
    core = lax.rem(b, 2)
    chip = b // 2
    piece = width // depths
    rows = p_ref.shape[0]

    def start(shard):
        return pl.multiple_of(shard * entries // 1024 * 8, 8)

    def send(src, dst, sems, slot, device):
        copy = pltpu.make_async_remote_copy(
            src_ref=src, dst_ref=dst, send_sem=sems.at[0, slot], recv_sem=sems.at[1, slot],
            device_id=device, device_id_type=pl.DeviceIdType.MESH,
        )
        copy.start()
        return copy

    barrier = pltpu.get_barrier_semaphore()
    for step in range(1, 2 * chips):
        pl.semaphore_signal(
            barrier, inc=1, device_id=(lax.rem(b + step, 2 * chips), z), device_id_type=pl.DeviceIdType.MESH
        )
    for step in range(1, depths):
        pl.semaphore_signal(
            barrier, inc=1, device_id=(b, lax.rem(z + step, depths)), device_id_type=pl.DeviceIdType.MESH
        )
    assemble(flat, (r0, r1, r2, r3))
    note[...] = jnp.broadcast_to(r0[LAYER_ROWS + 1:LAYER_ROWS + 2], note.shape)
    pl.semaphore_wait(barrier, 2 * chips - 1 + depths - 1)

    order = list(range(1, chips)) + [0]
    pairs = {}
    for step in order:
        other = 2 * lax.rem(chip + step, chips) + 1 - core
        pairs[step] = send(
            flat.at[pl.ds(start(other), width)], pair_in.at[step], pair_sem, step, (2 * chip + 1 - core, z)
        )
    loss_copies = [
        send(note, depth_notes.at[step - 1], note_sem, step - 1, (b, lax.rem(z + step, depths)))
        for step in range(1, depths)
    ]
    planes = []
    for step in order:
        pairs[step].wait_recv()
        owner = 2 * lax.rem(chip + step, chips) + core
        total = flat[pl.ds(start(owner), width), :] + pair_in[step]
        if step:
            sent[step - 1] = total
            planes.append(send(sent.at[step - 1], plane_in.at[step - 1], plane_sem, step - 1, (owner, z)))
        else:
            held[...] = total
    for step in order:
        pairs[step].wait_send()
    total = held[...]
    for step in range(1, chips):
        planes[step - 1].wait()
        total = total + plane_in[step - 1]
    held[...] = total
    copies = []
    for step in range(1, depths):
        other = lax.rem(z + step, depths)
        copies.append(
            send(held.at[pl.ds(pl.multiple_of(other * piece, 8), piece)], depth_in.at[step - 1], depth_sem, step - 1, (b, other))
        )
    here = pl.ds(pl.multiple_of(z * piece, 8), piece)
    total = held[here, :]
    for step in range(1, depths):
        copies[step - 1].wait()
        total = total + depth_in[step - 1]
    mine[...] = total
    copies = [
        send(mine, found.at[here], spread_sem, step - 1, (b, lax.rem(z + step, depths)))
        for step in range(1, depths)
    ]
    losses = note[...]
    for step in range(1, depths):
        loss_copies[step - 1].wait()
        losses = losses + depth_notes[step - 1]
    for copy in copies:
        copy.wait()
    found[here, :] = mine[...]

    at = b * entries - start(b) * 128
    row_at, lane_at = at // 128, lax.rem(at, 128)
    gradient = found[pl.ds(row_at, rows), :]
    counted = gradient
    if entries % 128:
        lane = lax.broadcasted_iota(jnp.int32, (rows, 128), 1)
        row = lax.broadcasted_iota(jnp.int32, (rows, 128), 0)
        turn = lax.rem(128 - lane_at, 128)
        gradient = jnp.where(
            lane < 128 - lane_at, pltpu.roll(gradient, turn, 1), pltpu.roll(found[pl.ds(row_at + 1, rows), :], turn, 1)
        )
        counted = jnp.where(128 * row + lane < entries, gradient, 0.0)
    squares = jnp.sum(jnp.sum(counted * counted, 0, keepdims=True), 1, keepdims=True)
    lane = lax.broadcasted_iota(jnp.int32, note.shape, 1)
    note[...] = jnp.where(lane == 2, squares, losses)
    copies = [
        send(note, notes.at[b], notes_sem, step - 1, (lax.rem(b + step, 2 * chips), z))
        for step in range(1, 2 * chips)
    ]
    for copy in copies:
        copy.wait()
    notes[b] = note[...]
    totals = notes[0]
    for other in range(1, 2 * chips):
        totals = totals + notes[other]
    count = jnp.sum(jnp.where(lane == 1, totals, 0.0), 1, keepdims=True)[0:1]
    norm = jnp.sqrt(jnp.sum(jnp.where(lane == 2, totals, 0.0), 1, keepdims=True)[0:1]) / count
    stats_ref[...] = jnp.where(lane == 2, norm, totals)
    clipped = gradient / count * (CLIP_AT / jnp.maximum(norm, CLIP_AT))
    new_first = BETA_ONE * m_ref[...] + (1.0 - BETA_ONE) * clipped
    new_second = BETA_TWO * v_ref[...] + (1.0 - BETA_TWO) * clipped * clipped
    step_size = (
        new_first / (1.0 - BETA_ONE**STEP) / (jnp.sqrt(new_second / (1.0 - BETA_TWO**STEP)) + ADAM_EPS)
    )
    params = p_ref[...]
    new_params = params - LEARN_RATE * (step_size + DECAY_RATE * params)
    new_ref[...] = new_params
    half_ref[...] = new_params.astype(BF16)
    first_ref[...] = new_first
    second_ref[...] = new_second


def sizes(inter, groups):
    if inter:
        return groups, 2 * HALF_PAD, 4
    return 2 * HOP, groups, 5


def whole(shape):
    return pl.BlockSpec(shape, lambda j: (0,) * len(shape))


def run_forward(layer_no, groups, stream, flat):
    inter = layer_no % 2 == 1
    length, rows, steps = sizes(inter, groups)
    stream_shape = (HALF_PAD * groups, 128)
    out = [
        (stream_shape, whole(stream_shape)),
        (stream_shape, whole(stream_shape)),
        ((8, 128), whole((8, 128))),
        ((length, rows, UNITS), pl.BlockSpec((2 * steps, rows, UNITS), lambda j: (j, 0, 0))),
        ((length, 6, rows, UNITS), pl.BlockSpec((2 * steps, 6, rows, UNITS), lambda j: (j, 0, 0, 0))),
    ]
    return pl.pallas_call(
        functools.partial(forward_kernel, layer_no, groups, steps),
        grid=(length // (2 * steps),),
        in_specs=[whole(stream_shape), pl.BlockSpec(memory_space=pl.ANY)],
        out_specs=[spec for _, spec in out],
        out_shape=[jax.ShapeDtypeStruct(shape, F32) for shape, _ in out],
        scratch_shapes=[
            pltpu.VMEM((2, 256, GATES), BF16), pltpu.VMEM((2, 128, GATES), BF16),
            pltpu.VMEM((256, GATES), BF16), pltpu.VMEM((128, GATES), BF16),
            pltpu.VMEM((2, 256, 128), BF16), pltpu.VMEM((2, 128, 128), BF16),
            pltpu.VMEM((UNITS, 128), F32),
            pltpu.VMEM((8, GATES), F32),
            pltpu.VMEM((steps * rows, GATES), F32), pltpu.VMEM((steps * rows, GATES), F32),
            pltpu.VMEM((steps * rows, UNITS), F32), pltpu.VMEM((steps * rows, UNITS), F32),
            pltpu.VMEM((rows, UNITS), F32),
            pltpu.VMEM(stream_shape, F32), pltpu.VMEM(stream_shape, F32), pltpu.SemaphoreType.DMA((2,)),
            pltpu.VMEM((WINDOW, 128), F32), pltpu.SemaphoreType.DMA,
        ],
        compiler_params=pltpu.CompilerParams(
            vmem_limit_bytes=VMEM_MAX, collective_id=2 + layer_no, has_side_effects=True
        ),
        name="forward_inter" if inter else "forward_intra",
    )(stream, flat)


def run_backward(layer_no, groups, grad, kept, flat, extra):
    inter = layer_no % 2 == 1
    last_layer = layer_no == 2 * BLOCKS - 1
    length, rows, steps = sizes(inter, groups)
    stream_shape = (HALF_PAD * groups, 128)
    count = length // (2 * steps)
    out = [(LAYER_ROWS + (HEAD_ROWS if last_layer else 0 if layer_no else 8), 128)]
    if layer_no:
        out = [stream_shape] + out
    x, normed, scale, h_all, coef = kept
    remote = dict(collective_id=6 + layer_no, has_side_effects=True) if layer_no else {}
    return pl.pallas_call(
        functools.partial(backward_kernel, layer_no, groups, steps),
        grid=(count,),
        in_specs=[whole(a.shape) for a in (grad, normed, scale, x, h_all)]
        + [pl.BlockSpec((2 * steps, 6, rows, UNITS), lambda j: (count - 1 - j, 0, 0, 0)), pl.BlockSpec(memory_space=pl.ANY)]
        + [whole(a.shape) for a in extra],
        out_specs=[whole(shape) for shape in out],
        out_shape=[jax.ShapeDtypeStruct(shape, F32) for shape in out],
        scratch_shapes=[
            pltpu.VMEM((2, 2 * GATES, 128), BF16), pltpu.VMEM((2, GATES, 128), BF16),
            pltpu.VMEM((GATES, 256), BF16), pltpu.VMEM((GATES, 128), BF16),
            pltpu.VMEM((2, 256, 128), BF16), pltpu.VMEM((2, 128, 128), BF16),
            pltpu.VMEM((UNITS, 128), F32),
            pltpu.VMEM(stream_shape, F32),
            pltpu.VMEM((steps * rows, UNITS), F32), pltpu.VMEM((steps * rows, UNITS), F32),
            pltpu.VMEM((steps * rows, GATES), F32), pltpu.VMEM((steps * rows, GATES), F32),
            pltpu.VMEM((rows, UNITS), F32),
            pltpu.VMEM((256, GATES), F32), pltpu.VMEM((2 * UNITS if inter else UNITS, 128), F32),
            pltpu.VMEM((8, GATES), F32),
            pltpu.VMEM(stream_shape, F32), pltpu.VMEM(stream_shape, F32), pltpu.SemaphoreType.DMA((2,)),
            pltpu.VMEM((WINDOW, 128), F32), pltpu.SemaphoreType.DMA,
        ],
        compiler_params=pltpu.CompilerParams(vmem_limit_bytes=VMEM_MAX, **remote),
        name="backward_inter" if inter else "backward_intra",
    )(grad, normed, scale, x, h_all, coef, flat, *extra)


def run_head(groups, separated, stream, column, active, masker, decoder):
    valid = HOP * groups
    stream_shape = (HALF_PAD * groups, 128)
    out = [stream_shape, (HEAD_ROWS, 128), (valid, FILTERS), (8, 128)]
    wide = SOURCES * FILTERS
    operands = (separated, stream, column, active, masker, decoder)
    return pl.pallas_call(
        functools.partial(head_kernel, groups),
        grid=(1,),
        in_specs=[whole(a.shape) for a in operands],
        out_specs=[whole(shape) for shape in out],
        out_shape=[jax.ShapeDtypeStruct(shape, F32) for shape in out],
        scratch_shapes=[
            pltpu.VMEM((valid, wide), F32), pltpu.VMEM((valid, 128), F32),
            pltpu.VMEM((valid + groups, 128), F32), pltpu.VMEM((valid + groups, 128), F32),
            pltpu.VMEM((2 * FILTERS, wide), BF16), pltpu.VMEM((FILTERS, wide), BF16),
            pltpu.VMEM((2 * wide, FILTERS), BF16), pltpu.VMEM((wide, FILTERS), BF16),
            pltpu.VMEM((2 * wide, 256), BF16), pltpu.VMEM((wide, 256), BF16),
            pltpu.VMEM((512, wide), BF16), pltpu.VMEM((256, wide), BF16),
            pltpu.VMEM((FILTERS, wide), F32), pltpu.VMEM((wide, 256), F32),
            pltpu.VMEM((FILTERS, 128), F32), pltpu.VMEM((FILTERS, 128), F32),
        ],
        compiler_params=pltpu.CompilerParams(vmem_limit_bytes=VMEM_MAX),
        name="head",
    )(*operands)


def run_finish(layers, params, first_moment, second_moment):
    entries = params.shape[0]
    rows = -(-entries // 128)
    depths = lax.axis_size("frames")
    chips = lax.axis_size("batch") // 2
    width = -(-(rows + 8) // (8 * depths)) * 8 * depths
    shards = [
        jnp.pad(a, (0, rows * 128 - entries)).reshape(rows, 128) for a in (params, first_moment, second_moment)
    ]
    out = [((rows, 128), F32), ((rows, 128), BF16), ((rows, 128), F32), ((rows, 128), F32), ((8, 128), F32)]
    vmem = pl.BlockSpec(memory_space=pltpu.VMEM)
    block = (width, 128)
    piece = (width // depths, 128)
    sems = pltpu.SemaphoreType.DMA
    found = pl.pallas_call(
        functools.partial(finish_kernel, chips, depths, entries, width),
        in_specs=[vmem] * 7,
        out_specs=[vmem] * 5,
        out_shape=[jax.ShapeDtypeStruct(shape, dtype) for shape, dtype in out],
        scratch_shapes=[
            pltpu.VMEM((6792 + width, 128), F32),
            pltpu.VMEM((chips,) + block, F32), pltpu.VMEM((chips - 1,) + block, F32),
            pltpu.VMEM((chips - 1,) + block, F32), pltpu.VMEM(block, F32),
            pltpu.VMEM((depths - 1,) + piece, F32), pltpu.VMEM(piece, F32), pltpu.VMEM(block, F32),
            pltpu.VMEM((8, 128), F32), pltpu.VMEM((depths - 1, 8, 128), F32), pltpu.VMEM((2 * chips, 8, 128), F32),
            sems((2, chips)), sems((2, chips - 1)), sems((2, depths - 1)), sems((2, depths - 1)),
            sems((2, depths - 1)), sems((2, 2 * chips - 1)),
        ],
        compiler_params=pltpu.CompilerParams(
            vmem_limit_bytes=VMEM_MAX, collective_id=1, has_side_effects=True
        ),
        name="finish",
    )(*layers, *shards)
    return [a.reshape(-1)[:entries] for a in found[:4]] + [found[4]]


def local(params, first_moment, second_moment, mixture, sources, speakers, lengths):
    flat = lax.all_gather(params, "batch", axis=0, tiled=True)
    items = mixture.shape[0]
    frames_size = lax.axis_size("frames")
    samples = mixture.shape[1] * frames_size
    groups = samples // HOP
    depth = lax.axis_index("frames")
    column = 2 * items
    copies = frames_size // column
    mine = depth // copies
    weight = jnp.where(depth % copies == 0, 1.0, 0.0).astype(F32)
    pairs = [[2 * b, 2 * b + 1] for b in range(lax.axis_size("batch") // 2)]

    signals = jnp.concatenate([mixture[:, None], sources], 1)
    signals = lax.all_gather(signals, "frames", axis=2, tiled=True)
    scalars = jnp.stack([speakers, lengths], 1).astype(F32)
    signals = lax.all_gather(signals, "batch", axis=0, tiled=True, axis_index_groups=pairs)
    scalars = lax.all_gather(scalars, "batch", axis=0, tiled=True, axis_index_groups=pairs)
    signal = lax.dynamic_slice_in_dim(signals, mine, 1, 0)[0]
    scalar = lax.dynamic_slice_in_dim(scalars, mine, 1, 0)[0]
    mix = signal[0]
    following = jnp.concatenate([mix[1:], jnp.zeros((1,), F32)])

    def by_row(array):
        return array.reshape(array.shape[:-1] + (groups, HOP)).swapaxes(-1, -2).reshape(array.shape[:-1] + (groups * HOP,))

    mix_row = by_row(mix)
    follow_row = by_row(following)
    encoder = flat[:2 * FILTERS].reshape(FILTERS, 2)
    raw = mix_row[:, None] * encoder[:, 0] + follow_row[:, None] * encoder[:, 1]
    encoded = jax.nn.softplus(raw)

    def later(array):
        three = array.reshape(HOP, groups, -1)
        return jnp.concatenate([three[:, 1:], jnp.zeros_like(three[:, :1])], 1).reshape(array.shape)

    def earlier(array):
        three = array.reshape(HOP, groups, -1)
        return jnp.concatenate([jnp.zeros_like(three[:, :1]), three[:, :-1]], 1).reshape(array.shape)

    pad = ((0, (HALF_PAD - HOP) * groups), (0, 0))
    stream = jnp.pad(jnp.concatenate([encoded, later(encoded)], 1), pad)
    view = flat.reshape(-1, 128)
    kept = []
    x = stream
    for layer_no in range(2 * BLOCKS):
        after, normed, scale, h_all, coef = run_forward(layer_no, groups, x, view)
        kept.append((x, normed, scale, h_all, coef))
        x = after

    position = by_row(jnp.arange(samples).astype(F32))
    valid = jnp.where(position < scalar[1], 1.0, 0.0) * weight
    active = jnp.where(jnp.arange(SOURCES).astype(F32) < scalar[0], 1.0, 0.0)
    target = by_row(signal[1:]) * active[:, None]
    wide = SOURCES * FILTERS
    masker = flat[-FILTERS * wide - 2 * FILTERS:-2 * FILTERS].reshape(FILTERS, wide)
    decoder = flat[-2 * FILTERS:].reshape(FILTERS, 2)
    column = jnp.pad(jnp.concatenate([target, valid[None]], 0).T, ((0, 0), (0, 124)))
    by_source = jnp.pad(jnp.eye(SOURCES, dtype=F32), ((0, 0), (0, 128 - SOURCES)))
    taps = (by_source[:, None, None, :] * decoder[None, :, :, None]).reshape(wide, 256)
    active_wide = jnp.broadcast_to(jnp.repeat(active, FILTERS)[None], (8, wide))
    grad, head_grads, grad_encoded, loss = run_head(groups, x, stream, column, active_wide, masker, taps)
    lane = jnp.arange(128)
    count_part = jnp.sum(scalars[:, 1]) / frames_size
    loss = jnp.where(lane == 0, loss, jnp.where(lane == 1, count_part, 0.0))
    signal_column = jnp.pad(jnp.stack([mix_row, follow_row], 1), ((0, 0), (0, 126)))
    encoder_rows = jnp.pad(encoder.T, ((0, 6), (0, 0)))
    sums = [None] * (2 * BLOCKS)
    extras = {0: (signal_column, grad_encoded, encoder_rows, loss), 2 * BLOCKS - 1: (head_grads,)}
    for layer_no in reversed(range(2 * BLOCKS)):
        *found, sums[layer_no] = run_backward(
            layer_no, groups, grad, kept[layer_no], view, extras.get(layer_no, ())
        )
        if layer_no:
            grad = found[0]
    *updated, stats = run_finish(sums, params, first_moment, second_moment)
    return (*updated, stats[0, 2], stats[0, :2])


def solution(mesh):
    placed = (
        P("batch"),
        P("batch"),
        P("batch"),
        P("batch", "frames"),
        P("batch", None, "frames"),
        P("batch"),
        P("batch"),
    )
    return jax.shard_map(
        local,
        mesh=mesh,
        in_specs=placed,
        out_specs=(P("batch"), P("batch"), P("batch"), P("batch"), P(), P()),
        check_vma=False,
    )
```

```python
import functools
import math

import jax
import jax.numpy as jnp
from jax import lax
from jax.experimental import pallas as pl
from jax.experimental.pallas import tpu as pltpu
from jax.sharding import PartitionSpec as P

FILTERS = 64
UNITS = 128
HOP = 50
HALF_PAD = 56
SOURCES = 3
BLOCKS = 2
STEP = 5
GATES = 4 * UNITS

HIGHEST = lax.Precision.HIGHEST
NORM_EPS = 1e-08
CLIP_AT = 0.001
BETA_ONE = 0.5
BETA_TWO = 0.5
LEARN_RATE = 0.05
DECAY_RATE = 0.01
ADAM_EPS = 1e-08
F32 = jnp.float32
BF16 = jnp.bfloat16
VMEM_MAX = 60 * 2**20


def split(a):
    hi = a.astype(BF16)
    return hi, (a - hi.astype(F32)).astype(BF16)


def dot(a, b):
    return jnp.dot(a, b, preferred_element_type=F32)


def dot3(a, w_twice, w_low):
    hi, lo = split(a)
    return dot(jnp.concatenate([hi, lo], 1), w_twice) + dot(hi, w_low)


def dot_rows(a, b):
    return lax.dot_general(a, b, (((0,), (0,)), ((), ())), preferred_element_type=F32)


def dot_rows3(a, b):
    a_hi, a_lo = split(a)
    b_hi, b_lo = split(b)
    return dot_rows(a_hi, b_hi) + dot_rows(a_lo, b_hi) + dot_rows(a_hi, b_lo)


SIDE_ROWS = 772
PROJ_ROWS = 2 * SIDE_ROWS
VEC_ROW = PROJ_ROWS + 128
LAYER_ROWS = 1680
HEAD_ROWS = 160
OWN_PROJ = SIDE_ROWS
OWN_VEC = SIDE_ROWS + 64
OWN_EXTRA = SIDE_ROWS + 68
OWN_ROWS = (OWN_EXTRA + 8, OWN_EXTRA, OWN_EXTRA, OWN_EXTRA + HEAD_ROWS)
WINDOW = 1688
TAIL_ROW = 6688
TAIL_ROWS = 104


def window(layer_no):
    at = 2 + 3347 * layer_no
    return at // 16 * 8, at // 2 % 8, at % 2


def pick(ref, base, odd, start, count, stride=1):
    def load(at):
        return ref[pl.ds(at, count, stride=stride), :] if stride > 1 else ref[pl.ds(at, count), :]

    first = load(base + start)
    if not odd:
        return first
    return jnp.concatenate([first[:, 64:], load(base + start + 1)[:, :64]], 1)


def load_weights(ref, base, odd, dir_no, proj_s):
    at = SIDE_ROWS * dir_no
    win = jnp.concatenate([pick(ref, base, odd, at + q, FILTERS, 4) for q in range(4)], 1)
    wrec = jnp.concatenate([pick(ref, base, odd, at + 256 + q, UNITS, 4) for q in range(4)], 1)
    bias = jnp.concatenate([pick(ref, base, odd, at + 768 + q, 1) for q in range(4)], 1)
    pairs = pick(ref, base, odd, PROJ_ROWS + 64 * dir_no, 64)
    proj_s[pl.ds(0, 64, stride=2), :] = pairs
    proj_s[pl.ds(1, 64, stride=2), :] = pltpu.roll(pairs, 64, 1)
    return win, wrec, bias, proj_s[:, :FILTERS]


def load_vec(ref, base, odd):
    first = pick(ref, base, odd, VEC_ROW, 1)
    turned = pltpu.roll(jnp.broadcast_to(first, (8, 128)), 64, 1)[0:1]
    if odd:
        last = ref[base + VEC_ROW + 1:base + VEC_ROW + 2, :]
        last = jnp.concatenate([last[:, 64:], last[:, 64:]], 1)
    else:
        last = ref[base + VEC_ROW + 1:base + VEC_ROW + 2, :]
        last = jnp.concatenate([last[:, :64], last[:, :64]], 1)
    low = lax.broadcasted_iota(jnp.int32, (1, 128), 1) < 64
    return jnp.where(low, first, turned), jnp.where(low, turned, first), last


def put_split(w, twice_ref, low_ref):
    hi, lo = split(w)
    twice_ref[...] = jnp.concatenate([hi, hi], 0)
    low_ref[...] = lo


def times(dir_no, chunk_no, length, steps):
    return [dir_no * (length - 1) + (1 - 2 * dir_no) * (chunk_no * steps + u) for u in range(steps)]


def stream_rows(inter, groups, at):
    if inter:
        return pl.ds(at, HALF_PAD, stride=groups)
    return pl.ds(pl.multiple_of(lax.rem(at, HOP) * groups, 8), groups)


def gather(ref, inter, groups, positions):
    return jnp.concatenate([ref[stream_rows(inter, groups, at), :] for at in positions], 0)


def to_sides(inter, steps, array):
    if not inter:
        return [array]
    three = array.reshape(steps, 2 * HALF_PAD, array.shape[-1])
    return [
        three[:, side * HALF_PAD:(side + 1) * HALF_PAD].reshape(steps * HALF_PAD, array.shape[-1]) for side in range(2)
    ]


SIDE_ROWS = 772
PROJ_ROWS = 2 * SIDE_ROWS
VEC_ROW = PROJ_ROWS + 128
LAYER_ROWS = 1680
HEAD_ROWS = 160
OWN_PROJ = SIDE_ROWS
OWN_VEC = SIDE_ROWS + 64
OWN_EXTRA = SIDE_ROWS + 68
OWN_ROWS = (OWN_EXTRA + 8, OWN_EXTRA, OWN_EXTRA, OWN_EXTRA + HEAD_ROWS)
WINDOW = 1688
TAIL_ROW = 6688
TAIL_ROWS = 104


def window(layer_no):
    at = 2 + 3347 * layer_no
    return at // 16 * 8, at // 2 % 8, at % 2


def pick(ref, base, odd, start, count, stride=1):
    def load(at):
        return ref[pl.ds(at, count, stride=stride), :] if stride > 1 else ref[pl.ds(at, count), :]

    first = load(base + start)
    if not odd:
        return first
    return jnp.concatenate([first[:, 64:], load(base + start + 1)[:, :64]], 1)


def load_weights(ref, base, odd, dir_no, proj_s):
    at = SIDE_ROWS * dir_no
    win = jnp.concatenate([pick(ref, base, odd, at + q, FILTERS, 4) for q in range(4)], 1)
    wrec = jnp.concatenate([pick(ref, base, odd, at + 256 + q, UNITS, 4) for q in range(4)], 1)
    bias = jnp.concatenate([pick(ref, base, odd, at + 768 + q, 1) for q in range(4)], 1)
    pairs = pick(ref, base, odd, PROJ_ROWS + 64 * dir_no, 64)
    proj_s[pl.ds(0, 64, stride=2), :] = pairs
    proj_s[pl.ds(1, 64, stride=2), :] = pltpu.roll(pairs, 64, 1)
    return win, wrec, bias, proj_s[:, :FILTERS]


def load_vec(ref, base, odd):
    first = pick(ref, base, odd, VEC_ROW, 1)
    turned = pltpu.roll(jnp.broadcast_to(first, (8, 128)), 64, 1)[0:1]
    if odd:
        last = ref[base + VEC_ROW + 1:base + VEC_ROW + 2, :]
        last = jnp.concatenate([last[:, 64:], last[:, 64:]], 1)
    else:
        last = ref[base + VEC_ROW + 1:base + VEC_ROW + 2, :]
        last = jnp.concatenate([last[:, :64], last[:, :64]], 1)
    low = lax.broadcasted_iota(jnp.int32, (1, 128), 1) < 64
    return jnp.where(low, first, turned), jnp.where(low, turned, first), last


def put_split(w, twice_ref, low_ref):
    hi, lo = split(w)
    twice_ref[...] = jnp.concatenate([hi, hi], 0)
    low_ref[...] = lo


def place(dir_no, chunk_no, count, steps, inter, groups):
    first = jnp.where(dir_no == 0, chunk_no * steps, (count - 1 - chunk_no) * steps)
    if inter:
        return first, 0, 0
    half = first // HOP
    return first, half, pl.multiple_of((first - HOP * half) * groups, 8)


def norm_stage(prev_ref, pa_ref, pb_ref, flat_ref, base, odd, valid, normed_ref, scale_ref, x_ref):
    offset, gain, shift = load_vec(flat_ref, base, odd)
    mixed = pa_ref[:valid] + pb_ref[:valid] + offset
    total = 2.0 * valid * FILTERS
    mean = jnp.sum(mixed) / total
    spread = jnp.sum(mixed * mixed) / total - mean * mean
    scale = lax.rsqrt(jnp.full((1, 128), spread + NORM_EPS, F32))
    normed = (mixed - mean) * scale
    normed_ref[:valid] = normed
    normed_ref[valid:] = jnp.zeros((normed_ref.shape[0] - valid, 128), F32)
    x_ref[:valid] = prev_ref[:valid] + gain * normed + shift
    x_ref[valid:] = jnp.zeros((x_ref.shape[0] - valid, 128), F32)
    scale_ref[...] = jnp.broadcast_to(scale, scale_ref.shape)


def greet_sibling():
    b = lax.axis_index("batch")
    device = (b + 1 - 2 * lax.rem(b, 2), lax.axis_index("frames"))
    return device, pltpu.get_barrier_semaphore()


def fetch(flat_ref, layer_no, window_s, sem):
    first, _, _ = window(layer_no)
    copy = pltpu.make_async_copy(flat_ref.at[pl.ds(first, WINDOW)], window_s, sem)
    copy.start()
    return copy


def swap_with_sibling(src_ref, dst_ref, sems, greeted=False):
    device, barrier = greet_sibling()
    if not greeted:
        pl.semaphore_wait(barrier, 1)
    copy = pltpu.make_async_remote_copy(
        src_ref=src_ref, dst_ref=dst_ref, send_sem=sems.at[0], recv_sem=sems.at[1],
        device_id=device, device_id_type=pl.DeviceIdType.MESH,
    )
    copy.start()
    return copy


def reduced_rows(rows, chips, depths):
    return -(-rows // (8 * chips * depths)) * 8 * chips * depths


def reducer_scratch(rows, chips, depths):
    quarter = rows // chips
    part = quarter // depths
    sems = pltpu.SemaphoreType.DMA
    return [
        pltpu.VMEM((2, rows, 128), F32), pltpu.VMEM((chips - 1, quarter, 128), F32), pltpu.VMEM((quarter, 128), F32),
        pltpu.VMEM((depths - 1, part, 128), F32), pltpu.VMEM((part, 128), F32), pltpu.VMEM((quarter, 128), F32),
        sems((2, chips - 1)), sems((2, depths - 1)), sems((2, depths - 1)), sems((2, chips - 1)), sems((2, 1)),
    ]


def greet_all(chips, depths):
    b = lax.axis_index("batch")
    z = lax.axis_index("frames")
    barrier = pltpu.get_barrier_semaphore()
    devices = [(b + 1 - 2 * lax.rem(b, 2), z)]
    devices += [(lax.rem(b + 2 * step, 2 * chips), z) for step in range(1, chips)]
    devices += [(b, lax.rem(z + step, depths)) for step in range(1, depths)]
    for device in devices:
        pl.semaphore_signal(barrier, inc=1, device_id=device, device_id_type=pl.DeviceIdType.MESH)
    return barrier, len(devices)


def reducer(src, chips, depths, refs):
    red, plane_in, mine, depth_in, piece, joined, s_plane, s_depth, s_spread, s_gather, s_back = refs
    b = lax.axis_index("batch")
    z = lax.axis_index("frames")
    core = lax.rem(b, 2)
    chip = lax.div(b, 2)
    quarter = mine.shape[0]
    part = piece.shape[0]

    def rows(at, count):
        return pl.ds(pl.multiple_of(at, 8), count)

    def send(src_ref, dst_ref, sems, slot, device):
        return pltpu.make_async_remote_copy(
            src_ref=src_ref, dst_ref=dst_ref, send_sem=sems.at[0, slot], recv_sem=sems.at[1, slot],
            device_id=device, device_id_type=pl.DeviceIdType.MESH,
        )

    over_plane = [(step, (lax.rem(b + 2 * step, 2 * chips), z)) for step in range(1, chips)]
    over_depth = [(step, (b, lax.rem(z + step, depths))) for step in range(1, depths)]
    own = rows(chip * quarter, quarter)
    mine_at = rows(z * part, part)

    def plane():
        return [
            send(src.at[rows(lax.rem(chip + step, chips) * quarter, quarter)], plane_in.at[step - 1], s_plane, step - 1, to)
            for step, to in over_plane
        ]

    def scatter():
        return [
            send(mine.at[rows(lax.rem(z + step, depths) * part, part)], depth_in.at[step - 1], s_depth, step - 1, to)
            for step, to in over_depth
        ]

    def spread():
        return [send(piece, joined.at[mine_at], s_spread, step - 1, to) for step, to in over_depth]

    def gather():
        return [send(joined, red.at[core, own], s_gather, step - 1, to) for step, to in over_plane]

    def back():
        return [send(red.at[core], red.at[core], s_back, 0, (b + 1 - 2 * core, z))]

    def start(copies):
        for copy in copies:
            copy.start()

    def wait(copies):
        for copy in copies:
            copy.wait()

    def first():
        start(plane())

    def third():
        wait(plane())
        total = src[own, :]
        for step in range(1, chips):
            total = total + plane_in[step - 1]
        mine[...] = total
        start(scatter())

    def fourth():
        wait(scatter())
        total = mine[mine_at, :]
        for step in range(1, depths):
            total = total + depth_in[step - 1]
        piece[...] = total
        joined[mine_at, :] = total
        start(spread())

    def fifth():
        wait(spread())
        red[core, own] = joined[...]
        start(gather())

    def sixth():
        wait(gather())
        start(back())

    def last():
        wait(back())

    return [first, third, fourth, fifth, sixth, last]


def forward_kernel(layer_no, groups, steps, *refs):
    inter = layer_no % 2 == 1
    (x_ref, flat_ref,
     next_ref, normed_ref, scale_ref, h_ref, coef_ref,
     wi2, wil, wr2, wrl, pj2, pjl, proj_s, bias_s, gin_a, gin_b, h_a, h_b, c_s, part_ref, peer_ref, sems, window_s, fetch_sem) = refs
    turn_no = pl.program_id(0)
    last_turn = pl.num_programs(0) - 1
    chunks = 2 * pl.num_programs(0)
    length = chunks * steps
    dir_no = lax.rem(lax.axis_index("batch"), 2)
    rows = 2 * HALF_PAD if inter else groups
    valid = HOP * groups

    def before(chunk_no, gin):
        chunk_no = lax.rem(chunk_no, chunks)
        positions = times(dir_no, chunk_no, length, steps)
        xs_hi, xs_lo = split(gather(x_ref, inter, groups, positions))
        both = jnp.concatenate([xs_hi, xs_lo], 1)
        half = 0 if inter else lax.div(positions[0], HOP)

        def gate(q):
            cut = slice(q * UNITS, (q + 1) * UNITS)
            for side in range(2) if inter else [half]:
                found = dot(both, wi2[side, :, cut]) + dot(xs_hi, wil[side, :, cut]) + bias_s[0:1, cut]
                if inter:
                    for u in range(steps):
                        at = u * rows + side * HALF_PAD
                        gin[at:at + HALF_PAD, cut] = found[u * HALF_PAD:(u + 1) * HALF_PAD]
                else:
                    gin[:, cut] = found

        return [functools.partial(gate, q) for q in range(4)]

    def after(chunk_no, hs):
        chunk_no = lax.rem(chunk_no + chunks, chunks)
        positions = times(dir_no, chunk_no, length, steps)

        def project():
            if inter:
                found = 0.0
                for side, part in enumerate(to_sides(inter, steps, hs[...])):
                    found = found + dot3(part, pj2[side], pjl[side])
                for u in range(steps):
                    part_ref[stream_rows(inter, groups, positions[u]), :] = found[u * HALF_PAD:(u + 1) * HALF_PAD]
            else:
                half = lax.div(positions[0], HOP)
                found = dot3(hs[...], pj2[half], pjl[half])
                for u in range(steps):
                    here = stream_rows(inter, groups, positions[u])
                    part_ref[here, :] = part_ref[here, :] + found[u * groups:(u + 1) * groups]

        return [project]

    def walk(gin, hs, h, c, sub, beside):
        for u in range(steps):
            hi, lo = split(h)
            z = dot(jnp.concatenate([hi, lo], 1), wr2[...]) + dot(hi, wrl[...])
            for task in beside[u::steps]:
                task()
            z = z + gin[u * rows:(u + 1) * rows]
            th = jnp.tanh(z)
            ti, tf, g, to = (th[:, q * UNITS:(q + 1) * UNITS] for q in range(4))
            i_g = 0.5 * ti + 0.5
            f_g = 0.5 * tf + 0.5
            o_g = 0.5 * to + 0.5
            c_prev = c
            c = f_g * c + i_g * g
            tc = jnp.tanh(c)
            h = o_g * tc
            at = sub * steps + u
            hs[u * rows:(u + 1) * rows] = h
            h_ref[at] = h
            coef_ref[at, 0] = tc * (0.25 - 0.25 * to * to)
            coef_ref[at, 1] = o_g * (1.0 - tc * tc)
            coef_ref[at, 2] = g * (0.25 - 0.25 * ti * ti)
            coef_ref[at, 3] = c_prev * (0.25 - 0.25 * tf * tf)
            coef_ref[at, 4] = i_g * (1.0 - g * g)
            coef_ref[at, 5] = f_g
        return h, c

    @pl.when(turn_no == 0)
    def _():
        device, barrier = greet_sibling()
        pl.semaphore_signal(barrier, inc=1, device_id=device, device_id_type=pl.DeviceIdType.MESH)
        fetch(flat_ref, layer_no, window_s, fetch_sem).wait()
        part_ref[...] = jnp.zeros_like(part_ref)
        column = lax.broadcasted_iota(jnp.int32, (1, GATES), 1)
        scaling = jnp.where((column >= 2 * UNITS) & (column < 3 * UNITS), 1.0, 0.5)
        _, base, odd = window(layer_no)
        win, wrec, bias, proj = load_weights(window_s, base, odd, dir_no, proj_s)
        win = win * scaling
        none = jnp.zeros_like(win)
        for half in range(2):
            put_split(jnp.concatenate([win, none] if half == 0 else [none, win], 0), wi2.at[half], wil.at[half])
        put_split(wrec * scaling, wr2, wrl)
        bias_s[...] = jnp.broadcast_to(bias * scaling, bias_s.shape)
        none = jnp.zeros_like(proj)
        for half in range(2):
            put_split(jnp.concatenate([proj, none] if half == 0 else [none, proj], 1), pj2.at[half], pjl.at[half])
        c_s[...] = jnp.zeros_like(c_s)
        h_b[...] = jnp.zeros_like(h_b)
        for task in before(0, gin_a):
            task()

    h, c = h_b[(steps - 1) * rows:], c_s[...]
    h, c = walk(gin_a, h_a, h, c, 0, after(2 * turn_no - 1, h_b) + before(2 * turn_no + 1, gin_b))
    h, c = walk(gin_b, h_b, h, c, 1, after(2 * turn_no, h_a) + before(2 * turn_no + 2, gin_a))
    c_s[...] = c

    @pl.when(turn_no == last_turn)
    def _():
        for task in after(chunks - 1, h_b):
            task()
        swap_with_sibling(part_ref, peer_ref, sems).wait()
        _, base, odd = window(layer_no)
        norm_stage(x_ref, part_ref, peer_ref, window_s, base, odd, valid, normed_ref, scale_ref, next_ref)


def backward_kernel(layer_no, groups, steps, chips, depths, *refs):
    inter = layer_no % 2 == 1
    last_layer = layer_no == 2 * BLOCKS - 1
    g_ref, normed_ref, scale_ref, x_ref, h_ref, coef_ref, flat_ref, *rest = refs
    if last_layer:
        hg_ref, *rest = rest
    if layer_no == 0:
        column_ref, denc_ref, encoder_ref, loss_ref, *rest = rest
    if not last_layer:
        upper_ref, *rest = rest
    if layer_no:
        below_ref, *rest = rest
    if not last_layer:
        red_ref, *rest = rest
    (grad_ref,
     wi2, wil, wrw, wrt, pj2, pjl, proj_s, dmx, dh_a, dh_b, dz_a, dz_b, dc_s, awin, aproj, abias,
     dx_ref, peer_ref, sems, window_s, fetch_sem, *rest) = rest
    stages = [] if last_layer else reducer(upper_ref, chips, depths, rest)
    turn_no = pl.program_id(0)
    last_turn = pl.num_programs(0) - 1
    chunks = 2 * pl.num_programs(0)
    length = chunks * steps
    dir_no = lax.rem(lax.axis_index("batch"), 2)
    rows = 2 * HALF_PAD if inter else groups
    valid = HOP * groups

    def before(back_no, dhc):
        chunk_no = chunks - 1 - lax.rem(back_no, chunks)
        positions = times(dir_no, chunk_no, length, steps)

        def outward():
            dms = gather(dmx, inter, groups, positions)
            if inter:
                for side in range(2):
                    found = dot3(dms, pj2[side], pjl[side])
                    for u in range(steps):
                        at = u * rows + side * HALF_PAD
                        dhc[at:at + HALF_PAD] = found[u * HALF_PAD:(u + 1) * HALF_PAD]
            else:
                half = lax.div(positions[0], HOP)
                dhc[...] = dot3(dms, pj2[half], pjl[half])

        return [outward]

    def after(back_no, dzs):
        used = back_no >= 0
        chunk_no = chunks - 1 - lax.rem(back_no + chunks, chunks)
        positions = times(dir_no, chunk_no, length, steps)
        half = 0 if inter else lax.div(positions[0], HOP)
        xs = gather(x_ref, inter, groups, positions)
        at = chunk_no * steps
        hs = h_ref[pl.ds(at, steps)].reshape(steps * rows, UNITS)
        early = h_ref[lax.rem(at + length - 1, length)] * jnp.where(at == 0, 0.0, 1.0)
        hp = jnp.concatenate([early, hs[:(steps - 1) * rows]], 0)
        if inter:
            lhs = [
                jnp.concatenate([xs if side == 0 else pltpu.roll(xs, FILTERS, 1), hp_side], 1)
                for side, hp_side in enumerate(to_sides(inter, steps, hp))
            ]
            lhs = jnp.concatenate(lhs, 0)
        else:
            lhs = jnp.concatenate([jnp.where(half == 0, xs, pltpu.roll(xs, FILTERS, 1)), hp], 1)
        lhs_t = lhs.T
        lhs_hi, lhs_lo = split(lhs_t)

        def gate(q):
            cut = slice(q * UNITS, (q + 1) * UNITS)
            dz = dzs[:, cut]
            abias[0:1, cut] += jnp.sum(dz, 0, keepdims=True)
            if inter:
                dz = jnp.concatenate(to_sides(inter, steps, dz), 0)
            dz_hi, dz_lo = split(dz)
            awin[:, cut] += dot(lhs_hi, dz_hi) + dot(lhs_lo, dz_hi) + dot(lhs_hi, dz_lo)

        def project():
            dms = gather(dmx, inter, groups, positions) * jnp.where(used, 1.0, 0.0)
            if inter:
                aproj[...] += dot_rows3(jnp.concatenate(to_sides(inter, steps, hs), 1), dms)
            else:
                turned = jnp.where(half == 0, dms, pltpu.roll(dms, FILTERS, 1))
                aproj[...] += dot_rows3(hs, turned)

        def inward():
            if inter:
                found = 0.0
                for side, dz_side in enumerate(to_sides(inter, steps, dzs[...])):
                    found = found + dot3(dz_side, wi2[side], wil[side])
                for u in range(steps):
                    dx_ref[stream_rows(inter, groups, positions[u]), :] = found[u * HALF_PAD:(u + 1) * HALF_PAD]
            else:
                found = dot3(dzs[...], wi2[half], wil[half])
                for u in range(steps):
                    here = stream_rows(inter, groups, positions[u])
                    dx_ref[here, :] = dx_ref[here, :] + found[u * groups:(u + 1) * groups]

        return [functools.partial(gate, q) for q in range(4)] + [inward, project]

    def walk(dhc, dzs, dz, dc_next, sub, beside):
        for u in reversed(range(steps)):
            at = sub * steps + u
            hi, lo = split(dz)
            wide = dot(hi, wrw[...])
            dh = wide[:, :UNITS] + wide[:, UNITS:] + dot(lo, wrt[...])
            for task in beside[steps - 1 - u::steps]:
                task()
            dh = dh + dhc[u * rows:(u + 1) * rows]
            dc = dh * coef_ref[at, 1] + dc_next
            dz = jnp.concatenate(
                [dc * coef_ref[at, 2], dc * coef_ref[at, 3], dc * coef_ref[at, 4], dh * coef_ref[at, 0]], 1
            )
            dc_next = dc * coef_ref[at, 5]
            dzs[u * rows:(u + 1) * rows] = dz
        return dz, dc_next

    @pl.when(turn_no == 0)
    def _():
        if last_layer:
            device, barrier = greet_sibling()
            pl.semaphore_signal(barrier, inc=1, device_id=device, device_id_type=pl.DeviceIdType.MESH)
        else:
            barrier, count = greet_all(chips, depths)
            pl.semaphore_wait(barrier, count)
            stages[0]()
        fetch(flat_ref, layer_no, window_s, fetch_sem).wait()
        dx_ref[...] = jnp.zeros_like(dx_ref)
        _, base, odd = window(layer_no)
        win, wrec, _, proj = load_weights(window_s, base, odd, dir_no, proj_s)
        win_t = win.T
        none = jnp.zeros_like(win_t)
        for half in range(2):
            put_split(jnp.concatenate([win_t, none] if half == 0 else [none, win_t], 1), wi2.at[half], wil.at[half])
        hi, lo = split(wrec.T)
        wrw[...] = jnp.concatenate([hi, lo], 1)
        wrt[...] = hi
        proj_t = proj.T
        none = jnp.zeros_like(proj_t)
        for half in range(2):
            put_split(jnp.concatenate([proj_t, none] if half == 0 else [none, proj_t], 0), pj2.at[half], pjl.at[half])
        dz_b[...] = jnp.zeros_like(dz_b)
        dc_s[...] = jnp.zeros_like(dc_s)
        awin[...] = jnp.zeros_like(awin)
        aproj[...] = jnp.zeros_like(aproj)
        abias[...] = jnp.zeros_like(abias)
        grad_ref[...] = jnp.zeros_like(grad_ref)
        g = g_ref[:valid]
        normed = normed_ref[:valid]
        _, gain, _ = load_vec(window_s, base, odd)
        g_n = g * gain
        total = 2.0 * valid * FILTERS
        mean_one = jnp.sum(g_n) / total
        mean_two = jnp.sum(g_n * normed) / total
        dmixed = scale_ref[0:1] * (g_n - mean_one - normed * mean_two)
        dmx[:valid] = dmixed
        dmx[valid:] = jnp.zeros((dmx.shape[0] - valid, 128), F32)
        lead = jnp.where(dir_no == 0, 1.0, 0.0)

        def fold(array):
            found = lead * jnp.sum(array, 0, keepdims=True)
            return found[:, :FILTERS] + found[:, FILTERS:]

        grad_ref[OWN_VEC:OWN_VEC + 1] = jnp.concatenate([fold(dmixed), fold(g * normed)], 1)
        grad_ref[OWN_VEC + 1:OWN_VEC + 2] = jnp.concatenate([fold(g), jnp.zeros((1, FILTERS), F32)], 1)
        if last_layer:
            grad_ref[OWN_EXTRA:OWN_EXTRA + HEAD_ROWS] = hg_ref[...] * lead

        for task in before(0, dh_a):
            task()

    for stage, at in zip(stages[1:], (2, 3, 4) if inter else (3, 5, 6, 9)):
        pl.when(turn_no == at)(stage)

    dz, dc_next = dz_b[:rows], dc_s[...]
    dz, dc_next = walk(dh_a, dz_a, dz, dc_next, 1, after(2 * turn_no - 1, dz_b) + before(2 * turn_no + 1, dh_b))
    dz, dc_next = walk(dh_b, dz_b, dz, dc_next, 0, after(2 * turn_no, dz_a) + before(2 * turn_no + 2, dh_a))
    dc_s[...] = dc_next

    @pl.when(turn_no == last_turn)
    def _():
        for task in after(chunks - 1, dz_b):
            task()
        if layer_no:
            swap = swap_with_sibling(dx_ref, peer_ref, sems, not last_layer)
        for stage in stages[4:] if inter else stages[5:]:
            stage()
        if not last_layer:
            red_ref[...] = rest[0][...]
        if layer_no:
            swap.wait()
            below_ref[:valid] = g_ref[:valid] + dx_ref[:valid] + peer_ref[:valid]
            below_ref[valid:] = jnp.zeros((below_ref.shape[0] - valid, 128), F32)
        for q in range(4):
            cut = slice(q * UNITS, (q + 1) * UNITS)
            grad_ref[pl.ds(q, FILTERS, stride=4), :] = awin[:FILTERS, cut]
            grad_ref[pl.ds(256 + q, UNITS, stride=4), :] = awin[2 * FILTERS:, cut]
            grad_ref[768 + q:769 + q, :] = abias[0:1, cut]
        proj_s[...] = aproj[:UNITS] + pltpu.roll(aproj[UNITS:], FILTERS, 1) if inter else aproj[...]
        even = proj_s[pl.ds(0, 64, stride=2), :]
        odd_rows = proj_s[pl.ds(1, 64, stride=2), :]
        grad_ref[OWN_PROJ:OWN_VEC, :] = jnp.concatenate(
            [even[:, :FILTERS], odd_rows[:, :FILTERS]], 1
        )
        if layer_no == 0:
            lead = jnp.where(dir_no == 0, 1.0, 0.0)
            streams = lead * g_ref[:valid] + dx_ref[:valid]
            column = column_ref[...]
            mix, following = column[:, 4:5], column[:, 5:6]
            raw = mix * encoder_ref[0:1, :FILTERS] + following * encoder_ref[1:2, :FILTERS]
            group_at = lax.broadcasted_iota(jnp.int32, (valid, FILTERS), 0) % groups
            shifted = jnp.where(group_at == 0, 0.0, pltpu.roll(pltpu.roll(streams, FILTERS, 1), 1, 0)[:, :FILTERS])
            grad_raw = (streams[:, :FILTERS] + shifted + lead * denc_ref[...]) * jax.nn.sigmoid(raw)
            grad_ref[OWN_EXTRA:OWN_EXTRA + 1] = jnp.concatenate(
                [jnp.sum(grad_raw * mix, 0, keepdims=True), jnp.sum(grad_raw * following, 0, keepdims=True)], 1
            )
            grad_ref[OWN_EXTRA + 1:OWN_EXTRA + 2] = loss_ref[0:1] * lead


def head_kernel(groups, sep, stream_ref, column_ref, active_ref, note_ref, flat_ref,
                g_ref, hg_ref, denc_ref, loss_ref,
                sig_s, now_s, before_s, slope_s, mk2, mkl, mt2, mtl, dk2, dkl, dt2, dtl, amask, adec, m_low, m_top, tail_s, tail_sem):
    valid = HOP * groups
    block = 10 * groups
    tail = pltpu.make_async_copy(flat_ref.at[pl.ds(TAIL_ROW, TAIL_ROWS)], tail_s, tail_sem)
    tail.start()
    tail.wait()
    first, second, third = (tail_s[pl.ds(6695 - TAIL_ROW + n, 32, stride=3), :] for n in range(3))
    m_low[pl.ds(0, 32, stride=2), :] = first
    m_low[pl.ds(1, 32, stride=2), :] = jnp.concatenate([second[:, FILTERS:], third[:, :FILTERS]], 1)
    m_top[pl.ds(0, 32, stride=2), :] = second
    m_top[pl.ds(1, 32, stride=2), :] = pltpu.roll(third, FILTERS, 1)
    masker = jnp.concatenate([m_low[...], m_top[:, :FILTERS]], 1)
    taps = tail_s[6791 - TAIL_ROW:6792 - TAIL_ROW]
    lane_at = lax.broadcasted_iota(jnp.int32, (FILTERS, 128), 1)
    row_at = lax.broadcasted_iota(jnp.int32, (FILTERS, 128), 0)
    upright = [
        jnp.sum(jnp.where(lane_at == 2 * row_at + tap, taps, 0.0), 1, keepdims=True) for tap in range(2)
    ]
    decoder = jnp.concatenate(
        [
            jnp.concatenate([jnp.where(lane_at == j, column, 0.0) for column in upright], 1)
            for j in range(SOURCES)
        ],
        0,
    )
    put_split(masker, mk2, mkl)
    put_split(masker.T, mt2, mtl)
    put_split(decoder, dk2, dkl)
    put_split(decoder.T, dt2, dtl)
    amask[...] = jnp.zeros_like(amask)
    adec[...] = jnp.zeros_like(adec)
    active = active_ref[0:1]

    def rows(n):
        return pl.ds(pl.multiple_of(n * block, 8), block)

    def summed_of(n):
        here = sep[rows(n), :]
        group_at = lax.broadcasted_iota(jnp.int32, (block, FILTERS), 0) % groups
        shifted = pltpu.roll(pltpu.roll(here, FILTERS, 1), 1, 0)[:, :FILTERS]
        return here[:, :FILTERS] + jnp.where(group_at == 0, 0.0, shifted)

    def frames_of(n):
        encoded = stream_ref[rows(n), :][:, :FILTERS]
        return jnp.concatenate([encoded, encoded, encoded], 1)

    def ahead(n, carry):
        logits = dot3(summed_of(n), mk2[...], mkl[...])
        sig = jax.nn.sigmoid(logits)
        sig_s[rows(n), :] = sig
        both = dot3(sig * active * frames_of(n), dk2[...], dkl[...])
        now_s[rows(n), :] = both[:, :128]
        before_s[pl.ds(pl.multiple_of(n * block + groups, 8), block), :] = both[:, 128:]
        return carry

    lax.fori_loop(0, HOP // 10, ahead, 0)
    at = lax.broadcasted_iota(jnp.int32, (groups, 128), 0)
    before_s[:groups] = jnp.where(at == 0, 0.0, pltpu.roll(before_s[valid:], 1, 0))

    def losses(n, total):
        column = column_ref[rows(n), :]
        lane = lax.broadcasted_iota(jnp.int32, (block, 128), 1)
        target = jnp.where(lane < SOURCES, column, 0.0)
        kept = jnp.broadcast_to(column[:, SOURCES:SOURCES + 1], (block, 128))
        differ = now_s[rows(n), :] + before_s[rows(n), :] - target
        root = jnp.sqrt(differ * differ + 1.0)
        slope_s[rows(n), :] = kept * differ / root
        return total + jnp.sum(kept * (root - 1.0), 0, keepdims=True)

    total = lax.fori_loop(0, HOP // 10, losses, jnp.zeros((1, 128), F32))
    first_lane = lax.broadcasted_iota(jnp.int32, (8, 128), 1) == 0
    loss_ref[...] = jnp.where(first_lane, jnp.sum(total, 1, keepdims=True), note_ref[...])
    slope_s[valid:] = jnp.where(at == groups - 1, 0.0, pltpu.roll(slope_s[:groups], groups - 1, 0))

    def back(n, carry):
        slopes = jnp.concatenate(
            [slope_s[rows(n), :], slope_s[pl.ds(pl.multiple_of(n * block + groups, 8), block), :]], 1
        )
        sig = sig_s[rows(n), :]
        frames = frames_of(n)
        dmasked = dot3(slopes, dt2[...], dtl[...]) * active
        by_sig = dmasked * sig
        denc_ref[rows(n), :] = (
            by_sig[:, :FILTERS] + by_sig[:, FILTERS:2 * FILTERS] + by_sig[:, 2 * FILTERS:]
        )
        dlogits = by_sig * frames * (1.0 - sig)
        dsummed = dot3(dlogits, mt2[...], mtl[...])
        group_at = lax.broadcasted_iota(jnp.int32, (block, FILTERS), 0) % groups
        shifted = jnp.where(group_at == groups - 1, 0.0, pltpu.roll(dsummed, block - 1, 0))
        g_ref[rows(n), :] = jnp.concatenate([dsummed, shifted], 1)
        amask[...] += dot_rows3(summed_of(n), dlogits)
        adec[...] += dot_rows3(sig * active * frames, slopes)
        return carry

    lax.fori_loop(0, HOP // 10, back, 0)
    g_ref[valid:] = jnp.zeros((g_ref.shape[0] - valid, 128), F32)
    m_low[...] = amask[:, :128]
    m_top[...] = jnp.concatenate([amask[:, 128:], jnp.zeros((FILTERS, FILTERS), F32)], 1)
    low_even, low_odd = m_low[pl.ds(0, 32, stride=2), :], m_low[pl.ds(1, 32, stride=2), :]
    top_even, top_odd = m_top[pl.ds(0, 32, stride=2), :], m_top[pl.ds(1, 32, stride=2), :]
    hg_ref[pl.ds(0, 32, stride=3), :] = low_even
    hg_ref[pl.ds(1, 32, stride=3), :] = jnp.concatenate([top_even[:, :FILTERS], low_odd[:, :FILTERS]], 1)
    hg_ref[pl.ds(2, 32, stride=3), :] = jnp.concatenate([low_odd[:, FILTERS:], top_odd[:, :FILTERS]], 1)
    columns = []
    for tap in range(2):
        found = 0.0
        for j in range(SOURCES):
            found = found + adec[j * FILTERS:(j + 1) * FILTERS, 128 * tap + j:128 * tap + j + 1]
        columns.append(jnp.broadcast_to(found, (FILTERS, 128)))
    lane = lax.broadcasted_iota(jnp.int32, (FILTERS, 128), 1)
    hg_ref[96:HEAD_ROWS] = jnp.where(lane == 0, columns[0], jnp.where(lane == 1, columns[1], 0.0))


def assemble(flat, layers):
    lane = lax.broadcasted_iota(jnp.int32, (FILTERS, 128), 1)
    row = lax.broadcasted_iota(jnp.int32, (FILTERS, 128), 0)

    def interleave(a, b):
        return jnp.sum(jnp.where(lane == 2 * row, a, jnp.where(lane == 2 * row + 1, b, 0.0)), 0, keepdims=True)

    for layer_no, ref in enumerate(layers):
        if ref is None:
            continue
        first, inner, odd = window(layer_no)
        at = first + inner
        parts = [(ref[0, :OWN_PROJ], False), (ref[1, :OWN_PROJ], False), (ref[0, OWN_PROJ:OWN_VEC], False)]
        parts += [(ref[1, OWN_PROJ:OWN_VEC], False), (ref[0, OWN_VEC:OWN_VEC + 2], True)]
        for rows, ends in parts:
            count = rows.shape[0]
            if odd:
                turned = pltpu.roll(rows, FILTERS, 1) if count >= 8 else jnp.concatenate(
                    [rows[:, FILTERS:], rows[:, :FILTERS]], 1
                )
                wide_low = lax.broadcasted_iota(jnp.int32, (count - 1, 128), 1) < FILTERS
                flat[at:at + 1, FILTERS:] = turned[0:1, FILTERS:]
                flat[at + 1:at + count] = jnp.where(wide_low, turned[:-1], turned[1:])
                if not ends:
                    flat[at + count:at + count + 1, :FILTERS] = turned[count - 1:, :FILTERS]
            elif ends:
                flat[at:at + 1] = rows[0:1]
                flat[at + 1:at + 2, :FILTERS] = rows[1:2, :FILTERS]
            else:
                flat[at:at + count] = rows
            at += count
        if layer_no == 0:
            encoder = ref[0, OWN_EXTRA:OWN_EXTRA + 1] + ref[1, OWN_EXTRA:OWN_EXTRA + 1]
            encoder = jnp.broadcast_to(encoder, (FILTERS, 128))
            first_tap = jnp.sum(jnp.where(lane == row, encoder, 0.0), 1, keepdims=True)
            second_tap = jnp.sum(jnp.where(lane == row + FILTERS, encoder, 0.0), 1, keepdims=True)
            flat[0:1] = interleave(first_tap, second_tap)
        if layer_no == 2 * BLOCKS - 1:
            flat[6695:6791] = ref[0, OWN_EXTRA:OWN_EXTRA + 96]
            decoder = ref[0, OWN_EXTRA + 96:OWN_EXTRA + HEAD_ROWS]
            flat[6791:6792] = interleave(decoder[:, 0:1], decoder[:, 1:2])
            flat[6792:] = jnp.zeros((flat.shape[0] - 6792, 128), F32)


def finish_kernel(chips, depths, entries, own_ref, r1, r2, r3, grad_ref, note_ref, flat, b1, b2, b3, sems, *rest):
    b = lax.axis_index("batch")
    barrier, count = greet_all(chips, depths)
    pairs = ((r1, b1), (r2, b2), (r3, b3))
    fetches = [pltpu.make_async_copy(src, dst, sems.at[n]) for n, (src, dst) in enumerate(pairs)]
    for copy in fetches:
        copy.start()
    pl.semaphore_wait(barrier, count)
    stages = reducer(own_ref, chips, depths, rest)
    stages[0]()
    for copy in fetches:
        copy.wait()
    assemble(flat, (None, b1, b2, b3))
    for stage in stages[1:]:
        stage()
    r0 = rest[0]
    assemble(flat, (r0, None, None, None))
    note_ref[...] = jnp.zeros_like(note_ref)
    squares = jnp.sum(jnp.sum(flat[...] * flat[...], 0, keepdims=True), 1, keepdims=True)
    lane = lax.broadcasted_iota(jnp.int32, (1, 128), 1)
    note_ref[0:1] = jnp.where(lane == 2, squares, r0[0, OWN_EXTRA + 1:OWN_EXTRA + 2])
    rows = grad_ref.shape[0]
    row_at, lane_at = lax.div(b * entries, 128), lax.rem(b * entries, 128)
    gradient = flat[pl.ds(row_at, rows), :]
    if entries % 128:
        lane = lax.broadcasted_iota(jnp.int32, (rows, 128), 1)
        turn = lax.rem(128 - lane_at, 128)
        gradient = jnp.where(
            lane < 128 - lane_at, pltpu.roll(gradient, turn, 1), pltpu.roll(flat[pl.ds(row_at + 1, rows), :], turn, 1)
        )
    grad_ref[...] = gradient


def update_kernel(grad_ref, note_ref, p_ref, m_ref, v_ref, new_ref, half_ref, first_ref, second_ref, norm_ref, loss_ref):
    rows = grad_ref.shape[0]
    note = note_ref[0:1]
    lane = lax.broadcasted_iota(jnp.int32, (1, 128), 1)
    count = jnp.sum(jnp.where(lane == 1, note, 0.0), 1, keepdims=True)
    norm = jnp.sqrt(jnp.sum(jnp.where(lane == 2, note, 0.0), 1, keepdims=True)) / count
    norm_ref[0] = norm[0, 0]
    loss_ref[0] = note[0, 0]
    loss_ref[1] = note[0, 1]
    clipped = grad_ref[...] / count * (CLIP_AT / jnp.maximum(norm, CLIP_AT))
    new_first = BETA_ONE * m_ref[...].reshape(rows, 128) + (1.0 - BETA_ONE) * clipped
    new_second = BETA_TWO * v_ref[...].reshape(rows, 128) + (1.0 - BETA_TWO) * clipped * clipped
    step_size = (
        new_first / (1.0 - BETA_ONE**STEP) / (jnp.sqrt(new_second / (1.0 - BETA_TWO**STEP)) + ADAM_EPS)
    )
    params = p_ref[...].reshape(rows, 128)
    new_params = params - LEARN_RATE * (step_size + DECAY_RATE * params)
    new_ref[...] = new_params.reshape(new_ref.shape)
    half_ref[...] = new_params.astype(BF16).reshape(half_ref.shape)
    first_ref[...] = new_first.reshape(first_ref.shape)
    second_ref[...] = new_second.reshape(second_ref.shape)


def start_kernel(chips, depths, items, groups, gathers, p_ref, mail_ref, *refs):
    if gathers:
        flat_ref, *refs = refs
    else:
        flat_ref = p_ref
    (stream_ref, column_ref, active_ref, encoder_ref, note_ref,
     inbox, planes, plane_sem, pair_sem, own_sem, mail_sem) = refs
    b = lax.axis_index("batch")
    z = lax.axis_index("frames")
    core = lax.rem(b, 2)
    chip = lax.div(b, 2)
    sibling = (b + 1 - 2 * core, z)
    entries = p_ref.shape[0]
    copies = depths // (2 * items)
    share = groups // depths
    valid = HOP * groups
    mail_rows = mail_ref.shape[0] // items
    mesh = pl.DeviceIdType.MESH

    barrier = pltpu.get_barrier_semaphore()
    for step in range(1, chips):
        pl.semaphore_signal(barrier, inc=1, device_id=(lax.rem(b + 2 * step, 2 * chips), z), device_id_type=mesh)
    for step in range(1, depths):
        pl.semaphore_signal(barrier, inc=1, device_id=(b, lax.rem(z + step, depths)), device_id_type=mesh)
    for step in range(depths):
        pl.semaphore_signal(barrier, inc=1, device_id=(sibling[0], lax.rem(z + step, depths)), device_id_type=mesh)
    pl.semaphore_wait(barrier, chips - 1 + 2 * depths - 1)

    def shard(at):
        return flat_ref.at[pl.ds(pl.multiple_of(at * entries, 128), entries)]

    def send(src, dst, sems, slot, device):
        return pltpu.make_async_remote_copy(
            src_ref=src, dst_ref=dst, send_sem=sems.at[0, slot], recv_sem=sems.at[1, slot],
            device_id=device, device_id_type=mesh,
        )

    if gathers:
        across = [
            send(p_ref, shard(b), plane_sem, step - 1, (lax.rem(b + 2 * step, 2 * chips), z))
            for step in range(1, chips)
        ]
        for copy in across:
            copy.start()
        beside = [send(p_ref, shard(b), pair_sem, 0, sibling)]
        beside[0].start()
        own = pltpu.make_async_copy(p_ref, shard(b), own_sem)
        own.start()
    letters = []
    for item in range(items):
        for other in range(2):
            for copy_no in range(copies):
                depth = (items * core + item) * copies + copy_no
                here = (core == other) & (z == depth)
                src = mail_ref.at[pl.ds(item * mail_rows, mail_rows)]
                far = pltpu.make_async_remote_copy(
                    src_ref=src, dst_ref=inbox.at[z], send_sem=mail_sem.at[1, len(letters)], recv_sem=mail_sem.at[0, z],
                    device_id=(2 * chip + other, depth), device_id_type=mesh,
                )
                near = pltpu.make_async_copy(src, inbox.at[z], mail_sem.at[0, z])

                @pl.when(here)
                def _():
                    near.start()

                @pl.when(jnp.logical_not(here))
                def _():
                    far.start()

                letters.append((here, far))
    for depth in range(depths):
        pltpu.make_async_copy(inbox.at[depth], inbox.at[depth], mail_sem.at[0, depth]).wait()
    for here, far in letters:
        @pl.when(jnp.logical_not(here))
        def _():
            far.wait_send()

    for signal in range(1 + SOURCES):
        planes[signal] = jnp.concatenate(
            [inbox[depth, signal * share:(signal + 1) * share] for depth in range(depths)], 0
        )
    facts = inbox[0, (1 + SOURCES) * share:(1 + SOURCES) * share + 1]
    speakers, length = facts[:, 0:1], facts[:, 1:2]
    whole_item = jnp.where(lax.rem(z, copies) == 0, 1.0, 0.0)
    lead = jnp.where(core == 0, whole_item, 0.0)
    lane = lax.broadcasted_iota(jnp.int32, (groups, 128), 1)
    group = lax.broadcasted_iota(jnp.int32, (groups, 128), 0)
    first_lane = lane[:8]
    note_ref[...] = jnp.where(first_lane == 1, lead * length, 0.0)
    wide = SOURCES * FILTERS
    source = lax.broadcasted_iota(jnp.int32, (8, wide), 1) // FILTERS
    active_ref[...] = jnp.where(source.astype(F32) < speakers, 1.0, 0.0)
    mix = planes[0]
    next_start = jnp.where(group == groups - 1, 0.0, pltpu.roll(mix, groups - 1, 0))
    following = jnp.where(lane == HOP - 1, pltpu.roll(next_start, HOP - 1, 1), pltpu.roll(mix, 127, 1))

    def columns(k, carry):
        def take(array):
            return jnp.broadcast_to(pltpu.roll(array, lax.rem(128 - k, 128), 1)[:, 0:1], (groups, 128))

        found = jnp.where((group * HOP + k).astype(F32) < length, whole_item, 0.0)
        for j in range(SOURCES):
            found = jnp.where(lane == j, jnp.where(speakers > j, take(planes[1 + j]), 0.0), found)
        found = jnp.where(lane == 4, take(mix), found)
        found = jnp.where(lane == 5, take(following), found)
        column_ref[pl.ds(pl.multiple_of(k * groups, 8), groups), :] = found
        return carry

    lax.fori_loop(0, HOP, columns, 0)

    if gathers:
        for step in range(1, chips):
            across[step - 1].wait_recv()
            at = lax.rem(b + 2 * chips - 2 * step, 2 * chips)
            beside.append(send(shard(at), shard(at), pair_sem, step, sibling))
            beside[-1].start()
        for copy in across:
            copy.wait_send()
        own.wait()
        for copy in beside:
            copy.wait()

    taps = flat_ref[0:128].reshape(1, 128)
    at_lane = lax.broadcasted_iota(jnp.int32, (128, 128), 1)
    at_row = lax.broadcasted_iota(jnp.int32, (128, 128), 0)
    upright = jnp.sum(jnp.where(at_lane == at_row, taps, 0.0), 1, keepdims=True)
    twice = 2 * lax.rem(at_lane, FILTERS)
    tap_rows = [jnp.sum(jnp.where(at_row == twice + tap, upright, 0.0), 0, keepdims=True) for tap in range(2)]
    encoder_ref[...] = jnp.where(at_row[:8] == 0, tap_rows[0], jnp.where(at_row[:8] == 1, tap_rows[1], 0.0))

    def encode(k, carry):
        rows = pl.ds(pl.multiple_of(k * groups, 8), groups)
        column = column_ref[rows, :]
        raw = column[:, 4:5] * tap_rows[0] + column[:, 5:6] * tap_rows[1]
        encoded = jnp.maximum(raw, 0.0) + jnp.log1p(jnp.exp(-jnp.abs(raw)))
        later = jnp.where(group == groups - 1, 0.0, pltpu.roll(encoded, groups - 1, 0))
        stream_ref[rows, :] = jnp.where(lane < FILTERS, encoded, later)
        return carry

    lax.fori_loop(0, HOP, encode, 0, unroll=5)
    stream_ref[valid:] = jnp.zeros((stream_ref.shape[0] - valid, 128), F32)


def sizes(inter, groups):
    if inter:
        return groups, 2 * HALF_PAD, 4
    return 2 * HOP, groups, 5


def whole(shape):
    return pl.BlockSpec(shape, lambda j: (0,) * len(shape))


def run_start(params, mixture, sources, speakers, lengths):
    items, samples_here = mixture.shape
    depths = lax.axis_size("frames")
    chips = lax.axis_size("batch") // 2
    groups = samples_here * depths // HOP
    share = groups // depths
    valid = HOP * groups
    copies = depths // (2 * items)
    signals = jnp.concatenate([mixture[:, None], sources], 1).reshape(items, (1 + SOURCES) * share, HOP)
    facts = jnp.stack([speakers, lengths], 1).astype(F32)[:, None]
    mail_rows = -(-((1 + SOURCES) * share + 1) // 8) * 8
    mail = jnp.concatenate(
        [jnp.pad(signals, ((0, 0), (0, 0), (0, 128 - HOP))), jnp.pad(facts, ((0, 0), (0, 0), (0, 126)))], 1
    )
    mail = jnp.pad(mail, ((0, 0), (0, mail_rows - mail.shape[1]), (0, 0))).reshape(items * mail_rows, 128)
    stream_shape = (HALF_PAD * groups, 128)
    out = [stream_shape, (valid, 128), (8, SOURCES * FILTERS), (8, 128), (8, 128)]
    gathers = params.shape[0] % 128 == 0
    if gathers:
        out = [(params.shape[0] * 2 * chips,)] + out
    else:
        params = lax.all_gather(params, "batch", axis=0, tiled=True)
    vmem = pl.BlockSpec(memory_space=pltpu.VMEM)
    sems = pltpu.SemaphoreType.DMA
    found = pl.pallas_call(
        functools.partial(start_kernel, chips, depths, items, groups, gathers),
        in_specs=[vmem] * 2,
        out_specs=[vmem] * len(out),
        out_shape=[jax.ShapeDtypeStruct(shape, F32) for shape in out],
        scratch_shapes=[
            pltpu.VMEM((depths, mail_rows, 128), F32), pltpu.VMEM((1 + SOURCES, groups, 128), F32),
            sems((2, chips - 1)), sems((2, chips)), sems, sems((2, max(depths, 2 * items * copies))),
        ],
        compiler_params=pltpu.CompilerParams(
            vmem_limit_bytes=VMEM_MAX, collective_id=10, has_side_effects=True
        ),
        name="start",
    )(params, mail)
    return found if gathers else [params, *found]


def run_forward(layer_no, groups, stream, flat):
    inter = layer_no % 2 == 1
    length, rows, steps = sizes(inter, groups)
    stream_shape = (HALF_PAD * groups, 128)
    out = [
        (stream_shape, whole(stream_shape)),
        (stream_shape, whole(stream_shape)),
        ((8, 128), whole((8, 128))),
        ((length, rows, UNITS), pl.BlockSpec((2 * steps, rows, UNITS), lambda j: (j, 0, 0))),
        ((length, 6, rows, UNITS), pl.BlockSpec((2 * steps, 6, rows, UNITS), lambda j: (j, 0, 0, 0))),
    ]
    return pl.pallas_call(
        functools.partial(forward_kernel, layer_no, groups, steps),
        grid=(length // (2 * steps),),
        in_specs=[whole(stream_shape), pl.BlockSpec(memory_space=pl.ANY)],
        out_specs=[spec for _, spec in out],
        out_shape=[jax.ShapeDtypeStruct(shape, F32) for shape, _ in out],
        scratch_shapes=[
            pltpu.VMEM((2, 256, GATES), BF16), pltpu.VMEM((2, 128, GATES), BF16),
            pltpu.VMEM((256, GATES), BF16), pltpu.VMEM((128, GATES), BF16),
            pltpu.VMEM((2, 256, 128), BF16), pltpu.VMEM((2, 128, 128), BF16),
            pltpu.VMEM((UNITS, 128), F32),
            pltpu.VMEM((8, GATES), F32),
            pltpu.VMEM((steps * rows, GATES), F32), pltpu.VMEM((steps * rows, GATES), F32),
            pltpu.VMEM((steps * rows, UNITS), F32), pltpu.VMEM((steps * rows, UNITS), F32),
            pltpu.VMEM((rows, UNITS), F32),
            pltpu.VMEM(stream_shape, F32), pltpu.VMEM(stream_shape, F32), pltpu.SemaphoreType.DMA((2,)),
            pltpu.VMEM((WINDOW, 128), F32), pltpu.SemaphoreType.DMA,
        ],
        compiler_params=pltpu.CompilerParams(
            vmem_limit_bytes=VMEM_MAX, collective_id=2 + layer_no, has_side_effects=True
        ),
        name="forward_inter" if inter else "forward_intra",
    )(stream, flat)


def run_backward(layer_no, groups, grad, kept, flat, extra):
    inter = layer_no % 2 == 1
    last_layer = layer_no == 2 * BLOCKS - 1
    length, rows, steps = sizes(inter, groups)
    stream_shape = (HALF_PAD * groups, 128)
    count = length // (2 * steps)
    depths = lax.axis_size("frames")
    chips = lax.axis_size("batch") // 2
    out = [(reduced_rows(OWN_ROWS[layer_no], chips, depths), 128)]
    scratch = []
    if not last_layer:
        upper_rows = reduced_rows(OWN_ROWS[layer_no + 1], chips, depths)
        out = [(2, upper_rows, 128)] + out
        scratch = reducer_scratch(upper_rows, chips, depths)
    if layer_no:
        out = [stream_shape] + out
    x, normed, scale, h_all, coef = kept
    return pl.pallas_call(
        functools.partial(backward_kernel, layer_no, groups, steps, chips, depths),
        grid=(count,),
        in_specs=[whole(a.shape) for a in (grad, normed, scale, x, h_all)]
        + [pl.BlockSpec((2 * steps, 6, rows, UNITS), lambda j: (count - 1 - j, 0, 0, 0)), pl.BlockSpec(memory_space=pl.ANY)]
        + [whole(a.shape) for a in extra],
        out_specs=[whole(shape) for shape in out],
        out_shape=[jax.ShapeDtypeStruct(shape, F32) for shape in out],
        scratch_shapes=[
            pltpu.VMEM((2, 2 * GATES, 128), BF16), pltpu.VMEM((2, GATES, 128), BF16),
            pltpu.VMEM((GATES, 256), BF16), pltpu.VMEM((GATES, 128), BF16),
            pltpu.VMEM((2, 256, 128), BF16), pltpu.VMEM((2, 128, 128), BF16),
            pltpu.VMEM((UNITS, 128), F32),
            pltpu.VMEM(stream_shape, F32),
            pltpu.VMEM((steps * rows, UNITS), F32), pltpu.VMEM((steps * rows, UNITS), F32),
            pltpu.VMEM((steps * rows, GATES), F32), pltpu.VMEM((steps * rows, GATES), F32),
            pltpu.VMEM((rows, UNITS), F32),
            pltpu.VMEM((256, GATES), F32), pltpu.VMEM((2 * UNITS if inter else UNITS, 128), F32),
            pltpu.VMEM((8, GATES), F32),
            pltpu.VMEM(stream_shape, F32), pltpu.VMEM(stream_shape, F32), pltpu.SemaphoreType.DMA((2,)),
            pltpu.VMEM((WINDOW, 128), F32), pltpu.SemaphoreType.DMA,
        ]
        + scratch,
        compiler_params=pltpu.CompilerParams(vmem_limit_bytes=VMEM_MAX, collective_id=6 + layer_no, has_side_effects=True),
        name="backward_inter" if inter else "backward_intra",
    )(grad, normed, scale, x, h_all, coef, flat, *extra)


def run_head(groups, separated, stream, column, active, note, flat):
    valid = HOP * groups
    stream_shape = (HALF_PAD * groups, 128)
    out = [stream_shape, (HEAD_ROWS, 128), (valid, FILTERS), (8, 128)]
    wide = SOURCES * FILTERS
    operands = (separated, stream, column, active, note)
    return pl.pallas_call(
        functools.partial(head_kernel, groups),
        grid=(1,),
        in_specs=[whole(a.shape) for a in operands] + [pl.BlockSpec(memory_space=pl.ANY)],
        out_specs=[whole(shape) for shape in out],
        out_shape=[jax.ShapeDtypeStruct(shape, F32) for shape in out],
        scratch_shapes=[
            pltpu.VMEM((valid, wide), F32), pltpu.VMEM((valid, 128), F32),
            pltpu.VMEM((valid + groups, 128), F32), pltpu.VMEM((valid + groups, 128), F32),
            pltpu.VMEM((2 * FILTERS, wide), BF16), pltpu.VMEM((FILTERS, wide), BF16),
            pltpu.VMEM((2 * wide, FILTERS), BF16), pltpu.VMEM((wide, FILTERS), BF16),
            pltpu.VMEM((2 * wide, 256), BF16), pltpu.VMEM((wide, 256), BF16),
            pltpu.VMEM((512, wide), BF16), pltpu.VMEM((256, wide), BF16),
            pltpu.VMEM((FILTERS, wide), F32), pltpu.VMEM((wide, 256), F32),
            pltpu.VMEM((FILTERS, 128), F32), pltpu.VMEM((FILTERS, 128), F32),
            pltpu.VMEM((TAIL_ROWS, 128), F32), pltpu.SemaphoreType.DMA,
        ],
        compiler_params=pltpu.CompilerParams(vmem_limit_bytes=VMEM_MAX),
        name="head",
    )(*operands, flat)


def run_finish(layers, params, first_moment, second_moment):
    entries = params.shape[0]
    rows = -(-entries // 128)
    depths = lax.axis_size("frames")
    chips = lax.axis_size("batch") // 2
    vmem = pl.BlockSpec(memory_space=pltpu.VMEM)
    gradient, note = pl.pallas_call(
        functools.partial(finish_kernel, chips, depths, entries),
        in_specs=[vmem] + [pl.BlockSpec(memory_space=pl.ANY)] * 3,
        out_specs=[vmem] * 2,
        out_shape=[jax.ShapeDtypeStruct(shape, F32) for shape in ((rows, 128), (8, 128))],
        scratch_shapes=[pltpu.VMEM((6808, 128), F32)]
        + [pltpu.VMEM(a.shape, F32) for a in layers[1:]]
        + [pltpu.SemaphoreType.DMA((3,))]
        + reducer_scratch(layers[0].shape[0], chips, depths),
        compiler_params=pltpu.CompilerParams(
            vmem_limit_bytes=VMEM_MAX, collective_id=1, has_side_effects=True
        ),
        name="finish",
    )(*layers)
    shards = [params, first_moment, second_moment]
    shape = (entries,)
    if entries % 128:
        shape = (rows, 128)
        shards = [jnp.pad(a, (0, rows * 128 - entries)).reshape(shape) for a in shards]
    smem = pl.BlockSpec(memory_space=pltpu.SMEM)
    out = [(shape, F32), (shape, BF16), (shape, F32), (shape, F32), ((1,), F32), ((2,), F32)]
    found = pl.pallas_call(
        update_kernel,
        in_specs=[vmem] * 5,
        out_specs=[vmem] * 4 + [smem] * 2,
        out_shape=[jax.ShapeDtypeStruct(shape, dtype) for shape, dtype in out],
        compiler_params=pltpu.CompilerParams(vmem_limit_bytes=VMEM_MAX),
        name="update",
    )(gradient, note, *shards)
    return [a.reshape(-1)[:entries] for a in found[:4]] + [found[4][0], found[5]]


def local(params, first_moment, second_moment, mixture, sources, speakers, lengths):
    groups = mixture.shape[1] * lax.axis_size("frames") // HOP
    flat, stream, column, active, encoder, note = run_start(params, mixture, sources, speakers, lengths)
    view = flat.reshape(-1, 128)
    kept = []
    x = stream
    for layer_no in range(2 * BLOCKS):
        after, normed, scale, h_all, coef = run_forward(layer_no, groups, x, view)
        kept.append((x, normed, scale, h_all, coef))
        x = after
    grad, head_grads, grad_encoded, loss = run_head(groups, x, stream, column, active, note, view)
    sums = [None] * (2 * BLOCKS)
    for layer_no in reversed(range(2 * BLOCKS)):
        extra = ()
        if layer_no == 2 * BLOCKS - 1:
            extra = (head_grads,)
        if layer_no == 0:
            extra = (column, grad_encoded, encoder, loss)
        if layer_no < 2 * BLOCKS - 1:
            extra = extra + (sums[layer_no + 1],)
        *found, sums[layer_no] = run_backward(layer_no, groups, grad, kept[layer_no], view, extra)
        if layer_no < 2 * BLOCKS - 1:
            sums[layer_no + 1] = found[-1]
        if layer_no:
            grad = found[0]
    return tuple(run_finish(sums, params, first_moment, second_moment))


def solution(mesh):
    placed = (
        P("batch"),
        P("batch"),
        P("batch"),
        P("batch", "frames"),
        P("batch", None, "frames"),
        P("batch"),
        P("batch"),
    )
    return jax.shard_map(
        local,
        mesh=mesh,
        in_specs=placed,
        out_specs=(P("batch"), P("batch"), P("batch"), P("batch"), P(), P()),
        check_vma=False,
    )
```

```python
import functools
import math

import jax
import jax.numpy as jnp
from jax import lax
from jax.experimental import pallas as pl
from jax.experimental.pallas import tpu as pltpu
from jax.sharding import PartitionSpec as P

FILTERS = 64
UNITS = 128
HOP = 50
HALF_PAD = 56
SOURCES = 3
BLOCKS = 2
STEP = 5
GATES = 4 * UNITS

HIGHEST = lax.Precision.HIGHEST
NORM_EPS = 1e-08
CLIP_AT = 0.001
BETA_ONE = 0.5
BETA_TWO = 0.5
LEARN_RATE = 0.05
DECAY_RATE = 0.01
ADAM_EPS = 1e-08
F32 = jnp.float32
BF16 = jnp.bfloat16
VMEM_MAX = 60 * 2**20


def split(a):
    hi = a.astype(BF16)
    return hi, (a - hi.astype(F32)).astype(BF16)


def dot(a, b):
    return jnp.dot(a, b, preferred_element_type=F32)


def dot3(a, w_twice, w_low):
    hi, lo = split(a)
    return dot(jnp.concatenate([hi, lo], 1), w_twice) + dot(hi, w_low)


def dot_rows(a, b):
    return lax.dot_general(a, b, (((0,), (0,)), ((), ())), preferred_element_type=F32)


def dot_rows3(a, b):
    a_hi, a_lo = split(a)
    b_hi, b_lo = split(b)
    return dot_rows(a_hi, b_hi) + dot_rows(a_lo, b_hi) + dot_rows(a_hi, b_lo)


SIDE_ROWS = 772
PROJ_ROWS = 2 * SIDE_ROWS
VEC_ROW = PROJ_ROWS + 128
LAYER_ROWS = 1680
HEAD_ROWS = 160
OWN_PROJ = SIDE_ROWS
OWN_VEC = SIDE_ROWS + 64
OWN_EXTRA = SIDE_ROWS + 68
OWN_ROWS = (OWN_EXTRA + 8, OWN_EXTRA, OWN_EXTRA, OWN_EXTRA + HEAD_ROWS)
WINDOW = 1688
TAIL_ROW = 6688
TAIL_ROWS = 104
FRAME_LANES = 8
MIX_LANE = SOURCES
NEXT_LANE = FRAME_LANES + MIX_LANE


def window(layer_no):
    at = 2 + 3347 * layer_no
    return at // 16 * 8, at // 2 % 8, at % 2


def pick(ref, base, odd, start, count, stride=1):
    def load(at):
        return ref[pl.ds(at, count, stride=stride), :] if stride > 1 else ref[pl.ds(at, count), :]

    first = load(base + start)
    if not odd:
        return first
    return jnp.concatenate([first[:, 64:], load(base + start + 1)[:, :64]], 1)


def load_weights(ref, base, odd, dir_no, proj_s):
    at = SIDE_ROWS * dir_no
    win = jnp.concatenate([pick(ref, base, odd, at + q, FILTERS, 4) for q in range(4)], 1)
    wrec = jnp.concatenate([pick(ref, base, odd, at + 256 + q, UNITS, 4) for q in range(4)], 1)
    bias = jnp.concatenate([pick(ref, base, odd, at + 768 + q, 1) for q in range(4)], 1)
    pairs = pick(ref, base, odd, PROJ_ROWS + 64 * dir_no, 64)
    proj_s[pl.ds(0, 64, stride=2), :] = pairs
    proj_s[pl.ds(1, 64, stride=2), :] = pltpu.roll(pairs, 64, 1)
    return win, wrec, bias, proj_s[:, :FILTERS]


def load_vec(ref, base, odd):
    first = pick(ref, base, odd, VEC_ROW, 1)
    turned = pltpu.roll(jnp.broadcast_to(first, (8, 128)), 64, 1)[0:1]
    if odd:
        last = ref[base + VEC_ROW + 1:base + VEC_ROW + 2, :]
        last = jnp.concatenate([last[:, 64:], last[:, 64:]], 1)
    else:
        last = ref[base + VEC_ROW + 1:base + VEC_ROW + 2, :]
        last = jnp.concatenate([last[:, :64], last[:, :64]], 1)
    low = lax.broadcasted_iota(jnp.int32, (1, 128), 1) < 64
    return jnp.where(low, first, turned), jnp.where(low, turned, first), last


def share_of(tasks, number, count):
    return tasks[number * len(tasks) // count:(number + 1) * len(tasks) // count]


def fold_halves(a):
    return a + pltpu.roll(a, FILTERS, 1)


def narrow(a, half):
    if isinstance(half, int):
        a = pltpu.roll(a, FILTERS, 1) if half else a
    else:
        a = jnp.where(half == 0, a, pltpu.roll(a, FILTERS, 1))
    low_lanes = lax.broadcasted_iota(jnp.int32, a.shape, 1) < FILTERS
    hi = a.astype(BF16).astype(F32)
    lo = pltpu.roll(a - hi, FILTERS, 1)
    return jnp.concatenate([jnp.where(low_lanes, hi, lo), jnp.where(low_lanes, hi, 0.0)], 1).astype(BF16)


def narrow_weights(w):
    hi, lo = split(w)
    return jnp.concatenate([hi, hi, lo, jnp.zeros_like(hi)], 0)


def side_weights(w):
    hi, lo = split(w)
    return jnp.concatenate([hi, lo], 1)


def dot_sides(a, w):
    hi, lo = split(a)
    return fold_halves(dot(hi, w) + dot(lo, w))


def put_split(w, twice_ref, low_ref):
    hi, lo = split(w)
    twice_ref[...] = jnp.concatenate([hi, hi], 0)
    low_ref[...] = lo


def times(dir_no, chunk_no, length, steps):
    return [dir_no * (length - 1) + (1 - 2 * dir_no) * (chunk_no * steps + u) for u in range(steps)]


def stream_rows(inter, groups, at):
    if inter:
        return pl.ds(at, HALF_PAD, stride=groups)
    return pl.ds(pl.multiple_of(lax.rem(at, HOP) * groups, 8), groups)


def gather(ref, inter, groups, positions):
    return jnp.concatenate([ref[stream_rows(inter, groups, at), :] for at in positions], 0)


def to_sides(inter, steps, array):
    if not inter:
        return [array]
    three = array.reshape(steps, 2 * HALF_PAD, array.shape[-1])
    return [
        three[:, side * HALF_PAD:(side + 1) * HALF_PAD].reshape(steps * HALF_PAD, array.shape[-1]) for side in range(2)
    ]


SIDE_ROWS = 772
PROJ_ROWS = 2 * SIDE_ROWS
VEC_ROW = PROJ_ROWS + 128
LAYER_ROWS = 1680
HEAD_ROWS = 160
OWN_PROJ = SIDE_ROWS
OWN_VEC = SIDE_ROWS + 64
OWN_EXTRA = SIDE_ROWS + 68
OWN_ROWS = (OWN_EXTRA + 8, OWN_EXTRA, OWN_EXTRA, OWN_EXTRA + HEAD_ROWS)
WINDOW = 1688
TAIL_ROW = 6688
TAIL_ROWS = 104
FRAME_LANES = 8
MIX_LANE = SOURCES
NEXT_LANE = FRAME_LANES + MIX_LANE


def window(layer_no):
    at = 2 + 3347 * layer_no
    return at // 16 * 8, at // 2 % 8, at % 2


def pick(ref, base, odd, start, count, stride=1):
    def load(at):
        return ref[pl.ds(at, count, stride=stride), :] if stride > 1 else ref[pl.ds(at, count), :]

    first = load(base + start)
    if not odd:
        return first
    return jnp.concatenate([first[:, 64:], load(base + start + 1)[:, :64]], 1)


def load_weights(ref, base, odd, dir_no, proj_s):
    at = SIDE_ROWS * dir_no
    win = jnp.concatenate([pick(ref, base, odd, at + q, FILTERS, 4) for q in range(4)], 1)
    wrec = jnp.concatenate([pick(ref, base, odd, at + 256 + q, UNITS, 4) for q in range(4)], 1)
    bias = jnp.concatenate([pick(ref, base, odd, at + 768 + q, 1) for q in range(4)], 1)
    pairs = pick(ref, base, odd, PROJ_ROWS + 64 * dir_no, 64)
    proj_s[pl.ds(0, 64, stride=2), :] = pairs
    proj_s[pl.ds(1, 64, stride=2), :] = pltpu.roll(pairs, 64, 1)
    return win, wrec, bias, proj_s[:, :FILTERS]


def load_vec(ref, base, odd):
    first = pick(ref, base, odd, VEC_ROW, 1)
    turned = pltpu.roll(jnp.broadcast_to(first, (8, 128)), 64, 1)[0:1]
    if odd:
        last = ref[base + VEC_ROW + 1:base + VEC_ROW + 2, :]
        last = jnp.concatenate([last[:, 64:], last[:, 64:]], 1)
    else:
        last = ref[base + VEC_ROW + 1:base + VEC_ROW + 2, :]
        last = jnp.concatenate([last[:, :64], last[:, :64]], 1)
    low = lax.broadcasted_iota(jnp.int32, (1, 128), 1) < 64
    return jnp.where(low, first, turned), jnp.where(low, turned, first), last


def put_split(w, twice_ref, low_ref):
    hi, lo = split(w)
    twice_ref[...] = jnp.concatenate([hi, hi], 0)
    low_ref[...] = lo


def place(dir_no, chunk_no, count, steps, inter, groups):
    first = jnp.where(dir_no == 0, chunk_no * steps, (count - 1 - chunk_no) * steps)
    if inter:
        return first, 0, 0
    half = first // HOP
    return first, half, pl.multiple_of((first - HOP * half) * groups, 8)


def norm_stage(prev_ref, pa_ref, pb_ref, flat_ref, base, odd, valid, normed_ref, scale_ref, x_ref):
    offset, gain, shift = load_vec(flat_ref, base, odd)
    mixed = pa_ref[:valid] + pb_ref[:valid] + offset
    total = 2.0 * valid * FILTERS
    mean = jnp.sum(mixed) / total
    spread = jnp.sum(mixed * mixed) / total - mean * mean
    scale = lax.rsqrt(jnp.full((1, 128), spread + NORM_EPS, F32))
    normed = (mixed - mean) * scale
    normed_ref[:valid] = normed
    normed_ref[valid:] = jnp.zeros((normed_ref.shape[0] - valid, 128), F32)
    x_ref[:valid] = prev_ref[:valid] + gain * normed + shift
    x_ref[valid:] = jnp.zeros((x_ref.shape[0] - valid, 128), F32)
    scale_ref[...] = jnp.broadcast_to(scale, scale_ref.shape)


def greet_sibling():
    b = lax.axis_index("batch")
    device = (b + 1 - 2 * lax.rem(b, 2), lax.axis_index("frames"))
    return device, pltpu.get_barrier_semaphore()


def swap_with_sibling(src_ref, dst_ref, sems, greeted=False):
    device, barrier = greet_sibling()
    if not greeted:
        pl.semaphore_wait(barrier, 1)
    copy = pltpu.make_async_remote_copy(
        src_ref=src_ref, dst_ref=dst_ref, send_sem=sems.at[0], recv_sem=sems.at[1],
        device_id=device, device_id_type=pl.DeviceIdType.MESH,
    )
    copy.start()
    return copy


def reduced_rows(rows, chips, depths):
    return -(-rows // (8 * chips * depths)) * 8 * chips * depths


def reducer_scratch(rows, chips, depths):
    quarter = rows // chips
    part = quarter // depths
    sems = pltpu.SemaphoreType.DMA
    return [
        pltpu.VMEM((2, rows, 128), F32), pltpu.VMEM((chips - 1, quarter, 128), F32), pltpu.VMEM((quarter, 128), F32),
        pltpu.VMEM((depths - 1, part, 128), F32), pltpu.VMEM((part, 128), F32), pltpu.VMEM((quarter, 128), F32),
        sems((2, chips - 1)), sems((2, depths - 1)), sems((2, depths - 1)), sems((2, chips - 1)), sems((2, 1)),
    ]


def greet_all(chips, depths):
    b = lax.axis_index("batch")
    z = lax.axis_index("frames")
    barrier = pltpu.get_barrier_semaphore()
    devices = [(b + 1 - 2 * lax.rem(b, 2), z)]
    devices += [(lax.rem(b + 2 * step, 2 * chips), z) for step in range(1, chips)]
    devices += [(b, lax.rem(z + step, depths)) for step in range(1, depths)]
    for device in devices:
        pl.semaphore_signal(barrier, inc=1, device_id=device, device_id_type=pl.DeviceIdType.MESH)
    return barrier, len(devices)


def reducer(src, chips, depths, refs):
    red, plane_in, mine, depth_in, piece, joined, s_plane, s_depth, s_spread, s_gather, s_back = refs
    b = lax.axis_index("batch")
    z = lax.axis_index("frames")
    core = lax.rem(b, 2)
    chip = lax.div(b, 2)
    quarter = mine.shape[0]
    part = piece.shape[0]

    def rows(at, count):
        return pl.ds(pl.multiple_of(at, 8), count)

    def send(src_ref, dst_ref, sems, slot, device):
        return pltpu.make_async_remote_copy(
            src_ref=src_ref, dst_ref=dst_ref, send_sem=sems.at[0, slot], recv_sem=sems.at[1, slot],
            device_id=device, device_id_type=pl.DeviceIdType.MESH,
        )

    over_plane = [(step, (lax.rem(b + 2 * step, 2 * chips), z)) for step in range(1, chips)]
    over_depth = [(step, (b, lax.rem(z + step, depths))) for step in range(1, depths)]
    own = rows(chip * quarter, quarter)
    mine_at = rows(z * part, part)

    def plane():
        return [
            send(src.at[rows(lax.rem(chip + step, chips) * quarter, quarter)], plane_in.at[step - 1], s_plane, step - 1, to)
            for step, to in over_plane
        ]

    def scatter():
        return [
            send(mine.at[rows(lax.rem(z + step, depths) * part, part)], depth_in.at[step - 1], s_depth, step - 1, to)
            for step, to in over_depth
        ]

    def spread():
        return [send(piece, joined.at[mine_at], s_spread, step - 1, to) for step, to in over_depth]

    def gather():
        return [send(joined, red.at[core, own], s_gather, step - 1, to) for step, to in over_plane]

    def back():
        return [send(red.at[core], red.at[core], s_back, 0, (b + 1 - 2 * core, z))]

    def start(copies):
        for copy in copies:
            copy.start()

    def wait(copies):
        for copy in copies:
            copy.wait()

    def first():
        start(plane())

    def third():
        wait(plane())
        total = src[own, :]
        for step in range(1, chips):
            total = total + plane_in[step - 1]
        mine[...] = total
        start(scatter())

    def fourth():
        wait(scatter())
        total = mine[mine_at, :]
        for step in range(1, depths):
            total = total + depth_in[step - 1]
        piece[...] = total
        joined[mine_at, :] = total
        start(spread())

    def fifth():
        wait(spread())
        red[core, own] = joined[...]
        start(gather())

    def sixth():
        wait(gather())
        start(back())

    def last():
        wait(back())

    return [first, third, fourth, fifth, sixth, last]


def forward_kernel(layer_no, groups, steps, *refs):
    inter = layer_no % 2 == 1
    (x_ref, flat_ref,
     next_ref, normed_ref, scale_ref, h_ref, coef_ref,
     wi4, wr2, wrl, pj, proj_s, bias_s, gin_a, gin_b, h_a, h_b, c_s, part_ref, peer_ref, sems) = refs
    turn_no = pl.program_id(0)
    last_turn = pl.num_programs(0) - 1
    chunks = 2 * pl.num_programs(0)
    length = chunks * steps
    dir_no = lax.rem(lax.axis_index("batch"), 2)
    rows = 2 * HALF_PAD if inter else groups
    valid = HOP * groups

    def before(chunk_no, gin):
        chunk_no = lax.rem(chunk_no, chunks)
        positions = times(dir_no, chunk_no, length, steps)
        sides = []

        def prepare():
            xs = gather(x_ref, inter, groups, positions)
            for half in [0, 1] if inter else [lax.div(positions[0], HOP)]:
                sides.append(narrow(xs, half))

        def gate(q):
            cut = slice(q * UNITS, (q + 1) * UNITS)
            for side, rows_of in enumerate(sides):
                found = dot(rows_of, wi4[:, cut]) + bias_s[0:1, cut]
                if inter:
                    for u in range(steps):
                        at = u * rows + side * HALF_PAD
                        gin[at:at + HALF_PAD, cut] = found[u * HALF_PAD:(u + 1) * HALF_PAD]
                else:
                    gin[:, cut] = found

        return [prepare] + [functools.partial(gate, q) for q in range(4)]

    def after(chunk_no, hs):
        chunk_no = lax.rem(chunk_no + chunks, chunks)
        positions = times(dir_no, chunk_no, length, steps)

        def project():
            found = [dot_sides(part, pj[...]) for part in to_sides(inter, steps, hs[...])]
            low_lanes = lax.broadcasted_iota(jnp.int32, found[0].shape, 1) < FILTERS
            if inter:
                found = jnp.where(low_lanes, found[0], found[1])
                for u in range(steps):
                    part_ref[stream_rows(inter, groups, positions[u]), :] = found[u * HALF_PAD:(u + 1) * HALF_PAD]
            else:
                half = lax.div(positions[0], HOP)
                found = jnp.where(low_lanes == (half == 0), found[0], 0.0)
                for u in range(steps):
                    here = stream_rows(inter, groups, positions[u])
                    part_ref[here, :] = part_ref[here, :] + found[u * groups:(u + 1) * groups]

        return [project]

    def walk(gin, hs, h, c, sub, beside):
        for u in range(steps):
            hi, lo = split(h)
            z = dot(jnp.concatenate([hi, lo], 1), wr2[...]) + dot(hi, wrl[...])
            for task in share_of(beside, u, steps):
                task()
            z = z + gin[u * rows:(u + 1) * rows]
            th = jnp.tanh(z)
            ti, tf, g, to = (th[:, q * UNITS:(q + 1) * UNITS] for q in range(4))
            i_g = 0.5 * ti + 0.5
            f_g = 0.5 * tf + 0.5
            o_g = 0.5 * to + 0.5
            c_prev = c
            c = f_g * c + i_g * g
            tc = jnp.tanh(c)
            h = o_g * tc
            at = sub * steps + u
            hs[u * rows:(u + 1) * rows] = h
            h_ref[at] = h
            coef_ref[at, 0] = tc * (0.25 - 0.25 * to * to)
            coef_ref[at, 1] = o_g * (1.0 - tc * tc)
            coef_ref[at, 2] = g * (0.25 - 0.25 * ti * ti)
            coef_ref[at, 3] = c_prev * (0.25 - 0.25 * tf * tf)
            coef_ref[at, 4] = i_g * (1.0 - g * g)
            coef_ref[at, 5] = f_g
        return h, c

    @pl.when(turn_no == 0)
    def _():
        device, barrier = greet_sibling()
        pl.semaphore_signal(barrier, inc=1, device_id=device, device_id_type=pl.DeviceIdType.MESH)
        part_ref[...] = jnp.zeros_like(part_ref)
        column = lax.broadcasted_iota(jnp.int32, (1, GATES), 1)
        scaling = jnp.where((column >= 2 * UNITS) & (column < 3 * UNITS), 1.0, 0.5)
        _, base, odd = window(layer_no)
        win, wrec, bias, proj = load_weights(flat_ref, base, odd, dir_no, proj_s)
        wi4[...] = narrow_weights(win * scaling)
        put_split(wrec * scaling, wr2, wrl)
        bias_s[...] = jnp.broadcast_to(bias * scaling, bias_s.shape)
        pj[...] = side_weights(proj)
        c_s[...] = jnp.zeros_like(c_s)
        h_b[...] = jnp.zeros_like(h_b)
        for task in before(0, gin_a):
            task()

    h, c = h_b[(steps - 1) * rows:], c_s[...]
    h, c = walk(gin_a, h_a, h, c, 0, after(2 * turn_no - 1, h_b) + before(2 * turn_no + 1, gin_b))
    h, c = walk(gin_b, h_b, h, c, 1, after(2 * turn_no, h_a) + before(2 * turn_no + 2, gin_a))
    c_s[...] = c

    @pl.when(turn_no == last_turn)
    def _():
        for task in after(chunks - 1, h_b):
            task()
        swap_with_sibling(part_ref, peer_ref, sems).wait()
        _, base, odd = window(layer_no)
        norm_stage(x_ref, part_ref, peer_ref, flat_ref, base, odd, valid, normed_ref, scale_ref, next_ref)


def backward_kernel(layer_no, groups, steps, chips, depths, *refs):
    inter = layer_no % 2 == 1
    last_layer = layer_no == 2 * BLOCKS - 1
    g_ref, normed_ref, scale_ref, x_ref, h_ref, coef_ref, flat_ref, *rest = refs
    if last_layer:
        hg_ref, *rest = rest
    if layer_no == 0:
        column_ref, denc_ref, encoder_ref, loss_ref, *rest = rest
    if not last_layer:
        upper_ref, *rest = rest
    if layer_no:
        below_ref, *rest = rest
    if not last_layer:
        red_ref, *rest = rest
    (grad_ref,
     wi4, wrw, wrt, pj, proj_s, dmx, dh_a, dh_b, dz_a, dz_b, dc_s, awin, aproj, abias,
     dx_ref, peer_ref, sems, *rest) = rest
    stages = [] if last_layer else reducer(upper_ref, chips, depths, rest)
    turn_no = pl.program_id(0)
    last_turn = pl.num_programs(0) - 1
    chunks = 2 * pl.num_programs(0)
    length = chunks * steps
    dir_no = lax.rem(lax.axis_index("batch"), 2)
    rows = 2 * HALF_PAD if inter else groups
    valid = HOP * groups

    def before(back_no, dhc):
        chunk_no = chunks - 1 - lax.rem(back_no, chunks)
        positions = times(dir_no, chunk_no, length, steps)

        def outward():
            dms = gather(dmx, inter, groups, positions)
            for side, half in enumerate([0, 1] if inter else [lax.div(positions[0], HOP)]):
                found = dot(narrow(dms, half), pj[...])
                if inter:
                    for u in range(steps):
                        at = u * rows + side * HALF_PAD
                        dhc[at:at + HALF_PAD] = found[u * HALF_PAD:(u + 1) * HALF_PAD]
                else:
                    dhc[...] = found

        return [outward]

    def after(back_no, dzs):
        used = back_no >= 0
        chunk_no = chunks - 1 - lax.rem(back_no + chunks, chunks)
        positions = times(dir_no, chunk_no, length, steps)
        half = 0 if inter else lax.div(positions[0], HOP)
        at = chunk_no * steps
        count = UNITS + FILTERS
        ready = []

        def prepare():
            xs = gather(x_ref, inter, groups, positions)
            hs = h_ref[pl.ds(at, steps)].reshape(steps * rows, UNITS)
            early = h_ref[lax.rem(at + length - 1, length)] * jnp.where(at == 0, 0.0, 1.0)
            hp = jnp.concatenate([early, hs[:(steps - 1) * rows]], 0)
            if inter:
                lhs = [
                    jnp.concatenate([hp_side, (xs if side == 0 else pltpu.roll(xs, FILTERS, 1))[:, :FILTERS]], 1)
                    for side, hp_side in enumerate(to_sides(inter, steps, hp))
                ]
                lhs = jnp.concatenate(lhs, 0)
            else:
                turned = jnp.where(half == 0, xs, pltpu.roll(xs, FILTERS, 1))
                lhs = jnp.concatenate([hp, turned[:, :FILTERS]], 1)
            lhs_hi, lhs_lo = split(lhs.T)
            ready.extend([lhs_hi, jnp.concatenate([lhs_hi, lhs_lo], 0)])

        def gate(q):
            cut = slice(q * UNITS, (q + 1) * UNITS)
            dz = dzs[:, cut]
            abias[0:1, cut] += jnp.sum(dz, 0, keepdims=True)
            if inter:
                dz = jnp.concatenate(to_sides(inter, steps, dz), 0)
            dz_hi, dz_lo = split(dz)
            both = dot(ready[1], dz_hi)
            awin[:, cut] += both[:count] + both[count:] + dot(ready[0], dz_lo)

        def project():
            hs = h_ref[pl.ds(at, steps)].reshape(steps * rows, UNITS)
            dms = gather(dmx, inter, groups, positions) * jnp.where(used, 1.0, 0.0)
            if inter:
                aproj[...] += dot_rows3(jnp.concatenate(to_sides(inter, steps, hs), 1), dms)
            else:
                turned = jnp.where(half == 0, dms, pltpu.roll(dms, FILTERS, 1))
                aproj[...] += dot_rows3(hs, turned)

        def inward():
            found = [dot_sides(part, wi4[...]) for part in to_sides(inter, steps, dzs[...])]
            low_lanes = lax.broadcasted_iota(jnp.int32, found[0].shape, 1) < FILTERS
            if inter:
                found = jnp.where(low_lanes, found[0], found[1])
                for u in range(steps):
                    dx_ref[stream_rows(inter, groups, positions[u]), :] = found[u * HALF_PAD:(u + 1) * HALF_PAD]
            else:
                found = jnp.where(low_lanes == (half == 0), found[0], 0.0)
                for u in range(steps):
                    here = stream_rows(inter, groups, positions[u])
                    dx_ref[here, :] = dx_ref[here, :] + found[u * groups:(u + 1) * groups]

        return [inward, project, prepare] + [functools.partial(gate, q) for q in range(4)]

    def walk(dhc, dzs, dz, dc_next, sub, beside):
        for u in reversed(range(steps)):
            at = sub * steps + u
            hi, lo = split(dz)
            wide = dot(hi, wrw[...])
            dh = wide[:, :UNITS] + wide[:, UNITS:] + dot(lo, wrt[...])
            for task in share_of(beside, steps - 1 - u, steps):
                task()
            dh = dh + dhc[u * rows:(u + 1) * rows]
            dc = dh * coef_ref[at, 1] + dc_next
            dz = jnp.concatenate(
                [dc * coef_ref[at, 2], dc * coef_ref[at, 3], dc * coef_ref[at, 4], dh * coef_ref[at, 0]], 1
            )
            dc_next = dc * coef_ref[at, 5]
            dzs[u * rows:(u + 1) * rows] = dz
        return dz, dc_next

    @pl.when(turn_no == 0)
    def _():
        if last_layer:
            device, barrier = greet_sibling()
            pl.semaphore_signal(barrier, inc=1, device_id=device, device_id_type=pl.DeviceIdType.MESH)
        else:
            barrier, count = greet_all(chips, depths)
            pl.semaphore_wait(barrier, count)
            stages[0]()
        dx_ref[...] = jnp.zeros_like(dx_ref)
        _, base, odd = window(layer_no)
        win, wrec, _, proj = load_weights(flat_ref, base, odd, dir_no, proj_s)
        wi4[...] = side_weights(win.T)
        hi, lo = split(wrec.T)
        wrw[...] = jnp.concatenate([hi, lo], 1)
        wrt[...] = hi
        pj[...] = narrow_weights(proj.T)
        dz_b[...] = jnp.zeros_like(dz_b)
        dc_s[...] = jnp.zeros_like(dc_s)
        awin[...] = jnp.zeros_like(awin)
        aproj[...] = jnp.zeros_like(aproj)
        abias[...] = jnp.zeros_like(abias)
        grad_ref[...] = jnp.zeros_like(grad_ref)
        g = g_ref[:valid]
        normed = normed_ref[:valid]
        _, gain, _ = load_vec(flat_ref, base, odd)
        g_n = g * gain
        total = 2.0 * valid * FILTERS
        mean_one = jnp.sum(g_n) / total
        mean_two = jnp.sum(g_n * normed) / total
        dmixed = scale_ref[0:1] * (g_n - mean_one - normed * mean_two)
        dmx[:valid] = dmixed
        dmx[valid:] = jnp.zeros((dmx.shape[0] - valid, 128), F32)
        lead = jnp.where(dir_no == 0, 1.0, 0.0)

        def fold(array):
            found = lead * jnp.sum(array, 0, keepdims=True)
            return found[:, :FILTERS] + found[:, FILTERS:]

        grad_ref[OWN_VEC:OWN_VEC + 1] = jnp.concatenate([fold(dmixed), fold(g * normed)], 1)
        grad_ref[OWN_VEC + 1:OWN_VEC + 2] = jnp.concatenate([fold(g), jnp.zeros((1, FILTERS), F32)], 1)
        if last_layer:
            grad_ref[OWN_EXTRA:OWN_EXTRA + HEAD_ROWS] = hg_ref[...] * lead

        for task in before(0, dh_a):
            task()

    for stage, at in zip(stages[1:], (2, 3, 4, None) if inter else (3, 5, 6, 9)):
        if at is not None:
            pl.when(turn_no == at)(stage)

    dz, dc_next = dz_b[:rows], dc_s[...]
    dz, dc_next = walk(dh_a, dz_a, dz, dc_next, 1, after(2 * turn_no - 1, dz_b) + before(2 * turn_no + 1, dh_b))
    dz, dc_next = walk(dh_b, dz_b, dz, dc_next, 0, after(2 * turn_no, dz_a) + before(2 * turn_no + 2, dh_a))
    dc_s[...] = dc_next

    @pl.when(turn_no == last_turn)
    def _():
        for task in after(chunks - 1, dz_b):
            task()
        if layer_no:
            swap = swap_with_sibling(dx_ref, peer_ref, sems, not last_layer)
        for stage in stages[4:] if inter else stages[5:]:
            stage()
        if not last_layer:
            red_ref[...] = rest[0][...]
        if layer_no:
            swap.wait()
            below_ref[:valid] = g_ref[:valid] + dx_ref[:valid] + peer_ref[:valid]
            below_ref[valid:] = jnp.zeros((below_ref.shape[0] - valid, 128), F32)
        for q in range(4):
            cut = slice(q * UNITS, (q + 1) * UNITS)
            grad_ref[pl.ds(q, FILTERS, stride=4), :] = awin[UNITS:, cut]
            grad_ref[pl.ds(256 + q, UNITS, stride=4), :] = awin[:UNITS, cut]
            grad_ref[768 + q:769 + q, :] = abias[0:1, cut]
        proj_s[...] = aproj[:UNITS] + pltpu.roll(aproj[UNITS:], FILTERS, 1) if inter else aproj[...]
        even = proj_s[pl.ds(0, 64, stride=2), :]
        odd_rows = proj_s[pl.ds(1, 64, stride=2), :]
        grad_ref[OWN_PROJ:OWN_VEC, :] = jnp.concatenate(
            [even[:, :FILTERS], odd_rows[:, :FILTERS]], 1
        )
        if layer_no == 0:
            lead = jnp.where(dir_no == 0, 1.0, 0.0)
            streams = lead * g_ref[:valid] + dx_ref[:valid]
            column = column_ref[...]
            mix, following = column[:, MIX_LANE:MIX_LANE + 1], column[:, NEXT_LANE:NEXT_LANE + 1]
            raw = mix * encoder_ref[0:1, :FILTERS] + following * encoder_ref[1:2, :FILTERS]
            group_at = lax.broadcasted_iota(jnp.int32, (valid, FILTERS), 0) % groups
            shifted = jnp.where(group_at == 0, 0.0, pltpu.roll(pltpu.roll(streams, FILTERS, 1), 1, 0)[:, :FILTERS])
            grad_raw = (streams[:, :FILTERS] + shifted + lead * denc_ref[...]) * jax.nn.sigmoid(raw)
            grad_ref[OWN_EXTRA:OWN_EXTRA + 1] = jnp.concatenate(
                [jnp.sum(grad_raw * mix, 0, keepdims=True), jnp.sum(grad_raw * following, 0, keepdims=True)], 1
            )
            grad_ref[OWN_EXTRA + 1:OWN_EXTRA + 2] = loss_ref[0:1] * lead


def head_kernel(groups, sep, stream_ref, column_ref, active_ref, note_ref, tail_s,
                g_ref, hg_ref, denc_ref, loss_ref,
                sig_s, now_s, before_s, slope_s, mk2, mkl, mt2, mtl, dk2, dkl, dt2, dtl, amask, adec, m_low, m_top):
    valid = HOP * groups
    block = 10 * groups
    first, second, third = (tail_s[pl.ds(6695 - TAIL_ROW + n, 32, stride=3), :] for n in range(3))
    m_low[pl.ds(0, 32, stride=2), :] = first
    m_low[pl.ds(1, 32, stride=2), :] = jnp.concatenate([second[:, FILTERS:], third[:, :FILTERS]], 1)
    m_top[pl.ds(0, 32, stride=2), :] = second
    m_top[pl.ds(1, 32, stride=2), :] = pltpu.roll(third, FILTERS, 1)
    masker = jnp.concatenate([m_low[...], m_top[:, :FILTERS]], 1)
    taps = tail_s[6791 - TAIL_ROW:6792 - TAIL_ROW]
    lane_at = lax.broadcasted_iota(jnp.int32, (FILTERS, 128), 1)
    row_at = lax.broadcasted_iota(jnp.int32, (FILTERS, 128), 0)
    upright = [
        jnp.sum(jnp.where(lane_at == 2 * row_at + tap, taps, 0.0), 1, keepdims=True) for tap in range(2)
    ]
    decoder = jnp.concatenate(
        [
            jnp.concatenate([jnp.where(lane_at == j, column, 0.0) for column in upright], 1)
            for j in range(SOURCES)
        ],
        0,
    )
    put_split(masker, mk2, mkl)
    put_split(masker.T, mt2, mtl)
    put_split(decoder, dk2, dkl)
    put_split(decoder.T, dt2, dtl)
    amask[...] = jnp.zeros_like(amask)
    adec[...] = jnp.zeros_like(adec)
    active = active_ref[0:1]

    def rows(n):
        return pl.ds(pl.multiple_of(n * block, 8), block)

    def summed_of(n):
        here = sep[rows(n), :]
        group_at = lax.broadcasted_iota(jnp.int32, (block, FILTERS), 0) % groups
        shifted = pltpu.roll(pltpu.roll(here, FILTERS, 1), 1, 0)[:, :FILTERS]
        return here[:, :FILTERS] + jnp.where(group_at == 0, 0.0, shifted)

    def frames_of(n):
        encoded = stream_ref[rows(n), :][:, :FILTERS]
        return jnp.concatenate([encoded, encoded, encoded], 1)

    def ahead(n, carry):
        logits = dot3(summed_of(n), mk2[...], mkl[...])
        sig = jax.nn.sigmoid(logits)
        sig_s[rows(n), :] = sig
        both = dot3(sig * active * frames_of(n), dk2[...], dkl[...])
        now_s[rows(n), :] = both[:, :128]
        before_s[pl.ds(pl.multiple_of(n * block + groups, 8), block), :] = both[:, 128:]
        return carry

    lax.fori_loop(0, HOP // 10, ahead, 0)
    at = lax.broadcasted_iota(jnp.int32, (groups, 128), 0)
    before_s[:groups] = jnp.where(at == 0, 0.0, pltpu.roll(before_s[valid:], 1, 0))

    def losses(n, total):
        column = column_ref[rows(n), :]
        lane = lax.broadcasted_iota(jnp.int32, (block, 128), 1)
        active_lane = (lane < SOURCES) & (lane.astype(F32) < active_ref[1:2, :128])
        target = jnp.where(active_lane, column, 0.0)
        row = lax.broadcasted_iota(jnp.int32, (block, 128), 0)
        frame = HOP * (row % groups) + row // groups + 10 * n
        kept = jnp.where(frame.astype(F32) < active_ref[2:3, :128], active_ref[3:4, :128], 0.0)
        differ = now_s[rows(n), :] + before_s[rows(n), :] - target
        root = jnp.sqrt(differ * differ + 1.0)
        slope_s[rows(n), :] = kept * differ / root
        return total + jnp.sum(kept * (root - 1.0), 0, keepdims=True)

    total = lax.fori_loop(0, HOP // 10, losses, jnp.zeros((1, 128), F32))
    first_lane = lax.broadcasted_iota(jnp.int32, (8, 128), 1) == 0
    loss_ref[...] = jnp.where(first_lane, jnp.sum(total, 1, keepdims=True), note_ref[...])
    slope_s[valid:] = jnp.where(at == groups - 1, 0.0, pltpu.roll(slope_s[:groups], groups - 1, 0))

    def back(n, carry):
        slopes = jnp.concatenate(
            [slope_s[rows(n), :], slope_s[pl.ds(pl.multiple_of(n * block + groups, 8), block), :]], 1
        )
        sig = sig_s[rows(n), :]
        frames = frames_of(n)
        dmasked = dot3(slopes, dt2[...], dtl[...]) * active
        by_sig = dmasked * sig
        denc_ref[rows(n), :] = (
            by_sig[:, :FILTERS] + by_sig[:, FILTERS:2 * FILTERS] + by_sig[:, 2 * FILTERS:]
        )
        dlogits = by_sig * frames * (1.0 - sig)
        dsummed = dot3(dlogits, mt2[...], mtl[...])
        group_at = lax.broadcasted_iota(jnp.int32, (block, FILTERS), 0) % groups
        shifted = jnp.where(group_at == groups - 1, 0.0, pltpu.roll(dsummed, block - 1, 0))
        g_ref[rows(n), :] = jnp.concatenate([dsummed, shifted], 1)
        amask[...] += dot_rows3(summed_of(n), dlogits)
        adec[...] += dot_rows3(sig * active * frames, slopes)
        return carry

    lax.fori_loop(0, HOP // 10, back, 0)
    g_ref[valid:] = jnp.zeros((g_ref.shape[0] - valid, 128), F32)
    m_low[...] = amask[:, :128]
    m_top[...] = jnp.concatenate([amask[:, 128:], jnp.zeros((FILTERS, FILTERS), F32)], 1)
    low_even, low_odd = m_low[pl.ds(0, 32, stride=2), :], m_low[pl.ds(1, 32, stride=2), :]
    top_even, top_odd = m_top[pl.ds(0, 32, stride=2), :], m_top[pl.ds(1, 32, stride=2), :]
    hg_ref[pl.ds(0, 32, stride=3), :] = low_even
    hg_ref[pl.ds(1, 32, stride=3), :] = jnp.concatenate([top_even[:, :FILTERS], low_odd[:, :FILTERS]], 1)
    hg_ref[pl.ds(2, 32, stride=3), :] = jnp.concatenate([low_odd[:, FILTERS:], top_odd[:, :FILTERS]], 1)
    columns = []
    for tap in range(2):
        found = 0.0
        for j in range(SOURCES):
            found = found + adec[j * FILTERS:(j + 1) * FILTERS, 128 * tap + j:128 * tap + j + 1]
        columns.append(jnp.broadcast_to(found, (FILTERS, 128)))
    lane = lax.broadcasted_iota(jnp.int32, (FILTERS, 128), 1)
    hg_ref[96:HEAD_ROWS] = jnp.where(lane == 0, columns[0], jnp.where(lane == 1, columns[1], 0.0))


def assemble(flat, layers):
    lane = lax.broadcasted_iota(jnp.int32, (FILTERS, 128), 1)
    row = lax.broadcasted_iota(jnp.int32, (FILTERS, 128), 0)

    def interleave(a, b):
        return jnp.sum(jnp.where(lane == 2 * row, a, jnp.where(lane == 2 * row + 1, b, 0.0)), 0, keepdims=True)

    for layer_no, ref in enumerate(layers):
        if ref is None:
            continue
        first, inner, odd = window(layer_no)
        at = first + inner
        parts = [(ref[0, :OWN_PROJ], False), (ref[1, :OWN_PROJ], False), (ref[0, OWN_PROJ:OWN_VEC], False)]
        parts += [(ref[1, OWN_PROJ:OWN_VEC], False), (ref[0, OWN_VEC:OWN_VEC + 2], True)]
        for rows, ends in parts:
            count = rows.shape[0]
            if odd:
                turned = pltpu.roll(rows, FILTERS, 1) if count >= 8 else jnp.concatenate(
                    [rows[:, FILTERS:], rows[:, :FILTERS]], 1
                )
                wide_low = lax.broadcasted_iota(jnp.int32, (count - 1, 128), 1) < FILTERS
                flat[at:at + 1, FILTERS:] = turned[0:1, FILTERS:]
                flat[at + 1:at + count] = jnp.where(wide_low, turned[:-1], turned[1:])
                if not ends:
                    flat[at + count:at + count + 1, :FILTERS] = turned[count - 1:, :FILTERS]
            elif ends:
                flat[at:at + 1] = rows[0:1]
                flat[at + 1:at + 2, :FILTERS] = rows[1:2, :FILTERS]
            else:
                flat[at:at + count] = rows
            at += count
        if layer_no == 0:
            encoder = ref[0, OWN_EXTRA:OWN_EXTRA + 1] + ref[1, OWN_EXTRA:OWN_EXTRA + 1]
            encoder = jnp.broadcast_to(encoder, (FILTERS, 128))
            first_tap = jnp.sum(jnp.where(lane == row, encoder, 0.0), 1, keepdims=True)
            second_tap = jnp.sum(jnp.where(lane == row + FILTERS, encoder, 0.0), 1, keepdims=True)
            flat[0:1] = interleave(first_tap, second_tap)
        if layer_no == 2 * BLOCKS - 1:
            flat[6695:6791] = ref[0, OWN_EXTRA:OWN_EXTRA + 96]
            decoder = ref[0, OWN_EXTRA + 96:OWN_EXTRA + HEAD_ROWS]
            flat[6791:6792] = interleave(decoder[:, 0:1], decoder[:, 1:2])
            flat[6792:] = jnp.zeros((flat.shape[0] - 6792, 128), F32)


def finish_kernel(chips, depths, entries, own_ref, r1, r2, r3, grad_ref, note_ref, flat, b1, b2, b3, sems, *rest):
    b = lax.axis_index("batch")
    barrier, count = greet_all(chips, depths)
    pairs = ((r1, b1), (r2, b2), (r3, b3))
    fetches = [pltpu.make_async_copy(src, dst, sems.at[n]) for n, (src, dst) in enumerate(pairs)]
    for copy in fetches:
        copy.start()
    pl.semaphore_wait(barrier, count)
    stages = reducer(own_ref, chips, depths, rest)
    stages[0]()
    for copy in fetches:
        copy.wait()
    assemble(flat, (None, b1, b2, b3))
    for stage in stages[1:]:
        stage()
    r0 = rest[0]
    assemble(flat, (r0, None, None, None))
    note_ref[...] = jnp.zeros_like(note_ref)
    squares = jnp.sum(jnp.sum(flat[...] * flat[...], 0, keepdims=True), 1, keepdims=True)
    lane = lax.broadcasted_iota(jnp.int32, (1, 128), 1)
    note_ref[0:1] = jnp.where(lane == 2, squares, r0[0, OWN_EXTRA + 1:OWN_EXTRA + 2])
    rows = grad_ref.shape[0]
    row_at, lane_at = lax.div(b * entries, 128), lax.rem(b * entries, 128)
    gradient = flat[pl.ds(row_at, rows), :]
    if entries % 128:
        lane = lax.broadcasted_iota(jnp.int32, (rows, 128), 1)
        turn = lax.rem(128 - lane_at, 128)
        gradient = jnp.where(
            lane < 128 - lane_at, pltpu.roll(gradient, turn, 1), pltpu.roll(flat[pl.ds(row_at + 1, rows), :], turn, 1)
        )
    grad_ref[...] = gradient


def update_kernel(grad_ref, note_ref, p_ref, m_ref, v_ref, new_ref, half_ref, first_ref, second_ref, norm_ref, loss_ref):
    rows = grad_ref.shape[0]
    note = note_ref[0:1]
    lane = lax.broadcasted_iota(jnp.int32, (1, 128), 1)
    count = jnp.sum(jnp.where(lane == 1, note, 0.0), 1, keepdims=True)
    norm = jnp.sqrt(jnp.sum(jnp.where(lane == 2, note, 0.0), 1, keepdims=True)) / count
    norm_ref[0] = norm[0, 0]
    loss_ref[0] = note[0, 0]
    loss_ref[1] = note[0, 1]
    clipped = grad_ref[...] / count * (CLIP_AT / jnp.maximum(norm, CLIP_AT))
    new_first = BETA_ONE * m_ref[...].reshape(rows, 128) + (1.0 - BETA_ONE) * clipped
    new_second = BETA_TWO * v_ref[...].reshape(rows, 128) + (1.0 - BETA_TWO) * clipped * clipped
    step_size = (
        new_first / (1.0 - BETA_ONE**STEP) / (jnp.sqrt(new_second / (1.0 - BETA_TWO**STEP)) + ADAM_EPS)
    )
    params = p_ref[...].reshape(rows, 128)
    new_params = params - LEARN_RATE * (step_size + DECAY_RATE * params)
    new_ref[...] = new_params.reshape(new_ref.shape)
    half_ref[...] = new_params.astype(BF16).reshape(half_ref.shape)
    first_ref[...] = new_first.reshape(first_ref.shape)
    second_ref[...] = new_second.reshape(second_ref.shape)


def start_kernel(chips, depths, items, groups, gathers, p_ref, mail_ref, *refs):
    *views, refs = *refs[:5], refs[5:]
    if gathers:
        *refs, flat_ref = refs
    else:
        flat_ref = p_ref
    *refs, view_sem = refs
    (stream_ref, column_ref, active_ref, encoder_ref, note_ref,
     inbox, planes, plane_sem, pair_sem, own_sem, mail_sem) = refs
    b = lax.axis_index("batch")
    z = lax.axis_index("frames")
    core = lax.rem(b, 2)
    chip = lax.div(b, 2)
    sibling = (b + 1 - 2 * core, z)
    entries = p_ref.shape[0]
    copies = depths // (2 * items)
    share = groups // depths
    valid = HOP * groups
    mail_rows = mail_ref.shape[0] // items
    mesh = pl.DeviceIdType.MESH

    barrier = pltpu.get_barrier_semaphore()
    for step in range(1, chips):
        pl.semaphore_signal(barrier, inc=1, device_id=(lax.rem(b + 2 * step, 2 * chips), z), device_id_type=mesh)
    for step in range(1, depths):
        pl.semaphore_signal(barrier, inc=1, device_id=(b, lax.rem(z + step, depths)), device_id_type=mesh)
    for step in range(depths):
        pl.semaphore_signal(barrier, inc=1, device_id=(sibling[0], lax.rem(z + step, depths)), device_id_type=mesh)
    pl.semaphore_wait(barrier, chips - 1 + 2 * depths - 1)

    def shard(at):
        return flat_ref.at[pl.ds(pl.multiple_of(at * entries, 128), entries)]

    def send(src, dst, sems, slot, device):
        return pltpu.make_async_remote_copy(
            src_ref=src, dst_ref=dst, send_sem=sems.at[0, slot], recv_sem=sems.at[1, slot],
            device_id=device, device_id_type=mesh,
        )

    if gathers:
        across = [
            send(p_ref, shard(b), plane_sem, step - 1, (lax.rem(b + 2 * step, 2 * chips), z))
            for step in range(1, chips)
        ]
        for copy in across:
            copy.start()
        beside = [send(p_ref, shard(b), pair_sem, 0, sibling)]
        beside[0].start()
        own = pltpu.make_async_copy(p_ref, shard(b), own_sem)
        own.start()
    letters = []
    for item in range(items):
        for other in range(2):
            for copy_no in range(copies):
                depth = (items * core + item) * copies + copy_no
                here = (core == other) & (z == depth)
                src = mail_ref.at[pl.ds(item * mail_rows, mail_rows)]
                far = pltpu.make_async_remote_copy(
                    src_ref=src, dst_ref=inbox.at[z], send_sem=mail_sem.at[1, len(letters)], recv_sem=mail_sem.at[0, z],
                    device_id=(2 * chip + other, depth), device_id_type=mesh,
                )
                near = pltpu.make_async_copy(src, inbox.at[z], mail_sem.at[0, z])

                @pl.when(here)
                def _():
                    near.start()

                @pl.when(jnp.logical_not(here))
                def _():
                    far.start()

                letters.append((here, far))
    for depth in range(depths):
        pltpu.make_async_copy(inbox.at[depth], inbox.at[depth], mail_sem.at[0, depth]).wait()
    for here, far in letters:
        @pl.when(jnp.logical_not(here))
        def _():
            far.wait_send()

    frames = jnp.concatenate([inbox[depth, :share] for depth in range(depths)], 0)
    facts = inbox[0, share:share + 1]
    speakers, length = facts[:, 0:1], facts[:, 1:2]
    whole_item = jnp.where(lax.rem(z, copies) == 0, 1.0, 0.0)
    lead = jnp.where(core == 0, whole_item, 0.0)
    lane = lax.broadcasted_iota(jnp.int32, (groups, 128), 1)
    group = lax.broadcasted_iota(jnp.int32, (groups, 128), 0)
    note_ref[...] = jnp.where(lane[:8] == 1, lead * length, 0.0)
    wide = SOURCES * FILTERS
    source = lax.broadcasted_iota(jnp.int32, (8, wide), 1) // FILTERS
    fact_at = lax.broadcasted_iota(jnp.int32, (8, wide), 0)
    active = jnp.where(source.astype(F32) < speakers, 1.0, 0.0)
    active = jnp.where(fact_at == 1, speakers, jnp.where(fact_at == 2, length, active))
    active_ref[...] = jnp.where(fact_at == 3, whole_item, active)
    end = HOP * FRAME_LANES
    tile = end // 128 * 128
    opening = jnp.where(group == groups - 1, 0.0, pltpu.roll(frames[:, :128], groups - 1, 0))
    ending = (lane >= end - tile) & (lane < end - tile + FRAME_LANES)
    planes[:, :tile] = frames[:, :tile]
    planes[:, tile:tile + 128] = jnp.where(ending, pltpu.roll(opening, end - tile, 1), frames[:, tile:tile + 128])
    planes[:, tile + 128:] = jnp.zeros((groups, planes.shape[1] - tile - 128), F32)
    for k in range(HOP):
        column_ref[k * groups:(k + 1) * groups] = planes[:, FRAME_LANES * k:FRAME_LANES * k + 128]

    if gathers:
        for step in range(1, chips):
            across[step - 1].wait_recv()
            at = lax.rem(b + 2 * chips - 2 * step, 2 * chips)
            beside.append(send(shard(at), shard(at), pair_sem, step, sibling))
            beside[-1].start()
        for copy in across:
            copy.wait_send()
        own.wait()
        for copy in beside:
            copy.wait()

    bounds = [(window(n)[0], WINDOW) for n in range(2 * BLOCKS)] + [(TAIL_ROW, TAIL_ROWS)]
    stores = [
        pltpu.make_async_copy(flat_ref.at[pl.ds(128 * at, 128 * count)], view, view_sem.at[n])
        for n, ((at, count), view) in enumerate(zip(bounds, views))
    ]
    for store in stores:
        store.start()
    taps = flat_ref[0:128].reshape(1, 128)
    at_lane = lax.broadcasted_iota(jnp.int32, (128, 128), 1)
    at_row = lax.broadcasted_iota(jnp.int32, (128, 128), 0)
    upright = jnp.sum(jnp.where(at_lane == at_row, taps, 0.0), 1, keepdims=True)
    twice = 2 * lax.rem(at_lane, FILTERS)
    tap_rows = [jnp.sum(jnp.where(at_row == twice + tap, upright, 0.0), 0, keepdims=True) for tap in range(2)]
    encoder_ref[...] = jnp.where(at_row[:8] == 0, tap_rows[0], jnp.where(at_row[:8] == 1, tap_rows[1], 0.0))

    block = 5 * groups
    block_lane = lax.broadcasted_iota(jnp.int32, (block, 128), 1)
    last_group = lax.broadcasted_iota(jnp.int32, (block, 128), 0) % groups == groups - 1

    def encode(n, carry):
        rows = pl.ds(pl.multiple_of(n * block, 8), block)
        column = column_ref[rows, :]
        raw = column[:, MIX_LANE:MIX_LANE + 1] * tap_rows[0] + column[:, NEXT_LANE:NEXT_LANE + 1] * tap_rows[1]
        encoded = jnp.maximum(raw, 0.0) + jnp.log1p(jnp.exp(-jnp.abs(raw)))
        later = jnp.where(last_group, 0.0, pltpu.roll(encoded, block - 1, 0))
        stream_ref[rows, :] = jnp.where(block_lane < FILTERS, encoded, later)
        return carry

    lax.fori_loop(0, HOP // 5, encode, 0)
    stream_ref[valid:] = jnp.zeros((stream_ref.shape[0] - valid, 128), F32)
    for store in stores:
        store.wait()


def sizes(inter, groups):
    if inter:
        return groups, 2 * HALF_PAD, 4
    return 2 * HOP, groups, 5


def whole(shape):
    return pl.BlockSpec(shape, lambda j: (0,) * len(shape))


def run_start(params, mixture, sources, speakers, lengths):
    items, samples_here = mixture.shape
    depths = lax.axis_size("frames")
    chips = lax.axis_size("batch") // 2
    groups = samples_here * depths // HOP
    share = groups // depths
    valid = HOP * groups
    copies = depths // (2 * items)
    signals = jnp.concatenate([sources, mixture[:, None]], 1).transpose(0, 2, 1)
    signals = jnp.pad(signals, ((0, 0), (0, 0), (0, FRAME_LANES - 1 - SOURCES)))
    signals = signals.reshape(items, share, HOP * FRAME_LANES)
    width = -(-HOP * FRAME_LANES // 128) * 128
    facts = jnp.stack([speakers, lengths], 1).astype(F32)[:, None]
    mail_rows = -(-(share + 1) // 8) * 8
    mail = jnp.concatenate(
        [
            jnp.pad(signals, ((0, 0), (0, 0), (0, width - HOP * FRAME_LANES))),
            jnp.pad(facts, ((0, 0), (0, mail_rows - share - 1), (0, width - 2))),
        ],
        1,
    ).reshape(items * mail_rows, width)
    stream_shape = (HALF_PAD * groups, 128)
    out = [stream_shape, (valid, 128), (8, SOURCES * FILTERS), (8, 128), (8, 128)]
    out = [(WINDOW * 128,)] * (2 * BLOCKS) + [(TAIL_ROWS * 128,)] + out
    gathers = params.shape[0] % 128 == 0
    whole_flat = [pltpu.VMEM((params.shape[0] * 2 * chips,), F32)] if gathers else []
    if not gathers:
        params = lax.all_gather(params, "batch", axis=0, tiled=True)
    vmem = pl.BlockSpec(memory_space=pltpu.VMEM)
    sems = pltpu.SemaphoreType.DMA
    found = pl.pallas_call(
        functools.partial(start_kernel, chips, depths, items, groups, gathers),
        in_specs=[vmem] * 2,
        out_specs=[pl.BlockSpec(memory_space=pl.ANY)] * 5 + [vmem] * 5,
        out_shape=[jax.ShapeDtypeStruct(shape, F32) for shape in out],
        scratch_shapes=[
            pltpu.VMEM((depths, mail_rows, width), F32), pltpu.VMEM((groups, width + 128), F32),
            sems((2, chips - 1)), sems((2, chips)), sems, sems((2, max(depths, 2 * items * copies))), sems((5,)),
        ]
        + whole_flat,
        compiler_params=pltpu.CompilerParams(
            vmem_limit_bytes=VMEM_MAX, collective_id=10, has_side_effects=True
        ),
        name="start",
    )(params, mail)
    return [a.reshape(-1, 128) for a in found[:5]], found[5:]


def run_forward(layer_no, groups, stream, flat):
    inter = layer_no % 2 == 1
    length, rows, steps = sizes(inter, groups)
    stream_shape = (HALF_PAD * groups, 128)
    out = [
        (stream_shape, whole(stream_shape)),
        (stream_shape, whole(stream_shape)),
        ((8, 128), whole((8, 128))),
        ((length, rows, UNITS), pl.BlockSpec((2 * steps, rows, UNITS), lambda j: (j, 0, 0))),
        ((length, 6, rows, UNITS), pl.BlockSpec((2 * steps, 6, rows, UNITS), lambda j: (j, 0, 0, 0))),
    ]
    return pl.pallas_call(
        functools.partial(forward_kernel, layer_no, groups, steps),
        grid=(length // (2 * steps),),
        in_specs=[whole(stream_shape), whole((WINDOW, 128))],
        out_specs=[spec for _, spec in out],
        out_shape=[jax.ShapeDtypeStruct(shape, F32) for shape, _ in out],
        scratch_shapes=[
            pltpu.VMEM((256, GATES), BF16),
            pltpu.VMEM((256, GATES), BF16), pltpu.VMEM((128, GATES), BF16),
            pltpu.VMEM((UNITS, 128), BF16),
            pltpu.VMEM((UNITS, 128), F32),
            pltpu.VMEM((8, GATES), F32),
            pltpu.VMEM((steps * rows, GATES), F32), pltpu.VMEM((steps * rows, GATES), F32),
            pltpu.VMEM((steps * rows, UNITS), F32), pltpu.VMEM((steps * rows, UNITS), F32),
            pltpu.VMEM((rows, UNITS), F32),
            pltpu.VMEM(stream_shape, F32), pltpu.VMEM(stream_shape, F32), pltpu.SemaphoreType.DMA((2,)),
        ],
        compiler_params=pltpu.CompilerParams(
            vmem_limit_bytes=VMEM_MAX, collective_id=2 + layer_no, has_side_effects=True
        ),
        name="forward_inter" if inter else "forward_intra",
    )(stream, flat)


def run_backward(layer_no, groups, grad, kept, flat, extra):
    inter = layer_no % 2 == 1
    last_layer = layer_no == 2 * BLOCKS - 1
    length, rows, steps = sizes(inter, groups)
    stream_shape = (HALF_PAD * groups, 128)
    count = length // (2 * steps)
    depths = lax.axis_size("frames")
    chips = lax.axis_size("batch") // 2
    out = [(reduced_rows(OWN_ROWS[layer_no], chips, depths), 128)]
    scratch = []
    if not last_layer:
        upper_rows = reduced_rows(OWN_ROWS[layer_no + 1], chips, depths)
        out = [(2, upper_rows, 128)] + out
        scratch = reducer_scratch(upper_rows, chips, depths)
    if layer_no:
        out = [stream_shape] + out
    x, normed, scale, h_all, coef = kept
    return pl.pallas_call(
        functools.partial(backward_kernel, layer_no, groups, steps, chips, depths),
        grid=(count,),
        in_specs=[whole(a.shape) for a in (grad, normed, scale, x, h_all)]
        + [pl.BlockSpec((2 * steps, 6, rows, UNITS), lambda j: (count - 1 - j, 0, 0, 0)), whole((WINDOW, 128))]
        + [whole(a.shape) for a in extra],
        out_specs=[whole(shape) for shape in out],
        out_shape=[jax.ShapeDtypeStruct(shape, F32) for shape in out],
        scratch_shapes=[
            pltpu.VMEM((GATES, 128), BF16),
            pltpu.VMEM((GATES, 256), BF16), pltpu.VMEM((GATES, 128), BF16),
            pltpu.VMEM((256, UNITS), BF16),
            pltpu.VMEM((UNITS, 128), F32),
            pltpu.VMEM(stream_shape, F32),
            pltpu.VMEM((steps * rows, UNITS), F32), pltpu.VMEM((steps * rows, UNITS), F32),
            pltpu.VMEM((steps * rows, GATES), F32), pltpu.VMEM((steps * rows, GATES), F32),
            pltpu.VMEM((rows, UNITS), F32),
            pltpu.VMEM((UNITS + FILTERS, GATES), F32), pltpu.VMEM((2 * UNITS if inter else UNITS, 128), F32),
            pltpu.VMEM((8, GATES), F32),
            pltpu.VMEM(stream_shape, F32), pltpu.VMEM(stream_shape, F32), pltpu.SemaphoreType.DMA((2,)),
        ]
        + scratch,
        compiler_params=pltpu.CompilerParams(vmem_limit_bytes=VMEM_MAX, collective_id=6 + layer_no, has_side_effects=True),
        name="backward_inter" if inter else "backward_intra",
    )(grad, normed, scale, x, h_all, coef, flat, *extra)


def run_head(groups, separated, stream, column, active, note, tail):
    valid = HOP * groups
    stream_shape = (HALF_PAD * groups, 128)
    out = [stream_shape, (HEAD_ROWS, 128), (valid, FILTERS), (8, 128)]
    wide = SOURCES * FILTERS
    operands = (separated, stream, column, active, note, tail)
    return pl.pallas_call(
        functools.partial(head_kernel, groups),
        grid=(1,),
        in_specs=[whole(a.shape) for a in operands],
        out_specs=[whole(shape) for shape in out],
        out_shape=[jax.ShapeDtypeStruct(shape, F32) for shape in out],
        scratch_shapes=[
            pltpu.VMEM((valid, wide), F32), pltpu.VMEM((valid, 128), F32),
            pltpu.VMEM((valid + groups, 128), F32), pltpu.VMEM((valid + groups, 128), F32),
            pltpu.VMEM((2 * FILTERS, wide), BF16), pltpu.VMEM((FILTERS, wide), BF16),
            pltpu.VMEM((2 * wide, FILTERS), BF16), pltpu.VMEM((wide, FILTERS), BF16),
            pltpu.VMEM((2 * wide, 256), BF16), pltpu.VMEM((wide, 256), BF16),
            pltpu.VMEM((512, wide), BF16), pltpu.VMEM((256, wide), BF16),
            pltpu.VMEM((FILTERS, wide), F32), pltpu.VMEM((wide, 256), F32),
            pltpu.VMEM((FILTERS, 128), F32), pltpu.VMEM((FILTERS, 128), F32),
        ],
        compiler_params=pltpu.CompilerParams(vmem_limit_bytes=VMEM_MAX),
        name="head",
    )(*operands)


def run_finish(layers, params, first_moment, second_moment):
    entries = params.shape[0]
    rows = -(-entries // 128)
    depths = lax.axis_size("frames")
    chips = lax.axis_size("batch") // 2
    vmem = pl.BlockSpec(memory_space=pltpu.VMEM)
    gradient, note = pl.pallas_call(
        functools.partial(finish_kernel, chips, depths, entries),
        in_specs=[vmem] + [pl.BlockSpec(memory_space=pl.ANY)] * 3,
        out_specs=[vmem] * 2,
        out_shape=[jax.ShapeDtypeStruct(shape, F32) for shape in ((rows, 128), (8, 128))],
        scratch_shapes=[pltpu.VMEM((6808, 128), F32)]
        + [pltpu.VMEM(a.shape, F32) for a in layers[1:]]
        + [pltpu.SemaphoreType.DMA((3,))]
        + reducer_scratch(layers[0].shape[0], chips, depths),
        compiler_params=pltpu.CompilerParams(
            vmem_limit_bytes=VMEM_MAX, collective_id=1, has_side_effects=True
        ),
        name="finish",
    )(*layers)
    shards = [params, first_moment, second_moment]
    shape = (entries,)
    if entries % 128:
        shape = (rows, 128)
        shards = [jnp.pad(a, (0, rows * 128 - entries)).reshape(shape) for a in shards]
    smem = pl.BlockSpec(memory_space=pltpu.SMEM)
    out = [(shape, F32), (shape, BF16), (shape, F32), (shape, F32), ((1,), F32), ((2,), F32)]
    found = pl.pallas_call(
        update_kernel,
        in_specs=[vmem] * 5,
        out_specs=[vmem] * 4 + [smem] * 2,
        out_shape=[jax.ShapeDtypeStruct(shape, dtype) for shape, dtype in out],
        compiler_params=pltpu.CompilerParams(vmem_limit_bytes=VMEM_MAX),
        name="update",
    )(gradient, note, *shards)
    return [a.reshape(-1)[:entries] for a in found[:4]] + [found[4][0], found[5]]


def local(params, first_moment, second_moment, mixture, sources, speakers, lengths):
    groups = mixture.shape[1] * lax.axis_size("frames") // HOP
    views, (stream, column, active, encoder, note) = run_start(params, mixture, sources, speakers, lengths)
    kept = []
    x = stream
    for layer_no in range(2 * BLOCKS):
        after, normed, scale, h_all, coef = run_forward(layer_no, groups, x, views[layer_no])
        kept.append((x, normed, scale, h_all, coef))
        x = after
    grad, head_grads, grad_encoded, loss = run_head(groups, x, stream, column, active, note, views[2 * BLOCKS])
    sums = [None] * (2 * BLOCKS)
    for layer_no in reversed(range(2 * BLOCKS)):
        extra = ()
        if layer_no == 2 * BLOCKS - 1:
            extra = (head_grads,)
        if layer_no == 0:
            extra = (column, grad_encoded, encoder, loss)
        if layer_no < 2 * BLOCKS - 1:
            extra = extra + (sums[layer_no + 1],)
        *found, sums[layer_no] = run_backward(layer_no, groups, grad, kept[layer_no], views[layer_no], extra)
        if layer_no < 2 * BLOCKS - 1:
            sums[layer_no + 1] = found[-1]
        if layer_no:
            grad = found[0]
    return tuple(run_finish(sums, params, first_moment, second_moment))


def solution(mesh):
    placed = (
        P("batch"),
        P("batch"),
        P("batch"),
        P("batch", "frames"),
        P("batch", None, "frames"),
        P("batch"),
        P("batch"),
    )
    return jax.shard_map(
        local,
        mesh=mesh,
        in_specs=placed,
        out_specs=(P("batch"), P("batch"), P("batch"), P("batch"), P(), P()),
        check_vma=False,
    )
```

```python
import functools
import math

import jax
import jax.numpy as jnp
from jax import lax
from jax.experimental import pallas as pl
from jax.experimental.pallas import tpu as pltpu
from jax.sharding import PartitionSpec as P

FILTERS = 64
UNITS = 128
HOP = 50
HALF_PAD = 56
SOURCES = 3
BLOCKS = 2
STEP = 5
GATES = 4 * UNITS

HIGHEST = lax.Precision.HIGHEST
NORM_EPS = 1e-08
CLIP_AT = 0.001
BETA_ONE = 0.5
BETA_TWO = 0.5
LEARN_RATE = 0.05
DECAY_RATE = 0.01
ADAM_EPS = 1e-08
F32 = jnp.float32
BF16 = jnp.bfloat16
VMEM_MAX = 60 * 2**20


def split(a):
    hi = a.astype(BF16)
    return hi, (a - hi.astype(F32)).astype(BF16)


def dot(a, b):
    return jnp.dot(a, b, preferred_element_type=F32)


def dot3(a, w_twice, w_low):
    hi, lo = split(a)
    return dot(jnp.concatenate([hi, lo], 1), w_twice) + dot(hi, w_low)


def dot_rows(a, b):
    return lax.dot_general(a, b, (((0,), (0,)), ((), ())), preferred_element_type=F32)


def dot_rows3(a, b):
    a_hi, a_lo = split(a)
    b_hi, b_lo = split(b)
    return dot_rows(a_hi, b_hi) + dot_rows(a_lo, b_hi) + dot_rows(a_hi, b_lo)


SIDE_ROWS = 772
PROJ_ROWS = 2 * SIDE_ROWS
VEC_ROW = PROJ_ROWS + 128
LAYER_ROWS = 1680
HEAD_ROWS = 160
OWN_PROJ = SIDE_ROWS
OWN_VEC = SIDE_ROWS + 64
OWN_EXTRA = SIDE_ROWS + 68
OWN_ROWS = (OWN_EXTRA + 8, OWN_EXTRA, OWN_EXTRA, OWN_EXTRA + HEAD_ROWS)
WINDOW = 1688
TAIL_ROW = 6688
TAIL_ROWS = 104
SHARE_ROWS = 256
FRAME_LANES = 8
MIX_LANE = SOURCES
NEXT_LANE = FRAME_LANES + MIX_LANE


def window(layer_no):
    at = 2 + 3347 * layer_no
    return at // 16 * 8, at // 2 % 8, at % 2


def pick(ref, base, odd, start, count, stride=1):
    def load(at):
        return ref[pl.ds(at, count, stride=stride), :] if stride > 1 else ref[pl.ds(at, count), :]

    first = load(base + start)
    if not odd:
        return first
    return jnp.concatenate([first[:, 64:], load(base + start + 1)[:, :64]], 1)


def load_weights(ref, base, odd, dir_no, proj_s):
    at = SIDE_ROWS * dir_no
    win = jnp.concatenate([pick(ref, base, odd, at + q, FILTERS, 4) for q in range(4)], 1)
    wrec = jnp.concatenate([pick(ref, base, odd, at + 256 + q, UNITS, 4) for q in range(4)], 1)
    bias = jnp.concatenate([pick(ref, base, odd, at + 768 + q, 1) for q in range(4)], 1)
    pairs = pick(ref, base, odd, PROJ_ROWS + 64 * dir_no, 64)
    proj_s[pl.ds(0, 64, stride=2), :] = pairs
    proj_s[pl.ds(1, 64, stride=2), :] = pltpu.roll(pairs, 64, 1)
    return win, wrec, bias, proj_s[:, :FILTERS]


def load_vec(ref, base, odd):
    first = pick(ref, base, odd, VEC_ROW, 1)
    turned = pltpu.roll(jnp.broadcast_to(first, (8, 128)), 64, 1)[0:1]
    if odd:
        last = ref[base + VEC_ROW + 1:base + VEC_ROW + 2, :]
        last = jnp.concatenate([last[:, 64:], last[:, 64:]], 1)
    else:
        last = ref[base + VEC_ROW + 1:base + VEC_ROW + 2, :]
        last = jnp.concatenate([last[:, :64], last[:, :64]], 1)
    low = lax.broadcasted_iota(jnp.int32, (1, 128), 1) < 64
    return jnp.where(low, first, turned), jnp.where(low, turned, first), last


def share_of(tasks, number, count):
    return tasks[number * len(tasks) // count:(number + 1) * len(tasks) // count]


def fold_halves(a):
    return a + pltpu.roll(a, FILTERS, 1)


def narrow(a, half):
    if isinstance(half, int):
        a = pltpu.roll(a, FILTERS, 1) if half else a
    else:
        a = jnp.where(half == 0, a, pltpu.roll(a, FILTERS, 1))
    low_lanes = lax.broadcasted_iota(jnp.int32, a.shape, 1) < FILTERS
    hi = a.astype(BF16).astype(F32)
    lo = pltpu.roll(a - hi, FILTERS, 1)
    return jnp.concatenate([jnp.where(low_lanes, hi, lo), jnp.where(low_lanes, hi, 0.0)], 1).astype(BF16)


def narrow_weights(w):
    hi, lo = split(w)
    return jnp.concatenate([hi, hi, lo, jnp.zeros_like(hi)], 0)


def side_weights(w):
    hi, lo = split(w)
    return jnp.concatenate([hi, lo], 1)


def dot_sides(a, w):
    hi, lo = split(a)
    return fold_halves(dot(hi, w) + dot(lo, w))


def put_split(w, twice_ref, low_ref):
    hi, lo = split(w)
    twice_ref[...] = jnp.concatenate([hi, hi], 0)
    low_ref[...] = lo


def times(dir_no, chunk_no, length, steps):
    return [dir_no * (length - 1) + (1 - 2 * dir_no) * (chunk_no * steps + u) for u in range(steps)]


def stream_rows(inter, groups, at):
    if inter:
        return pl.ds(at, HALF_PAD, stride=groups)
    return pl.ds(pl.multiple_of(lax.rem(at, HOP) * groups, 8), groups)


def gather(ref, inter, groups, positions):
    return jnp.concatenate([ref[stream_rows(inter, groups, at), :] for at in positions], 0)


def to_sides(inter, steps, array):
    if not inter:
        return [array]
    three = array.reshape(steps, 2 * HALF_PAD, array.shape[-1])
    return [
        three[:, side * HALF_PAD:(side + 1) * HALF_PAD].reshape(steps * HALF_PAD, array.shape[-1]) for side in range(2)
    ]


SIDE_ROWS = 772
PROJ_ROWS = 2 * SIDE_ROWS
VEC_ROW = PROJ_ROWS + 128
LAYER_ROWS = 1680
HEAD_ROWS = 160
OWN_PROJ = SIDE_ROWS
OWN_VEC = SIDE_ROWS + 64
OWN_EXTRA = SIDE_ROWS + 68
OWN_ROWS = (OWN_EXTRA + 8, OWN_EXTRA, OWN_EXTRA, OWN_EXTRA + HEAD_ROWS)
WINDOW = 1688
TAIL_ROW = 6688
TAIL_ROWS = 104
SHARE_ROWS = 256
FRAME_LANES = 8
MIX_LANE = SOURCES
NEXT_LANE = FRAME_LANES + MIX_LANE


def window(layer_no):
    at = 2 + 3347 * layer_no
    return at // 16 * 8, at // 2 % 8, at % 2


def pick(ref, base, odd, start, count, stride=1):
    def load(at):
        return ref[pl.ds(at, count, stride=stride), :] if stride > 1 else ref[pl.ds(at, count), :]

    first = load(base + start)
    if not odd:
        return first
    return jnp.concatenate([first[:, 64:], load(base + start + 1)[:, :64]], 1)


def load_weights(ref, base, odd, dir_no, proj_s):
    at = SIDE_ROWS * dir_no
    win = jnp.concatenate([pick(ref, base, odd, at + q, FILTERS, 4) for q in range(4)], 1)
    wrec = jnp.concatenate([pick(ref, base, odd, at + 256 + q, UNITS, 4) for q in range(4)], 1)
    bias = jnp.concatenate([pick(ref, base, odd, at + 768 + q, 1) for q in range(4)], 1)
    pairs = pick(ref, base, odd, PROJ_ROWS + 64 * dir_no, 64)
    proj_s[pl.ds(0, 64, stride=2), :] = pairs
    proj_s[pl.ds(1, 64, stride=2), :] = pltpu.roll(pairs, 64, 1)
    return win, wrec, bias, proj_s[:, :FILTERS]


def load_vec(ref, base, odd):
    first = pick(ref, base, odd, VEC_ROW, 1)
    turned = pltpu.roll(jnp.broadcast_to(first, (8, 128)), 64, 1)[0:1]
    if odd:
        last = ref[base + VEC_ROW + 1:base + VEC_ROW + 2, :]
        last = jnp.concatenate([last[:, 64:], last[:, 64:]], 1)
    else:
        last = ref[base + VEC_ROW + 1:base + VEC_ROW + 2, :]
        last = jnp.concatenate([last[:, :64], last[:, :64]], 1)
    low = lax.broadcasted_iota(jnp.int32, (1, 128), 1) < 64
    return jnp.where(low, first, turned), jnp.where(low, turned, first), last


def put_split(w, twice_ref, low_ref):
    hi, lo = split(w)
    twice_ref[...] = jnp.concatenate([hi, hi], 0)
    low_ref[...] = lo


def place(dir_no, chunk_no, count, steps, inter, groups):
    first = jnp.where(dir_no == 0, chunk_no * steps, (count - 1 - chunk_no) * steps)
    if inter:
        return first, 0, 0
    half = first // HOP
    return first, half, pl.multiple_of((first - HOP * half) * groups, 8)


def norm_stage(prev_ref, pa_ref, pb_ref, flat_ref, base, odd, valid, normed_ref, scale_ref, x_ref):
    offset, gain, shift = load_vec(flat_ref, base, odd)
    mixed = pa_ref[:valid] + pb_ref[:valid] + offset
    total = 2.0 * valid * FILTERS
    mean = jnp.sum(mixed) / total
    spread = jnp.sum(mixed * mixed) / total - mean * mean
    scale = lax.rsqrt(jnp.full((1, 128), spread + NORM_EPS, F32))
    normed = (mixed - mean) * scale
    normed_ref[:valid] = normed
    normed_ref[valid:] = jnp.zeros((normed_ref.shape[0] - valid, 128), F32)
    x_ref[:valid] = prev_ref[:valid] + gain * normed + shift
    x_ref[valid:] = jnp.zeros((x_ref.shape[0] - valid, 128), F32)
    scale_ref[...] = jnp.broadcast_to(scale, scale_ref.shape)


def greet_sibling():
    b = lax.axis_index("batch")
    device = (b + 1 - 2 * lax.rem(b, 2), lax.axis_index("frames"))
    return device, pltpu.get_barrier_semaphore()


def swap_with_sibling(src_ref, dst_ref, sems, greeted=False):
    device, barrier = greet_sibling()
    if not greeted:
        pl.semaphore_wait(barrier, 1)
    copy = pltpu.make_async_remote_copy(
        src_ref=src_ref, dst_ref=dst_ref, send_sem=sems.at[0], recv_sem=sems.at[1],
        device_id=device, device_id_type=pl.DeviceIdType.MESH,
    )
    copy.start()
    return copy


def reduced_rows(rows, chips, depths):
    return -(-rows // (8 * chips * depths)) * 8 * chips * depths


def reducer_scratch(rows, chips, depths):
    quarter = rows // chips
    part = quarter // depths
    sems = pltpu.SemaphoreType.DMA
    return [
        pltpu.VMEM((2, rows, 128), F32), pltpu.VMEM((chips - 1, quarter, 128), F32), pltpu.VMEM((quarter, 128), F32),
        pltpu.VMEM((depths - 1, part, 128), F32), pltpu.VMEM((part, 128), F32), pltpu.VMEM((quarter, 128), F32),
        sems((2, chips - 1)), sems((2, depths - 1)), sems((2, depths - 1)), sems((2, chips - 1)), sems((2, 1)),
    ]


def greet_all(chips, depths):
    b = lax.axis_index("batch")
    z = lax.axis_index("frames")
    barrier = pltpu.get_barrier_semaphore()
    devices = [(b + 1 - 2 * lax.rem(b, 2), z)]
    devices += [(lax.rem(b + 2 * step, 2 * chips), z) for step in range(1, chips)]
    devices += [(b, lax.rem(z + step, depths)) for step in range(1, depths)]
    for device in devices:
        pl.semaphore_signal(barrier, inc=1, device_id=device, device_id_type=pl.DeviceIdType.MESH)
    return barrier, len(devices)


def reducer(src, chips, depths, refs):
    red, plane_in, mine, depth_in, piece, joined, s_plane, s_depth, s_spread, s_gather, s_back = refs
    b = lax.axis_index("batch")
    z = lax.axis_index("frames")
    core = lax.rem(b, 2)
    chip = lax.div(b, 2)
    quarter = mine.shape[0]
    part = piece.shape[0]

    def rows(at, count):
        return pl.ds(pl.multiple_of(at, 8), count)

    def send(src_ref, dst_ref, sems, slot, device):
        return pltpu.make_async_remote_copy(
            src_ref=src_ref, dst_ref=dst_ref, send_sem=sems.at[0, slot], recv_sem=sems.at[1, slot],
            device_id=device, device_id_type=pl.DeviceIdType.MESH,
        )

    over_plane = [(step, (lax.rem(b + 2 * step, 2 * chips), z)) for step in range(1, chips)]
    over_depth = [(step, (b, lax.rem(z + step, depths))) for step in range(1, depths)]
    own = rows(chip * quarter, quarter)
    mine_at = rows(z * part, part)

    def plane():
        return [
            send(src.at[rows(lax.rem(chip + step, chips) * quarter, quarter)], plane_in.at[step - 1], s_plane, step - 1, to)
            for step, to in over_plane
        ]

    def scatter():
        return [
            send(mine.at[rows(lax.rem(z + step, depths) * part, part)], depth_in.at[step - 1], s_depth, step - 1, to)
            for step, to in over_depth
        ]

    def spread():
        return [send(piece, joined.at[mine_at], s_spread, step - 1, to) for step, to in over_depth]

    def gather():
        return [send(joined, red.at[core, own], s_gather, step - 1, to) for step, to in over_plane]

    def back():
        return [send(red.at[core], red.at[core], s_back, 0, (b + 1 - 2 * core, z))]

    def start(copies):
        for copy in copies:
            copy.start()

    def wait(copies):
        for copy in copies:
            copy.wait()

    def first():
        start(plane())

    def third():
        wait(plane())
        total = src[own, :]
        for step in range(1, chips):
            total = total + plane_in[step - 1]
        mine[...] = total
        start(scatter())

    def fourth():
        wait(scatter())
        total = mine[mine_at, :]
        for step in range(1, depths):
            total = total + depth_in[step - 1]
        piece[...] = total
        joined[mine_at, :] = total
        start(spread())

    def fifth():
        wait(spread())
        red[core, own] = joined[...]
        start(gather())

    def sixth():
        wait(gather())
        start(back())

    def last():
        wait(back())

    return [first, third, fourth, fifth, sixth, last]


def forward_kernel(layer_no, groups, steps, *refs):
    inter = layer_no % 2 == 1
    (x_ref, flat_ref,
     next_ref, normed_ref, scale_ref, h_ref, coef_ref,
     wi4, wr2, wrl, pj, proj_s, bias_s, gin_a, gin_b, h_a, h_b, c_s, part_ref, peer_ref, sems) = refs
    turn_no = pl.program_id(0)
    last_turn = pl.num_programs(0) - 1
    turn = per_turn(inter)
    chunks = turn * pl.num_programs(0)
    length = chunks * steps
    dir_no = lax.rem(lax.axis_index("batch"), 2)
    rows = 2 * HALF_PAD if inter else groups
    valid = HOP * groups

    def before(chunk_no, gin):
        chunk_no = lax.rem(chunk_no, chunks)
        positions = times(dir_no, chunk_no, length, steps)
        sides = []

        def prepare():
            xs = gather(x_ref, inter, groups, positions)
            for half in [0, 1] if inter else [lax.div(positions[0], HOP)]:
                sides.append(narrow(xs, half))

        def gate(q):
            cut = slice(q * UNITS, (q + 1) * UNITS)
            for side, rows_of in enumerate(sides):
                found = dot(rows_of, wi4[:, cut]) + bias_s[0:1, cut]
                if inter:
                    for u in range(steps):
                        at = u * rows + side * HALF_PAD
                        gin[at:at + HALF_PAD, cut] = found[u * HALF_PAD:(u + 1) * HALF_PAD]
                else:
                    gin[:, cut] = found

        return [prepare] + [functools.partial(gate, q) for q in range(4)]

    def after(chunk_no, hs):
        chunk_no = lax.rem(chunk_no + chunks, chunks)
        positions = times(dir_no, chunk_no, length, steps)

        def project():
            found = [dot_sides(part, pj[...]) for part in to_sides(inter, steps, hs[...])]
            low_lanes = lax.broadcasted_iota(jnp.int32, found[0].shape, 1) < FILTERS
            if inter:
                found = jnp.where(low_lanes, found[0], found[1])
                for u in range(steps):
                    part_ref[stream_rows(inter, groups, positions[u]), :] = found[u * HALF_PAD:(u + 1) * HALF_PAD]
            else:
                half = lax.div(positions[0], HOP)
                found = jnp.where(low_lanes == (half == 0), found[0], 0.0)
                for u in range(steps):
                    here = stream_rows(inter, groups, positions[u])
                    part_ref[here, :] = part_ref[here, :] + found[u * groups:(u + 1) * groups]

        return [project]

    def walk(gin, hs, h, c, sub, beside):
        for u in range(steps):
            hi, lo = split(h)
            z = dot(jnp.concatenate([hi, lo], 1), wr2[...]) + dot(hi, wrl[...])
            for task in share_of(beside, u, steps):
                task()
            z = z + gin[u * rows:(u + 1) * rows]
            th = jnp.tanh(z)
            ti, tf, g, to = (th[:, q * UNITS:(q + 1) * UNITS] for q in range(4))
            i_g = 0.5 * ti + 0.5
            f_g = 0.5 * tf + 0.5
            o_g = 0.5 * to + 0.5
            c_prev = c
            c = f_g * c + i_g * g
            tc = jnp.tanh(c)
            h = o_g * tc
            at = sub * steps + u
            hs[u * rows:(u + 1) * rows] = h
            h_ref[at] = h
            coef_ref[at, 0] = tc * (0.25 - 0.25 * to * to)
            coef_ref[at, 1] = o_g * (1.0 - tc * tc)
            coef_ref[at, 2] = g * (0.25 - 0.25 * ti * ti)
            coef_ref[at, 3] = c_prev * (0.25 - 0.25 * tf * tf)
            coef_ref[at, 4] = i_g * (1.0 - g * g)
            coef_ref[at, 5] = f_g
        return h, c

    @pl.when(turn_no == 0)
    def _():
        device, barrier = greet_sibling()
        pl.semaphore_signal(barrier, inc=1, device_id=device, device_id_type=pl.DeviceIdType.MESH)
        part_ref[...] = jnp.zeros_like(part_ref)
        column = lax.broadcasted_iota(jnp.int32, (1, GATES), 1)
        scaling = jnp.where((column >= 2 * UNITS) & (column < 3 * UNITS), 1.0, 0.5)
        _, base, odd = window(layer_no)
        win, wrec, bias, proj = load_weights(flat_ref, base, odd, dir_no, proj_s)
        wi4[...] = narrow_weights(win * scaling)
        put_split(wrec * scaling, wr2, wrl)
        bias_s[...] = jnp.broadcast_to(bias * scaling, bias_s.shape)
        pj[...] = side_weights(proj)
        c_s[...] = jnp.zeros_like(c_s)
        h_b[...] = jnp.zeros_like(h_b)
        for task in before(0, gin_a):
            task()

    h, c = h_b[(steps - 1) * rows:], c_s[...]
    for n in range(turn):
        (gin, hs), (next_gin, past_hs) = ((gin_a, h_a), (gin_b, h_b))[::1 - 2 * (n % 2)]
        number = turn * turn_no + n
        h, c = walk(gin, hs, h, c, n, after(number - 1, past_hs) + before(number + 1, next_gin))
    c_s[...] = c

    @pl.when(turn_no == last_turn)
    def _():
        for task in after(chunks - 1, h_b):
            task()
        swap_with_sibling(part_ref, peer_ref, sems).wait()
        _, base, odd = window(layer_no)
        norm_stage(x_ref, part_ref, peer_ref, flat_ref, base, odd, valid, normed_ref, scale_ref, next_ref)


def backward_kernel(layer_no, groups, steps, chips, depths, *refs):
    inter = layer_no % 2 == 1
    last_layer = layer_no == 2 * BLOCKS - 1
    g_ref, normed_ref, scale_ref, x_ref, h_ref, coef_ref, flat_ref, *rest = refs
    if last_layer:
        hg_ref, *rest = rest
    if layer_no == 0:
        column_ref, denc_ref, encoder_ref, loss_ref, *rest = rest
    if not last_layer:
        upper_ref, *rest = rest
    if layer_no:
        below_ref, *rest = rest
    if not last_layer:
        red_ref, *rest = rest
    (grad_ref,
     wi4, wrw, wrt, pj, proj_s, dmx, dh_a, dh_b, dz_a, dz_b, dc_s, awin, aproj, abias,
     dx_ref, peer_ref, sems, *rest) = rest
    stages = [] if last_layer else reducer(upper_ref, chips, depths, rest)
    turn_no = pl.program_id(0)
    last_turn = pl.num_programs(0) - 1
    chunks = 2 * pl.num_programs(0)
    length = chunks * steps
    dir_no = lax.rem(lax.axis_index("batch"), 2)
    rows = 2 * HALF_PAD if inter else groups
    valid = HOP * groups

    def before(back_no, dhc):
        chunk_no = chunks - 1 - lax.rem(back_no, chunks)
        positions = times(dir_no, chunk_no, length, steps)

        def outward():
            dms = gather(dmx, inter, groups, positions)
            for side, half in enumerate([0, 1] if inter else [lax.div(positions[0], HOP)]):
                found = dot(narrow(dms, half), pj[...])
                if inter:
                    for u in range(steps):
                        at = u * rows + side * HALF_PAD
                        dhc[at:at + HALF_PAD] = found[u * HALF_PAD:(u + 1) * HALF_PAD]
                else:
                    dhc[...] = found

        return [outward]

    def after(back_no, dzs):
        used = back_no >= 0
        chunk_no = chunks - 1 - lax.rem(back_no + chunks, chunks)
        positions = times(dir_no, chunk_no, length, steps)
        half = 0 if inter else lax.div(positions[0], HOP)
        at = chunk_no * steps
        count = UNITS + FILTERS
        ready = []

        def prepare():
            xs = gather(x_ref, inter, groups, positions)
            hs = h_ref[pl.ds(at, steps)].reshape(steps * rows, UNITS)
            early = h_ref[lax.rem(at + length - 1, length)] * jnp.where(at == 0, 0.0, 1.0)
            hp = jnp.concatenate([early, hs[:(steps - 1) * rows]], 0)
            if inter:
                lhs = [
                    jnp.concatenate([hp_side, (xs if side == 0 else pltpu.roll(xs, FILTERS, 1))[:, :FILTERS]], 1)
                    for side, hp_side in enumerate(to_sides(inter, steps, hp))
                ]
                lhs = jnp.concatenate(lhs, 0)
            else:
                turned = jnp.where(half == 0, xs, pltpu.roll(xs, FILTERS, 1))
                lhs = jnp.concatenate([hp, turned[:, :FILTERS]], 1)
            lhs_hi, lhs_lo = split(lhs.T)
            ready.extend([lhs_hi, jnp.concatenate([lhs_hi, lhs_lo], 0)])

        def gate(q):
            cut = slice(q * UNITS, (q + 1) * UNITS)
            dz = dzs[:, cut]
            abias[0:1, cut] += jnp.sum(dz, 0, keepdims=True)
            if inter:
                dz = jnp.concatenate(to_sides(inter, steps, dz), 0)
            dz_hi, dz_lo = split(dz)
            both = dot(ready[1], dz_hi)
            awin[:, cut] += both[:count] + both[count:] + dot(ready[0], dz_lo)

        def project():
            hs = h_ref[pl.ds(at, steps)].reshape(steps * rows, UNITS)
            dms = gather(dmx, inter, groups, positions) * jnp.where(used, 1.0, 0.0)
            if inter:
                aproj[...] += dot_rows3(jnp.concatenate(to_sides(inter, steps, hs), 1), dms)
            else:
                turned = jnp.where(half == 0, dms, pltpu.roll(dms, FILTERS, 1))
                aproj[...] += dot_rows3(hs, turned)

        def inward():
            found = [dot_sides(part, wi4[...]) for part in to_sides(inter, steps, dzs[...])]
            low_lanes = lax.broadcasted_iota(jnp.int32, found[0].shape, 1) < FILTERS
            if inter:
                found = jnp.where(low_lanes, found[0], found[1])
                for u in range(steps):
                    dx_ref[stream_rows(inter, groups, positions[u]), :] = found[u * HALF_PAD:(u + 1) * HALF_PAD]
            else:
                found = jnp.where(low_lanes == (half == 0), found[0], 0.0)
                for u in range(steps):
                    here = stream_rows(inter, groups, positions[u])
                    dx_ref[here, :] = dx_ref[here, :] + found[u * groups:(u + 1) * groups]

        return [inward, project, prepare] + [functools.partial(gate, q) for q in range(4)]

    def walk(dhc, dzs, dz, dc_next, sub, beside):
        for u in reversed(range(steps)):
            at = sub * steps + u
            hi, lo = split(dz)
            wide = dot(hi, wrw[...])
            dh = wide[:, :UNITS] + wide[:, UNITS:] + dot(lo, wrt[...])
            for task in share_of(beside, steps - 1 - u, steps):
                task()
            dh = dh + dhc[u * rows:(u + 1) * rows]
            dc = dh * coef_ref[at, 1] + dc_next
            dz = jnp.concatenate(
                [dc * coef_ref[at, 2], dc * coef_ref[at, 3], dc * coef_ref[at, 4], dh * coef_ref[at, 0]], 1
            )
            dc_next = dc * coef_ref[at, 5]
            dzs[u * rows:(u + 1) * rows] = dz
        return dz, dc_next

    @pl.when(turn_no == 0)
    def _():
        if last_layer:
            device, barrier = greet_sibling()
            pl.semaphore_signal(barrier, inc=1, device_id=device, device_id_type=pl.DeviceIdType.MESH)
        else:
            barrier, count = greet_all(chips, depths)
            pl.semaphore_wait(barrier, count)
            stages[0]()
        dx_ref[...] = jnp.zeros_like(dx_ref)
        _, base, odd = window(layer_no)
        win, wrec, _, proj = load_weights(flat_ref, base, odd, dir_no, proj_s)
        wi4[...] = side_weights(win.T)
        hi, lo = split(wrec.T)
        wrw[...] = jnp.concatenate([hi, lo], 1)
        wrt[...] = hi
        pj[...] = narrow_weights(proj.T)
        dz_b[...] = jnp.zeros_like(dz_b)
        dc_s[...] = jnp.zeros_like(dc_s)
        awin[...] = jnp.zeros_like(awin)
        aproj[...] = jnp.zeros_like(aproj)
        abias[...] = jnp.zeros_like(abias)
        grad_ref[...] = jnp.zeros_like(grad_ref)
        g = g_ref[:valid]
        normed = normed_ref[:valid]
        _, gain, _ = load_vec(flat_ref, base, odd)
        g_n = g * gain
        total = 2.0 * valid * FILTERS
        mean_one = jnp.sum(g_n) / total
        mean_two = jnp.sum(g_n * normed) / total
        dmixed = scale_ref[0:1] * (g_n - mean_one - normed * mean_two)
        dmx[:valid] = dmixed
        dmx[valid:] = jnp.zeros((dmx.shape[0] - valid, 128), F32)
        lead = jnp.where(dir_no == 0, 1.0, 0.0)

        def fold(array):
            found = lead * jnp.sum(array, 0, keepdims=True)
            return found[:, :FILTERS] + found[:, FILTERS:]

        grad_ref[OWN_VEC:OWN_VEC + 1] = jnp.concatenate([fold(dmixed), fold(g * normed)], 1)
        grad_ref[OWN_VEC + 1:OWN_VEC + 2] = jnp.concatenate([fold(g), jnp.zeros((1, FILTERS), F32)], 1)
        if last_layer:
            grad_ref[OWN_EXTRA:OWN_EXTRA + HEAD_ROWS] = hg_ref[...] * lead

        for task in before(0, dh_a):
            task()

    for stage, at in zip(stages[1:], (2, 3, 4, None) if inter else (3, 5, 6, 9)):
        if at is not None:
            pl.when(turn_no == at)(stage)

    dz, dc_next = dz_b[:rows], dc_s[...]
    dz, dc_next = walk(dh_a, dz_a, dz, dc_next, 1, after(2 * turn_no - 1, dz_b) + before(2 * turn_no + 1, dh_b))
    dz, dc_next = walk(dh_b, dz_b, dz, dc_next, 0, after(2 * turn_no, dz_a) + before(2 * turn_no + 2, dh_a))
    dc_s[...] = dc_next

    @pl.when(turn_no == last_turn)
    def _():
        for task in after(chunks - 1, dz_b):
            task()
        if layer_no:
            swap = swap_with_sibling(dx_ref, peer_ref, sems, not last_layer)
        for stage in stages[4:] if inter else stages[5:]:
            stage()
        if not last_layer:
            red_ref[...] = rest[0][...]
        if layer_no:
            swap.wait()
            below_ref[:valid] = g_ref[:valid] + dx_ref[:valid] + peer_ref[:valid]
            below_ref[valid:] = jnp.zeros((below_ref.shape[0] - valid, 128), F32)
        for q in range(4):
            cut = slice(q * UNITS, (q + 1) * UNITS)
            grad_ref[pl.ds(q, FILTERS, stride=4), :] = awin[UNITS:, cut]
            grad_ref[pl.ds(256 + q, UNITS, stride=4), :] = awin[:UNITS, cut]
            grad_ref[768 + q:769 + q, :] = abias[0:1, cut]
        proj_s[...] = aproj[:UNITS] + pltpu.roll(aproj[UNITS:], FILTERS, 1) if inter else aproj[...]
        even = proj_s[pl.ds(0, 64, stride=2), :]
        odd_rows = proj_s[pl.ds(1, 64, stride=2), :]
        grad_ref[OWN_PROJ:OWN_VEC, :] = jnp.concatenate(
            [even[:, :FILTERS], odd_rows[:, :FILTERS]], 1
        )
        if layer_no == 0:
            lead = jnp.where(dir_no == 0, 1.0, 0.0)
            streams = lead * g_ref[:valid] + dx_ref[:valid]
            column = column_ref[...]
            mix, following = column[:, MIX_LANE:MIX_LANE + 1], column[:, NEXT_LANE:NEXT_LANE + 1]
            raw = mix * encoder_ref[0:1, :FILTERS] + following * encoder_ref[1:2, :FILTERS]
            group_at = lax.broadcasted_iota(jnp.int32, (valid, FILTERS), 0) % groups
            shifted = jnp.where(group_at == 0, 0.0, pltpu.roll(pltpu.roll(streams, FILTERS, 1), 1, 0)[:, :FILTERS])
            grad_raw = (streams[:, :FILTERS] + shifted + lead * denc_ref[...]) * jax.nn.sigmoid(raw)
            grad_ref[OWN_EXTRA:OWN_EXTRA + 1] = jnp.concatenate(
                [jnp.sum(grad_raw * mix, 0, keepdims=True), jnp.sum(grad_raw * following, 0, keepdims=True)], 1
            )
            grad_ref[OWN_EXTRA + 1:OWN_EXTRA + 2] = loss_ref[0:1] * lead


def head_kernel(groups, sep, stream_ref, column_ref, active_ref, note_ref, tail_s,
                g_ref, hg_ref, denc_ref, loss_ref,
                sig_s, now_s, before_s, slope_s, mk2, mkl, mt2, mtl, dk2, dkl, dt2, dtl, amask, adec, m_low, m_top):
    valid = HOP * groups
    block = 10 * groups
    first, second, third = (tail_s[pl.ds(6695 - TAIL_ROW + n, 32, stride=3), :] for n in range(3))
    m_low[pl.ds(0, 32, stride=2), :] = first
    m_low[pl.ds(1, 32, stride=2), :] = jnp.concatenate([second[:, FILTERS:], third[:, :FILTERS]], 1)
    m_top[pl.ds(0, 32, stride=2), :] = second
    m_top[pl.ds(1, 32, stride=2), :] = pltpu.roll(third, FILTERS, 1)
    masker = jnp.concatenate([m_low[...], m_top[:, :FILTERS]], 1)
    taps = tail_s[6791 - TAIL_ROW:6792 - TAIL_ROW]
    lane_at = lax.broadcasted_iota(jnp.int32, (FILTERS, 128), 1)
    row_at = lax.broadcasted_iota(jnp.int32, (FILTERS, 128), 0)
    upright = [
        jnp.sum(jnp.where(lane_at == 2 * row_at + tap, taps, 0.0), 1, keepdims=True) for tap in range(2)
    ]
    decoder = jnp.concatenate(
        [
            jnp.concatenate([jnp.where(lane_at == j, column, 0.0) for column in upright], 1)
            for j in range(SOURCES)
        ],
        0,
    )
    put_split(masker, mk2, mkl)
    put_split(masker.T, mt2, mtl)
    put_split(decoder, dk2, dkl)
    put_split(decoder.T, dt2, dtl)
    amask[...] = jnp.zeros_like(amask)
    adec[...] = jnp.zeros_like(adec)
    active = active_ref[0:1]

    def rows(n):
        return pl.ds(pl.multiple_of(n * block, 8), block)

    def summed_of(n):
        here = sep[rows(n), :]
        group_at = lax.broadcasted_iota(jnp.int32, (block, FILTERS), 0) % groups
        shifted = pltpu.roll(pltpu.roll(here, FILTERS, 1), 1, 0)[:, :FILTERS]
        return here[:, :FILTERS] + jnp.where(group_at == 0, 0.0, shifted)

    def frames_of(n):
        encoded = stream_ref[rows(n), :][:, :FILTERS]
        return jnp.concatenate([encoded, encoded, encoded], 1)

    def ahead(n, carry):
        logits = dot3(summed_of(n), mk2[...], mkl[...])
        sig = jax.nn.sigmoid(logits)
        sig_s[rows(n), :] = sig
        both = dot3(sig * active * frames_of(n), dk2[...], dkl[...])
        now_s[rows(n), :] = both[:, :128]
        before_s[pl.ds(pl.multiple_of(n * block + groups, 8), block), :] = both[:, 128:]
        return carry

    lax.fori_loop(0, HOP // 10, ahead, 0)
    at = lax.broadcasted_iota(jnp.int32, (groups, 128), 0)
    before_s[:groups] = jnp.where(at == 0, 0.0, pltpu.roll(before_s[valid:], 1, 0))

    def losses(n, total):
        column = column_ref[rows(n), :]
        lane = lax.broadcasted_iota(jnp.int32, (block, 128), 1)
        active_lane = (lane < SOURCES) & (lane.astype(F32) < active_ref[1:2, :128])
        target = jnp.where(active_lane, column, 0.0)
        row = lax.broadcasted_iota(jnp.int32, (block, 128), 0)
        frame = HOP * (row % groups) + row // groups + 10 * n
        kept = jnp.where(frame.astype(F32) < active_ref[2:3, :128], active_ref[3:4, :128], 0.0)
        differ = now_s[rows(n), :] + before_s[rows(n), :] - target
        root = jnp.sqrt(differ * differ + 1.0)
        slope_s[rows(n), :] = kept * differ / root
        return total + jnp.sum(kept * (root - 1.0), 0, keepdims=True)

    total = lax.fori_loop(0, HOP // 10, losses, jnp.zeros((1, 128), F32))
    first_lane = lax.broadcasted_iota(jnp.int32, (8, 128), 1) == 0
    loss_ref[...] = jnp.where(first_lane, jnp.sum(total, 1, keepdims=True), note_ref[...])
    slope_s[valid:] = jnp.where(at == groups - 1, 0.0, pltpu.roll(slope_s[:groups], groups - 1, 0))

    def back(n, carry):
        slopes = jnp.concatenate(
            [slope_s[rows(n), :], slope_s[pl.ds(pl.multiple_of(n * block + groups, 8), block), :]], 1
        )
        sig = sig_s[rows(n), :]
        frames = frames_of(n)
        dmasked = dot3(slopes, dt2[...], dtl[...]) * active
        by_sig = dmasked * sig
        denc_ref[rows(n), :] = (
            by_sig[:, :FILTERS] + by_sig[:, FILTERS:2 * FILTERS] + by_sig[:, 2 * FILTERS:]
        )
        dlogits = by_sig * frames * (1.0 - sig)
        dsummed = dot3(dlogits, mt2[...], mtl[...])
        group_at = lax.broadcasted_iota(jnp.int32, (block, FILTERS), 0) % groups
        shifted = jnp.where(group_at == groups - 1, 0.0, pltpu.roll(dsummed, block - 1, 0))
        g_ref[rows(n), :] = jnp.concatenate([dsummed, shifted], 1)
        amask[...] += dot_rows3(summed_of(n), dlogits)
        adec[...] += dot_rows3(sig * active * frames, slopes)
        return carry

    lax.fori_loop(0, HOP // 10, back, 0)
    g_ref[valid:] = jnp.zeros((g_ref.shape[0] - valid, 128), F32)
    m_low[...] = amask[:, :128]
    m_top[...] = jnp.concatenate([amask[:, 128:], jnp.zeros((FILTERS, FILTERS), F32)], 1)
    low_even, low_odd = m_low[pl.ds(0, 32, stride=2), :], m_low[pl.ds(1, 32, stride=2), :]
    top_even, top_odd = m_top[pl.ds(0, 32, stride=2), :], m_top[pl.ds(1, 32, stride=2), :]
    hg_ref[pl.ds(0, 32, stride=3), :] = low_even
    hg_ref[pl.ds(1, 32, stride=3), :] = jnp.concatenate([top_even[:, :FILTERS], low_odd[:, :FILTERS]], 1)
    hg_ref[pl.ds(2, 32, stride=3), :] = jnp.concatenate([low_odd[:, FILTERS:], top_odd[:, :FILTERS]], 1)
    columns = []
    for tap in range(2):
        found = 0.0
        for j in range(SOURCES):
            found = found + adec[j * FILTERS:(j + 1) * FILTERS, 128 * tap + j:128 * tap + j + 1]
        columns.append(jnp.broadcast_to(found, (FILTERS, 128)))
    lane = lax.broadcasted_iota(jnp.int32, (FILTERS, 128), 1)
    hg_ref[96:HEAD_ROWS] = jnp.where(lane == 0, columns[0], jnp.where(lane == 1, columns[1], 0.0))


def assemble(flat, layers):
    lane = lax.broadcasted_iota(jnp.int32, (FILTERS, 128), 1)
    row = lax.broadcasted_iota(jnp.int32, (FILTERS, 128), 0)

    def interleave(a, b):
        return jnp.sum(jnp.where(lane == 2 * row, a, jnp.where(lane == 2 * row + 1, b, 0.0)), 0, keepdims=True)

    for layer_no, ref in enumerate(layers):
        if ref is None:
            continue
        first, inner, odd = window(layer_no)
        at = first + inner
        parts = [(ref[0, :OWN_PROJ], False), (ref[1, :OWN_PROJ], False), (ref[0, OWN_PROJ:OWN_VEC], False)]
        parts += [(ref[1, OWN_PROJ:OWN_VEC], False), (ref[0, OWN_VEC:OWN_VEC + 2], True)]
        for rows, ends in parts:
            count = rows.shape[0]
            if odd:
                turned = pltpu.roll(rows, FILTERS, 1) if count >= 8 else jnp.concatenate(
                    [rows[:, FILTERS:], rows[:, :FILTERS]], 1
                )
                wide_low = lax.broadcasted_iota(jnp.int32, (count - 1, 128), 1) < FILTERS
                flat[at:at + 1, FILTERS:] = turned[0:1, FILTERS:]
                flat[at + 1:at + count] = jnp.where(wide_low, turned[:-1], turned[1:])
                if not ends:
                    flat[at + count:at + count + 1, :FILTERS] = turned[count - 1:, :FILTERS]
            elif ends:
                flat[at:at + 1] = rows[0:1]
                flat[at + 1:at + 2, :FILTERS] = rows[1:2, :FILTERS]
            else:
                flat[at:at + count] = rows
            at += count
        if layer_no == 0:
            encoder = ref[0, OWN_EXTRA:OWN_EXTRA + 1] + ref[1, OWN_EXTRA:OWN_EXTRA + 1]
            encoder = jnp.broadcast_to(encoder, (FILTERS, 128))
            first_tap = jnp.sum(jnp.where(lane == row, encoder, 0.0), 1, keepdims=True)
            second_tap = jnp.sum(jnp.where(lane == row + FILTERS, encoder, 0.0), 1, keepdims=True)
            flat[0:1] = interleave(first_tap, second_tap)
        if layer_no == 2 * BLOCKS - 1:
            flat[6695:6791] = ref[0, OWN_EXTRA:OWN_EXTRA + 96]
            decoder = ref[0, OWN_EXTRA + 96:OWN_EXTRA + HEAD_ROWS]
            flat[6791:6792] = interleave(decoder[:, 0:1], decoder[:, 1:2])
            flat[6792:] = jnp.zeros((flat.shape[0] - 6792, 128), F32)


def finish_kernel(chips, depths, entries, own_ref, r1, r2, r3, grad_ref, note_ref, flat, b1, b2, b3, sems, *rest):
    b = lax.axis_index("batch")
    barrier, count = greet_all(chips, depths)
    pairs = ((r1, b1), (r2, b2), (r3, b3))
    fetches = [pltpu.make_async_copy(src, dst, sems.at[n]) for n, (src, dst) in enumerate(pairs)]
    for copy in fetches:
        copy.start()
    pl.semaphore_wait(barrier, count)
    stages = reducer(own_ref, chips, depths, rest)
    stages[0]()
    for copy in fetches:
        copy.wait()
    assemble(flat, (None, b1, b2, b3))
    for stage in stages[1:]:
        stage()
    r0 = rest[0]
    assemble(flat, (r0, None, None, None))
    note_ref[...] = jnp.zeros_like(note_ref)
    squares = jnp.sum(jnp.sum(flat[...] * flat[...], 0, keepdims=True), 1, keepdims=True)
    lane = lax.broadcasted_iota(jnp.int32, (1, 128), 1)
    note_ref[0:1] = jnp.where(lane == 2, squares, r0[0, OWN_EXTRA + 1:OWN_EXTRA + 2])
    rows = grad_ref.shape[0]
    row_at, lane_at = lax.div(b * entries, 128), lax.rem(b * entries, 128)
    gradient = flat[pl.ds(row_at, rows), :]
    if entries % 128:
        lane = lax.broadcasted_iota(jnp.int32, (rows, 128), 1)
        turn = lax.rem(128 - lane_at, 128)
        gradient = jnp.where(
            lane < 128 - lane_at, pltpu.roll(gradient, turn, 1), pltpu.roll(flat[pl.ds(row_at + 1, rows), :], turn, 1)
        )
    grad_ref[...] = gradient


def update_kernel(grad_ref, note_ref, p_ref, m_ref, v_ref, new_ref, half_ref, first_ref, second_ref, norm_ref, loss_ref):
    rows = grad_ref.shape[0]
    note = note_ref[0:1]
    lane = lax.broadcasted_iota(jnp.int32, (1, 128), 1)
    count = jnp.sum(jnp.where(lane == 1, note, 0.0), 1, keepdims=True)
    norm = jnp.sqrt(jnp.sum(jnp.where(lane == 2, note, 0.0), 1, keepdims=True)) / count
    norm_ref[0] = norm[0, 0]
    loss_ref[0] = note[0, 0]
    loss_ref[1] = note[0, 1]
    clipped = grad_ref[...] / count * (CLIP_AT / jnp.maximum(norm, CLIP_AT))
    new_first = BETA_ONE * m_ref[...].reshape(rows, 128) + (1.0 - BETA_ONE) * clipped
    new_second = BETA_TWO * v_ref[...].reshape(rows, 128) + (1.0 - BETA_TWO) * clipped * clipped
    step_size = (
        new_first / (1.0 - BETA_ONE**STEP) / (jnp.sqrt(new_second / (1.0 - BETA_TWO**STEP)) + ADAM_EPS)
    )
    params = p_ref[...].reshape(rows, 128)
    new_params = params - LEARN_RATE * (step_size + DECAY_RATE * params)
    new_ref[...] = new_params.reshape(new_ref.shape)
    half_ref[...] = new_params.astype(BF16).reshape(half_ref.shape)
    first_ref[...] = new_first.reshape(first_ref.shape)
    second_ref[...] = new_second.reshape(second_ref.shape)


def start_kernel(chips, depths, items, groups, gathers, p_ref, mail_ref, *refs):
    *views, refs = *refs[:5], refs[5:]
    if gathers:
        *refs, flat_ref = refs
    else:
        flat_ref = p_ref
    *refs, view_sem = refs
    (stream_ref, column_ref, active_ref, encoder_ref, note_ref,
     inbox, planes, plane_sem, pair_sem, top_sem, own_sem, mail_sem) = refs
    b = lax.axis_index("batch")
    z = lax.axis_index("frames")
    core = lax.rem(b, 2)
    chip = lax.div(b, 2)
    sibling = (b + 1 - 2 * core, z)
    entries = p_ref.shape[0]
    copies = depths // (2 * items)
    share = groups // depths
    valid = HOP * groups
    mail_rows = mail_ref.shape[0] // items
    mesh = pl.DeviceIdType.MESH

    barrier = pltpu.get_barrier_semaphore()
    for step in range(1, chips):
        pl.semaphore_signal(barrier, inc=1, device_id=(lax.rem(b + 2 * step, 2 * chips), z), device_id_type=mesh)
    for step in range(1, depths):
        pl.semaphore_signal(barrier, inc=1, device_id=(b, lax.rem(z + step, depths)), device_id_type=mesh)
    for step in range(depths):
        pl.semaphore_signal(barrier, inc=1, device_id=(sibling[0], lax.rem(z + step, depths)), device_id_type=mesh)
    pl.semaphore_wait(barrier, chips - 1 + 2 * depths - 1)

    def shard(at):
        return flat_ref.at[pl.ds(pl.multiple_of(at * entries, 128), entries)]

    def send(src, dst, sems, slot, device):
        return pltpu.make_async_remote_copy(
            src_ref=src, dst_ref=dst, send_sem=sems.at[0, slot], recv_sem=sems.at[1, slot],
            device_id=device, device_id_type=mesh,
        )

    def tail_of(at):
        return flat_ref.at[pl.ds(pl.multiple_of((at + 1) * entries - 128 * SHARE_ROWS, 128), 128 * SHARE_ROWS)]

    def forward_to_sibling(at, slot):
        for src, sems in ((tail_of(at), pair_sem), (flat_ref.at[pl.ds(pl.multiple_of(at * entries, 128), 128)], top_sem)):
            copy = send(src, src, sems, slot, sibling)
            copy.start()
            beside.append(copy)

    beside = []
    if gathers:
        by_x = b + 2 - 4 * lax.rem(chip, 2)
        by_y = b + 4 - 8 * lax.div(chip, 2)
        beyond = by_x + by_y - b
        half_rows = entries // 256

        def piece(ref, at, second):
            first_row, count = (half_rows, entries // 128 - half_rows) if second else (0, half_rows)
            return ref.at[pl.ds(pl.multiple_of(at * entries + 128 * first_row, 128), 128 * count)]

        across = [
            send(piece(p_ref, 0, second), piece(flat_ref, b, second), plane_sem, slot, (to, z))
            for slot, (second, to) in enumerate(((0, by_x), (1, by_y), (1, by_x), (0, by_y)))
        ]
        for copy in across:
            copy.start()
        own = pltpu.make_async_copy(p_ref, shard(b), own_sem)
        own.start()
        own.wait()
        forward_to_sibling(b, 0)
    letters = []
    for item in range(items):
        for other in range(2):
            for copy_no in range(copies):
                depth = (items * core + item) * copies + copy_no
                here = (core == other) & (z == depth)
                src = mail_ref.at[pl.ds(item * mail_rows, mail_rows)]
                far = pltpu.make_async_remote_copy(
                    src_ref=src, dst_ref=inbox.at[z], send_sem=mail_sem.at[1, len(letters)], recv_sem=mail_sem.at[0, z],
                    device_id=(2 * chip + other, depth), device_id_type=mesh,
                )
                near = pltpu.make_async_copy(src, inbox.at[z], mail_sem.at[0, z])

                @pl.when(here)
                def _():
                    near.start()

                @pl.when(jnp.logical_not(here))
                def _():
                    far.start()

                letters.append((here, far))
    for depth in range(depths):
        pltpu.make_async_copy(inbox.at[depth], inbox.at[depth], mail_sem.at[0, depth]).wait()
    for here, far in letters:
        @pl.when(jnp.logical_not(here))
        def _():
            far.wait_send()

    frames = jnp.concatenate([inbox[depth, :share] for depth in range(depths)], 0)
    facts = inbox[0, share:share + 1]
    speakers, length = facts[:, 0:1], facts[:, 1:2]
    whole_item = jnp.where(lax.rem(z, copies) == 0, 1.0, 0.0)
    lead = jnp.where(core == 0, whole_item, 0.0)
    lane = lax.broadcasted_iota(jnp.int32, (groups, 128), 1)
    group = lax.broadcasted_iota(jnp.int32, (groups, 128), 0)
    note_ref[...] = jnp.where(lane[:8] == 1, lead * length, 0.0)
    wide = SOURCES * FILTERS
    source = lax.broadcasted_iota(jnp.int32, (8, wide), 1) // FILTERS
    fact_at = lax.broadcasted_iota(jnp.int32, (8, wide), 0)
    active = jnp.where(source.astype(F32) < speakers, 1.0, 0.0)
    active = jnp.where(fact_at == 1, speakers, jnp.where(fact_at == 2, length, active))
    active_ref[...] = jnp.where(fact_at == 3, whole_item, active)
    end = HOP * FRAME_LANES
    tile = end // 128 * 128
    opening = jnp.where(group == groups - 1, 0.0, pltpu.roll(frames[:, :128], groups - 1, 0))
    ending = (lane >= end - tile) & (lane < end - tile + FRAME_LANES)
    planes[:, :tile] = frames[:, :tile]
    planes[:, tile:tile + 128] = jnp.where(ending, pltpu.roll(opening, end - tile, 1), frames[:, tile:tile + 128])
    planes[:, tile + 128:] = jnp.zeros((groups, planes.shape[1] - tile - 128), F32)
    for k in range(HOP):
        column_ref[k * groups:(k + 1) * groups] = planes[:, FRAME_LANES * k:FRAME_LANES * k + 128]

    if gathers:
        across[0].wait_recv()
        across.append(send(piece(flat_ref, by_x, 0), piece(flat_ref, by_x, 0), plane_sem, 4, (by_y, z)))
        across[4].start()
        across[1].wait_recv()
        across.append(send(piece(flat_ref, by_y, 1), piece(flat_ref, by_y, 1), plane_sem, 5, (by_x, z)))
        across[5].start()
        across[2].wait_recv()
        forward_to_sibling(by_x, 1)
        across[3].wait_recv()
        forward_to_sibling(by_y, 2)
        across[4].wait_recv()
        across[5].wait_recv()
        forward_to_sibling(beyond, 3)
        for copy in across:
            copy.wait_send()
        for copy in beside:
            copy.wait()

    bounds = [(window(n)[0], WINDOW) for n in range(2 * BLOCKS)] + [(TAIL_ROW, TAIL_ROWS)]
    stores = [
        pltpu.make_async_copy(flat_ref.at[pl.ds(128 * at, 128 * count)], view, view_sem.at[n])
        for n, ((at, count), view) in enumerate(zip(bounds, views))
    ]
    for store in stores:
        store.start()
    taps = flat_ref[0:128].reshape(1, 128)
    at_lane = lax.broadcasted_iota(jnp.int32, (128, 128), 1)
    at_row = lax.broadcasted_iota(jnp.int32, (128, 128), 0)
    upright = jnp.sum(jnp.where(at_lane == at_row, taps, 0.0), 1, keepdims=True)
    twice = 2 * lax.rem(at_lane, FILTERS)
    tap_rows = [jnp.sum(jnp.where(at_row == twice + tap, upright, 0.0), 0, keepdims=True) for tap in range(2)]
    encoder_ref[...] = jnp.where(at_row[:8] == 0, tap_rows[0], jnp.where(at_row[:8] == 1, tap_rows[1], 0.0))

    block = 5 * groups
    block_lane = lax.broadcasted_iota(jnp.int32, (block, 128), 1)
    last_group = lax.broadcasted_iota(jnp.int32, (block, 128), 0) % groups == groups - 1

    def encode(n, carry):
        rows = pl.ds(pl.multiple_of(n * block, 8), block)
        column = column_ref[rows, :]
        raw = column[:, MIX_LANE:MIX_LANE + 1] * tap_rows[0] + column[:, NEXT_LANE:NEXT_LANE + 1] * tap_rows[1]
        encoded = jnp.maximum(raw, 0.0) + jnp.log1p(jnp.exp(-jnp.abs(raw)))
        later = jnp.where(last_group, 0.0, pltpu.roll(encoded, block - 1, 0))
        stream_ref[rows, :] = jnp.where(block_lane < FILTERS, encoded, later)
        return carry

    lax.fori_loop(0, HOP // 5, encode, 0)
    stream_ref[valid:] = jnp.zeros((stream_ref.shape[0] - valid, 128), F32)
    for store in stores:
        store.wait()


def per_turn(inter):
    return 2 if inter else 4


def sizes(inter, groups):
    if inter:
        return groups, 2 * HALF_PAD, 4
    return 2 * HOP, groups, 5


def whole(shape):
    return pl.BlockSpec(shape, lambda j: (0,) * len(shape))


def run_start(params, mixture, sources, speakers, lengths):
    items, samples_here = mixture.shape
    depths = lax.axis_size("frames")
    chips = lax.axis_size("batch") // 2
    groups = samples_here * depths // HOP
    share = groups // depths
    valid = HOP * groups
    copies = depths // (2 * items)
    signals = jnp.concatenate([sources, mixture[:, None]], 1).transpose(0, 2, 1)
    signals = jnp.pad(signals, ((0, 0), (0, 0), (0, FRAME_LANES - 1 - SOURCES)))
    signals = signals.reshape(items, share, HOP * FRAME_LANES)
    width = -(-HOP * FRAME_LANES // 128) * 128
    facts = jnp.stack([speakers, lengths], 1).astype(F32)[:, None]
    mail_rows = -(-(share + 1) // 8) * 8
    mail = jnp.concatenate(
        [
            jnp.pad(signals, ((0, 0), (0, 0), (0, width - HOP * FRAME_LANES))),
            jnp.pad(facts, ((0, 0), (0, mail_rows - share - 1), (0, width - 2))),
        ],
        1,
    ).reshape(items * mail_rows, width)
    stream_shape = (HALF_PAD * groups, 128)
    out = [stream_shape, (valid, 128), (8, SOURCES * FILTERS), (8, 128), (8, 128)]
    out = [(WINDOW * 128,)] * (2 * BLOCKS) + [(TAIL_ROWS * 128,)] + out
    gathers = params.shape[0] % 128 == 0 and chips == 4
    whole_flat = [pltpu.VMEM((params.shape[0] * 2 * chips,), F32)] if gathers else []
    if not gathers:
        params = lax.all_gather(params, "batch", axis=0, tiled=True)
    vmem = pl.BlockSpec(memory_space=pltpu.VMEM)
    sems = pltpu.SemaphoreType.DMA
    found = pl.pallas_call(
        functools.partial(start_kernel, chips, depths, items, groups, gathers),
        in_specs=[vmem] * 2,
        out_specs=[pl.BlockSpec(memory_space=pl.ANY)] * 5 + [vmem] * 5,
        out_shape=[jax.ShapeDtypeStruct(shape, F32) for shape in out],
        scratch_shapes=[
            pltpu.VMEM((depths, mail_rows, width), F32), pltpu.VMEM((groups, width + 128), F32),
            sems((2, 6)), sems((2, chips)), sems((2, chips)), sems, sems((2, max(depths, 2 * items * copies))), sems((5,)),
        ]
        + whole_flat,
        compiler_params=pltpu.CompilerParams(
            vmem_limit_bytes=VMEM_MAX, collective_id=10, has_side_effects=True
        ),
        name="start",
    )(params, mail)
    return [a.reshape(-1, 128) for a in found[:5]], found[5:]


def run_forward(layer_no, groups, stream, flat):
    inter = layer_no % 2 == 1
    length, rows, steps = sizes(inter, groups)
    turn = per_turn(inter)
    stream_shape = (HALF_PAD * groups, 128)
    out = [
        (stream_shape, whole(stream_shape)),
        (stream_shape, whole(stream_shape)),
        ((8, 128), whole((8, 128))),
        ((length, rows, UNITS), pl.BlockSpec((turn * steps, rows, UNITS), lambda j: (j, 0, 0))),
        ((length, 6, rows, UNITS), pl.BlockSpec((turn * steps, 6, rows, UNITS), lambda j: (j, 0, 0, 0))),
    ]
    return pl.pallas_call(
        functools.partial(forward_kernel, layer_no, groups, steps),
        grid=(length // (turn * steps),),
        in_specs=[whole(stream_shape), whole((WINDOW, 128))],
        out_specs=[spec for _, spec in out],
        out_shape=[jax.ShapeDtypeStruct(shape, F32) for shape, _ in out],
        scratch_shapes=[
            pltpu.VMEM((256, GATES), BF16),
            pltpu.VMEM((256, GATES), BF16), pltpu.VMEM((128, GATES), BF16),
            pltpu.VMEM((UNITS, 128), BF16),
            pltpu.VMEM((UNITS, 128), F32),
            pltpu.VMEM((8, GATES), F32),
            pltpu.VMEM((steps * rows, GATES), F32), pltpu.VMEM((steps * rows, GATES), F32),
            pltpu.VMEM((steps * rows, UNITS), F32), pltpu.VMEM((steps * rows, UNITS), F32),
            pltpu.VMEM((rows, UNITS), F32),
            pltpu.VMEM(stream_shape, F32), pltpu.VMEM(stream_shape, F32), pltpu.SemaphoreType.DMA((2,)),
        ],
        compiler_params=pltpu.CompilerParams(
            vmem_limit_bytes=VMEM_MAX, collective_id=2 + layer_no, has_side_effects=True
        ),
        name="forward_inter" if inter else "forward_intra",
    )(stream, flat)


def run_backward(layer_no, groups, grad, kept, flat, extra):
    inter = layer_no % 2 == 1
    last_layer = layer_no == 2 * BLOCKS - 1
    length, rows, steps = sizes(inter, groups)
    stream_shape = (HALF_PAD * groups, 128)
    count = length // (2 * steps)
    depths = lax.axis_size("frames")
    chips = lax.axis_size("batch") // 2
    out = [(reduced_rows(OWN_ROWS[layer_no], chips, depths), 128)]
    scratch = []
    if not last_layer:
        upper_rows = reduced_rows(OWN_ROWS[layer_no + 1], chips, depths)
        out = [(2, upper_rows, 128)] + out
        scratch = reducer_scratch(upper_rows, chips, depths)
    if layer_no:
        out = [stream_shape] + out
    x, normed, scale, h_all, coef = kept
    return pl.pallas_call(
        functools.partial(backward_kernel, layer_no, groups, steps, chips, depths),
        grid=(count,),
        in_specs=[whole(a.shape) for a in (grad, normed, scale, x, h_all)]
        + [pl.BlockSpec((2 * steps, 6, rows, UNITS), lambda j: (count - 1 - j, 0, 0, 0)), whole((WINDOW, 128))]
        + [whole(a.shape) for a in extra],
        out_specs=[whole(shape) for shape in out],
        out_shape=[jax.ShapeDtypeStruct(shape, F32) for shape in out],
        scratch_shapes=[
            pltpu.VMEM((GATES, 128), BF16),
            pltpu.VMEM((GATES, 256), BF16), pltpu.VMEM((GATES, 128), BF16),
            pltpu.VMEM((256, UNITS), BF16),
            pltpu.VMEM((UNITS, 128), F32),
            pltpu.VMEM(stream_shape, F32),
            pltpu.VMEM((steps * rows, UNITS), F32), pltpu.VMEM((steps * rows, UNITS), F32),
            pltpu.VMEM((steps * rows, GATES), F32), pltpu.VMEM((steps * rows, GATES), F32),
            pltpu.VMEM((rows, UNITS), F32),
            pltpu.VMEM((UNITS + FILTERS, GATES), F32), pltpu.VMEM((2 * UNITS if inter else UNITS, 128), F32),
            pltpu.VMEM((8, GATES), F32),
            pltpu.VMEM(stream_shape, F32), pltpu.VMEM(stream_shape, F32), pltpu.SemaphoreType.DMA((2,)),
        ]
        + scratch,
        compiler_params=pltpu.CompilerParams(vmem_limit_bytes=VMEM_MAX, collective_id=6 + layer_no, has_side_effects=True),
        name="backward_inter" if inter else "backward_intra",
    )(grad, normed, scale, x, h_all, coef, flat, *extra)


def run_head(groups, separated, stream, column, active, note, tail):
    valid = HOP * groups
    stream_shape = (HALF_PAD * groups, 128)
    out = [stream_shape, (HEAD_ROWS, 128), (valid, FILTERS), (8, 128)]
    wide = SOURCES * FILTERS
    operands = (separated, stream, column, active, note, tail)
    return pl.pallas_call(
        functools.partial(head_kernel, groups),
        grid=(1,),
        in_specs=[whole(a.shape) for a in operands],
        out_specs=[whole(shape) for shape in out],
        out_shape=[jax.ShapeDtypeStruct(shape, F32) for shape in out],
        scratch_shapes=[
            pltpu.VMEM((valid, wide), F32), pltpu.VMEM((valid, 128), F32),
            pltpu.VMEM((valid + groups, 128), F32), pltpu.VMEM((valid + groups, 128), F32),
            pltpu.VMEM((2 * FILTERS, wide), BF16), pltpu.VMEM((FILTERS, wide), BF16),
            pltpu.VMEM((2 * wide, FILTERS), BF16), pltpu.VMEM((wide, FILTERS), BF16),
            pltpu.VMEM((2 * wide, 256), BF16), pltpu.VMEM((wide, 256), BF16),
            pltpu.VMEM((512, wide), BF16), pltpu.VMEM((256, wide), BF16),
            pltpu.VMEM((FILTERS, wide), F32), pltpu.VMEM((wide, 256), F32),
            pltpu.VMEM((FILTERS, 128), F32), pltpu.VMEM((FILTERS, 128), F32),
        ],
        compiler_params=pltpu.CompilerParams(vmem_limit_bytes=VMEM_MAX),
        name="head",
    )(*operands)


def run_finish(layers, params, first_moment, second_moment):
    entries = params.shape[0]
    rows = -(-entries // 128)
    depths = lax.axis_size("frames")
    chips = lax.axis_size("batch") // 2
    vmem = pl.BlockSpec(memory_space=pltpu.VMEM)
    gradient, note = pl.pallas_call(
        functools.partial(finish_kernel, chips, depths, entries),
        in_specs=[vmem] + [pl.BlockSpec(memory_space=pl.ANY)] * 3,
        out_specs=[vmem] * 2,
        out_shape=[jax.ShapeDtypeStruct(shape, F32) for shape in ((rows, 128), (8, 128))],
        scratch_shapes=[pltpu.VMEM((6808, 128), F32)]
        + [pltpu.VMEM(a.shape, F32) for a in layers[1:]]
        + [pltpu.SemaphoreType.DMA((3,))]
        + reducer_scratch(layers[0].shape[0], chips, depths),
        compiler_params=pltpu.CompilerParams(
            vmem_limit_bytes=VMEM_MAX, collective_id=1, has_side_effects=True
        ),
        name="finish",
    )(*layers)
    shards = [params, first_moment, second_moment]
    shape = (entries,)
    if entries % 128:
        shape = (rows, 128)
        shards = [jnp.pad(a, (0, rows * 128 - entries)).reshape(shape) for a in shards]
    smem = pl.BlockSpec(memory_space=pltpu.SMEM)
    out = [(shape, F32), (shape, BF16), (shape, F32), (shape, F32), ((1,), F32), ((2,), F32)]
    found = pl.pallas_call(
        update_kernel,
        in_specs=[vmem] * 5,
        out_specs=[vmem] * 4 + [smem] * 2,
        out_shape=[jax.ShapeDtypeStruct(shape, dtype) for shape, dtype in out],
        compiler_params=pltpu.CompilerParams(vmem_limit_bytes=VMEM_MAX),
        name="update",
    )(gradient, note, *shards)
    return [a.reshape(-1)[:entries] for a in found[:4]] + [found[4][0], found[5]]


def local(params, first_moment, second_moment, mixture, sources, speakers, lengths):
    groups = mixture.shape[1] * lax.axis_size("frames") // HOP
    views, (stream, column, active, encoder, note) = run_start(params, mixture, sources, speakers, lengths)
    kept = []
    x = stream
    for layer_no in range(2 * BLOCKS):
        after, normed, scale, h_all, coef = run_forward(layer_no, groups, x, views[layer_no])
        kept.append((x, normed, scale, h_all, coef))
        x = after
    grad, head_grads, grad_encoded, loss = run_head(groups, x, stream, column, active, note, views[2 * BLOCKS])
    sums = [None] * (2 * BLOCKS)
    for layer_no in reversed(range(2 * BLOCKS)):
        extra = ()
        if layer_no == 2 * BLOCKS - 1:
            extra = (head_grads,)
        if layer_no == 0:
            extra = (column, grad_encoded, encoder, loss)
        if layer_no < 2 * BLOCKS - 1:
            extra = extra + (sums[layer_no + 1],)
        *found, sums[layer_no] = run_backward(layer_no, groups, grad, kept[layer_no], views[layer_no], extra)
        if layer_no < 2 * BLOCKS - 1:
            sums[layer_no + 1] = found[-1]
        if layer_no:
            grad = found[0]
    return tuple(run_finish(sums, params, first_moment, second_moment))


def solution(mesh):
    placed = (
        P("batch"),
        P("batch"),
        P("batch"),
        P("batch", "frames"),
        P("batch", None, "frames"),
        P("batch"),
        P("batch"),
    )
    return jax.shard_map(
        local,
        mesh=mesh,
        in_specs=placed,
        out_specs=(P("batch"), P("batch"), P("batch"), P("batch"), P(), P()),
        check_vma=False,
    )
```

```python
import functools
import math

import jax
import jax.numpy as jnp
from jax import lax
from jax.experimental import pallas as pl
from jax.experimental.pallas import tpu as pltpu
from jax.sharding import PartitionSpec as P

FILTERS = 64
UNITS = 128
HOP = 50
HALF_PAD = 56
SOURCES = 3
BLOCKS = 2
STEP = 5
GATES = 4 * UNITS

HIGHEST = lax.Precision.HIGHEST
NORM_EPS = 1e-08
CLIP_AT = 0.001
BETA_ONE = 0.5
BETA_TWO = 0.5
LEARN_RATE = 0.05
DECAY_RATE = 0.01
ADAM_EPS = 1e-08
F32 = jnp.float32
BF16 = jnp.bfloat16
VMEM_MAX = 60 * 2**20


def split(a):
    hi = a.astype(BF16)
    return hi, (a - hi.astype(F32)).astype(BF16)


def dot(a, b):
    return jnp.dot(a, b, preferred_element_type=F32)


def dot3(a, w_twice, w_low):
    hi, lo = split(a)
    return dot(jnp.concatenate([hi, lo], 1), w_twice) + dot(hi, w_low)


def dot_rows(a, b):
    return lax.dot_general(a, b, (((0,), (0,)), ((), ())), preferred_element_type=F32)


def dot_rows3(a, b):
    a_hi, a_lo = split(a)
    b_hi, b_lo = split(b)
    return dot_rows(a_hi, b_hi) + dot_rows(a_lo, b_hi) + dot_rows(a_hi, b_lo)


SIDE_ROWS = 772
PROJ_ROWS = 2 * SIDE_ROWS
VEC_ROW = PROJ_ROWS + 128
LAYER_ROWS = 1680
HEAD_ROWS = 160
OWN_PROJ = SIDE_ROWS
OWN_VEC = SIDE_ROWS + 64
OWN_EXTRA = SIDE_ROWS + 68
OWN_ROWS = (OWN_EXTRA + 8, OWN_EXTRA, OWN_EXTRA, OWN_EXTRA + HEAD_ROWS)
WINDOW = 1688
TAIL_ROW = 6688
TAIL_ROWS = 104
SHARE_ROWS = 256
FRAME_LANES = 8
MIX_LANE = SOURCES
NEXT_LANE = FRAME_LANES + MIX_LANE


def window(layer_no):
    at = 2 + 3347 * layer_no
    return at // 16 * 8, at // 2 % 8, at % 2


def pick(ref, base, odd, start, count, stride=1):
    def load(at):
        return ref[pl.ds(at, count, stride=stride), :] if stride > 1 else ref[pl.ds(at, count), :]

    first = load(base + start)
    if not odd:
        return first
    return jnp.concatenate([first[:, 64:], load(base + start + 1)[:, :64]], 1)


def load_weights(ref, base, odd, dir_no, proj_s):
    at = SIDE_ROWS * dir_no
    win = jnp.concatenate([pick(ref, base, odd, at + q, FILTERS, 4) for q in range(4)], 1)
    wrec = jnp.concatenate([pick(ref, base, odd, at + 256 + q, UNITS, 4) for q in range(4)], 1)
    bias = jnp.concatenate([pick(ref, base, odd, at + 768 + q, 1) for q in range(4)], 1)
    pairs = pick(ref, base, odd, PROJ_ROWS + 64 * dir_no, 64)
    proj_s[pl.ds(0, 64, stride=2), :] = pairs
    proj_s[pl.ds(1, 64, stride=2), :] = pltpu.roll(pairs, 64, 1)
    return win, wrec, bias, proj_s[:, :FILTERS]


def load_vec(ref, base, odd):
    first = pick(ref, base, odd, VEC_ROW, 1)
    turned = pltpu.roll(jnp.broadcast_to(first, (8, 128)), 64, 1)[0:1]
    if odd:
        last = ref[base + VEC_ROW + 1:base + VEC_ROW + 2, :]
        last = jnp.concatenate([last[:, 64:], last[:, 64:]], 1)
    else:
        last = ref[base + VEC_ROW + 1:base + VEC_ROW + 2, :]
        last = jnp.concatenate([last[:, :64], last[:, :64]], 1)
    low = lax.broadcasted_iota(jnp.int32, (1, 128), 1) < 64
    return jnp.where(low, first, turned), jnp.where(low, turned, first), last


def share_of(tasks, number, count):
    return tasks[number * len(tasks) // count:(number + 1) * len(tasks) // count]


def fold_halves(a):
    return a + pltpu.roll(a, FILTERS, 1)


def narrow(a, half):
    if isinstance(half, int):
        a = pltpu.roll(a, FILTERS, 1) if half else a
    else:
        a = jnp.where(half == 0, a, pltpu.roll(a, FILTERS, 1))
    low_lanes = lax.broadcasted_iota(jnp.int32, a.shape, 1) < FILTERS
    hi = a.astype(BF16).astype(F32)
    lo = pltpu.roll(a - hi, FILTERS, 1)
    return jnp.concatenate([jnp.where(low_lanes, hi, lo), jnp.where(low_lanes, hi, 0.0)], 1).astype(BF16)


def narrow_weights(w):
    hi, lo = split(w)
    return jnp.concatenate([hi, hi, lo, jnp.zeros_like(hi)], 0)


def side_weights(w):
    hi, lo = split(w)
    return jnp.concatenate([hi, lo], 1)


def dot_sides(a, w):
    hi, lo = split(a)
    return fold_halves(dot(hi, w) + dot(lo, w))


def put_split(w, twice_ref, low_ref):
    hi, lo = split(w)
    twice_ref[...] = jnp.concatenate([hi, hi], 0)
    low_ref[...] = lo


def times(dir_no, chunk_no, length, steps):
    return [dir_no * (length - 1) + (1 - 2 * dir_no) * (chunk_no * steps + u) for u in range(steps)]


def stream_rows(inter, groups, at):
    if inter:
        return pl.ds(at, HALF_PAD, stride=groups)
    return pl.ds(pl.multiple_of(lax.rem(at, HOP) * groups, 8), groups)


def gather(ref, inter, groups, positions):
    return jnp.concatenate([ref[stream_rows(inter, groups, at), :] for at in positions], 0)


def to_sides(inter, steps, array):
    if not inter:
        return [array]
    three = array.reshape(steps, 2 * HALF_PAD, array.shape[-1])
    return [
        three[:, side * HALF_PAD:(side + 1) * HALF_PAD].reshape(steps * HALF_PAD, array.shape[-1]) for side in range(2)
    ]


SIDE_ROWS = 772
PROJ_ROWS = 2 * SIDE_ROWS
VEC_ROW = PROJ_ROWS + 128
LAYER_ROWS = 1680
HEAD_ROWS = 160
OWN_PROJ = SIDE_ROWS
OWN_VEC = SIDE_ROWS + 64
OWN_EXTRA = SIDE_ROWS + 68
OWN_ROWS = (OWN_EXTRA + 8, OWN_EXTRA, OWN_EXTRA, OWN_EXTRA + HEAD_ROWS)
WINDOW = 1688
TAIL_ROW = 6688
TAIL_ROWS = 104
SHARE_ROWS = 256
FRAME_LANES = 8
MIX_LANE = SOURCES
NEXT_LANE = FRAME_LANES + MIX_LANE


def window(layer_no):
    at = 2 + 3347 * layer_no
    return at // 16 * 8, at // 2 % 8, at % 2


def pick(ref, base, odd, start, count, stride=1):
    def load(at):
        return ref[pl.ds(at, count, stride=stride), :] if stride > 1 else ref[pl.ds(at, count), :]

    first = load(base + start)
    if not odd:
        return first
    return jnp.concatenate([first[:, 64:], load(base + start + 1)[:, :64]], 1)


def load_weights(ref, base, odd, dir_no, proj_s):
    at = SIDE_ROWS * dir_no
    win = jnp.concatenate([pick(ref, base, odd, at + q, FILTERS, 4) for q in range(4)], 1)
    wrec = jnp.concatenate([pick(ref, base, odd, at + 256 + q, UNITS, 4) for q in range(4)], 1)
    bias = jnp.concatenate([pick(ref, base, odd, at + 768 + q, 1) for q in range(4)], 1)
    pairs = pick(ref, base, odd, PROJ_ROWS + 64 * dir_no, 64)
    proj_s[pl.ds(0, 64, stride=2), :] = pairs
    proj_s[pl.ds(1, 64, stride=2), :] = pltpu.roll(pairs, 64, 1)
    return win, wrec, bias, proj_s[:, :FILTERS]


def load_vec(ref, base, odd):
    first = pick(ref, base, odd, VEC_ROW, 1)
    turned = pltpu.roll(jnp.broadcast_to(first, (8, 128)), 64, 1)[0:1]
    if odd:
        last = ref[base + VEC_ROW + 1:base + VEC_ROW + 2, :]
        last = jnp.concatenate([last[:, 64:], last[:, 64:]], 1)
    else:
        last = ref[base + VEC_ROW + 1:base + VEC_ROW + 2, :]
        last = jnp.concatenate([last[:, :64], last[:, :64]], 1)
    low = lax.broadcasted_iota(jnp.int32, (1, 128), 1) < 64
    return jnp.where(low, first, turned), jnp.where(low, turned, first), last


def put_split(w, twice_ref, low_ref):
    hi, lo = split(w)
    twice_ref[...] = jnp.concatenate([hi, hi], 0)
    low_ref[...] = lo


def place(dir_no, chunk_no, count, steps, inter, groups):
    first = jnp.where(dir_no == 0, chunk_no * steps, (count - 1 - chunk_no) * steps)
    if inter:
        return first, 0, 0
    half = first // HOP
    return first, half, pl.multiple_of((first - HOP * half) * groups, 8)


def norm_stage(prev_ref, pa_ref, pb_ref, flat_ref, base, odd, valid, normed_ref, scale_ref, x_ref):
    offset, gain, shift = load_vec(flat_ref, base, odd)
    mixed = pa_ref[:valid] + pb_ref[:valid] + offset
    total = 2.0 * valid * FILTERS
    mean = jnp.sum(mixed) / total
    spread = jnp.sum(mixed * mixed) / total - mean * mean
    scale = lax.rsqrt(jnp.full((1, 128), spread + NORM_EPS, F32))
    normed = (mixed - mean) * scale
    normed_ref[:valid] = normed
    normed_ref[valid:] = jnp.zeros((normed_ref.shape[0] - valid, 128), F32)
    x_ref[:valid] = prev_ref[:valid] + gain * normed + shift
    x_ref[valid:] = jnp.zeros((x_ref.shape[0] - valid, 128), F32)
    scale_ref[...] = jnp.broadcast_to(scale, scale_ref.shape)


def greet_sibling():
    b = lax.axis_index("batch")
    device = (b + 1 - 2 * lax.rem(b, 2), lax.axis_index("frames"))
    return device, pltpu.get_barrier_semaphore()


def swap_with_sibling(src_ref, dst_ref, sems, greeted=False):
    device, barrier = greet_sibling()
    if not greeted:
        pl.semaphore_wait(barrier, 1)
    copy = pltpu.make_async_remote_copy(
        src_ref=src_ref, dst_ref=dst_ref, send_sem=sems.at[0], recv_sem=sems.at[1],
        device_id=device, device_id_type=pl.DeviceIdType.MESH,
    )
    copy.start()
    return copy


def reduced_rows(rows, chips, depths):
    return -(-rows // (8 * chips * depths)) * 8 * chips * depths


def reducer_scratch(rows, chips, depths):
    quarter = rows // chips
    part = quarter // depths
    sems = pltpu.SemaphoreType.DMA
    return [
        pltpu.VMEM((2, rows, 128), F32), pltpu.VMEM((chips - 1, quarter, 128), F32), pltpu.VMEM((quarter, 128), F32),
        pltpu.VMEM((depths - 1, part, 128), F32), pltpu.VMEM((part, 128), F32), pltpu.VMEM((quarter, 128), F32),
        sems((2, chips - 1)), sems((2, depths - 1)), sems((2, depths - 1)), sems((2, chips - 1)), sems((2, 1)),
    ]


def greet_all(chips, depths):
    b = lax.axis_index("batch")
    z = lax.axis_index("frames")
    barrier = pltpu.get_barrier_semaphore()
    devices = [(b + 1 - 2 * lax.rem(b, 2), z)]
    devices += [(lax.rem(b + 2 * step, 2 * chips), z) for step in range(1, chips)]
    devices += [(b, lax.rem(z + step, depths)) for step in range(1, depths)]
    for device in devices:
        pl.semaphore_signal(barrier, inc=1, device_id=device, device_id_type=pl.DeviceIdType.MESH)
    return barrier, len(devices)


def reducer(src, chips, depths, refs):
    red, plane_in, mine, depth_in, piece, joined, s_plane, s_depth, s_spread, s_gather, s_back = refs
    b = lax.axis_index("batch")
    z = lax.axis_index("frames")
    core = lax.rem(b, 2)
    chip = lax.div(b, 2)
    quarter = mine.shape[0]
    part = piece.shape[0]

    def rows(at, count):
        return pl.ds(pl.multiple_of(at, 8), count)

    def send(src_ref, dst_ref, sems, slot, device):
        return pltpu.make_async_remote_copy(
            src_ref=src_ref, dst_ref=dst_ref, send_sem=sems.at[0, slot], recv_sem=sems.at[1, slot],
            device_id=device, device_id_type=pl.DeviceIdType.MESH,
        )

    over_plane = [(step, (lax.rem(b + 2 * step, 2 * chips), z)) for step in range(1, chips)]
    over_depth = [(step, (b, lax.rem(z + step, depths))) for step in range(1, depths)]
    own = rows(chip * quarter, quarter)
    mine_at = rows(z * part, part)

    def plane():
        return [
            send(src.at[rows(lax.rem(chip + step, chips) * quarter, quarter)], plane_in.at[step - 1], s_plane, step - 1, to)
            for step, to in over_plane
        ]

    def scatter():
        return [
            send(mine.at[rows(lax.rem(z + step, depths) * part, part)], depth_in.at[step - 1], s_depth, step - 1, to)
            for step, to in over_depth
        ]

    def spread():
        return [send(piece, joined.at[mine_at], s_spread, step - 1, to) for step, to in over_depth]

    def gather():
        return [send(joined, red.at[core, own], s_gather, step - 1, to) for step, to in over_plane]

    def back():
        return [send(red.at[core], red.at[core], s_back, 0, (b + 1 - 2 * core, z))]

    def start(copies):
        for copy in copies:
            copy.start()

    def wait(copies):
        for copy in copies:
            copy.wait()

    def first():
        start(plane())

    def third():
        wait(plane())
        total = src[own, :]
        for step in range(1, chips):
            total = total + plane_in[step - 1]
        mine[...] = total
        start(scatter())

    def fourth():
        wait(scatter())
        total = mine[mine_at, :]
        for step in range(1, depths):
            total = total + depth_in[step - 1]
        piece[...] = total
        joined[mine_at, :] = total
        start(spread())

    def fifth():
        wait(spread())
        red[core, own] = joined[...]
        start(gather())

    def sixth():
        wait(gather())
        start(back())

    def last():
        wait(back())

    return [first, third, fourth, fifth, sixth, last]


def forward_kernel(layer_no, groups, steps, *refs):
    inter = layer_no % 2 == 1
    (x_ref, flat_ref,
     next_ref, normed_ref, scale_ref, h_ref, coef_ref,
     wi4, wr2, wrl, pj, proj_s, bias_s, gin_a, gin_b, h_a, h_b, c_s, part_ref, peer_ref, sems) = refs
    turn_no = pl.program_id(0)
    last_turn = pl.num_programs(0) - 1
    turn = per_turn(inter)
    chunks = turn * pl.num_programs(0)
    length = chunks * steps
    dir_no = lax.rem(lax.axis_index("batch"), 2)
    rows = 2 * HALF_PAD if inter else groups
    valid = HOP * groups

    def before(chunk_no, gin):
        chunk_no = lax.rem(chunk_no, chunks)
        positions = times(dir_no, chunk_no, length, steps)
        sides = []

        def prepare():
            xs = gather(x_ref, inter, groups, positions)
            for half in [0, 1] if inter else [lax.div(positions[0], HOP)]:
                sides.append(narrow(xs, half))

        def gate(q):
            cut = slice(q * UNITS, (q + 1) * UNITS)
            for side, rows_of in enumerate(sides):
                found = dot(rows_of, wi4[:, cut]) + bias_s[0:1, cut]
                if inter:
                    for u in range(steps):
                        at = u * rows + side * HALF_PAD
                        gin[at:at + HALF_PAD, cut] = found[u * HALF_PAD:(u + 1) * HALF_PAD]
                else:
                    gin[:, cut] = found

        return [prepare] + [functools.partial(gate, q) for q in range(4)]

    def after(chunk_no, hs):
        chunk_no = lax.rem(chunk_no + chunks, chunks)
        positions = times(dir_no, chunk_no, length, steps)

        def project():
            found = [dot_sides(part, pj[...]) for part in to_sides(inter, steps, hs[...])]
            low_lanes = lax.broadcasted_iota(jnp.int32, found[0].shape, 1) < FILTERS
            if inter:
                found = jnp.where(low_lanes, found[0], found[1])
                for u in range(steps):
                    part_ref[stream_rows(inter, groups, positions[u]), :] = found[u * HALF_PAD:(u + 1) * HALF_PAD]
            else:
                half = lax.div(positions[0], HOP)
                found = jnp.where(low_lanes == (half == 0), found[0], 0.0)
                for u in range(steps):
                    here = stream_rows(inter, groups, positions[u])
                    part_ref[here, :] = part_ref[here, :] + found[u * groups:(u + 1) * groups]

        return [project]

    def walk(gin, hs, h, c, sub, beside):
        for u in range(steps):
            hi, lo = split(h)
            z = dot(jnp.concatenate([hi, lo], 1), wr2[...]) + dot(hi, wrl[...])
            for task in share_of(beside, u, steps):
                task()
            z = z + gin[u * rows:(u + 1) * rows]
            th = jnp.tanh(z)
            ti, tf, g, to = (th[:, q * UNITS:(q + 1) * UNITS] for q in range(4))
            i_g = 0.5 * ti + 0.5
            f_g = 0.5 * tf + 0.5
            o_g = 0.5 * to + 0.5
            c_prev = c
            c = f_g * c + i_g * g
            tc = jnp.tanh(c)
            h = o_g * tc
            at = sub * steps + u
            hs[u * rows:(u + 1) * rows] = h
            h_ref[at] = h
            coef_ref[at, 0] = tc * (0.25 - 0.25 * to * to)
            coef_ref[at, 1] = o_g * (1.0 - tc * tc)
            coef_ref[at, 2] = g * (0.25 - 0.25 * ti * ti)
            coef_ref[at, 3] = c_prev * (0.25 - 0.25 * tf * tf)
            coef_ref[at, 4] = i_g * (1.0 - g * g)
            coef_ref[at, 5] = f_g
        return h, c

    @pl.when(turn_no == 0)
    def _():
        device, barrier = greet_sibling()
        pl.semaphore_signal(barrier, inc=1, device_id=device, device_id_type=pl.DeviceIdType.MESH)
        part_ref[...] = jnp.zeros_like(part_ref)
        column = lax.broadcasted_iota(jnp.int32, (1, GATES), 1)
        scaling = jnp.where((column >= 2 * UNITS) & (column < 3 * UNITS), 1.0, 0.5)
        _, base, odd = window(layer_no)
        win, wrec, bias, proj = load_weights(flat_ref, base, odd, dir_no, proj_s)
        wi4[...] = narrow_weights(win * scaling)
        put_split(wrec * scaling, wr2, wrl)
        bias_s[...] = jnp.broadcast_to(bias * scaling, bias_s.shape)
        pj[...] = side_weights(proj)
        c_s[...] = jnp.zeros_like(c_s)
        h_b[...] = jnp.zeros_like(h_b)
        for task in before(0, gin_a):
            task()

    h, c = h_b[(steps - 1) * rows:], c_s[...]
    for n in range(turn):
        (gin, hs), (next_gin, past_hs) = ((gin_a, h_a), (gin_b, h_b))[::1 - 2 * (n % 2)]
        number = turn * turn_no + n
        h, c = walk(gin, hs, h, c, n, after(number - 1, past_hs) + before(number + 1, next_gin))
    c_s[...] = c

    @pl.when(turn_no == last_turn)
    def _():
        for task in after(chunks - 1, h_b):
            task()
        swap_with_sibling(part_ref, peer_ref, sems).wait()
        _, base, odd = window(layer_no)
        norm_stage(x_ref, part_ref, peer_ref, flat_ref, base, odd, valid, normed_ref, scale_ref, next_ref)


def backward_kernel(layer_no, groups, steps, chips, depths, *refs):
    inter = layer_no % 2 == 1
    last_layer = layer_no == 2 * BLOCKS - 1
    g_ref, normed_ref, scale_ref, x_hbm, h_hbm, coef_ref, flat_ref, *rest = refs
    if last_layer:
        hg_ref, *rest = rest
    if layer_no == 0:
        column_ref, denc_ref, encoder_ref, loss_ref, *rest = rest
    if not last_layer:
        upper_ref, *rest = rest
    if layer_no:
        below_ref, *rest = rest
    if not last_layer:
        red_ref, *rest = rest
    (grad_ref,
     wi4, wrw, wrt, pj, proj_s, dmx, dh_a, dh_b, dz_a, dz_b, dc_s, awin, aproj, abias,
     dx_ref, peer_ref, sems, x_ref, h_ref, kept_sem, *rest) = rest
    stages = [] if last_layer else reducer(upper_ref, chips, depths, rest)
    turn_no = pl.program_id(0)
    last_turn = pl.num_programs(0) - 1
    chunks = 2 * pl.num_programs(0)
    length = chunks * steps
    dir_no = lax.rem(lax.axis_index("batch"), 2)
    rows = 2 * HALF_PAD if inter else groups
    valid = HOP * groups

    def before(back_no, dhc):
        chunk_no = chunks - 1 - lax.rem(back_no, chunks)
        positions = times(dir_no, chunk_no, length, steps)

        def outward():
            dms = gather(dmx, inter, groups, positions)
            for side, half in enumerate([0, 1] if inter else [lax.div(positions[0], HOP)]):
                found = dot(narrow(dms, half), pj[...])
                if inter:
                    for u in range(steps):
                        at = u * rows + side * HALF_PAD
                        dhc[at:at + HALF_PAD] = found[u * HALF_PAD:(u + 1) * HALF_PAD]
                else:
                    dhc[...] = found

        return [outward]

    def after(back_no, dzs):
        used = back_no >= 0
        chunk_no = chunks - 1 - lax.rem(back_no + chunks, chunks)
        positions = times(dir_no, chunk_no, length, steps)
        half = 0 if inter else lax.div(positions[0], HOP)
        at = chunk_no * steps
        count = UNITS + FILTERS
        ready = []

        def prepare():
            xs = gather(x_ref, inter, groups, positions)
            hs = h_ref[pl.ds(at, steps)].reshape(steps * rows, UNITS)
            early = h_ref[lax.rem(at + length - 1, length)] * jnp.where(at == 0, 0.0, 1.0)
            hp = jnp.concatenate([early, hs[:(steps - 1) * rows]], 0)
            if inter:
                lhs = [
                    jnp.concatenate([hp_side, (xs if side == 0 else pltpu.roll(xs, FILTERS, 1))[:, :FILTERS]], 1)
                    for side, hp_side in enumerate(to_sides(inter, steps, hp))
                ]
                lhs = jnp.concatenate(lhs, 0)
            else:
                turned = jnp.where(half == 0, xs, pltpu.roll(xs, FILTERS, 1))
                lhs = jnp.concatenate([hp, turned[:, :FILTERS]], 1)
            lhs_hi, lhs_lo = split(lhs.T)
            ready.extend([lhs_hi, jnp.concatenate([lhs_hi, lhs_lo], 0)])

        def gate(q):
            cut = slice(q * UNITS, (q + 1) * UNITS)
            dz = dzs[:, cut]
            abias[0:1, cut] += jnp.sum(dz, 0, keepdims=True)
            if inter:
                dz = jnp.concatenate(to_sides(inter, steps, dz), 0)
            dz_hi, dz_lo = split(dz)
            both = dot(ready[1], dz_hi)
            awin[:, cut] += both[:count] + both[count:] + dot(ready[0], dz_lo)

        def project():
            hs = h_ref[pl.ds(at, steps)].reshape(steps * rows, UNITS)
            dms = gather(dmx, inter, groups, positions) * jnp.where(used, 1.0, 0.0)
            if inter:
                aproj[...] += dot_rows3(jnp.concatenate(to_sides(inter, steps, hs), 1), dms)
            else:
                turned = jnp.where(half == 0, dms, pltpu.roll(dms, FILTERS, 1))
                aproj[...] += dot_rows3(hs, turned)

        def inward():
            found = [dot_sides(part, wi4[...]) for part in to_sides(inter, steps, dzs[...])]
            low_lanes = lax.broadcasted_iota(jnp.int32, found[0].shape, 1) < FILTERS
            if inter:
                found = jnp.where(low_lanes, found[0], found[1])
                for u in range(steps):
                    dx_ref[stream_rows(inter, groups, positions[u]), :] = found[u * HALF_PAD:(u + 1) * HALF_PAD]
            else:
                found = jnp.where(low_lanes == (half == 0), found[0], 0.0)
                for u in range(steps):
                    here = stream_rows(inter, groups, positions[u])
                    dx_ref[here, :] = dx_ref[here, :] + found[u * groups:(u + 1) * groups]

        return [inward, project, prepare] + [functools.partial(gate, q) for q in range(4)]

    def walk(dhc, dzs, dz, dc_next, sub, beside):
        for u in reversed(range(steps)):
            at = sub * steps + u
            hi, lo = split(dz)
            wide = dot(hi, wrw[...])
            dh = wide[:, :UNITS] + wide[:, UNITS:] + dot(lo, wrt[...])
            for task in share_of(beside, steps - 1 - u, steps):
                task()
            dh = dh + dhc[u * rows:(u + 1) * rows]
            dc = dh * coef_ref[at, 1] + dc_next
            dz = jnp.concatenate(
                [dc * coef_ref[at, 2], dc * coef_ref[at, 3], dc * coef_ref[at, 4], dh * coef_ref[at, 0]], 1
            )
            dc_next = dc * coef_ref[at, 5]
            dzs[u * rows:(u + 1) * rows] = dz
        return dz, dc_next

    @pl.when(turn_no == 0)
    def _():
        kept = [
            pltpu.make_async_copy(src, dst, kept_sem.at[n])
            for n, (src, dst) in enumerate(((x_hbm, x_ref), (h_hbm, h_ref)))
        ]
        for copy in kept:
            copy.start()
        if last_layer:
            device, barrier = greet_sibling()
            pl.semaphore_signal(barrier, inc=1, device_id=device, device_id_type=pl.DeviceIdType.MESH)
        else:
            barrier, count = greet_all(chips, depths)
            pl.semaphore_wait(barrier, count)
            stages[0]()
        dx_ref[...] = jnp.zeros_like(dx_ref)
        _, base, odd = window(layer_no)
        win, wrec, _, proj = load_weights(flat_ref, base, odd, dir_no, proj_s)
        wi4[...] = side_weights(win.T)
        hi, lo = split(wrec.T)
        wrw[...] = jnp.concatenate([hi, lo], 1)
        wrt[...] = hi
        pj[...] = narrow_weights(proj.T)
        dz_b[...] = jnp.zeros_like(dz_b)
        dc_s[...] = jnp.zeros_like(dc_s)
        awin[...] = jnp.zeros_like(awin)
        aproj[...] = jnp.zeros_like(aproj)
        abias[...] = jnp.zeros_like(abias)
        grad_ref[...] = jnp.zeros_like(grad_ref)
        g = g_ref[:valid]
        normed = normed_ref[:valid]
        _, gain, _ = load_vec(flat_ref, base, odd)
        g_n = g * gain
        total = 2.0 * valid * FILTERS
        mean_one = jnp.sum(g_n) / total
        mean_two = jnp.sum(g_n * normed) / total
        dmixed = scale_ref[0:1] * (g_n - mean_one - normed * mean_two)
        dmx[:valid] = dmixed
        dmx[valid:] = jnp.zeros((dmx.shape[0] - valid, 128), F32)
        lead = jnp.where(dir_no == 0, 1.0, 0.0)

        def fold(array):
            found = lead * jnp.sum(array, 0, keepdims=True)
            return found[:, :FILTERS] + found[:, FILTERS:]

        grad_ref[OWN_VEC:OWN_VEC + 1] = jnp.concatenate([fold(dmixed), fold(g * normed)], 1)
        grad_ref[OWN_VEC + 1:OWN_VEC + 2] = jnp.concatenate([fold(g), jnp.zeros((1, FILTERS), F32)], 1)
        if last_layer:
            grad_ref[OWN_EXTRA:OWN_EXTRA + HEAD_ROWS] = hg_ref[...] * lead

        for task in before(0, dh_a):
            task()
        for copy in kept:
            copy.wait()

    for stage, at in zip(stages[1:], (2, 3, 4, None) if inter else (3, 5, 6, 9)):
        if at is not None:
            pl.when(turn_no == at)(stage)

    dz, dc_next = dz_b[:rows], dc_s[...]
    dz, dc_next = walk(dh_a, dz_a, dz, dc_next, 1, after(2 * turn_no - 1, dz_b) + before(2 * turn_no + 1, dh_b))
    dz, dc_next = walk(dh_b, dz_b, dz, dc_next, 0, after(2 * turn_no, dz_a) + before(2 * turn_no + 2, dh_a))
    dc_s[...] = dc_next

    @pl.when(turn_no == last_turn)
    def _():
        for task in after(chunks - 1, dz_b):
            task()
        if layer_no:
            swap = swap_with_sibling(dx_ref, peer_ref, sems, not last_layer)
        for stage in stages[4:] if inter else stages[5:]:
            stage()
        if not last_layer:
            red_ref[...] = rest[0][...]
        if layer_no:
            swap.wait()
            below_ref[:valid] = g_ref[:valid] + dx_ref[:valid] + peer_ref[:valid]
            below_ref[valid:] = jnp.zeros((below_ref.shape[0] - valid, 128), F32)
        for q in range(4):
            cut = slice(q * UNITS, (q + 1) * UNITS)
            grad_ref[pl.ds(q, FILTERS, stride=4), :] = awin[UNITS:, cut]
            grad_ref[pl.ds(256 + q, UNITS, stride=4), :] = awin[:UNITS, cut]
            grad_ref[768 + q:769 + q, :] = abias[0:1, cut]
        proj_s[...] = aproj[:UNITS] + pltpu.roll(aproj[UNITS:], FILTERS, 1) if inter else aproj[...]
        even = proj_s[pl.ds(0, 64, stride=2), :]
        odd_rows = proj_s[pl.ds(1, 64, stride=2), :]
        grad_ref[OWN_PROJ:OWN_VEC, :] = jnp.concatenate(
            [even[:, :FILTERS], odd_rows[:, :FILTERS]], 1
        )
        if layer_no == 0:
            lead = jnp.where(dir_no == 0, 1.0, 0.0)
            streams = lead * g_ref[:valid] + dx_ref[:valid]
            column = column_ref[...]
            mix, following = column[:, MIX_LANE:MIX_LANE + 1], column[:, NEXT_LANE:NEXT_LANE + 1]
            raw = mix * encoder_ref[0:1, :FILTERS] + following * encoder_ref[1:2, :FILTERS]
            group_at = lax.broadcasted_iota(jnp.int32, (valid, FILTERS), 0) % groups
            shifted = jnp.where(group_at == 0, 0.0, pltpu.roll(pltpu.roll(streams, FILTERS, 1), 1, 0)[:, :FILTERS])
            grad_raw = (streams[:, :FILTERS] + shifted + lead * denc_ref[...]) * jax.nn.sigmoid(raw)
            grad_ref[OWN_EXTRA:OWN_EXTRA + 1] = jnp.concatenate(
                [jnp.sum(grad_raw * mix, 0, keepdims=True), jnp.sum(grad_raw * following, 0, keepdims=True)], 1
            )
            grad_ref[OWN_EXTRA + 1:OWN_EXTRA + 2] = loss_ref[0:1] * lead


def head_kernel(groups, sep, stream_ref, column_ref, active_ref, note_ref, tail_s,
                g_ref, hg_ref, denc_ref, loss_ref,
                sig_s, now_s, before_s, slope_s, mk2, mkl, mt2, mtl, dk2, dkl, dt2, dtl, amask, adec, m_low, m_top):
    valid = HOP * groups
    block = 10 * groups
    first, second, third = (tail_s[pl.ds(6695 - TAIL_ROW + n, 32, stride=3), :] for n in range(3))
    m_low[pl.ds(0, 32, stride=2), :] = first
    m_low[pl.ds(1, 32, stride=2), :] = jnp.concatenate([second[:, FILTERS:], third[:, :FILTERS]], 1)
    m_top[pl.ds(0, 32, stride=2), :] = second
    m_top[pl.ds(1, 32, stride=2), :] = pltpu.roll(third, FILTERS, 1)
    masker = jnp.concatenate([m_low[...], m_top[:, :FILTERS]], 1)
    taps = tail_s[6791 - TAIL_ROW:6792 - TAIL_ROW]
    lane_at = lax.broadcasted_iota(jnp.int32, (FILTERS, 128), 1)
    row_at = lax.broadcasted_iota(jnp.int32, (FILTERS, 128), 0)
    upright = [
        jnp.sum(jnp.where(lane_at == 2 * row_at + tap, taps, 0.0), 1, keepdims=True) for tap in range(2)
    ]
    decoder = jnp.concatenate(
        [
            jnp.concatenate([jnp.where(lane_at == j, column, 0.0) for column in upright], 1)
            for j in range(SOURCES)
        ],
        0,
    )
    put_split(masker, mk2, mkl)
    put_split(masker.T, mt2, mtl)
    put_split(decoder, dk2, dkl)
    put_split(decoder.T, dt2, dtl)
    amask[...] = jnp.zeros_like(amask)
    adec[...] = jnp.zeros_like(adec)
    active = active_ref[0:1]

    def rows(n):
        return pl.ds(pl.multiple_of(n * block, 8), block)

    def summed_of(n):
        here = sep[rows(n), :]
        group_at = lax.broadcasted_iota(jnp.int32, (block, FILTERS), 0) % groups
        shifted = pltpu.roll(pltpu.roll(here, FILTERS, 1), 1, 0)[:, :FILTERS]
        return here[:, :FILTERS] + jnp.where(group_at == 0, 0.0, shifted)

    def frames_of(n):
        encoded = stream_ref[rows(n), :][:, :FILTERS]
        return jnp.concatenate([encoded, encoded, encoded], 1)

    def ahead(n, carry):
        logits = dot3(summed_of(n), mk2[...], mkl[...])
        sig = jax.nn.sigmoid(logits)
        sig_s[rows(n), :] = sig
        both = dot3(sig * active * frames_of(n), dk2[...], dkl[...])
        now_s[rows(n), :] = both[:, :128]
        before_s[pl.ds(pl.multiple_of(n * block + groups, 8), block), :] = both[:, 128:]
        return carry

    lax.fori_loop(0, HOP // 10, ahead, 0)
    at = lax.broadcasted_iota(jnp.int32, (groups, 128), 0)
    before_s[:groups] = jnp.where(at == 0, 0.0, pltpu.roll(before_s[valid:], 1, 0))

    def losses(n, total):
        column = column_ref[rows(n), :]
        lane = lax.broadcasted_iota(jnp.int32, (block, 128), 1)
        active_lane = (lane < SOURCES) & (lane.astype(F32) < active_ref[1:2, :128])
        target = jnp.where(active_lane, column, 0.0)
        row = lax.broadcasted_iota(jnp.int32, (block, 128), 0)
        frame = HOP * (row % groups) + row // groups + 10 * n
        kept = jnp.where(frame.astype(F32) < active_ref[2:3, :128], active_ref[3:4, :128], 0.0)
        differ = now_s[rows(n), :] + before_s[rows(n), :] - target
        root = jnp.sqrt(differ * differ + 1.0)
        slope_s[rows(n), :] = kept * differ / root
        return total + jnp.sum(kept * (root - 1.0), 0, keepdims=True)

    total = lax.fori_loop(0, HOP // 10, losses, jnp.zeros((1, 128), F32))
    first_lane = lax.broadcasted_iota(jnp.int32, (8, 128), 1) == 0
    loss_ref[...] = jnp.where(first_lane, jnp.sum(total, 1, keepdims=True), note_ref[...])
    slope_s[valid:] = jnp.where(at == groups - 1, 0.0, pltpu.roll(slope_s[:groups], groups - 1, 0))

    def back(n, carry):
        slopes = jnp.concatenate(
            [slope_s[rows(n), :], slope_s[pl.ds(pl.multiple_of(n * block + groups, 8), block), :]], 1
        )
        sig = sig_s[rows(n), :]
        frames = frames_of(n)
        dmasked = dot3(slopes, dt2[...], dtl[...]) * active
        by_sig = dmasked * sig
        denc_ref[rows(n), :] = (
            by_sig[:, :FILTERS] + by_sig[:, FILTERS:2 * FILTERS] + by_sig[:, 2 * FILTERS:]
        )
        dlogits = by_sig * frames * (1.0 - sig)
        dsummed = dot3(dlogits, mt2[...], mtl[...])
        group_at = lax.broadcasted_iota(jnp.int32, (block, FILTERS), 0) % groups
        shifted = jnp.where(group_at == groups - 1, 0.0, pltpu.roll(dsummed, block - 1, 0))
        g_ref[rows(n), :] = jnp.concatenate([dsummed, shifted], 1)
        amask[...] += dot_rows3(summed_of(n), dlogits)
        adec[...] += dot_rows3(sig * active * frames, slopes)
        return carry

    lax.fori_loop(0, HOP // 10, back, 0)
    g_ref[valid:] = jnp.zeros((g_ref.shape[0] - valid, 128), F32)
    m_low[...] = amask[:, :128]
    m_top[...] = jnp.concatenate([amask[:, 128:], jnp.zeros((FILTERS, FILTERS), F32)], 1)
    low_even, low_odd = m_low[pl.ds(0, 32, stride=2), :], m_low[pl.ds(1, 32, stride=2), :]
    top_even, top_odd = m_top[pl.ds(0, 32, stride=2), :], m_top[pl.ds(1, 32, stride=2), :]
    hg_ref[pl.ds(0, 32, stride=3), :] = low_even
    hg_ref[pl.ds(1, 32, stride=3), :] = jnp.concatenate([top_even[:, :FILTERS], low_odd[:, :FILTERS]], 1)
    hg_ref[pl.ds(2, 32, stride=3), :] = jnp.concatenate([low_odd[:, FILTERS:], top_odd[:, :FILTERS]], 1)
    columns = []
    for tap in range(2):
        found = 0.0
        for j in range(SOURCES):
            found = found + adec[j * FILTERS:(j + 1) * FILTERS, 128 * tap + j:128 * tap + j + 1]
        columns.append(jnp.broadcast_to(found, (FILTERS, 128)))
    lane = lax.broadcasted_iota(jnp.int32, (FILTERS, 128), 1)
    hg_ref[96:HEAD_ROWS] = jnp.where(lane == 0, columns[0], jnp.where(lane == 1, columns[1], 0.0))


def assemble(flat, layers):
    lane = lax.broadcasted_iota(jnp.int32, (FILTERS, 128), 1)
    row = lax.broadcasted_iota(jnp.int32, (FILTERS, 128), 0)

    def interleave(a, b):
        return jnp.sum(jnp.where(lane == 2 * row, a, jnp.where(lane == 2 * row + 1, b, 0.0)), 0, keepdims=True)

    for layer_no, ref in enumerate(layers):
        if ref is None:
            continue
        first, inner, odd = window(layer_no)
        at = first + inner
        parts = [(ref[0, :OWN_PROJ], False), (ref[1, :OWN_PROJ], False), (ref[0, OWN_PROJ:OWN_VEC], False)]
        parts += [(ref[1, OWN_PROJ:OWN_VEC], False), (ref[0, OWN_VEC:OWN_VEC + 2], True)]
        for rows, ends in parts:
            count = rows.shape[0]
            if odd:
                turned = pltpu.roll(rows, FILTERS, 1) if count >= 8 else jnp.concatenate(
                    [rows[:, FILTERS:], rows[:, :FILTERS]], 1
                )
                wide_low = lax.broadcasted_iota(jnp.int32, (count - 1, 128), 1) < FILTERS
                flat[at:at + 1, FILTERS:] = turned[0:1, FILTERS:]
                flat[at + 1:at + count] = jnp.where(wide_low, turned[:-1], turned[1:])
                if not ends:
                    flat[at + count:at + count + 1, :FILTERS] = turned[count - 1:, :FILTERS]
            elif ends:
                flat[at:at + 1] = rows[0:1]
                flat[at + 1:at + 2, :FILTERS] = rows[1:2, :FILTERS]
            else:
                flat[at:at + count] = rows
            at += count
        if layer_no == 0:
            encoder = ref[0, OWN_EXTRA:OWN_EXTRA + 1] + ref[1, OWN_EXTRA:OWN_EXTRA + 1]
            encoder = jnp.broadcast_to(encoder, (FILTERS, 128))
            first_tap = jnp.sum(jnp.where(lane == row, encoder, 0.0), 1, keepdims=True)
            second_tap = jnp.sum(jnp.where(lane == row + FILTERS, encoder, 0.0), 1, keepdims=True)
            flat[0:1] = interleave(first_tap, second_tap)
        if layer_no == 2 * BLOCKS - 1:
            flat[6695:6791] = ref[0, OWN_EXTRA:OWN_EXTRA + 96]
            decoder = ref[0, OWN_EXTRA + 96:OWN_EXTRA + HEAD_ROWS]
            flat[6791:6792] = interleave(decoder[:, 0:1], decoder[:, 1:2])
            flat[6792:] = jnp.zeros((flat.shape[0] - 6792, 128), F32)


def finish_kernel(chips, depths, entries, own_ref, r1, r2, r3, grad_ref, note_ref, flat, b1, b2, b3, sems, *rest):
    b = lax.axis_index("batch")
    barrier, count = greet_all(chips, depths)
    pairs = ((r1, b1), (r2, b2), (r3, b3))
    fetches = [pltpu.make_async_copy(src, dst, sems.at[n]) for n, (src, dst) in enumerate(pairs)]
    for copy in fetches:
        copy.start()
    pl.semaphore_wait(barrier, count)
    stages = reducer(own_ref, chips, depths, rest)
    stages[0]()
    for copy in fetches:
        copy.wait()
    assemble(flat, (None, b1, b2, b3))
    for stage in stages[1:]:
        stage()
    r0 = rest[0]
    assemble(flat, (r0, None, None, None))
    note_ref[...] = jnp.zeros_like(note_ref)
    squares = jnp.sum(jnp.sum(flat[...] * flat[...], 0, keepdims=True), 1, keepdims=True)
    lane = lax.broadcasted_iota(jnp.int32, (1, 128), 1)
    note_ref[0:1] = jnp.where(lane == 2, squares, r0[0, OWN_EXTRA + 1:OWN_EXTRA + 2])
    rows = grad_ref.shape[0]
    row_at, lane_at = lax.div(b * entries, 128), lax.rem(b * entries, 128)
    gradient = flat[pl.ds(row_at, rows), :]
    if entries % 128:
        lane = lax.broadcasted_iota(jnp.int32, (rows, 128), 1)
        turn = lax.rem(128 - lane_at, 128)
        gradient = jnp.where(
            lane < 128 - lane_at, pltpu.roll(gradient, turn, 1), pltpu.roll(flat[pl.ds(row_at + 1, rows), :], turn, 1)
        )
    grad_ref[...] = gradient


def update_kernel(grad_ref, note_ref, p_ref, m_ref, v_ref, new_ref, half_ref, first_ref, second_ref, norm_ref, loss_ref):
    rows = grad_ref.shape[0]
    note = note_ref[0:1]
    lane = lax.broadcasted_iota(jnp.int32, (1, 128), 1)
    count = jnp.sum(jnp.where(lane == 1, note, 0.0), 1, keepdims=True)
    norm = jnp.sqrt(jnp.sum(jnp.where(lane == 2, note, 0.0), 1, keepdims=True)) / count
    norm_ref[0] = norm[0, 0]
    loss_ref[0] = note[0, 0]
    loss_ref[1] = note[0, 1]
    clipped = grad_ref[...] / count * (CLIP_AT / jnp.maximum(norm, CLIP_AT))
    new_first = BETA_ONE * m_ref[...].reshape(rows, 128) + (1.0 - BETA_ONE) * clipped
    new_second = BETA_TWO * v_ref[...].reshape(rows, 128) + (1.0 - BETA_TWO) * clipped * clipped
    step_size = (
        new_first / (1.0 - BETA_ONE**STEP) / (jnp.sqrt(new_second / (1.0 - BETA_TWO**STEP)) + ADAM_EPS)
    )
    params = p_ref[...].reshape(rows, 128)
    new_params = params - LEARN_RATE * (step_size + DECAY_RATE * params)
    new_ref[...] = new_params.reshape(new_ref.shape)
    half_ref[...] = new_params.astype(BF16).reshape(half_ref.shape)
    first_ref[...] = new_first.reshape(first_ref.shape)
    second_ref[...] = new_second.reshape(second_ref.shape)


def start_kernel(chips, depths, items, groups, gathers, p_ref, mail_ref, *refs):
    *views, refs = *refs[:5], refs[5:]
    if gathers:
        *refs, flat_ref = refs
    else:
        flat_ref = p_ref
    *refs, view_sem = refs
    (stream_ref, column_ref, active_ref, encoder_ref, note_ref,
     inbox, planes, plane_sem, pair_sem, top_sem, own_sem, mail_sem) = refs
    b = lax.axis_index("batch")
    z = lax.axis_index("frames")
    core = lax.rem(b, 2)
    chip = lax.div(b, 2)
    sibling = (b + 1 - 2 * core, z)
    entries = p_ref.shape[0]
    copies = depths // (2 * items)
    share = groups // depths
    valid = HOP * groups
    mail_rows = mail_ref.shape[0] // items
    mesh = pl.DeviceIdType.MESH

    barrier = pltpu.get_barrier_semaphore()
    for step in range(1, chips):
        pl.semaphore_signal(barrier, inc=1, device_id=(lax.rem(b + 2 * step, 2 * chips), z), device_id_type=mesh)
    for step in range(1, depths):
        pl.semaphore_signal(barrier, inc=1, device_id=(b, lax.rem(z + step, depths)), device_id_type=mesh)
    for step in range(depths):
        pl.semaphore_signal(barrier, inc=1, device_id=(sibling[0], lax.rem(z + step, depths)), device_id_type=mesh)
    pl.semaphore_wait(barrier, chips - 1 + 2 * depths - 1)

    def shard(at):
        return flat_ref.at[pl.ds(pl.multiple_of(at * entries, 128), entries)]

    def send(src, dst, sems, slot, device):
        return pltpu.make_async_remote_copy(
            src_ref=src, dst_ref=dst, send_sem=sems.at[0, slot], recv_sem=sems.at[1, slot],
            device_id=device, device_id_type=mesh,
        )

    def tail_of(at):
        return flat_ref.at[pl.ds(pl.multiple_of((at + 1) * entries - 128 * SHARE_ROWS, 128), 128 * SHARE_ROWS)]

    def forward_to_sibling(at, slot):
        for src, sems in ((tail_of(at), pair_sem), (flat_ref.at[pl.ds(pl.multiple_of(at * entries, 128), 128)], top_sem)):
            copy = send(src, src, sems, slot, sibling)
            copy.start()
            beside.append(copy)

    beside = []
    if gathers:
        by_x = b + 2 - 4 * lax.rem(chip, 2)
        by_y = b + 4 - 8 * lax.div(chip, 2)
        beyond = by_x + by_y - b
        half_rows = entries // 256

        def piece(ref, at, second):
            first_row, count = (half_rows, entries // 128 - half_rows) if second else (0, half_rows)
            return ref.at[pl.ds(pl.multiple_of(at * entries + 128 * first_row, 128), 128 * count)]

        across = [
            send(piece(p_ref, 0, second), piece(flat_ref, b, second), plane_sem, slot, (to, z))
            for slot, (second, to) in enumerate(((0, by_x), (1, by_y), (1, by_x), (0, by_y)))
        ]
        for copy in across:
            copy.start()
        own = pltpu.make_async_copy(p_ref, shard(b), own_sem)
        own.start()
        own.wait()
        forward_to_sibling(b, 0)
    letters = []
    for item in range(items):
        for other in range(2):
            for copy_no in range(copies):
                depth = (items * core + item) * copies + copy_no
                here = (core == other) & (z == depth)
                src = mail_ref.at[pl.ds(item * mail_rows, mail_rows)]
                far = pltpu.make_async_remote_copy(
                    src_ref=src, dst_ref=inbox.at[z], send_sem=mail_sem.at[1, len(letters)], recv_sem=mail_sem.at[0, z],
                    device_id=(2 * chip + other, depth), device_id_type=mesh,
                )
                near = pltpu.make_async_copy(src, inbox.at[z], mail_sem.at[0, z])

                @pl.when(here)
                def _():
                    near.start()

                @pl.when(jnp.logical_not(here))
                def _():
                    far.start()

                letters.append((here, far))
    for depth in range(depths):
        pltpu.make_async_copy(inbox.at[depth], inbox.at[depth], mail_sem.at[0, depth]).wait()
    for here, far in letters:
        @pl.when(jnp.logical_not(here))
        def _():
            far.wait_send()

    frames = jnp.concatenate([inbox[depth, :share] for depth in range(depths)], 0)
    facts = inbox[0, share:share + 1]
    speakers, length = facts[:, 0:1], facts[:, 1:2]
    whole_item = jnp.where(lax.rem(z, copies) == 0, 1.0, 0.0)
    lead = jnp.where(core == 0, whole_item, 0.0)
    lane = lax.broadcasted_iota(jnp.int32, (groups, 128), 1)
    group = lax.broadcasted_iota(jnp.int32, (groups, 128), 0)
    note_ref[...] = jnp.where(lane[:8] == 1, lead * length, 0.0)
    wide = SOURCES * FILTERS
    source = lax.broadcasted_iota(jnp.int32, (8, wide), 1) // FILTERS
    fact_at = lax.broadcasted_iota(jnp.int32, (8, wide), 0)
    active = jnp.where(source.astype(F32) < speakers, 1.0, 0.0)
    active = jnp.where(fact_at == 1, speakers, jnp.where(fact_at == 2, length, active))
    active_ref[...] = jnp.where(fact_at == 3, whole_item, active)
    end = HOP * FRAME_LANES
    tile = end // 128 * 128
    opening = jnp.where(group == groups - 1, 0.0, pltpu.roll(frames[:, :128], groups - 1, 0))
    ending = (lane >= end - tile) & (lane < end - tile + FRAME_LANES)
    planes[:, :tile] = frames[:, :tile]
    planes[:, tile:tile + 128] = jnp.where(ending, pltpu.roll(opening, end - tile, 1), frames[:, tile:tile + 128])
    planes[:, tile + 128:] = jnp.zeros((groups, planes.shape[1] - tile - 128), F32)
    for k in range(HOP):
        column_ref[k * groups:(k + 1) * groups] = planes[:, FRAME_LANES * k:FRAME_LANES * k + 128]

    if gathers:
        across[0].wait_recv()
        across.append(send(piece(flat_ref, by_x, 0), piece(flat_ref, by_x, 0), plane_sem, 4, (by_y, z)))
        across[4].start()
        across[1].wait_recv()
        across.append(send(piece(flat_ref, by_y, 1), piece(flat_ref, by_y, 1), plane_sem, 5, (by_x, z)))
        across[5].start()
        across[2].wait_recv()
        forward_to_sibling(by_x, 1)
        across[3].wait_recv()
        forward_to_sibling(by_y, 2)
        across[4].wait_recv()
        across[5].wait_recv()
        forward_to_sibling(beyond, 3)
        for copy in across:
            copy.wait_send()
        for copy in beside:
            copy.wait()

    bounds = [(window(n)[0], WINDOW) for n in range(2 * BLOCKS)] + [(TAIL_ROW, TAIL_ROWS)]
    stores = [
        pltpu.make_async_copy(flat_ref.at[pl.ds(128 * at, 128 * count)], view, view_sem.at[n])
        for n, ((at, count), view) in enumerate(zip(bounds, views))
    ]
    for store in stores:
        store.start()
    taps = flat_ref[0:128].reshape(1, 128)
    at_lane = lax.broadcasted_iota(jnp.int32, (128, 128), 1)
    at_row = lax.broadcasted_iota(jnp.int32, (128, 128), 0)
    upright = jnp.sum(jnp.where(at_lane == at_row, taps, 0.0), 1, keepdims=True)
    twice = 2 * lax.rem(at_lane, FILTERS)
    tap_rows = [jnp.sum(jnp.where(at_row == twice + tap, upright, 0.0), 0, keepdims=True) for tap in range(2)]
    encoder_ref[...] = jnp.where(at_row[:8] == 0, tap_rows[0], jnp.where(at_row[:8] == 1, tap_rows[1], 0.0))

    block = 5 * groups
    block_lane = lax.broadcasted_iota(jnp.int32, (block, 128), 1)
    last_group = lax.broadcasted_iota(jnp.int32, (block, 128), 0) % groups == groups - 1

    def encode(n, carry):
        rows = pl.ds(pl.multiple_of(n * block, 8), block)
        column = column_ref[rows, :]
        raw = column[:, MIX_LANE:MIX_LANE + 1] * tap_rows[0] + column[:, NEXT_LANE:NEXT_LANE + 1] * tap_rows[1]
        encoded = jnp.maximum(raw, 0.0) + jnp.log1p(jnp.exp(-jnp.abs(raw)))
        later = jnp.where(last_group, 0.0, pltpu.roll(encoded, block - 1, 0))
        stream_ref[rows, :] = jnp.where(block_lane < FILTERS, encoded, later)
        return carry

    lax.fori_loop(0, HOP // 5, encode, 0)
    stream_ref[valid:] = jnp.zeros((stream_ref.shape[0] - valid, 128), F32)
    for store in stores:
        store.wait()


def per_turn(inter):
    return 2 if inter else 4


def sizes(inter, groups):
    if inter:
        return groups, 2 * HALF_PAD, 4
    return 2 * HOP, groups, 5


def whole(shape):
    return pl.BlockSpec(shape, lambda j: (0,) * len(shape))


def run_start(params, mixture, sources, speakers, lengths):
    items, samples_here = mixture.shape
    depths = lax.axis_size("frames")
    chips = lax.axis_size("batch") // 2
    groups = samples_here * depths // HOP
    share = groups // depths
    valid = HOP * groups
    copies = depths // (2 * items)
    signals = jnp.concatenate([sources, mixture[:, None]], 1).transpose(0, 2, 1)
    signals = jnp.pad(signals, ((0, 0), (0, 0), (0, FRAME_LANES - 1 - SOURCES)))
    signals = signals.reshape(items, share, HOP * FRAME_LANES)
    width = -(-HOP * FRAME_LANES // 128) * 128
    facts = jnp.stack([speakers, lengths], 1).astype(F32)[:, None]
    mail_rows = -(-(share + 1) // 8) * 8
    mail = jnp.concatenate(
        [
            jnp.pad(signals, ((0, 0), (0, 0), (0, width - HOP * FRAME_LANES))),
            jnp.pad(facts, ((0, 0), (0, mail_rows - share - 1), (0, width - 2))),
        ],
        1,
    ).reshape(items * mail_rows, width)
    stream_shape = (HALF_PAD * groups, 128)
    out = [stream_shape, (valid, 128), (8, SOURCES * FILTERS), (8, 128), (8, 128)]
    out = [(WINDOW * 128,)] * (2 * BLOCKS) + [(TAIL_ROWS * 128,)] + out
    gathers = params.shape[0] % 128 == 0 and chips == 4
    whole_flat = [pltpu.VMEM((params.shape[0] * 2 * chips,), F32)] if gathers else []
    if not gathers:
        params = lax.all_gather(params, "batch", axis=0, tiled=True)
    vmem = pl.BlockSpec(memory_space=pltpu.VMEM)
    sems = pltpu.SemaphoreType.DMA
    found = pl.pallas_call(
        functools.partial(start_kernel, chips, depths, items, groups, gathers),
        in_specs=[vmem] * 2,
        out_specs=[pl.BlockSpec(memory_space=pl.ANY)] * 5 + [vmem] * 5,
        out_shape=[jax.ShapeDtypeStruct(shape, F32) for shape in out],
        scratch_shapes=[
            pltpu.VMEM((depths, mail_rows, width), F32), pltpu.VMEM((groups, width + 128), F32),
            sems((2, 6)), sems((2, chips)), sems((2, chips)), sems, sems((2, max(depths, 2 * items * copies))), sems((5,)),
        ]
        + whole_flat,
        compiler_params=pltpu.CompilerParams(
            vmem_limit_bytes=VMEM_MAX, collective_id=10, has_side_effects=True
        ),
        name="start",
    )(params, mail)
    return [a.reshape(-1, 128) for a in found[:5]], found[5:]


def run_forward(layer_no, groups, stream, flat):
    inter = layer_no % 2 == 1
    length, rows, steps = sizes(inter, groups)
    turn = per_turn(inter)
    stream_shape = (HALF_PAD * groups, 128)
    out = [
        (stream_shape, whole(stream_shape)),
        (stream_shape, whole(stream_shape)),
        ((8, 128), whole((8, 128))),
        ((length, rows, UNITS), pl.BlockSpec((turn * steps, rows, UNITS), lambda j: (j, 0, 0))),
        ((length, 6, rows, UNITS), pl.BlockSpec((turn * steps, 6, rows, UNITS), lambda j: (j, 0, 0, 0))),
    ]
    return pl.pallas_call(
        functools.partial(forward_kernel, layer_no, groups, steps),
        grid=(length // (turn * steps),),
        in_specs=[whole(stream_shape), whole((WINDOW, 128))],
        out_specs=[spec for _, spec in out],
        out_shape=[jax.ShapeDtypeStruct(shape, F32) for shape, _ in out],
        scratch_shapes=[
            pltpu.VMEM((256, GATES), BF16),
            pltpu.VMEM((256, GATES), BF16), pltpu.VMEM((128, GATES), BF16),
            pltpu.VMEM((UNITS, 128), BF16),
            pltpu.VMEM((UNITS, 128), F32),
            pltpu.VMEM((8, GATES), F32),
            pltpu.VMEM((steps * rows, GATES), F32), pltpu.VMEM((steps * rows, GATES), F32),
            pltpu.VMEM((steps * rows, UNITS), F32), pltpu.VMEM((steps * rows, UNITS), F32),
            pltpu.VMEM((rows, UNITS), F32),
            pltpu.VMEM(stream_shape, F32), pltpu.VMEM(stream_shape, F32), pltpu.SemaphoreType.DMA((2,)),
        ],
        compiler_params=pltpu.CompilerParams(
            vmem_limit_bytes=VMEM_MAX, collective_id=2 + layer_no, has_side_effects=True
        ),
        name="forward_inter" if inter else "forward_intra",
    )(stream, flat)


def run_backward(layer_no, groups, grad, kept, flat, extra):
    inter = layer_no % 2 == 1
    last_layer = layer_no == 2 * BLOCKS - 1
    length, rows, steps = sizes(inter, groups)
    stream_shape = (HALF_PAD * groups, 128)
    count = length // (2 * steps)
    depths = lax.axis_size("frames")
    chips = lax.axis_size("batch") // 2
    out = [(reduced_rows(OWN_ROWS[layer_no], chips, depths), 128)]
    scratch = []
    if not last_layer:
        upper_rows = reduced_rows(OWN_ROWS[layer_no + 1], chips, depths)
        out = [(2, upper_rows, 128)] + out
        scratch = reducer_scratch(upper_rows, chips, depths)
    if layer_no:
        out = [stream_shape] + out
    x, normed, scale, h_all, coef = kept
    return pl.pallas_call(
        functools.partial(backward_kernel, layer_no, groups, steps, chips, depths),
        grid=(count,),
        in_specs=[whole(a.shape) for a in (grad, normed, scale)]
        + [pl.BlockSpec(memory_space=pl.ANY)] * 2
        + [pl.BlockSpec((2 * steps, 6, rows, UNITS), lambda j: (count - 1 - j, 0, 0, 0)), whole((WINDOW, 128))]
        + [whole(a.shape) for a in extra],
        out_specs=[whole(shape) for shape in out],
        out_shape=[jax.ShapeDtypeStruct(shape, F32) for shape in out],
        scratch_shapes=[
            pltpu.VMEM((GATES, 128), BF16),
            pltpu.VMEM((GATES, 256), BF16), pltpu.VMEM((GATES, 128), BF16),
            pltpu.VMEM((256, UNITS), BF16),
            pltpu.VMEM((UNITS, 128), F32),
            pltpu.VMEM(stream_shape, F32),
            pltpu.VMEM((steps * rows, UNITS), F32), pltpu.VMEM((steps * rows, UNITS), F32),
            pltpu.VMEM((steps * rows, GATES), F32), pltpu.VMEM((steps * rows, GATES), F32),
            pltpu.VMEM((rows, UNITS), F32),
            pltpu.VMEM((UNITS + FILTERS, GATES), F32), pltpu.VMEM((2 * UNITS if inter else UNITS, 128), F32),
            pltpu.VMEM((8, GATES), F32),
            pltpu.VMEM(stream_shape, F32), pltpu.VMEM(stream_shape, F32), pltpu.SemaphoreType.DMA((2,)),
            pltpu.VMEM(x.shape, F32), pltpu.VMEM(h_all.shape, F32), pltpu.SemaphoreType.DMA((2,)),
        ]
        + scratch,
        compiler_params=pltpu.CompilerParams(vmem_limit_bytes=VMEM_MAX, collective_id=6 + layer_no, has_side_effects=True),
        name="backward_inter" if inter else "backward_intra",
    )(grad, normed, scale, x, h_all, coef, flat, *extra)


def run_head(groups, separated, stream, column, active, note, tail):
    valid = HOP * groups
    stream_shape = (HALF_PAD * groups, 128)
    out = [stream_shape, (HEAD_ROWS, 128), (valid, FILTERS), (8, 128)]
    wide = SOURCES * FILTERS
    operands = (separated, stream, column, active, note, tail)
    return pl.pallas_call(
        functools.partial(head_kernel, groups),
        grid=(1,),
        in_specs=[whole(a.shape) for a in operands],
        out_specs=[whole(shape) for shape in out],
        out_shape=[jax.ShapeDtypeStruct(shape, F32) for shape in out],
        scratch_shapes=[
            pltpu.VMEM((valid, wide), F32), pltpu.VMEM((valid, 128), F32),
            pltpu.VMEM((valid + groups, 128), F32), pltpu.VMEM((valid + groups, 128), F32),
            pltpu.VMEM((2 * FILTERS, wide), BF16), pltpu.VMEM((FILTERS, wide), BF16),
            pltpu.VMEM((2 * wide, FILTERS), BF16), pltpu.VMEM((wide, FILTERS), BF16),
            pltpu.VMEM((2 * wide, 256), BF16), pltpu.VMEM((wide, 256), BF16),
            pltpu.VMEM((512, wide), BF16), pltpu.VMEM((256, wide), BF16),
            pltpu.VMEM((FILTERS, wide), F32), pltpu.VMEM((wide, 256), F32),
            pltpu.VMEM((FILTERS, 128), F32), pltpu.VMEM((FILTERS, 128), F32),
        ],
        compiler_params=pltpu.CompilerParams(vmem_limit_bytes=VMEM_MAX),
        name="head",
    )(*operands)


def run_finish(layers, params, first_moment, second_moment):
    entries = params.shape[0]
    rows = -(-entries // 128)
    depths = lax.axis_size("frames")
    chips = lax.axis_size("batch") // 2
    vmem = pl.BlockSpec(memory_space=pltpu.VMEM)
    gradient, note = pl.pallas_call(
        functools.partial(finish_kernel, chips, depths, entries),
        in_specs=[vmem] + [pl.BlockSpec(memory_space=pl.ANY)] * 3,
        out_specs=[vmem] * 2,
        out_shape=[jax.ShapeDtypeStruct(shape, F32) for shape in ((rows, 128), (8, 128))],
        scratch_shapes=[pltpu.VMEM((6808, 128), F32)]
        + [pltpu.VMEM(a.shape, F32) for a in layers[1:]]
        + [pltpu.SemaphoreType.DMA((3,))]
        + reducer_scratch(layers[0].shape[0], chips, depths),
        compiler_params=pltpu.CompilerParams(
            vmem_limit_bytes=VMEM_MAX, collective_id=1, has_side_effects=True
        ),
        name="finish",
    )(*layers)
    shards = [params, first_moment, second_moment]
    shape = (entries,)
    if entries % 128:
        shape = (rows, 128)
        shards = [jnp.pad(a, (0, rows * 128 - entries)).reshape(shape) for a in shards]
    smem = pl.BlockSpec(memory_space=pltpu.SMEM)
    out = [(shape, F32), (shape, BF16), (shape, F32), (shape, F32), ((1,), F32), ((2,), F32)]
    found = pl.pallas_call(
        update_kernel,
        in_specs=[vmem] * 5,
        out_specs=[vmem] * 4 + [smem] * 2,
        out_shape=[jax.ShapeDtypeStruct(shape, dtype) for shape, dtype in out],
        compiler_params=pltpu.CompilerParams(vmem_limit_bytes=VMEM_MAX),
        name="update",
    )(gradient, note, *shards)
    return [a.reshape(-1)[:entries] for a in found[:4]] + [found[4][0], found[5]]


def local(params, first_moment, second_moment, mixture, sources, speakers, lengths):
    groups = mixture.shape[1] * lax.axis_size("frames") // HOP
    views, (stream, column, active, encoder, note) = run_start(params, mixture, sources, speakers, lengths)
    kept = []
    x = stream
    for layer_no in range(2 * BLOCKS):
        after, normed, scale, h_all, coef = run_forward(layer_no, groups, x, views[layer_no])
        kept.append((x, normed, scale, h_all, coef))
        x = after
    grad, head_grads, grad_encoded, loss = run_head(groups, x, stream, column, active, note, views[2 * BLOCKS])
    sums = [None] * (2 * BLOCKS)
    for layer_no in reversed(range(2 * BLOCKS)):
        extra = ()
        if layer_no == 2 * BLOCKS - 1:
            extra = (head_grads,)
        if layer_no == 0:
            extra = (column, grad_encoded, encoder, loss)
        if layer_no < 2 * BLOCKS - 1:
            extra = extra + (sums[layer_no + 1],)
        *found, sums[layer_no] = run_backward(layer_no, groups, grad, kept[layer_no], views[layer_no], extra)
        if layer_no < 2 * BLOCKS - 1:
            sums[layer_no + 1] = found[-1]
        if layer_no:
            grad = found[0]
    return tuple(run_finish(sums, params, first_moment, second_moment))


def solution(mesh):
    placed = (
        P("batch"),
        P("batch"),
        P("batch"),
        P("batch", "frames"),
        P("batch", None, "frames"),
        P("batch"),
        P("batch"),
    )
    return jax.shard_map(
        local,
        mesh=mesh,
        in_specs=placed,
        out_specs=(P("batch"), P("batch"), P("batch"), P("batch"), P(), P()),
        check_vma=False,
    )
```

```python
import functools
import math

import jax
import jax.numpy as jnp
from jax import lax
from jax.experimental import pallas as pl
from jax.experimental.pallas import tpu as pltpu
from jax.sharding import PartitionSpec as P

FILTERS = 64
UNITS = 128
HOP = 50
HALF_PAD = 56
SOURCES = 3
BLOCKS = 2
STEP = 5
GATES = 4 * UNITS

HIGHEST = lax.Precision.HIGHEST
NORM_EPS = 1e-08
CLIP_AT = 0.001
BETA_ONE = 0.5
BETA_TWO = 0.5
LEARN_RATE = 0.05
DECAY_RATE = 0.01
ADAM_EPS = 1e-08
F32 = jnp.float32
BF16 = jnp.bfloat16
VMEM_MAX = 60 * 2**20


def split(a):
    hi = a.astype(BF16)
    return hi, (a - hi.astype(F32)).astype(BF16)


def dot(a, b):
    return jnp.dot(a, b, preferred_element_type=F32)


def dot3(a, w_twice, w_low):
    hi, lo = split(a)
    return dot(jnp.concatenate([hi, lo], 1), w_twice) + dot(hi, w_low)


def dot_rows(a, b):
    return lax.dot_general(a, b, (((0,), (0,)), ((), ())), preferred_element_type=F32)


def dot_rows3(a, b):
    a_hi, a_lo = split(a)
    b_hi, b_lo = split(b)
    return dot_rows(a_hi, b_hi) + dot_rows(a_lo, b_hi) + dot_rows(a_hi, b_lo)


SIDE_ROWS = 772
PROJ_ROWS = 2 * SIDE_ROWS
VEC_ROW = PROJ_ROWS + 128
LAYER_ROWS = 1680
HEAD_ROWS = 160
OWN_PROJ = SIDE_ROWS
OWN_VEC = SIDE_ROWS + 64
OWN_EXTRA = SIDE_ROWS + 68
OWN_ROWS = (OWN_EXTRA + 8, OWN_EXTRA, OWN_EXTRA, OWN_EXTRA + HEAD_ROWS)
WINDOW = 1688
TAIL_ROW = 6688
TAIL_ROWS = 104
SHARE_ROWS = 256
FRAME_LANES = 8
MIX_LANE = SOURCES
NEXT_LANE = FRAME_LANES + MIX_LANE


def window(layer_no):
    at = 2 + 3347 * layer_no
    return at // 16 * 8, at // 2 % 8, at % 2


def pick(ref, base, odd, start, count, stride=1):
    def load(at):
        return ref[pl.ds(at, count, stride=stride), :] if stride > 1 else ref[pl.ds(at, count), :]

    first = load(base + start)
    if not odd:
        return first
    return jnp.concatenate([first[:, 64:], load(base + start + 1)[:, :64]], 1)


def load_weights(ref, base, odd, dir_no, proj_s):
    at = SIDE_ROWS * dir_no
    win = jnp.concatenate([pick(ref, base, odd, at + q, FILTERS, 4) for q in range(4)], 1)
    wrec = jnp.concatenate([pick(ref, base, odd, at + 256 + q, UNITS, 4) for q in range(4)], 1)
    bias = jnp.concatenate([pick(ref, base, odd, at + 768 + q, 1) for q in range(4)], 1)
    pairs = pick(ref, base, odd, PROJ_ROWS + 64 * dir_no, 64)
    proj_s[pl.ds(0, 64, stride=2), :] = pairs
    proj_s[pl.ds(1, 64, stride=2), :] = pltpu.roll(pairs, 64, 1)
    return win, wrec, bias, proj_s[:, :FILTERS]


def load_vec(ref, base, odd):
    first = pick(ref, base, odd, VEC_ROW, 1)
    turned = pltpu.roll(jnp.broadcast_to(first, (8, 128)), 64, 1)[0:1]
    if odd:
        last = ref[base + VEC_ROW + 1:base + VEC_ROW + 2, :]
        last = jnp.concatenate([last[:, 64:], last[:, 64:]], 1)
    else:
        last = ref[base + VEC_ROW + 1:base + VEC_ROW + 2, :]
        last = jnp.concatenate([last[:, :64], last[:, :64]], 1)
    low = lax.broadcasted_iota(jnp.int32, (1, 128), 1) < 64
    return jnp.where(low, first, turned), jnp.where(low, turned, first), last


def share_of(tasks, number, count):
    return tasks[number * len(tasks) // count:(number + 1) * len(tasks) // count]


def fold_halves(a):
    return a + pltpu.roll(a, FILTERS, 1)


def narrow(a, half):
    if isinstance(half, int):
        a = pltpu.roll(a, FILTERS, 1) if half else a
    else:
        a = jnp.where(half == 0, a, pltpu.roll(a, FILTERS, 1))
    low_lanes = lax.broadcasted_iota(jnp.int32, a.shape, 1) < FILTERS
    hi = a.astype(BF16).astype(F32)
    lo = pltpu.roll(a - hi, FILTERS, 1)
    return jnp.concatenate([jnp.where(low_lanes, hi, lo), jnp.where(low_lanes, hi, 0.0)], 1).astype(BF16)


def narrow_weights(w):
    hi, lo = split(w)
    return jnp.concatenate([hi, hi, lo, jnp.zeros_like(hi)], 0)


def side_weights(w):
    hi, lo = split(w)
    return jnp.concatenate([hi, lo], 1)


def dot_sides(a, w):
    hi, lo = split(a)
    return fold_halves(dot(hi, w) + dot(lo, w))


def put_split(w, twice_ref, low_ref):
    hi, lo = split(w)
    twice_ref[...] = jnp.concatenate([hi, hi], 0)
    low_ref[...] = lo


def times(dir_no, chunk_no, length, steps):
    return [dir_no * (length - 1) + (1 - 2 * dir_no) * (chunk_no * steps + u) for u in range(steps)]


def stream_rows(inter, groups, at):
    if inter:
        return pl.ds(at, HALF_PAD, stride=groups)
    return pl.ds(pl.multiple_of(lax.rem(at, HOP) * groups, 8), groups)


def gather(ref, inter, groups, positions):
    return jnp.concatenate([ref[stream_rows(inter, groups, at), :] for at in positions], 0)


def to_sides(inter, steps, array):
    if not inter:
        return [array]
    three = array.reshape(steps, 2 * HALF_PAD, array.shape[-1])
    return [
        three[:, side * HALF_PAD:(side + 1) * HALF_PAD].reshape(steps * HALF_PAD, array.shape[-1]) for side in range(2)
    ]


SIDE_ROWS = 772
PROJ_ROWS = 2 * SIDE_ROWS
VEC_ROW = PROJ_ROWS + 128
LAYER_ROWS = 1680
HEAD_ROWS = 160
OWN_PROJ = SIDE_ROWS
OWN_VEC = SIDE_ROWS + 64
OWN_EXTRA = SIDE_ROWS + 68
OWN_ROWS = (OWN_EXTRA + 8, OWN_EXTRA, OWN_EXTRA, OWN_EXTRA + HEAD_ROWS)
WINDOW = 1688
TAIL_ROW = 6688
TAIL_ROWS = 104
SHARE_ROWS = 256
FRAME_LANES = 8
MIX_LANE = SOURCES
NEXT_LANE = FRAME_LANES + MIX_LANE


def window(layer_no):
    at = 2 + 3347 * layer_no
    return at // 16 * 8, at // 2 % 8, at % 2


def pick(ref, base, odd, start, count, stride=1):
    def load(at):
        return ref[pl.ds(at, count, stride=stride), :] if stride > 1 else ref[pl.ds(at, count), :]

    first = load(base + start)
    if not odd:
        return first
    return jnp.concatenate([first[:, 64:], load(base + start + 1)[:, :64]], 1)


def load_weights(ref, base, odd, dir_no, proj_s):
    at = SIDE_ROWS * dir_no
    win = jnp.concatenate([pick(ref, base, odd, at + q, FILTERS, 4) for q in range(4)], 1)
    wrec = jnp.concatenate([pick(ref, base, odd, at + 256 + q, UNITS, 4) for q in range(4)], 1)
    bias = jnp.concatenate([pick(ref, base, odd, at + 768 + q, 1) for q in range(4)], 1)
    pairs = pick(ref, base, odd, PROJ_ROWS + 64 * dir_no, 64)
    proj_s[pl.ds(0, 64, stride=2), :] = pairs
    proj_s[pl.ds(1, 64, stride=2), :] = pltpu.roll(pairs, 64, 1)
    return win, wrec, bias, proj_s[:, :FILTERS]


def load_vec(ref, base, odd):
    first = pick(ref, base, odd, VEC_ROW, 1)
    turned = pltpu.roll(jnp.broadcast_to(first, (8, 128)), 64, 1)[0:1]
    if odd:
        last = ref[base + VEC_ROW + 1:base + VEC_ROW + 2, :]
        last = jnp.concatenate([last[:, 64:], last[:, 64:]], 1)
    else:
        last = ref[base + VEC_ROW + 1:base + VEC_ROW + 2, :]
        last = jnp.concatenate([last[:, :64], last[:, :64]], 1)
    low = lax.broadcasted_iota(jnp.int32, (1, 128), 1) < 64
    return jnp.where(low, first, turned), jnp.where(low, turned, first), last


def put_split(w, twice_ref, low_ref):
    hi, lo = split(w)
    twice_ref[...] = jnp.concatenate([hi, hi], 0)
    low_ref[...] = lo


def place(dir_no, chunk_no, count, steps, inter, groups):
    first = jnp.where(dir_no == 0, chunk_no * steps, (count - 1 - chunk_no) * steps)
    if inter:
        return first, 0, 0
    half = first // HOP
    return first, half, pl.multiple_of((first - HOP * half) * groups, 8)


def norm_stage(prev_ref, pa_ref, pb_ref, flat_ref, base, odd, valid, normed_ref, scale_ref, x_ref):
    offset, gain, shift = load_vec(flat_ref, base, odd)
    mixed = pa_ref[:valid] + pb_ref[:valid] + offset
    total = 2.0 * valid * FILTERS
    mean = jnp.sum(mixed) / total
    spread = jnp.sum(mixed * mixed) / total - mean * mean
    scale = lax.rsqrt(jnp.full((1, 128), spread + NORM_EPS, F32))
    normed = (mixed - mean) * scale
    normed_ref[:valid] = normed
    normed_ref[valid:] = jnp.zeros((normed_ref.shape[0] - valid, 128), F32)
    x_ref[:valid] = prev_ref[:valid] + gain * normed + shift
    x_ref[valid:] = jnp.zeros((x_ref.shape[0] - valid, 128), F32)
    scale_ref[...] = jnp.broadcast_to(scale, scale_ref.shape)


def greet_sibling():
    b = lax.axis_index("batch")
    device = (b + 1 - 2 * lax.rem(b, 2), lax.axis_index("frames"))
    return device, pltpu.get_barrier_semaphore()


def swap_with_sibling(src_ref, dst_ref, sems, greeted=False):
    device, barrier = greet_sibling()
    if not greeted:
        pl.semaphore_wait(barrier, 1)
    copy = pltpu.make_async_remote_copy(
        src_ref=src_ref, dst_ref=dst_ref, send_sem=sems.at[0], recv_sem=sems.at[1],
        device_id=device, device_id_type=pl.DeviceIdType.MESH,
    )
    copy.start()
    return copy


def reduced_rows(rows, chips, depths):
    return -(-rows // (8 * chips * depths)) * 8 * chips * depths


def reducer_scratch(rows, chips, depths):
    quarter = rows // chips
    part = quarter // depths
    sems = pltpu.SemaphoreType.DMA
    return [
        pltpu.VMEM((2, rows, 128), F32), pltpu.VMEM((chips - 1, quarter, 128), F32), pltpu.VMEM((quarter, 128), F32),
        pltpu.VMEM((depths - 1, part, 128), F32), pltpu.VMEM((part, 128), F32), pltpu.VMEM((quarter, 128), F32),
        sems((2, chips - 1)), sems((2, depths - 1)), sems((2, depths - 1)), sems((2, chips - 1)), sems((2, 1)),
    ]


def greet_all(chips, depths):
    b = lax.axis_index("batch")
    z = lax.axis_index("frames")
    barrier = pltpu.get_barrier_semaphore()
    devices = [(b + 1 - 2 * lax.rem(b, 2), z)]
    devices += [(lax.rem(b + 2 * step, 2 * chips), z) for step in range(1, chips)]
    devices += [(b, lax.rem(z + step, depths)) for step in range(1, depths)]
    for device in devices:
        pl.semaphore_signal(barrier, inc=1, device_id=device, device_id_type=pl.DeviceIdType.MESH)
    return barrier, len(devices)


def reducer(src, chips, depths, refs):
    red, plane_in, mine, depth_in, piece, joined, s_plane, s_depth, s_spread, s_gather, s_back = refs
    b = lax.axis_index("batch")
    z = lax.axis_index("frames")
    core = lax.rem(b, 2)
    chip = lax.div(b, 2)
    quarter = mine.shape[0]
    part = piece.shape[0]

    def rows(at, count):
        return pl.ds(pl.multiple_of(at, 8), count)

    def send(src_ref, dst_ref, sems, slot, device):
        return pltpu.make_async_remote_copy(
            src_ref=src_ref, dst_ref=dst_ref, send_sem=sems.at[0, slot], recv_sem=sems.at[1, slot],
            device_id=device, device_id_type=pl.DeviceIdType.MESH,
        )

    over_plane = [(step, (lax.rem(b + 2 * step, 2 * chips), z)) for step in range(1, chips)]
    over_depth = [(step, (b, lax.rem(z + step, depths))) for step in range(1, depths)]
    own = rows(chip * quarter, quarter)
    mine_at = rows(z * part, part)

    def plane():
        return [
            send(src.at[rows(lax.rem(chip + step, chips) * quarter, quarter)], plane_in.at[step - 1], s_plane, step - 1, to)
            for step, to in over_plane
        ]

    def scatter():
        return [
            send(mine.at[rows(lax.rem(z + step, depths) * part, part)], depth_in.at[step - 1], s_depth, step - 1, to)
            for step, to in over_depth
        ]

    def spread():
        return [send(piece, joined.at[mine_at], s_spread, step - 1, to) for step, to in over_depth]

    def gather():
        return [send(joined, red.at[core, own], s_gather, step - 1, to) for step, to in over_plane]

    def back():
        return [send(red.at[core], red.at[core], s_back, 0, (b + 1 - 2 * core, z))]

    def start(copies):
        for copy in copies:
            copy.start()

    def wait(copies):
        for copy in copies:
            copy.wait()

    def first():
        start(plane())

    def third():
        wait(plane())
        total = src[own, :]
        for step in range(1, chips):
            total = total + plane_in[step - 1]
        mine[...] = total
        start(scatter())

    def fourth():
        wait(scatter())
        total = mine[mine_at, :]
        for step in range(1, depths):
            total = total + depth_in[step - 1]
        piece[...] = total
        joined[mine_at, :] = total
        start(spread())

    def fifth():
        wait(spread())
        red[core, own] = joined[...]
        start(gather())

    def sixth():
        wait(gather())
        start(back())

    def last():
        wait(back())

    return [first, third, fourth, fifth, sixth, last]


def forward_kernel(layer_no, groups, steps, *refs):
    inter = layer_no % 2 == 1
    (x_ref, flat_ref,
     next_ref, normed_ref, scale_ref, h_ref, coef_ref,
     wi4, wr2, wrl, pj, proj_s, bias_s, gin_a, gin_b, h_a, h_b, c_s, part_ref, peer_ref, sems) = refs
    turn_no = pl.program_id(0)
    last_turn = pl.num_programs(0) - 1
    turn = per_turn(inter)
    chunks = turn * pl.num_programs(0)
    length = chunks * steps
    dir_no = lax.rem(lax.axis_index("batch"), 2)
    rows = 2 * HALF_PAD if inter else groups
    valid = HOP * groups

    def before(chunk_no, gin):
        chunk_no = lax.rem(chunk_no, chunks)
        positions = times(dir_no, chunk_no, length, steps)
        sides = []

        def prepare():
            xs = gather(x_ref, inter, groups, positions)
            for half in [0, 1] if inter else [lax.div(positions[0], HOP)]:
                sides.append(narrow(xs, half))

        def gate(q):
            cut = slice(q * UNITS, (q + 1) * UNITS)
            for side, rows_of in enumerate(sides):
                found = dot(rows_of, wi4[:, cut]) + bias_s[0:1, cut]
                if inter:
                    for u in range(steps):
                        at = u * rows + side * HALF_PAD
                        gin[at:at + HALF_PAD, cut] = found[u * HALF_PAD:(u + 1) * HALF_PAD]
                else:
                    gin[:, cut] = found

        return [prepare] + [functools.partial(gate, q) for q in range(4)]

    def after(chunk_no, hs):
        chunk_no = lax.rem(chunk_no + chunks, chunks)
        positions = times(dir_no, chunk_no, length, steps)

        def project():
            found = [dot_sides(part, pj[...]) for part in to_sides(inter, steps, hs[...])]
            low_lanes = lax.broadcasted_iota(jnp.int32, found[0].shape, 1) < FILTERS
            if inter:
                found = jnp.where(low_lanes, found[0], found[1])
                for u in range(steps):
                    part_ref[stream_rows(inter, groups, positions[u]), :] = found[u * HALF_PAD:(u + 1) * HALF_PAD]
            else:
                half = lax.div(positions[0], HOP)
                found = jnp.where(low_lanes == (half == 0), found[0], 0.0)
                for u in range(steps):
                    here = stream_rows(inter, groups, positions[u])
                    part_ref[here, :] = part_ref[here, :] + found[u * groups:(u + 1) * groups]

        return [project]

    def walk(gin, hs, h, c, sub, beside):
        for u in range(steps):
            hi, lo = split(h)
            z = dot(jnp.concatenate([hi, lo], 1), wr2[...]) + dot(hi, wrl[...])
            for task in share_of(beside, u, steps):
                task()
            z = z + gin[u * rows:(u + 1) * rows]
            th = jnp.tanh(z)
            ti, tf, g, to = (th[:, q * UNITS:(q + 1) * UNITS] for q in range(4))
            i_g = 0.5 * ti + 0.5
            f_g = 0.5 * tf + 0.5
            o_g = 0.5 * to + 0.5
            c_prev = c
            c = f_g * c + i_g * g
            tc = jnp.tanh(c)
            h = o_g * tc
            at = sub * steps + u
            hs[u * rows:(u + 1) * rows] = h
            h_ref[at] = h
            coef_ref[at, 0] = tc * (0.25 - 0.25 * to * to)
            coef_ref[at, 1] = o_g * (1.0 - tc * tc)
            coef_ref[at, 2] = g * (0.25 - 0.25 * ti * ti)
            coef_ref[at, 3] = c_prev * (0.25 - 0.25 * tf * tf)
            coef_ref[at, 4] = i_g * (1.0 - g * g)
            coef_ref[at, 5] = f_g
        return h, c

    @pl.when(turn_no == 0)
    def _():
        device, barrier = greet_sibling()
        pl.semaphore_signal(barrier, inc=1, device_id=device, device_id_type=pl.DeviceIdType.MESH)
        part_ref[...] = jnp.zeros_like(part_ref)
        column = lax.broadcasted_iota(jnp.int32, (1, GATES), 1)
        scaling = jnp.where((column >= 2 * UNITS) & (column < 3 * UNITS), 1.0, 0.5)
        _, base, odd = window(layer_no)
        win, wrec, bias, proj = load_weights(flat_ref, base, odd, dir_no, proj_s)
        wi4[...] = narrow_weights(win * scaling)
        put_split(wrec * scaling, wr2, wrl)
        bias_s[...] = jnp.broadcast_to(bias * scaling, bias_s.shape)
        pj[...] = side_weights(proj)
        c_s[...] = jnp.zeros_like(c_s)
        h_b[...] = jnp.zeros_like(h_b)
        for task in before(0, gin_a):
            task()

    h, c = h_b[(steps - 1) * rows:], c_s[...]
    for n in range(turn):
        (gin, hs), (next_gin, past_hs) = ((gin_a, h_a), (gin_b, h_b))[::1 - 2 * (n % 2)]
        number = turn * turn_no + n
        h, c = walk(gin, hs, h, c, n, after(number - 1, past_hs) + before(number + 1, next_gin))
    c_s[...] = c

    @pl.when(turn_no == last_turn)
    def _():
        for task in after(chunks - 1, h_b):
            task()
        swap_with_sibling(part_ref, peer_ref, sems).wait()
        _, base, odd = window(layer_no)
        norm_stage(x_ref, part_ref, peer_ref, flat_ref, base, odd, valid, normed_ref, scale_ref, next_ref)


def backward_kernel(layer_no, groups, steps, chips, depths, *refs):
    inter = layer_no % 2 == 1
    last_layer = layer_no == 2 * BLOCKS - 1
    g_ref, normed_ref, scale_ref, x_hbm, h_hbm, coef_ref, flat_ref, *rest = refs
    if last_layer:
        hg_ref, *rest = rest
    if layer_no == 0:
        column_ref, denc_ref, encoder_ref, loss_ref, *rest = rest
    if not last_layer:
        upper_ref, *rest = rest
    if layer_no:
        below_ref, *rest = rest
    if not last_layer:
        red_ref, *rest = rest
    (grad_ref,
     wi4, wrw, wrt, pj, proj_s, dmx, dh_a, dh_b, dz_a, dz_b, dc_s, awin, aproj, abias,
     dx_ref, peer_ref, sems, x_ref, h_ref, kept_sem, *rest) = rest
    stages = [] if last_layer else reducer(upper_ref, chips, depths, rest)
    turn_no = pl.program_id(0)
    last_turn = pl.num_programs(0) - 1
    chunks = 2 * pl.num_programs(0)
    length = chunks * steps
    dir_no = lax.rem(lax.axis_index("batch"), 2)
    rows = 2 * HALF_PAD if inter else groups
    valid = HOP * groups

    def before(back_no, dhc):
        chunk_no = chunks - 1 - lax.rem(back_no, chunks)
        positions = times(dir_no, chunk_no, length, steps)

        def outward():
            dms = gather(dmx, inter, groups, positions)
            for side, half in enumerate([0, 1] if inter else [lax.div(positions[0], HOP)]):
                found = dot(narrow(dms, half), pj[...])
                if inter:
                    for u in range(steps):
                        at = u * rows + side * HALF_PAD
                        dhc[at:at + HALF_PAD] = found[u * HALF_PAD:(u + 1) * HALF_PAD]
                else:
                    dhc[...] = found

        return [outward]

    def after(back_no, dzs):
        used = back_no >= 0
        chunk_no = chunks - 1 - lax.rem(back_no + chunks, chunks)
        positions = times(dir_no, chunk_no, length, steps)
        half = 0 if inter else lax.div(positions[0], HOP)
        at = chunk_no * steps
        count = UNITS + FILTERS
        ready = []

        def prepare():
            xs = gather(x_ref, inter, groups, positions)
            hs = h_ref[pl.ds(at, steps)].reshape(steps * rows, UNITS)
            early = h_ref[lax.rem(at + length - 1, length)] * jnp.where(at == 0, 0.0, 1.0)
            hp = jnp.concatenate([early, hs[:(steps - 1) * rows]], 0)
            if inter:
                lhs = [
                    jnp.concatenate([hp_side, (xs if side == 0 else pltpu.roll(xs, FILTERS, 1))[:, :FILTERS]], 1)
                    for side, hp_side in enumerate(to_sides(inter, steps, hp))
                ]
                lhs = jnp.concatenate(lhs, 0)
            else:
                turned = jnp.where(half == 0, xs, pltpu.roll(xs, FILTERS, 1))
                lhs = jnp.concatenate([hp, turned[:, :FILTERS]], 1)
            lhs_hi, lhs_lo = split(lhs.T)
            ready.extend([lhs_hi, jnp.concatenate([lhs_hi, lhs_lo], 0)])

        def gate(q):
            cut = slice(q * UNITS, (q + 1) * UNITS)
            dz = dzs[:, cut]
            abias[0:1, cut] += jnp.sum(dz, 0, keepdims=True)
            if inter:
                dz = jnp.concatenate(to_sides(inter, steps, dz), 0)
            dz_hi, dz_lo = split(dz)
            both = dot(ready[1], dz_hi)
            awin[:, cut] += both[:count] + both[count:] + dot(ready[0], dz_lo)

        def project():
            hs = h_ref[pl.ds(at, steps)].reshape(steps * rows, UNITS)
            dms = gather(dmx, inter, groups, positions) * jnp.where(used, 1.0, 0.0)
            if inter:
                aproj[...] += dot_rows3(jnp.concatenate(to_sides(inter, steps, hs), 1), dms)
            else:
                turned = jnp.where(half == 0, dms, pltpu.roll(dms, FILTERS, 1))
                aproj[...] += dot_rows3(hs, turned)

        def inward():
            found = [dot_sides(part, wi4[...]) for part in to_sides(inter, steps, dzs[...])]
            low_lanes = lax.broadcasted_iota(jnp.int32, found[0].shape, 1) < FILTERS
            if inter:
                found = jnp.where(low_lanes, found[0], found[1])
                for u in range(steps):
                    dx_ref[stream_rows(inter, groups, positions[u]), :] = found[u * HALF_PAD:(u + 1) * HALF_PAD]
            else:
                found = jnp.where(low_lanes == (half == 0), found[0], 0.0)
                for u in range(steps):
                    here = stream_rows(inter, groups, positions[u])
                    dx_ref[here, :] = dx_ref[here, :] + found[u * groups:(u + 1) * groups]

        return [inward, project, prepare] + [functools.partial(gate, q) for q in range(4)]

    def walk(dhc, dzs, dz, dc_next, sub, beside):
        for u in reversed(range(steps)):
            at = sub * steps + u
            hi, lo = split(dz)
            if inter:
                wide = dot(hi, wrw[...])
                dh = wide[:, :UNITS] + wide[:, UNITS:] + dot(lo, wrt[...])
            else:
                wide = dot(jnp.concatenate([hi, lo], 0), wrw[...])
                dh = wide[:rows, :UNITS] + wide[:rows, UNITS:] + wide[rows:, :UNITS]
            for task in share_of(beside, steps - 1 - u, steps):
                task()
            dh = dh + dhc[u * rows:(u + 1) * rows]
            dc = dh * coef_ref[at, 1] + dc_next
            dz = jnp.concatenate(
                [dc * coef_ref[at, 2], dc * coef_ref[at, 3], dc * coef_ref[at, 4], dh * coef_ref[at, 0]], 1
            )
            dc_next = dc * coef_ref[at, 5]
            dzs[u * rows:(u + 1) * rows] = dz
        return dz, dc_next

    @pl.when(turn_no == 0)
    def _():
        kept = [
            pltpu.make_async_copy(src, dst, kept_sem.at[n])
            for n, (src, dst) in enumerate(((x_hbm, x_ref), (h_hbm, h_ref)))
        ]
        for copy in kept:
            copy.start()
        if last_layer:
            device, barrier = greet_sibling()
            pl.semaphore_signal(barrier, inc=1, device_id=device, device_id_type=pl.DeviceIdType.MESH)
        else:
            barrier, count = greet_all(chips, depths)
            pl.semaphore_wait(barrier, count)
            stages[0]()
        dx_ref[...] = jnp.zeros_like(dx_ref)
        _, base, odd = window(layer_no)
        win, wrec, _, proj = load_weights(flat_ref, base, odd, dir_no, proj_s)
        wi4[...] = side_weights(win.T)
        hi, lo = split(wrec.T)
        wrw[...] = jnp.concatenate([hi, lo], 1)
        wrt[...] = hi
        pj[...] = narrow_weights(proj.T)
        dz_b[...] = jnp.zeros_like(dz_b)
        dc_s[...] = jnp.zeros_like(dc_s)
        awin[...] = jnp.zeros_like(awin)
        aproj[...] = jnp.zeros_like(aproj)
        abias[...] = jnp.zeros_like(abias)
        grad_ref[...] = jnp.zeros_like(grad_ref)
        g = g_ref[:valid]
        normed = normed_ref[:valid]
        _, gain, _ = load_vec(flat_ref, base, odd)
        g_n = g * gain
        total = 2.0 * valid * FILTERS
        mean_one = jnp.sum(g_n) / total
        mean_two = jnp.sum(g_n * normed) / total
        dmixed = scale_ref[0:1] * (g_n - mean_one - normed * mean_two)
        dmx[:valid] = dmixed
        dmx[valid:] = jnp.zeros((dmx.shape[0] - valid, 128), F32)
        lead = jnp.where(dir_no == 0, 1.0, 0.0)

        def fold(array):
            found = lead * jnp.sum(array, 0, keepdims=True)
            return found[:, :FILTERS] + found[:, FILTERS:]

        grad_ref[OWN_VEC:OWN_VEC + 1] = jnp.concatenate([fold(dmixed), fold(g * normed)], 1)
        grad_ref[OWN_VEC + 1:OWN_VEC + 2] = jnp.concatenate([fold(g), jnp.zeros((1, FILTERS), F32)], 1)
        if last_layer:
            grad_ref[OWN_EXTRA:OWN_EXTRA + HEAD_ROWS] = hg_ref[...] * lead

        for task in before(0, dh_a):
            task()
        for copy in kept:
            copy.wait()

    for stage, at in zip(stages[1:], (2, 3, 4, None) if inter else (3, 5, 6, 9)):
        if at is not None:
            pl.when(turn_no == at)(stage)

    dz, dc_next = dz_b[:rows], dc_s[...]
    dz, dc_next = walk(dh_a, dz_a, dz, dc_next, 1, after(2 * turn_no - 1, dz_b) + before(2 * turn_no + 1, dh_b))
    dz, dc_next = walk(dh_b, dz_b, dz, dc_next, 0, after(2 * turn_no, dz_a) + before(2 * turn_no + 2, dh_a))
    dc_s[...] = dc_next

    @pl.when(turn_no == last_turn)
    def _():
        for task in after(chunks - 1, dz_b):
            task()
        if layer_no:
            swap = swap_with_sibling(dx_ref, peer_ref, sems, not last_layer)
        for stage in stages[4:] if inter else stages[5:]:
            stage()
        if not last_layer:
            red_ref[...] = rest[0][...]
        if layer_no:
            swap.wait()
            below_ref[:valid] = g_ref[:valid] + dx_ref[:valid] + peer_ref[:valid]
            below_ref[valid:] = jnp.zeros((below_ref.shape[0] - valid, 128), F32)
        for q in range(4):
            cut = slice(q * UNITS, (q + 1) * UNITS)
            grad_ref[pl.ds(q, FILTERS, stride=4), :] = awin[UNITS:, cut]
            grad_ref[pl.ds(256 + q, UNITS, stride=4), :] = awin[:UNITS, cut]
            grad_ref[768 + q:769 + q, :] = abias[0:1, cut]
        proj_s[...] = aproj[:UNITS] + pltpu.roll(aproj[UNITS:], FILTERS, 1) if inter else aproj[...]
        even = proj_s[pl.ds(0, 64, stride=2), :]
        odd_rows = proj_s[pl.ds(1, 64, stride=2), :]
        grad_ref[OWN_PROJ:OWN_VEC, :] = jnp.concatenate(
            [even[:, :FILTERS], odd_rows[:, :FILTERS]], 1
        )
        if layer_no == 0:
            lead = jnp.where(dir_no == 0, 1.0, 0.0)
            streams = lead * g_ref[:valid] + dx_ref[:valid]
            column = column_ref[...]
            mix, following = column[:, MIX_LANE:MIX_LANE + 1], column[:, NEXT_LANE:NEXT_LANE + 1]
            raw = mix * encoder_ref[0:1, :FILTERS] + following * encoder_ref[1:2, :FILTERS]
            group_at = lax.broadcasted_iota(jnp.int32, (valid, FILTERS), 0) % groups
            shifted = jnp.where(group_at == 0, 0.0, pltpu.roll(pltpu.roll(streams, FILTERS, 1), 1, 0)[:, :FILTERS])
            grad_raw = (streams[:, :FILTERS] + shifted + lead * denc_ref[...]) * jax.nn.sigmoid(raw)
            grad_ref[OWN_EXTRA:OWN_EXTRA + 1] = jnp.concatenate(
                [jnp.sum(grad_raw * mix, 0, keepdims=True), jnp.sum(grad_raw * following, 0, keepdims=True)], 1
            )
            grad_ref[OWN_EXTRA + 1:OWN_EXTRA + 2] = loss_ref[0:1] * lead


def head_kernel(groups, sep, stream_ref, column_ref, active_ref, note_ref, tail_s,
                g_ref, hg_ref, denc_ref, loss_ref,
                sig_s, now_s, before_s, slope_s, mk2, mkl, mt2, mtl, dk2, dkl, dt2, dtl, amask, adec, m_low, m_top):
    valid = HOP * groups
    block = 10 * groups
    first, second, third = (tail_s[pl.ds(6695 - TAIL_ROW + n, 32, stride=3), :] for n in range(3))
    m_low[pl.ds(0, 32, stride=2), :] = first
    m_low[pl.ds(1, 32, stride=2), :] = jnp.concatenate([second[:, FILTERS:], third[:, :FILTERS]], 1)
    m_top[pl.ds(0, 32, stride=2), :] = second
    m_top[pl.ds(1, 32, stride=2), :] = pltpu.roll(third, FILTERS, 1)
    masker = jnp.concatenate([m_low[...], m_top[:, :FILTERS]], 1)
    taps = tail_s[6791 - TAIL_ROW:6792 - TAIL_ROW]
    lane_at = lax.broadcasted_iota(jnp.int32, (FILTERS, 128), 1)
    row_at = lax.broadcasted_iota(jnp.int32, (FILTERS, 128), 0)
    upright = [
        jnp.sum(jnp.where(lane_at == 2 * row_at + tap, taps, 0.0), 1, keepdims=True) for tap in range(2)
    ]
    decoder = jnp.concatenate(
        [
            jnp.concatenate([jnp.where(lane_at == j, column, 0.0) for column in upright], 1)
            for j in range(SOURCES)
        ],
        0,
    )
    put_split(masker, mk2, mkl)
    put_split(masker.T, mt2, mtl)
    put_split(decoder, dk2, dkl)
    put_split(decoder.T, dt2, dtl)
    amask[...] = jnp.zeros_like(amask)
    adec[...] = jnp.zeros_like(adec)
    active = active_ref[0:1]

    def rows(n):
        return pl.ds(pl.multiple_of(n * block, 8), block)

    def summed_of(n):
        here = sep[rows(n), :]
        group_at = lax.broadcasted_iota(jnp.int32, (block, FILTERS), 0) % groups
        shifted = pltpu.roll(pltpu.roll(here, FILTERS, 1), 1, 0)[:, :FILTERS]
        return here[:, :FILTERS] + jnp.where(group_at == 0, 0.0, shifted)

    def frames_of(n):
        encoded = stream_ref[rows(n), :][:, :FILTERS]
        return jnp.concatenate([encoded, encoded, encoded], 1)

    def ahead(n, carry):
        logits = dot3(summed_of(n), mk2[...], mkl[...])
        sig = jax.nn.sigmoid(logits)
        sig_s[rows(n), :] = sig
        both = dot3(sig * active * frames_of(n), dk2[...], dkl[...])
        now_s[rows(n), :] = both[:, :128]
        before_s[pl.ds(pl.multiple_of(n * block + groups, 8), block), :] = both[:, 128:]
        return carry

    lax.fori_loop(0, HOP // 10, ahead, 0)
    at = lax.broadcasted_iota(jnp.int32, (groups, 128), 0)
    before_s[:groups] = jnp.where(at == 0, 0.0, pltpu.roll(before_s[valid:], 1, 0))

    def losses(n, total):
        column = column_ref[rows(n), :]
        lane = lax.broadcasted_iota(jnp.int32, (block, 128), 1)
        active_lane = (lane < SOURCES) & (lane.astype(F32) < active_ref[1:2, :128])
        target = jnp.where(active_lane, column, 0.0)
        row = lax.broadcasted_iota(jnp.int32, (block, 128), 0)
        frame = HOP * (row % groups) + row // groups + 10 * n
        kept = jnp.where(frame.astype(F32) < active_ref[2:3, :128], active_ref[3:4, :128], 0.0)
        differ = now_s[rows(n), :] + before_s[rows(n), :] - target
        root = jnp.sqrt(differ * differ + 1.0)
        slope_s[rows(n), :] = kept * differ / root
        return total + jnp.sum(kept * (root - 1.0), 0, keepdims=True)

    total = lax.fori_loop(0, HOP // 10, losses, jnp.zeros((1, 128), F32))
    first_lane = lax.broadcasted_iota(jnp.int32, (8, 128), 1) == 0
    loss_ref[...] = jnp.where(first_lane, jnp.sum(total, 1, keepdims=True), note_ref[...])
    slope_s[valid:] = jnp.where(at == groups - 1, 0.0, pltpu.roll(slope_s[:groups], groups - 1, 0))

    def back(n, carry):
        slopes = jnp.concatenate(
            [slope_s[rows(n), :], slope_s[pl.ds(pl.multiple_of(n * block + groups, 8), block), :]], 1
        )
        sig = sig_s[rows(n), :]
        frames = frames_of(n)
        dmasked = dot3(slopes, dt2[...], dtl[...]) * active
        by_sig = dmasked * sig
        denc_ref[rows(n), :] = (
            by_sig[:, :FILTERS] + by_sig[:, FILTERS:2 * FILTERS] + by_sig[:, 2 * FILTERS:]
        )
        dlogits = by_sig * frames * (1.0 - sig)
        dsummed = dot3(dlogits, mt2[...], mtl[...])
        group_at = lax.broadcasted_iota(jnp.int32, (block, FILTERS), 0) % groups
        shifted = jnp.where(group_at == groups - 1, 0.0, pltpu.roll(dsummed, block - 1, 0))
        g_ref[rows(n), :] = jnp.concatenate([dsummed, shifted], 1)
        amask[...] += dot_rows3(summed_of(n), dlogits)
        adec[...] += dot_rows3(sig * active * frames, slopes)
        return carry

    lax.fori_loop(0, HOP // 10, back, 0)
    g_ref[valid:] = jnp.zeros((g_ref.shape[0] - valid, 128), F32)
    m_low[...] = amask[:, :128]
    m_top[...] = jnp.concatenate([amask[:, 128:], jnp.zeros((FILTERS, FILTERS), F32)], 1)
    low_even, low_odd = m_low[pl.ds(0, 32, stride=2), :], m_low[pl.ds(1, 32, stride=2), :]
    top_even, top_odd = m_top[pl.ds(0, 32, stride=2), :], m_top[pl.ds(1, 32, stride=2), :]
    hg_ref[pl.ds(0, 32, stride=3), :] = low_even
    hg_ref[pl.ds(1, 32, stride=3), :] = jnp.concatenate([top_even[:, :FILTERS], low_odd[:, :FILTERS]], 1)
    hg_ref[pl.ds(2, 32, stride=3), :] = jnp.concatenate([low_odd[:, FILTERS:], top_odd[:, :FILTERS]], 1)
    columns = []
    for tap in range(2):
        found = 0.0
        for j in range(SOURCES):
            found = found + adec[j * FILTERS:(j + 1) * FILTERS, 128 * tap + j:128 * tap + j + 1]
        columns.append(jnp.broadcast_to(found, (FILTERS, 128)))
    lane = lax.broadcasted_iota(jnp.int32, (FILTERS, 128), 1)
    hg_ref[96:HEAD_ROWS] = jnp.where(lane == 0, columns[0], jnp.where(lane == 1, columns[1], 0.0))


def assemble(flat, layers):
    lane = lax.broadcasted_iota(jnp.int32, (FILTERS, 128), 1)
    row = lax.broadcasted_iota(jnp.int32, (FILTERS, 128), 0)

    def interleave(a, b):
        return jnp.sum(jnp.where(lane == 2 * row, a, jnp.where(lane == 2 * row + 1, b, 0.0)), 0, keepdims=True)

    for layer_no, ref in enumerate(layers):
        if ref is None:
            continue
        first, inner, odd = window(layer_no)
        at = first + inner
        parts = [(ref[0, :OWN_PROJ], False), (ref[1, :OWN_PROJ], False), (ref[0, OWN_PROJ:OWN_VEC], False)]
        parts += [(ref[1, OWN_PROJ:OWN_VEC], False), (ref[0, OWN_VEC:OWN_VEC + 2], True)]
        for rows, ends in parts:
            count = rows.shape[0]
            if odd:
                turned = pltpu.roll(rows, FILTERS, 1) if count >= 8 else jnp.concatenate(
                    [rows[:, FILTERS:], rows[:, :FILTERS]], 1
                )
                wide_low = lax.broadcasted_iota(jnp.int32, (count - 1, 128), 1) < FILTERS
                flat[at:at + 1, FILTERS:] = turned[0:1, FILTERS:]
                flat[at + 1:at + count] = jnp.where(wide_low, turned[:-1], turned[1:])
                if not ends:
                    flat[at + count:at + count + 1, :FILTERS] = turned[count - 1:, :FILTERS]
            elif ends:
                flat[at:at + 1] = rows[0:1]
                flat[at + 1:at + 2, :FILTERS] = rows[1:2, :FILTERS]
            else:
                flat[at:at + count] = rows
            at += count
        if layer_no == 0:
            encoder = ref[0, OWN_EXTRA:OWN_EXTRA + 1] + ref[1, OWN_EXTRA:OWN_EXTRA + 1]
            encoder = jnp.broadcast_to(encoder, (FILTERS, 128))
            first_tap = jnp.sum(jnp.where(lane == row, encoder, 0.0), 1, keepdims=True)
            second_tap = jnp.sum(jnp.where(lane == row + FILTERS, encoder, 0.0), 1, keepdims=True)
            flat[0:1] = interleave(first_tap, second_tap)
        if layer_no == 2 * BLOCKS - 1:
            flat[6695:6791] = ref[0, OWN_EXTRA:OWN_EXTRA + 96]
            decoder = ref[0, OWN_EXTRA + 96:OWN_EXTRA + HEAD_ROWS]
            flat[6791:6792] = interleave(decoder[:, 0:1], decoder[:, 1:2])
            flat[6792:] = jnp.zeros((flat.shape[0] - 6792, 128), F32)


def finish_kernel(chips, depths, entries, own_ref, r1, r2, r3, grad_ref, note_ref, flat, b1, b2, b3, sems, *rest):
    b = lax.axis_index("batch")
    barrier, count = greet_all(chips, depths)
    pairs = ((r1, b1), (r2, b2), (r3, b3))
    fetches = [pltpu.make_async_copy(src, dst, sems.at[n]) for n, (src, dst) in enumerate(pairs)]
    for copy in fetches:
        copy.start()
    pl.semaphore_wait(barrier, count)
    stages = reducer(own_ref, chips, depths, rest)
    stages[0]()
    for copy in fetches:
        copy.wait()
    assemble(flat, (None, b1, b2, b3))
    for stage in stages[1:]:
        stage()
    r0 = rest[0]
    assemble(flat, (r0, None, None, None))
    note_ref[...] = jnp.zeros_like(note_ref)
    squares = jnp.sum(jnp.sum(flat[...] * flat[...], 0, keepdims=True), 1, keepdims=True)
    lane = lax.broadcasted_iota(jnp.int32, (1, 128), 1)
    note_ref[0:1] = jnp.where(lane == 2, squares, r0[0, OWN_EXTRA + 1:OWN_EXTRA + 2])
    rows = grad_ref.shape[0]
    row_at, lane_at = lax.div(b * entries, 128), lax.rem(b * entries, 128)
    gradient = flat[pl.ds(row_at, rows), :]
    if entries % 128:
        lane = lax.broadcasted_iota(jnp.int32, (rows, 128), 1)
        turn = lax.rem(128 - lane_at, 128)
        gradient = jnp.where(
            lane < 128 - lane_at, pltpu.roll(gradient, turn, 1), pltpu.roll(flat[pl.ds(row_at + 1, rows), :], turn, 1)
        )
    grad_ref[...] = gradient


def update_kernel(grad_ref, note_ref, p_ref, m_ref, v_ref, new_ref, half_ref, first_ref, second_ref, norm_ref, loss_ref):
    rows = grad_ref.shape[0]
    note = note_ref[0:1]
    lane = lax.broadcasted_iota(jnp.int32, (1, 128), 1)
    count = jnp.sum(jnp.where(lane == 1, note, 0.0), 1, keepdims=True)
    norm = jnp.sqrt(jnp.sum(jnp.where(lane == 2, note, 0.0), 1, keepdims=True)) / count
    norm_ref[0] = norm[0, 0]
    loss_ref[0] = note[0, 0]
    loss_ref[1] = note[0, 1]
    clipped = grad_ref[...] / count * (CLIP_AT / jnp.maximum(norm, CLIP_AT))
    new_first = BETA_ONE * m_ref[...].reshape(rows, 128) + (1.0 - BETA_ONE) * clipped
    new_second = BETA_TWO * v_ref[...].reshape(rows, 128) + (1.0 - BETA_TWO) * clipped * clipped
    step_size = (
        new_first / (1.0 - BETA_ONE**STEP) / (jnp.sqrt(new_second / (1.0 - BETA_TWO**STEP)) + ADAM_EPS)
    )
    params = p_ref[...].reshape(rows, 128)
    new_params = params - LEARN_RATE * (step_size + DECAY_RATE * params)
    new_ref[...] = new_params.reshape(new_ref.shape)
    half_ref[...] = new_params.astype(BF16).reshape(half_ref.shape)
    first_ref[...] = new_first.reshape(first_ref.shape)
    second_ref[...] = new_second.reshape(second_ref.shape)


def start_kernel(chips, depths, items, groups, gathers, p_ref, mail_ref, *refs):
    *views, refs = *refs[:5], refs[5:]
    if gathers:
        *refs, flat_ref = refs
    else:
        flat_ref = p_ref
    *refs, view_sem = refs
    (stream_ref, column_ref, active_ref, encoder_ref, note_ref,
     inbox, planes, plane_sem, pair_sem, top_sem, own_sem, mail_sem) = refs
    b = lax.axis_index("batch")
    z = lax.axis_index("frames")
    core = lax.rem(b, 2)
    chip = lax.div(b, 2)
    sibling = (b + 1 - 2 * core, z)
    entries = p_ref.shape[0]
    copies = depths // (2 * items)
    share = groups // depths
    valid = HOP * groups
    mail_rows = mail_ref.shape[0] // items
    mesh = pl.DeviceIdType.MESH

    barrier = pltpu.get_barrier_semaphore()
    for step in range(1, chips):
        pl.semaphore_signal(barrier, inc=1, device_id=(lax.rem(b + 2 * step, 2 * chips), z), device_id_type=mesh)
    for step in range(1, depths):
        pl.semaphore_signal(barrier, inc=1, device_id=(b, lax.rem(z + step, depths)), device_id_type=mesh)
    for step in range(depths):
        pl.semaphore_signal(barrier, inc=1, device_id=(sibling[0], lax.rem(z + step, depths)), device_id_type=mesh)
    pl.semaphore_wait(barrier, chips - 1 + 2 * depths - 1)

    def shard(at):
        return flat_ref.at[pl.ds(pl.multiple_of(at * entries, 128), entries)]

    def send(src, dst, sems, slot, device):
        return pltpu.make_async_remote_copy(
            src_ref=src, dst_ref=dst, send_sem=sems.at[0, slot], recv_sem=sems.at[1, slot],
            device_id=device, device_id_type=mesh,
        )

    def tail_of(at):
        return flat_ref.at[pl.ds(pl.multiple_of((at + 1) * entries - 128 * SHARE_ROWS, 128), 128 * SHARE_ROWS)]

    def forward_to_sibling(at, slot):
        for src, sems in ((tail_of(at), pair_sem), (flat_ref.at[pl.ds(pl.multiple_of(at * entries, 128), 128)], top_sem)):
            copy = send(src, src, sems, slot, sibling)
            copy.start()
            beside.append(copy)

    beside = []
    if gathers:
        by_x = b + 2 - 4 * lax.rem(chip, 2)
        by_y = b + 4 - 8 * lax.div(chip, 2)
        beyond = by_x + by_y - b
        half_rows = entries // 256

        def piece(ref, at, second):
            first_row, count = (half_rows, entries // 128 - half_rows) if second else (0, half_rows)
            return ref.at[pl.ds(pl.multiple_of(at * entries + 128 * first_row, 128), 128 * count)]

        across = [
            send(piece(p_ref, 0, second), piece(flat_ref, b, second), plane_sem, slot, (to, z))
            for slot, (second, to) in enumerate(((0, by_x), (1, by_y), (1, by_x), (0, by_y)))
        ]
        for copy in across:
            copy.start()
        own = pltpu.make_async_copy(p_ref, shard(b), own_sem)
        own.start()
        own.wait()
        forward_to_sibling(b, 0)
    letters = []
    for item in range(items):
        for other in range(2):
            for copy_no in range(copies):
                depth = (items * core + item) * copies + copy_no
                here = (core == other) & (z == depth)
                src = mail_ref.at[pl.ds(item * mail_rows, mail_rows)]
                far = pltpu.make_async_remote_copy(
                    src_ref=src, dst_ref=inbox.at[z], send_sem=mail_sem.at[1, len(letters)], recv_sem=mail_sem.at[0, z],
                    device_id=(2 * chip + other, depth), device_id_type=mesh,
                )
                near = pltpu.make_async_copy(src, inbox.at[z], mail_sem.at[0, z])

                @pl.when(here)
                def _():
                    near.start()

                @pl.when(jnp.logical_not(here))
                def _():
                    far.start()

                letters.append((here, far))
    for depth in range(depths):
        pltpu.make_async_copy(inbox.at[depth], inbox.at[depth], mail_sem.at[0, depth]).wait()
    for here, far in letters:
        @pl.when(jnp.logical_not(here))
        def _():
            far.wait_send()

    frames = jnp.concatenate([inbox[depth, :share] for depth in range(depths)], 0)
    facts = inbox[0, share:share + 1]
    speakers, length = facts[:, 0:1], facts[:, 1:2]
    whole_item = jnp.where(lax.rem(z, copies) == 0, 1.0, 0.0)
    lead = jnp.where(core == 0, whole_item, 0.0)
    lane = lax.broadcasted_iota(jnp.int32, (groups, 128), 1)
    group = lax.broadcasted_iota(jnp.int32, (groups, 128), 0)
    note_ref[...] = jnp.where(lane[:8] == 1, lead * length, 0.0)
    wide = SOURCES * FILTERS
    source = lax.broadcasted_iota(jnp.int32, (8, wide), 1) // FILTERS
    fact_at = lax.broadcasted_iota(jnp.int32, (8, wide), 0)
    active = jnp.where(source.astype(F32) < speakers, 1.0, 0.0)
    active = jnp.where(fact_at == 1, speakers, jnp.where(fact_at == 2, length, active))
    active_ref[...] = jnp.where(fact_at == 3, whole_item, active)
    end = HOP * FRAME_LANES
    tile = end // 128 * 128
    opening = jnp.where(group == groups - 1, 0.0, pltpu.roll(frames[:, :128], groups - 1, 0))
    ending = (lane >= end - tile) & (lane < end - tile + FRAME_LANES)
    planes[:, :tile] = frames[:, :tile]
    planes[:, tile:tile + 128] = jnp.where(ending, pltpu.roll(opening, end - tile, 1), frames[:, tile:tile + 128])
    planes[:, tile + 128:] = jnp.zeros((groups, planes.shape[1] - tile - 128), F32)
    for k in range(HOP):
        column_ref[k * groups:(k + 1) * groups] = planes[:, FRAME_LANES * k:FRAME_LANES * k + 128]

    if gathers:
        across[0].wait_recv()
        across.append(send(piece(flat_ref, by_x, 0), piece(flat_ref, by_x, 0), plane_sem, 4, (by_y, z)))
        across[4].start()
        across[1].wait_recv()
        across.append(send(piece(flat_ref, by_y, 1), piece(flat_ref, by_y, 1), plane_sem, 5, (by_x, z)))
        across[5].start()
        across[2].wait_recv()
        forward_to_sibling(by_x, 1)
        across[3].wait_recv()
        forward_to_sibling(by_y, 2)
        across[4].wait_recv()
        across[5].wait_recv()
        forward_to_sibling(beyond, 3)
        for copy in across:
            copy.wait_send()
        for copy in beside:
            copy.wait()

    bounds = [(window(n)[0], WINDOW) for n in range(2 * BLOCKS)] + [(TAIL_ROW, TAIL_ROWS)]
    stores = [
        pltpu.make_async_copy(flat_ref.at[pl.ds(128 * at, 128 * count)], view, view_sem.at[n])
        for n, ((at, count), view) in enumerate(zip(bounds, views))
    ]
    for store in stores:
        store.start()
    taps = flat_ref[0:128].reshape(1, 128)
    at_lane = lax.broadcasted_iota(jnp.int32, (128, 128), 1)
    at_row = lax.broadcasted_iota(jnp.int32, (128, 128), 0)
    upright = jnp.sum(jnp.where(at_lane == at_row, taps, 0.0), 1, keepdims=True)
    twice = 2 * lax.rem(at_lane, FILTERS)
    tap_rows = [jnp.sum(jnp.where(at_row == twice + tap, upright, 0.0), 0, keepdims=True) for tap in range(2)]
    encoder_ref[...] = jnp.where(at_row[:8] == 0, tap_rows[0], jnp.where(at_row[:8] == 1, tap_rows[1], 0.0))

    block = 5 * groups
    block_lane = lax.broadcasted_iota(jnp.int32, (block, 128), 1)
    last_group = lax.broadcasted_iota(jnp.int32, (block, 128), 0) % groups == groups - 1

    def encode(n, carry):
        rows = pl.ds(pl.multiple_of(n * block, 8), block)
        column = column_ref[rows, :]
        raw = column[:, MIX_LANE:MIX_LANE + 1] * tap_rows[0] + column[:, NEXT_LANE:NEXT_LANE + 1] * tap_rows[1]
        encoded = jnp.maximum(raw, 0.0) + jnp.log1p(jnp.exp(-jnp.abs(raw)))
        later = jnp.where(last_group, 0.0, pltpu.roll(encoded, block - 1, 0))
        stream_ref[rows, :] = jnp.where(block_lane < FILTERS, encoded, later)
        return carry

    lax.fori_loop(0, HOP // 5, encode, 0)
    stream_ref[valid:] = jnp.zeros((stream_ref.shape[0] - valid, 128), F32)
    for store in stores:
        store.wait()


def per_turn(inter):
    return 2 if inter else 4


def sizes(inter, groups):
    if inter:
        return groups, 2 * HALF_PAD, 4
    return 2 * HOP, groups, 5


def whole(shape):
    return pl.BlockSpec(shape, lambda j: (0,) * len(shape))


def run_start(params, mixture, sources, speakers, lengths):
    items, samples_here = mixture.shape
    depths = lax.axis_size("frames")
    chips = lax.axis_size("batch") // 2
    groups = samples_here * depths // HOP
    share = groups // depths
    valid = HOP * groups
    copies = depths // (2 * items)
    signals = jnp.concatenate([sources, mixture[:, None]], 1).transpose(0, 2, 1)
    signals = jnp.pad(signals, ((0, 0), (0, 0), (0, FRAME_LANES - 1 - SOURCES)))
    signals = signals.reshape(items, share, HOP * FRAME_LANES)
    width = -(-HOP * FRAME_LANES // 128) * 128
    facts = jnp.stack([speakers, lengths], 1).astype(F32)[:, None]
    mail_rows = -(-(share + 1) // 8) * 8
    mail = jnp.concatenate(
        [
            jnp.pad(signals, ((0, 0), (0, 0), (0, width - HOP * FRAME_LANES))),
            jnp.pad(facts, ((0, 0), (0, mail_rows - share - 1), (0, width - 2))),
        ],
        1,
    ).reshape(items * mail_rows, width)
    stream_shape = (HALF_PAD * groups, 128)
    out = [stream_shape, (valid, 128), (8, SOURCES * FILTERS), (8, 128), (8, 128)]
    out = [(WINDOW * 128,)] * (2 * BLOCKS) + [(TAIL_ROWS * 128,)] + out
    gathers = params.shape[0] % 128 == 0 and chips == 4
    whole_flat = [pltpu.VMEM((params.shape[0] * 2 * chips,), F32)] if gathers else []
    if not gathers:
        params = lax.all_gather(params, "batch", axis=0, tiled=True)
    vmem = pl.BlockSpec(memory_space=pltpu.VMEM)
    sems = pltpu.SemaphoreType.DMA
    found = pl.pallas_call(
        functools.partial(start_kernel, chips, depths, items, groups, gathers),
        in_specs=[vmem] * 2,
        out_specs=[pl.BlockSpec(memory_space=pl.ANY)] * 5 + [vmem] * 5,
        out_shape=[jax.ShapeDtypeStruct(shape, F32) for shape in out],
        scratch_shapes=[
            pltpu.VMEM((depths, mail_rows, width), F32), pltpu.VMEM((groups, width + 128), F32),
            sems((2, 6)), sems((2, chips)), sems((2, chips)), sems, sems((2, max(depths, 2 * items * copies))), sems((5,)),
        ]
        + whole_flat,
        compiler_params=pltpu.CompilerParams(
            vmem_limit_bytes=VMEM_MAX, collective_id=10, has_side_effects=True
        ),
        name="start",
    )(params, mail)
    return [a.reshape(-1, 128) for a in found[:5]], found[5:]


def run_forward(layer_no, groups, stream, flat):
    inter = layer_no % 2 == 1
    length, rows, steps = sizes(inter, groups)
    turn = per_turn(inter)
    stream_shape = (HALF_PAD * groups, 128)
    out = [
        (stream_shape, whole(stream_shape)),
        (stream_shape, whole(stream_shape)),
        ((8, 128), whole((8, 128))),
        ((length, rows, UNITS), pl.BlockSpec((turn * steps, rows, UNITS), lambda j: (j, 0, 0))),
        ((length, 6, rows, UNITS), pl.BlockSpec((turn * steps, 6, rows, UNITS), lambda j: (j, 0, 0, 0))),
    ]
    return pl.pallas_call(
        functools.partial(forward_kernel, layer_no, groups, steps),
        grid=(length // (turn * steps),),
        in_specs=[whole(stream_shape), whole((WINDOW, 128))],
        out_specs=[spec for _, spec in out],
        out_shape=[jax.ShapeDtypeStruct(shape, F32) for shape, _ in out],
        scratch_shapes=[
            pltpu.VMEM((256, GATES), BF16),
            pltpu.VMEM((256, GATES), BF16), pltpu.VMEM((128, GATES), BF16),
            pltpu.VMEM((UNITS, 128), BF16),
            pltpu.VMEM((UNITS, 128), F32),
            pltpu.VMEM((8, GATES), F32),
            pltpu.VMEM((steps * rows, GATES), F32), pltpu.VMEM((steps * rows, GATES), F32),
            pltpu.VMEM((steps * rows, UNITS), F32), pltpu.VMEM((steps * rows, UNITS), F32),
            pltpu.VMEM((rows, UNITS), F32),
            pltpu.VMEM(stream_shape, F32), pltpu.VMEM(stream_shape, F32), pltpu.SemaphoreType.DMA((2,)),
        ],
        compiler_params=pltpu.CompilerParams(
            vmem_limit_bytes=VMEM_MAX, collective_id=2 + layer_no, has_side_effects=True
        ),
        name="forward_inter" if inter else "forward_intra",
    )(stream, flat)


def run_backward(layer_no, groups, grad, kept, flat, extra):
    inter = layer_no % 2 == 1
    last_layer = layer_no == 2 * BLOCKS - 1
    length, rows, steps = sizes(inter, groups)
    stream_shape = (HALF_PAD * groups, 128)
    count = length // (2 * steps)
    depths = lax.axis_size("frames")
    chips = lax.axis_size("batch") // 2
    out = [(reduced_rows(OWN_ROWS[layer_no], chips, depths), 128)]
    scratch = []
    if not last_layer:
        upper_rows = reduced_rows(OWN_ROWS[layer_no + 1], chips, depths)
        out = [(2, upper_rows, 128)] + out
        scratch = reducer_scratch(upper_rows, chips, depths)
    if layer_no:
        out = [stream_shape] + out
    x, normed, scale, h_all, coef = kept
    return pl.pallas_call(
        functools.partial(backward_kernel, layer_no, groups, steps, chips, depths),
        grid=(count,),
        in_specs=[whole(a.shape) for a in (grad, normed, scale)]
        + [pl.BlockSpec(memory_space=pl.ANY)] * 2
        + [pl.BlockSpec((2 * steps, 6, rows, UNITS), lambda j: (count - 1 - j, 0, 0, 0)), whole((WINDOW, 128))]
        + [whole(a.shape) for a in extra],
        out_specs=[whole(shape) for shape in out],
        out_shape=[jax.ShapeDtypeStruct(shape, F32) for shape in out],
        scratch_shapes=[
            pltpu.VMEM((GATES, 128), BF16),
            pltpu.VMEM((GATES, 256), BF16), pltpu.VMEM((GATES, 128), BF16),
            pltpu.VMEM((256, UNITS), BF16),
            pltpu.VMEM((UNITS, 128), F32),
            pltpu.VMEM(stream_shape, F32),
            pltpu.VMEM((steps * rows, UNITS), F32), pltpu.VMEM((steps * rows, UNITS), F32),
            pltpu.VMEM((steps * rows, GATES), F32), pltpu.VMEM((steps * rows, GATES), F32),
            pltpu.VMEM((rows, UNITS), F32),
            pltpu.VMEM((UNITS + FILTERS, GATES), F32), pltpu.VMEM((2 * UNITS if inter else UNITS, 128), F32),
            pltpu.VMEM((8, GATES), F32),
            pltpu.VMEM(stream_shape, F32), pltpu.VMEM(stream_shape, F32), pltpu.SemaphoreType.DMA((2,)),
            pltpu.VMEM(x.shape, F32), pltpu.VMEM(h_all.shape, F32), pltpu.SemaphoreType.DMA((2,)),
        ]
        + scratch,
        compiler_params=pltpu.CompilerParams(vmem_limit_bytes=VMEM_MAX, collective_id=6 + layer_no, has_side_effects=True),
        name="backward_inter" if inter else "backward_intra",
    )(grad, normed, scale, x, h_all, coef, flat, *extra)


def run_head(groups, separated, stream, column, active, note, tail):
    valid = HOP * groups
    stream_shape = (HALF_PAD * groups, 128)
    out = [stream_shape, (HEAD_ROWS, 128), (valid, FILTERS), (8, 128)]
    wide = SOURCES * FILTERS
    operands = (separated, stream, column, active, note, tail)
    return pl.pallas_call(
        functools.partial(head_kernel, groups),
        grid=(1,),
        in_specs=[whole(a.shape) for a in operands],
        out_specs=[whole(shape) for shape in out],
        out_shape=[jax.ShapeDtypeStruct(shape, F32) for shape in out],
        scratch_shapes=[
            pltpu.VMEM((valid, wide), F32), pltpu.VMEM((valid, 128), F32),
            pltpu.VMEM((valid + groups, 128), F32), pltpu.VMEM((valid + groups, 128), F32),
            pltpu.VMEM((2 * FILTERS, wide), BF16), pltpu.VMEM((FILTERS, wide), BF16),
            pltpu.VMEM((2 * wide, FILTERS), BF16), pltpu.VMEM((wide, FILTERS), BF16),
            pltpu.VMEM((2 * wide, 256), BF16), pltpu.VMEM((wide, 256), BF16),
            pltpu.VMEM((512, wide), BF16), pltpu.VMEM((256, wide), BF16),
            pltpu.VMEM((FILTERS, wide), F32), pltpu.VMEM((wide, 256), F32),
            pltpu.VMEM((FILTERS, 128), F32), pltpu.VMEM((FILTERS, 128), F32),
        ],
        compiler_params=pltpu.CompilerParams(vmem_limit_bytes=VMEM_MAX),
        name="head",
    )(*operands)


def run_finish(layers, params, first_moment, second_moment):
    entries = params.shape[0]
    rows = -(-entries // 128)
    depths = lax.axis_size("frames")
    chips = lax.axis_size("batch") // 2
    vmem = pl.BlockSpec(memory_space=pltpu.VMEM)
    gradient, note = pl.pallas_call(
        functools.partial(finish_kernel, chips, depths, entries),
        in_specs=[vmem] + [pl.BlockSpec(memory_space=pl.ANY)] * 3,
        out_specs=[vmem] * 2,
        out_shape=[jax.ShapeDtypeStruct(shape, F32) for shape in ((rows, 128), (8, 128))],
        scratch_shapes=[pltpu.VMEM((6808, 128), F32)]
        + [pltpu.VMEM(a.shape, F32) for a in layers[1:]]
        + [pltpu.SemaphoreType.DMA((3,))]
        + reducer_scratch(layers[0].shape[0], chips, depths),
        compiler_params=pltpu.CompilerParams(
            vmem_limit_bytes=VMEM_MAX, collective_id=1, has_side_effects=True
        ),
        name="finish",
    )(*layers)
    shards = [params, first_moment, second_moment]
    shape = (entries,)
    if entries % 128:
        shape = (rows, 128)
        shards = [jnp.pad(a, (0, rows * 128 - entries)).reshape(shape) for a in shards]
    smem = pl.BlockSpec(memory_space=pltpu.SMEM)
    out = [(shape, F32), (shape, BF16), (shape, F32), (shape, F32), ((1,), F32), ((2,), F32)]
    found = pl.pallas_call(
        update_kernel,
        in_specs=[vmem] * 5,
        out_specs=[vmem] * 4 + [smem] * 2,
        out_shape=[jax.ShapeDtypeStruct(shape, dtype) for shape, dtype in out],
        compiler_params=pltpu.CompilerParams(vmem_limit_bytes=VMEM_MAX),
        name="update",
    )(gradient, note, *shards)
    return [a.reshape(-1)[:entries] for a in found[:4]] + [found[4][0], found[5]]


def local(params, first_moment, second_moment, mixture, sources, speakers, lengths):
    groups = mixture.shape[1] * lax.axis_size("frames") // HOP
    views, (stream, column, active, encoder, note) = run_start(params, mixture, sources, speakers, lengths)
    kept = []
    x = stream
    for layer_no in range(2 * BLOCKS):
        after, normed, scale, h_all, coef = run_forward(layer_no, groups, x, views[layer_no])
        kept.append((x, normed, scale, h_all, coef))
        x = after
    grad, head_grads, grad_encoded, loss = run_head(groups, x, stream, column, active, note, views[2 * BLOCKS])
    sums = [None] * (2 * BLOCKS)
    for layer_no in reversed(range(2 * BLOCKS)):
        extra = ()
        if layer_no == 2 * BLOCKS - 1:
            extra = (head_grads,)
        if layer_no == 0:
            extra = (column, grad_encoded, encoder, loss)
        if layer_no < 2 * BLOCKS - 1:
            extra = extra + (sums[layer_no + 1],)
        *found, sums[layer_no] = run_backward(layer_no, groups, grad, kept[layer_no], views[layer_no], extra)
        if layer_no < 2 * BLOCKS - 1:
            sums[layer_no + 1] = found[-1]
        if layer_no:
            grad = found[0]
    return tuple(run_finish(sums, params, first_moment, second_moment))


def solution(mesh):
    placed = (
        P("batch"),
        P("batch"),
        P("batch"),
        P("batch", "frames"),
        P("batch", None, "frames"),
        P("batch"),
        P("batch"),
    )
    return jax.shard_map(
        local,
        mesh=mesh,
        in_specs=placed,
        out_specs=(P("batch"), P("batch"), P("batch"), P("batch"), P(), P()),
        check_vma=False,
    )
```
